32 devices in a mesh: dp: 4 (over y, core), ctx: 4 (over z), tp: 2 (over x).
Axes of the slice: x: 2, y: 2, z: 4, core: 2. Of those that a mesh axis runs over, the one named last changes fastest.
Arguments:
- tokens: bfloat16 [8192, 1536], P(('dp', 'ctx')), may hold values from -6 to 6
- cotangent: bfloat16 [8192, 1536], P(('dp', 'ctx')), may hold values from -6 to 6
- lengths: int32 [4, 4], P('dp'), may hold values from 1 to 1024, as said below
- block_order: int32 [4, 8, 4], P('dp'), may hold values from 0 to 3, each once within a row
- pre_gain: bfloat16 [1536], P(('dp', 'ctx')), may hold values from 0.5 to 1.5
- query_weight: bfloat16 [1536, 1536], P(('dp', 'ctx'), 'tp'), may hold values from -0.15625 to 0.15625
- key_weight: bfloat16 [1536, 768], P(('dp', 'ctx'), 'tp'), may hold values from -0.15625 to 0.15625
- value_weight: bfloat16 [1536, 768], P(('dp', 'ctx'), 'tp'), may hold values from -0.15625 to 0.15625
- output_weight: bfloat16 [1536, 1536], P(('dp', 'ctx'), 'tp'), may hold values from -2.5 to 2.5
- mid_gain: bfloat16 [1536], P(('dp', 'ctx')), may hold values from 0.5 to 1.5
- gate_weight: bfloat16 [1536, 4096], P(('dp', 'ctx'), 'tp'), may hold values from -0.15625 to 0.15625
- up_weight: bfloat16 [1536, 4096], P(('dp', 'ctx'), 'tp'), may hold values from -0.15625 to 0.15625
- down_weight: bfloat16 [1536, 4096], P(('dp', 'ctx'), 'tp'), may hold values from -0.09375 to 0.09375
Outputs:
- result: bfloat16 [8192, 1536], P(('dp', 'ctx'))
- token_gradient: bfloat16 [8192, 1536], P(('dp', 'ctx'))
- pre_gradient: float32 [1536], P(('dp', 'ctx'))
- query_gradient: float32 [1536, 1536], P(('dp', 'ctx'), 'tp')
- key_gradient: float32 [1536, 768], P(('dp', 'ctx'), 'tp')
- value_gradient: float32 [1536, 768], P(('dp', 'ctx'), 'tp')
- output_gradient: float32 [1536, 1536], P(('dp', 'ctx'), 'tp')
- mid_gradient: float32 [1536], P(('dp', 'ctx'))
- gate_gradient: float32 [1536, 4096], P(('dp', 'ctx'), 'tp')
- up_gradient: float32 [1536, 4096], P(('dp', 'ctx'), 'tp')
- down_gradient: float32 [1536, 4096], P(('dp', 'ctx'), 'tp')
The draws below stay inside these ranges and needn't reach their ends.
Inputs may be any that keep to these rules, and one draw needn't show every extreme that they name: The lengths of a data index sum to 2048; the longest is max(1024, 1023).
All inputs are finite; a program needn't handle non-finite values.
Results may differ from the reference program's by a relative error of at most 0.019.
Values may be sent and summed in bfloat16 or wider, within the bound.
A program may use at most 192 MiB of HBM per device.

```python
import math
import jax
import jax.numpy as jnp
from jax import lax

D = 1536
HQ = 16
KV = 8
HEAD_SIZE = 96
FF = 4096
TOK_DEV = 512
BLOCK = 64
SEQ_MIN = 1024
SEQS = 4
TOKENS = 8192
N_DP = 4
N_CTX = 4


def draw_lengths(key, part):
    key = jax.random.fold_in(key, 11)
    group_rows = N_CTX * TOK_DEV
    longest_size = max(SEQ_MIN, (group_rows - SEQS + 3) // 2)
    cut_key, spot_key = jax.random.split(key, 2)
    remain = group_rows - longest_size - (SEQS - 1)
    fraction = jax.random.randint(cut_key, (N_DP, SEQS - 2), 0, 65536)
    fraction = fraction * (jnp.arange(SEQS - 2, dtype=jnp.int32)[None, :] > 0).astype(jnp.int32)
    cuts = jnp.sort(fraction * remain // 65536, axis=1)
    edges = jnp.concatenate([jnp.zeros((N_DP, 1), jnp.int32), cuts.astype(jnp.int32), jnp.full((N_DP, 1), remain, jnp.int32)], axis=1)
    others = 1 + edges[:, 1:] - edges[:, :-1]
    joined = jnp.concatenate([jnp.full((N_DP, 1), longest_size, jnp.int32), others.astype(jnp.int32)], axis=1)
    spot = jax.random.randint(spot_key, (N_DP, 1), 0, SEQS)
    index = (jnp.arange(SEQS, dtype=jnp.int32)[None, :] - spot) % SEQS
    return jnp.take_along_axis(joined, index, axis=1).astype(jnp.int32)


def strengthened(values, own_key, source, target, blocks, factor):
    def block_of(dim):
        return (jnp.arange(values.shape[dim]) // (values.shape[dim] // blocks)).reshape((-1,) + (1,) * (values.ndim - 1 - dim))

    one_side = jax.random.permutation(own_key, blocks)[block_of(target)]
    other_side = (block_of(target) + blocks // 2) % blocks
    return jnp.where((block_of(source) == one_side) | (block_of(source) == other_side), factor * values, values)


def steps_of(key, extent, cuts, least, largest):
    def one(dim, blocks):
        draws = jax.random.uniform(jax.random.fold_in(jax.random.fold_in(key, 6), dim), (blocks,), jnp.float32, least / len(cuts), largest / len(cuts))
        return jnp.repeat(jnp.exp(draws), extent[dim] // blocks).reshape((-1,) + (1,) * (len(extent) - dim - 1))

    loudness = one(*cuts[0])
    for cut in cuts[1:]:
        loudness = loudness * one(*cut)
    return loudness


def scatter_about(stream_key, extent, deviation, most, cuts=(), kind=jnp.bfloat16):
    values = jax.random.normal(stream_key, extent, jnp.float32) * deviation
    if len(cuts) > 0:
        values = steps_of(stream_key, extent, cuts, -0.22, 0.18) * values
    return jnp.clip(values, min=-most, max=most).astype(kind)


def heavy_noise(stream_key, dims, spread, most, shards, heavy, kind=jnp.bfloat16):
    values = spread * jax.random.normal(stream_key, dims, jnp.float32)
    if shards:
        values = values * steps_of(stream_key, dims, shards, -0.22, 0.18)
    return jnp.clip(strengthened(values, jax.random.fold_in(stream_key, 3), *heavy), -most, most).astype(kind)


def setup_inputs(seed: int = 0) -> dict:
    streams_of = jax.random.split(jax.random.key(seed), 14)
    return {
        "tokens": scatter_about(streams_of[0], (TOKENS, D), 1.0, 6.0, ((0, 16),)),
        "cotangent": heavy_noise(streams_of[1], (TOKENS, D), 1.0, 6.0, ((0, 16),), (0, 1, 16, 2.0)),
        "lengths": draw_lengths(jax.random.fold_in(streams_of[13], 71), 0),
        "block_order": jax.vmap(lambda own: jax.random.permutation(own, N_CTX))(jax.random.split(streams_of[3], N_DP * (TOK_DEV // BLOCK))).reshape((N_DP, TOK_DEV // BLOCK, N_CTX)).astype(jnp.int32),
        "pre_gain": jnp.clip(1.0 + 0.1 * jax.random.normal(streams_of[4], (D,), jnp.float32), 0.5, 1.5).astype(jnp.bfloat16),
        "query_weight": scatter_about(streams_of[5], (D, HQ * HEAD_SIZE), D ** -0.5, 0.15625, ((0, 16), (1, 2))),
        "key_weight": scatter_about(streams_of[6], (D, KV * HEAD_SIZE), D ** -0.5, 0.15625, ((0, 16), (1, 2))),
        "value_weight": scatter_about(streams_of[7], (D, KV * HEAD_SIZE), D ** -0.5, 0.15625, ((0, 16), (1, 2))),
        "output_weight": scatter_about(streams_of[8], (D, HQ * HEAD_SIZE), (HQ * HEAD_SIZE * 4 // SEQ_MIN) ** -0.5, 2.5, ((0, 16), (1, 2))),
        "mid_gain": jnp.clip(1.0 + 0.1 * jax.random.normal(streams_of[9], (D,), jnp.float32), 0.5, 1.5).astype(jnp.bfloat16),
        "gate_weight": scatter_about(streams_of[10], (D, FF), D ** -0.5, 0.15625, ((0, 16), (1, 2))),
        "up_weight": scatter_about(streams_of[11], (D, FF), D ** -0.5, 0.15625, ((0, 16), (1, 2))),
        "down_weight": scatter_about(streams_of[12], (D, FF), FF ** -0.5, 0.09375, ((0, 16), (1, 2))),
    }


epsilon = 1e-05
rotary_base = 100000.0
masked_score = -1e+30

@jax.custom_vjp
def lower_precision(v):
    return lax.optimization_barrier(v.astype(jnp.bfloat16)).astype(jnp.float32)

@jax.custom_vjp
def lower_backward(v):
    return v

def low_keep(v):
    return (lower_precision(v), None)

def low_pass(kept, grad):
    return (grad,)

def back_keep(v):
    return (v, None)

def back_low(kept, grad):
    return (lower_precision(grad),)
lower_precision.defvjp(low_keep, low_pass)
lower_backward.defvjp(back_keep, back_low)

def times(left, right):
    return jnp.dot(left, right, precision=lax.Precision.HIGHEST, preferred_element_type=jnp.float32)

def places(lengths, block_order, count):
    rounds = block_order.shape[0]
    within = jnp.arange(rounds * BLOCK, dtype=jnp.int32)
    owner = jnp.repeat(block_order.T, BLOCK, axis=1).astype(jnp.int32)
    stream = ((owner + (within // BLOCK)[None, :] * count) * BLOCK + (within % BLOCK)[None, :]).reshape(-1).astype(jnp.int32)
    ends = jnp.cumsum(lengths).astype(jnp.int32)
    starts = (ends - lengths).astype(jnp.int32)
    segment = lax.optimization_barrier(jnp.sum((stream[:, None] >= ends[None, :]).astype(jnp.int32), axis=1)).astype(jnp.int32)
    labels = jnp.arange(lengths.shape[0], dtype=jnp.int32)
    first = lax.optimization_barrier(jnp.sum(jnp.where(segment[:, None] == labels[None, :], starts[None, :], 0), axis=1)).astype(jnp.int32)
    return (segment, (stream - first).astype(jnp.int32))

def group_places(group_lengths, group_order):
    return places(group_lengths, group_order, N_CTX)

def angles(place):
    half = HEAD_SIZE // 2
    frequency = rotary_base ** (-(jnp.arange(half, dtype=jnp.float32) * 2.0 / HEAD_SIZE))
    turn = place.astype(jnp.float32)[:, None] * frequency[None, :]
    return (jnp.cos(turn), jnp.sin(turn))

def rotate(field, cosine, sine, sign):
    rows = field.shape[0]
    head_outputs = field.shape[1] // HEAD_SIZE
    half = HEAD_SIZE // 2
    shaped = field.reshape(rows, head_outputs, HEAD_SIZE)
    first = shaped[:, :, :half]
    second = shaped[:, :, half:]
    across = cosine[:, None, :]
    along = sign * sine[:, None, :]
    output = jnp.concatenate([first * across - second * along, second * across + first * along], axis=2)
    return output.reshape(rows, head_outputs * HEAD_SIZE)

def norm_scale(field, gain):
    return field * lax.rsqrt(lax.optimization_barrier(jnp.mean(field * field, axis=1, keepdims=True)) + epsilon) * gain

def attend_block(queries, segment, place, keys, values, key_segment, key_place):
    head_outputs = queries.reshape(queries.shape[0], KV, HQ // KV, HEAD_SIZE)
    key_split = keys.reshape(keys.shape[0], KV, HEAD_SIZE)
    value_split = values.reshape(values.shape[0], KV, HEAD_SIZE)
    attention_scores = lower_backward(jnp.einsum('nixv,wiv->ixnw', head_outputs, key_split, precision=lax.Precision.HIGHEST) * HEAD_SIZE ** (-0.5))
    allowed = (segment[:, None] == key_segment[None, :]) & (key_place[None, :] <= place[:, None])
    masked = jnp.where(allowed[None, None], attention_scores, masked_score)
    top = lax.optimization_barrier(jnp.max(masked, axis=3, keepdims=True))
    weights = jnp.exp(masked - top)
    softmax_weights = weights / lax.optimization_barrier(jnp.sum(weights, axis=3, keepdims=True))
    attended_rows = jnp.einsum('omkw,woq->komq', lower_precision(softmax_weights), value_split, precision=lax.Precision.HIGHEST)
    return attended_rows.reshape(queries.shape[0], HQ * HEAD_SIZE)

def attention(queries, keys, values, segment, place):
    group_rows = N_CTX * TOK_DEV
    query_rows = math.gcd(group_rows, 512)
    blocks = group_rows // query_rows

    def group(pieces):
        group_queries, group_keys, group_values, group_segment, group_place = pieces

        def block(parts):
            return attend_block(parts[0], parts[1], parts[2], group_keys, group_values, group_segment, group_place)
        output = lax.map(jax.checkpoint(block), (group_queries.reshape(blocks, query_rows, HQ * HEAD_SIZE), group_segment.reshape(blocks, query_rows), group_place.reshape(blocks, query_rows)))
        return output.reshape(group_rows, HQ * HEAD_SIZE)
    output = lax.map(group, (queries.reshape(N_DP, group_rows, HQ * HEAD_SIZE), keys.reshape(N_DP, group_rows, KV * HEAD_SIZE), values.reshape(N_DP, group_rows, KV * HEAD_SIZE), segment.reshape(N_DP, group_rows), place.reshape(N_DP, group_rows)))
    return output.reshape(N_DP * group_rows, HQ * HEAD_SIZE)

def layer(inputs, pre_gain, query_weight, key_weight, value_weight, output_weight, mid_gain, gate_weight, up_weight, down_weight, segment, place):
    cosine, sine = angles(place)
    normed = lower_precision(norm_scale(inputs, pre_gain))
    queries = lower_precision(rotate(lower_backward(times(normed, query_weight)), cosine, sine, 1.0))
    keys = lower_precision(rotate(lower_backward(times(normed, key_weight)), cosine, sine, 1.0))
    values = lower_precision(lower_backward(times(normed, value_weight)))
    attended_rows = lower_precision(lower_backward(attention(queries, keys, values, segment, place)))
    middle = inputs + lower_backward(times(attended_rows, output_weight.T))
    mid_normed = lower_precision(norm_scale(middle, mid_gain))
    gate = lower_backward(times(mid_normed, gate_weight))
    upward = lower_backward(times(mid_normed, up_weight))
    mixed = lower_precision(jax.nn.silu(gate) * upward)
    return middle + lower_backward(times(mixed, down_weight.T))

def reference(tokens, cotangent, lengths, block_order, pre_gain, query_weight, key_weight, value_weight, output_weight, mid_gain, gate_weight, up_weight, down_weight):
    segment, place = jax.vmap(group_places)(lengths, block_order)
    segment = segment.reshape(-1)
    place = place.reshape(-1)

    def forward(inputs, gain_one, query_full, key_full, value_full, output_full, gain_two, gate_full, up_full, down_full):
        return layer(inputs, gain_one, query_full, key_full, value_full, output_full, gain_two, gate_full, up_full, down_full, segment, place)
    result, pull = jax.vjp(forward, tokens.astype(jnp.float32), pre_gain.astype(jnp.float32), query_weight.astype(jnp.float32), key_weight.astype(jnp.float32), value_weight.astype(jnp.float32), output_weight.astype(jnp.float32), mid_gain.astype(jnp.float32), gate_weight.astype(jnp.float32), up_weight.astype(jnp.float32), down_weight.astype(jnp.float32))
    slopes = pull(cotangent.astype(jnp.float32))
    return (result.astype(jnp.bfloat16), slopes[0].astype(jnp.bfloat16), slopes[1], slopes[2], slopes[3], slopes[4], slopes[5], slopes[6], slopes[7], slopes[8], slopes[9])
```

```python
import functools
import math

import jax
import jax.numpy as jnp
from jax import lax
from jax.experimental import pallas as pl
from jax.experimental.pallas import tpu as pltpu
from jax.sharding import PartitionSpec as P

HEAD_SIZE = 96
HALF = HEAD_SIZE // 2
BLOCK = 64
SPAN = 256
TILE = 512
LANES = 128

epsilon = 1e-05
rotary_base = 100000.0
masked_score = -1e30
SCALE = HEAD_SIZE**-0.5
SCALE2 = SCALE / math.log(2.0)

f32 = jnp.float32
bf16 = jnp.bfloat16
ROWS = ("dp", "ctx")
MIB = 2**20


def dot(left, right, contract):
    return lax.dot_general(
        left, right, ((contract[:1], contract[1:]), ((), ())), preferred_element_type=f32
    )


NN, NT, TN = (1, 0), (1, 1), (0, 0)


def cost(flops, moved):
    return pl.CostEstimate(flops=int(flops), bytes_accessed=int(moved), transcendentals=0)


def params(mib):
    return pltpu.CompilerParams(vmem_limit_bytes=mib * MIB)


def whole(shape):
    return pl.BlockSpec(shape, lambda *_: (0,) * len(shape))


SCALARS = pl.BlockSpec(memory_space=pltpu.SMEM)


def angles(place):
    frequency = rotary_base ** (-(jnp.arange(HALF, dtype=f32) * 2.0 / HEAD_SIZE))
    turn = place.astype(f32)[:, None] * frequency[None, :]
    return (jnp.cos(turn), jnp.sin(turn))


def own_places(starts, order, ctx, count):
    rounds = order.shape[0]
    within = jnp.arange(rounds * BLOCK, dtype=jnp.int32)
    owner = jnp.repeat(lax.dynamic_index_in_dim(order, ctx, 1, keepdims=False), BLOCK)
    stream = (owner + (within // BLOCK) * count) * BLOCK + within % BLOCK
    first = jnp.max(jnp.where(starts[None, :] <= stream[:, None], starts[None, :], 0), axis=1)
    return stream - first


def turned(head, cosine, sine, sign):
    first, second = head[:, :HALF], head[:, HALF:]
    along = sine if sign > 0 else -sine
    return jnp.concatenate(
        [first * cosine - second * along, second * cosine + first * along], axis=1
    )


def project_kernel(x_ref, gain_ref, cos_ref, sin_ref, w_ref, q_ref, kv_ref, normed_ref):
    step = pl.program_id(0)
    tile = w_ref.shape[1]

    @pl.when(step == 0)
    def _():
        x = x_ref[...].astype(f32)
        scale = lax.rsqrt(jnp.mean(x * x, axis=1, keepdims=True) + epsilon)
        normed_ref[...] = (x * scale * gain_ref[0:1, :]).astype(bf16)

    out = dot(normed_ref[...], w_ref[...], NN)

    def rotated(ref):
        for h in range(tile // HEAD_SIZE):
            lanes = slice(h * HEAD_SIZE, (h + 1) * HEAD_SIZE)
            ref[:, lanes] = turned(out[:, lanes], cos_ref[...], sin_ref[...], 1).astype(bf16)

    @pl.when(step < 2)
    def _():
        rotated(q_ref)

    @pl.when(step == 2)
    def _():
        rotated(kv_ref)

    @pl.when(step == 3)
    def _():
        kv_ref[...] = out.astype(bf16)


def project(x, gains, cosine, sine, weights, q_cols):
    rows, width = x.shape
    tile = q_cols // 2
    return pl.pallas_call(
        project_kernel,
        grid=(4,),
        in_specs=[
            whole(x.shape),
            whole(gains.shape),
            whole(cosine.shape),
            whole(sine.shape),
            pl.BlockSpec((width, tile), lambda j: (0, j)),
        ],
        out_specs=[
            pl.BlockSpec((rows, tile), lambda j: (0, jnp.minimum(j, 1))),
            pl.BlockSpec((rows, tile), lambda j: (0, jnp.maximum(j - 2, 0))),
            whole((rows, width)),
        ],
        out_shape=[
            jax.ShapeDtypeStruct((rows, q_cols), bf16),
            jax.ShapeDtypeStruct((rows, q_cols), bf16),
            jax.ShapeDtypeStruct((rows, width), bf16),
        ],
        compiler_params=params(40),
        cost_estimate=cost(2 * rows * width * 4 * tile, 2 * width * 4 * tile),
        name="project",
    )(x, gains, cosine, sine, weights)


def gather_stream(order, ctx, pieces, k_ref, v_ref):
    count, groups = len(pieces), k_ref.shape[0]
    width = groups * HEAD_SIZE

    def fill(i, unused):
        source = pl.ds(pl.multiple_of(i * BLOCK, BLOCK), BLOCK)
        for k, piece in enumerate(pieces):
            block = i * count + order[i, lax.rem(ctx - k + count, count)]
            target = pl.ds(pl.multiple_of(block * BLOCK, BLOCK), BLOCK)
            for g in range(groups):
                lanes = slice(g * HEAD_SIZE, (g + 1) * HEAD_SIZE)
                k_ref[g, target, :] = piece[source, lanes]
                v_ref[g, target, :] = piece[
                    source, width + g * HEAD_SIZE : width + (g + 1) * HEAD_SIZE
                ]
        return unused

    lax.fori_loop(0, order.shape[0], fill, 0)


def reach(starts, first):
    low = jnp.int32(0)
    for j in range(starts.shape[0]):
        low = jnp.where(starts[j] <= first, starts[j], low)
    return low


def row_limits(starts, first, lanes):
    row = first + lax.rem(lax.broadcasted_iota(jnp.int32, (1, lanes), 1), BLOCK)
    low = jnp.zeros((1, lanes), jnp.int32)
    for j in range(starts.shape[0]):
        low = jnp.where(row >= starts[j], starts[j], low)
    return row, low


def stacked(ref, rows, group, ratio):
    return jnp.concatenate(
        [
            ref[rows, (group * ratio + h) * HEAD_SIZE : (group * ratio + h + 1) * HEAD_SIZE]
            for h in range(ratio)
        ],
        axis=0,
    )


def attend_kernel(count, order, starts, place, q_ref, *refs):
    pieces = refs[:count]
    low_ref, att_ref, sum_ref, k_ref, v_ref = refs[count:]
    groups = k_ref.shape[0]
    ratio = q_ref.shape[1] // (groups * HEAD_SIZE)
    lanes = ratio * BLOCK
    ctx = place[0]
    gather_stream(order, ctx, pieces, k_ref, v_ref)

    def one(i, unused):
        first = (i * count + order[i, ctx]) * BLOCK
        row, low = row_limits(starts, first, lanes)
        begin = reach(starts, first) // SPAN
        end = (first + BLOCK - 1) // SPAN + 1
        rows = pl.ds(pl.multiple_of(i * BLOCK, BLOCK), BLOCK)
        queries = [stacked(q_ref, rows, g, ratio) for g in range(groups)]

        def chunk(c, carry):
            keys = pl.ds(pl.multiple_of(c * SPAN, SPAN), SPAN)
            index = c * SPAN + lax.broadcasted_iota(jnp.int32, (SPAN, lanes), 0)
            allowed = (index <= row) & (index >= low)
            new = []
            for g in range(groups):
                top, total, out = carry[g]
                raw = dot(k_ref[g, keys, :], queries[g], NT) * SCALE2
                raw = jnp.where(allowed, raw, masked_score)
                new_top = jnp.maximum(top, jnp.max(raw, axis=0, keepdims=True))
                weights = jnp.where(allowed, jnp.exp2(raw - new_top), 0.0)
                back = jnp.exp2(top - new_top)
                total = total * back + jnp.sum(weights, axis=0, keepdims=True)
                out = out * back + dot(v_ref[g, keys, :], weights.astype(bf16), TN)
                new.append((new_top, total, out))
            return tuple(new)

        blank = (
            jnp.full((1, lanes), masked_score, f32),
            jnp.zeros((1, lanes), f32),
            jnp.zeros((HEAD_SIZE, lanes), f32),
        )
        result = lax.fori_loop(begin, end, chunk, (blank,) * groups)
        for g in range(groups):
            top, total, out = result[g]
            out = out / total
            att_ref[i * groups + g] = out
            sum_ref[pl.ds(i * groups + g, 1), :] = top + jnp.log2(total)
            flat = out.T.astype(bf16)
            for h in range(ratio):
                head = g * ratio + h
                low_ref[rows, head * HEAD_SIZE : (head + 1) * HEAD_SIZE] = flat[
                    h * BLOCK : (h + 1) * BLOCK
                ]
        return unused

    lax.fori_loop(0, order.shape[0], one, 0)


def attend(order, starts, place, queries, pieces):
    count, rows = len(pieces), queries.shape[0]
    groups = pieces[0].shape[1] // (2 * HEAD_SIZE)
    ratio = queries.shape[1] // (groups * HEAD_SIZE)
    rounds, lanes = order.shape[0], ratio * BLOCK
    return pl.pallas_call(
        functools.partial(attend_kernel, count),
        in_specs=[SCALARS] * 3 + [pl.BlockSpec(memory_space=pltpu.VMEM)] * (1 + count),
        out_specs=[pl.BlockSpec(memory_space=pltpu.VMEM)] * 3,
        out_shape=[
            jax.ShapeDtypeStruct(queries.shape, bf16),
            jax.ShapeDtypeStruct((rounds * groups, HEAD_SIZE, lanes), f32),
            jax.ShapeDtypeStruct((rounds * groups, lanes), f32),
        ],
        scratch_shapes=[pltpu.VMEM((groups, count * rows, HEAD_SIZE), bf16)] * 2,
        compiler_params=params(40),
        cost_estimate=cost(8e9, 1e7),
        name="attend",
    )(order, starts, place, queries, *pieces)


def attend_back_kernel(count, order, starts, place, q_ref, d_ref, att_ref, sum_ref, cos_ref, sin_ref, *refs):
    pieces = refs[:count]
    qc_ref = refs[count]
    outs = refs[count + 1 : 2 * count + 1]
    k_ref, v_ref, dk_ref, dv_ref = refs[2 * count + 1 :]
    groups = k_ref.shape[0]
    ratio = q_ref.shape[1] // (groups * HEAD_SIZE)
    lanes = ratio * BLOCK
    width = groups * HEAD_SIZE
    ctx = place[0]
    gather_stream(order, ctx, pieces, k_ref, v_ref)
    dk_ref[...] = jnp.zeros_like(dk_ref)
    dv_ref[...] = jnp.zeros_like(dv_ref)

    def one(i, unused):
        first = (i * count + order[i, ctx]) * BLOCK
        row, low = row_limits(starts, first, lanes)
        begin = reach(starts, first) // SPAN
        end = (first + BLOCK - 1) // SPAN + 1
        rows = pl.ds(pl.multiple_of(i * BLOCK, BLOCK), BLOCK)
        queries = [stacked(q_ref, rows, g, ratio) for g in range(groups)]
        slopes = [stacked(d_ref, rows, g, ratio) for g in range(groups)]
        sums, deltas = [], []
        for g in range(groups):
            sums.append(sum_ref[pl.ds(i * groups + g, 1), :])
            across = slopes[g].astype(f32).T
            deltas.append(jnp.sum(across * att_ref[i * groups + g], axis=0, keepdims=True))

        def chunk(c, carry):
            keys = pl.ds(pl.multiple_of(c * SPAN, SPAN), SPAN)
            index = c * SPAN + lax.broadcasted_iota(jnp.int32, (SPAN, lanes), 0)
            allowed = (index <= row) & (index >= low)
            new = []
            for g in range(groups):
                key, value = k_ref[g, keys, :], v_ref[g, keys, :]
                raw = dot(key, queries[g], NT) * SCALE2
                share = jnp.where(allowed, jnp.exp2(jnp.minimum(raw - sums[g], 0.0)), 0.0)
                back_share = dot(value, slopes[g], NT)
                back = (share * (back_share - deltas[g])).astype(bf16)
                dv_ref[g, keys, :] += dot(share.astype(bf16), slopes[g], NN)
                dk_ref[g, keys, :] += dot(back, queries[g], NN)
                new.append(carry[g] + dot(key, back, TN))
            return tuple(new)

        blank = jnp.zeros((HEAD_SIZE, lanes), f32)
        result = lax.fori_loop(begin, end, chunk, (blank,) * groups)
        cosine, sine = cos_ref[rows, :], sin_ref[rows, :]
        for g in range(groups):
            flat = result[g].T * SCALE
            for h in range(ratio):
                head = g * ratio + h
                qc_ref[rows, head * HEAD_SIZE : (head + 1) * HEAD_SIZE] = turned(
                    flat[h * BLOCK : (h + 1) * BLOCK], cosine, sine, -1
                ).astype(bf16)
        return unused

    lax.fori_loop(0, order.shape[0], one, 0)

    def spread(i, unused):
        target = pl.ds(pl.multiple_of(i * BLOCK, BLOCK), BLOCK)
        for k, out in enumerate(outs):
            block = i * count + order[i, lax.rem(ctx - k + count, count)]
            source = pl.ds(pl.multiple_of(block * BLOCK, BLOCK), BLOCK)
            for g in range(groups):
                out[target, g * HEAD_SIZE : (g + 1) * HEAD_SIZE] = (
                    dk_ref[g, source, :] * SCALE
                ).astype(bf16)
                out[target, width + g * HEAD_SIZE : width + (g + 1) * HEAD_SIZE] = dv_ref[
                    g, source, :
                ].astype(bf16)
        return unused

    lax.fori_loop(0, order.shape[0], spread, 0)


def attend_back(order, starts, place, queries, slopes, att, sums, cosine, sine, pieces):
    count, rows = len(pieces), queries.shape[0]
    groups = pieces[0].shape[1] // (2 * HEAD_SIZE)
    keys = (groups, count * rows, HEAD_SIZE)
    return pl.pallas_call(
        functools.partial(attend_back_kernel, count),
        in_specs=[SCALARS] * 3 + [pl.BlockSpec(memory_space=pltpu.VMEM)] * (6 + count),
        out_specs=[pl.BlockSpec(memory_space=pltpu.VMEM)] * (1 + count),
        out_shape=[jax.ShapeDtypeStruct(queries.shape, bf16)]
        + [jax.ShapeDtypeStruct(pieces[0].shape, bf16)] * count,
        scratch_shapes=[pltpu.VMEM(keys, bf16)] * 2 + [pltpu.VMEM(keys, f32)] * 2,
        compiler_params=params(56),
        cost_estimate=cost(16e9, 2e7),
        name="attend_back",
    )(order, starts, place, queries, slopes, att, sums, cosine, sine, *pieces)


def output_kernel(a_ref, w_ref, o_ref):
    o_ref[...] = dot(a_ref[...], w_ref[...], NT).astype(bf16)


def output_product(attended, weights, column, features):
    rows, inner = attended.shape
    return pl.pallas_call(
        output_kernel,
        grid=(2,),
        in_specs=[
            whole(attended.shape),
            pl.BlockSpec((features // 2, inner), lambda j: (j, column)),
        ],
        out_specs=pl.BlockSpec((rows, features // 2), lambda j: (0, j)),
        out_shape=jax.ShapeDtypeStruct((rows, features), bf16),
        compiler_params=params(40),
        cost_estimate=cost(2 * rows * inner * features, 2 * inner * features),
        name="output_product",
    )(attended, weights)


def feed_kernel(
    x_ref, mine_ref, other_ref, gain_ref, cot_ref, gate_ref, up_ref, down_ref,
    middle_ref, normed_ref, mixed_ref, bg_ref, bu_ref, back_ref, total_ref,
):
    step = pl.program_id(0)

    @pl.when(step == 0)
    def _():
        middle = (
            x_ref[...].astype(f32) + mine_ref[...].astype(f32) + other_ref[...].astype(f32)
        )
        middle_ref[...] = middle
        scale = lax.rsqrt(jnp.mean(middle * middle, axis=1, keepdims=True) + epsilon)
        normed_ref[...] = (middle * scale * gain_ref[1:2, :]).astype(bf16)

    gate = dot(normed_ref[...], gate_ref[...], NN)
    upward = dot(normed_ref[...], up_ref[...], NN)
    back_mixed = dot(cot_ref[...], down_ref[...], NN)
    sigmoid = 1.0 / (1.0 + jnp.exp(-gate))
    activated = gate * sigmoid
    mixed_ref[...] = (activated * upward).astype(bf16)
    back_gate = (back_mixed * upward * sigmoid * (1.0 + gate * (1.0 - sigmoid))).astype(bf16)
    back_up = (back_mixed * activated).astype(bf16)
    bg_ref[...] = back_gate
    bu_ref[...] = back_up
    part = dot(back_gate, gate_ref[...], NT) + dot(back_up, up_ref[...], NT)

    @pl.when(step == 0)
    def _():
        total_ref[...] = part

    @pl.when(step > 0)
    def _():
        total_ref[...] += part

    @pl.when(step == pl.num_programs(0) - 1)
    def _():
        back_ref[...] = total_ref[...].astype(bf16)


def feed_forward(x, mine, other, gains, cotangent, weights, hidden):
    rows, width = x.shape
    steps = hidden // TILE
    tile_of = lambda which: pl.BlockSpec((width, TILE), lambda j: (0, which * steps + j))
    rows_of = pl.BlockSpec((rows, TILE), lambda j: (0, j))
    full = whole((rows, width))
    return pl.pallas_call(
        feed_kernel,
        grid=(steps,),
        in_specs=[full, full, full, whole(gains.shape), full]
        + [tile_of(0), tile_of(1), tile_of(2)],
        out_specs=[full, full, rows_of, rows_of, rows_of, full],
        out_shape=[
            jax.ShapeDtypeStruct((rows, width), f32),
            jax.ShapeDtypeStruct((rows, width), bf16),
            jax.ShapeDtypeStruct((rows, hidden), bf16),
            jax.ShapeDtypeStruct((rows, hidden), bf16),
            jax.ShapeDtypeStruct((rows, hidden), bf16),
            jax.ShapeDtypeStruct((rows, width), bf16),
        ],
        scratch_shapes=[pltpu.VMEM((rows, width), f32)],
        compiler_params=params(56),
        cost_estimate=cost(10 * rows * width * hidden, 6 * width * hidden),
        name="feed_forward",
    )(x, mine, other, gains, cotangent, weights, weights, weights)


def down_kernel(mixed_ref, w_ref, o_ref):
    o_ref[...] = dot(mixed_ref[...], w_ref[...], NT).astype(bf16)


def down_product(mixed, weights, column):
    rows, hidden = mixed.shape
    width = weights.shape[0]
    return pl.pallas_call(
        down_kernel,
        grid=(3,),
        in_specs=[
            whole(mixed.shape),
            pl.BlockSpec((width // 3, hidden), lambda j: (j, column)),
        ],
        out_specs=pl.BlockSpec((rows, width // 3), lambda j: (0, j)),
        out_shape=jax.ShapeDtypeStruct((rows, width), bf16),
        compiler_params=params(40),
        cost_estimate=cost(2 * rows * width * hidden, 2 * width * hidden),
        name="down_product",
    )(mixed, weights)


def middle_kernel(cot_ref, mine_ref, other_ref, middle_ref, gain_ref, w_ref, bm_ref, bb_ref, ba_ref, grad_ref):
    middle = middle_ref[...]
    scale = lax.rsqrt(jnp.mean(middle * middle, axis=1, keepdims=True) + epsilon)
    unit = middle * scale
    back = mine_ref[...].astype(f32) + other_ref[...].astype(f32)
    grad_ref[...] = jnp.sum(back * unit, axis=0, keepdims=True)
    inner = back * gain_ref[1:2, :]
    out = cot_ref[...].astype(f32) + scale * (
        inner - unit * jnp.mean(inner * unit, axis=1, keepdims=True)
    )
    bm_ref[...] = out
    low = out.astype(bf16)
    bb_ref[...] = low
    ba_ref[...] = dot(low, w_ref[...], NN).astype(bf16)


def middle_back(cotangent, mine, other, middle, gains, weights, column, inner):
    rows, width = middle.shape
    full = whole((rows, width))
    return pl.pallas_call(
        middle_kernel,
        grid=(1,),
        in_specs=[full, full, full, full, whole(gains.shape)]
        + [pl.BlockSpec((width, inner), lambda j: (0, column))],
        out_specs=[full, full, whole((rows, inner)), whole((1, width))],
        out_shape=[
            jax.ShapeDtypeStruct((rows, width), f32),
            jax.ShapeDtypeStruct((rows, width), bf16),
            jax.ShapeDtypeStruct((rows, inner), bf16),
            jax.ShapeDtypeStruct((1, width), f32),
        ],
        compiler_params=params(56),
        cost_estimate=cost(2 * rows * width * inner, 1.5e7),
        name="middle_back",
    )(cotangent, mine, other, middle, gains, weights)


def inputs_kernel(count, x_ref, qc_ref, cos_ref, sin_ref, w_ref, *refs):
    parts = refs[:count]
    cot_ref, back_ref, grad_ref = refs[count:]
    half = qc_ref.shape[1] // 2
    cot_ref[:, : 2 * half] = qc_ref[...]
    total = parts[0][...].astype(f32)
    for part in parts[1:]:
        total += part[...].astype(f32)
    for h in range(half // HEAD_SIZE):
        lanes = slice(h * HEAD_SIZE, (h + 1) * HEAD_SIZE)
        there = slice(2 * half + h * HEAD_SIZE, 2 * half + (h + 1) * HEAD_SIZE)
        cot_ref[:, there] = turned(total[:, lanes], cos_ref[...], sin_ref[...], -1).astype(bf16)
    cot_ref[:, 3 * half :] = total[:, half:].astype(bf16)
    back = dot(cot_ref[...], w_ref[...], NT)
    back_ref[...] = back.astype(bf16)
    x = x_ref[...].astype(f32)
    unit = x * lax.rsqrt(jnp.mean(x * x, axis=1, keepdims=True) + epsilon)
    grad_ref[...] = jnp.sum(back * unit, axis=0, keepdims=True)


def inputs_back(x, qc, cosine, sine, weights, parts):
    rows, width = x.shape
    inner = 2 * qc.shape[1]
    full = whole((rows, width))
    return pl.pallas_call(
        functools.partial(inputs_kernel, len(parts)),
        grid=(1,),
        in_specs=[full, whole(qc.shape), whole(cosine.shape), whole(sine.shape)]
        + [pl.BlockSpec((width, inner), lambda j: (0, 0))]
        + [whole(parts[0].shape)] * len(parts),
        out_specs=[whole((rows, inner)), full, whole((1, width))],
        out_shape=[
            jax.ShapeDtypeStruct((rows, inner), bf16),
            jax.ShapeDtypeStruct((rows, width), bf16),
            jax.ShapeDtypeStruct((1, width), f32),
        ],
        compiler_params=params(56),
        cost_estimate=cost(2 * rows * width * inner, 1.5e7),
        name="inputs_back",
    )(x, qc, cosine, sine, weights, *parts)


def final_kernel(bm_ref, mine_ref, other_ref, x_ref, gain_ref, o_ref):
    x = x_ref[...].astype(f32)
    scale = lax.rsqrt(jnp.mean(x * x, axis=1, keepdims=True) + epsilon)
    unit = x * scale
    inner = (mine_ref[...].astype(f32) + other_ref[...].astype(f32)) * gain_ref[0:1, :]
    out = bm_ref[...] + scale * (inner - unit * jnp.mean(inner * unit, axis=1, keepdims=True))
    o_ref[...] = out.astype(bf16)


def final_back(back_middle, mine, other, x, gains):
    rows, width = x.shape
    block = pl.BlockSpec((rows // 4, width), lambda j: (j, 0))
    return pl.pallas_call(
        final_kernel,
        grid=(4,),
        in_specs=[block] * 4 + [whole(gains.shape)],
        out_specs=block,
        out_shape=jax.ShapeDtypeStruct((rows, width), bf16),
        compiler_params=params(40),
        cost_estimate=cost(1e6, 1e7),
        name="final_back",
    )(back_middle, mine, other, x, gains)


def relative(field, pairs, ctxs):
    dp, ctx = lax.axis_index("dp"), lax.axis_index("ctx")
    shaped = field.reshape((pairs, 2, ctxs, -1) + field.shape[1:])
    for axis, shift in ((0, dp // 2 + 1), (1, dp % 2 + 1), (2, ctx + 1)):
        shaped = jnp.roll(shaped, -shift, axis)
    return shaped.swapaxes(0, 1).reshape(field.shape)


def gradient_kernel(pairs, ctxs, place, a_ref, b_ref, send_ref, keep_ref):
    width = a_ref.shape[1]
    section = width // (2 * pairs)
    piece = section // ctxs
    for c, out in ((1, send_ref), (0, keep_ref)):
        for y in range(pairs):
            pair = lax.rem(place[0] + y + 1, pairs)
            core = lax.rem(place[1] + c, 2)
            lanes = pl.ds(pl.multiple_of((pair * 2 + core) * section, LANES), section)
            result = dot(a_ref[:, lanes], b_ref[...], TN).astype(bf16)
            for z in range(ctxs):
                far = lax.rem(z + ctxs - place[2] - 1 + ctxs, ctxs)
                rows = pl.ds(pl.multiple_of(y * section + far * piece, piece), piece)
                out[rows, :] = result[z * piece : (z + 1) * piece]


def gradient(a, b, pairs, ctxs):
    rows, width = a.shape
    columns = b.shape[1]
    section = width // (2 * pairs)
    if section % LANES or (section // ctxs) % 32:
        ordered = relative(dot(a, b, TN).astype(bf16), pairs, ctxs)
        return ordered[: width // 2], ordered[width // 2 :]
    dp, ctx = lax.axis_index("dp"), lax.axis_index("ctx")
    place = jnp.stack([dp // 2, dp % 2, ctx]).astype(jnp.int32)
    tile = TILE if columns % TILE == 0 else columns // 2
    block = pl.BlockSpec((width // 2, tile), lambda j: (0, j))
    return pl.pallas_call(
        functools.partial(gradient_kernel, pairs, ctxs),
        grid=(columns // tile,),
        in_specs=[SCALARS, whole(a.shape), pl.BlockSpec((rows, tile), lambda j: (0, j))],
        out_specs=[block, block],
        out_shape=[jax.ShapeDtypeStruct((width // 2, columns), bf16)] * 2,
        compiler_params=params(40),
        cost_estimate=cost(2 * rows * width * columns, 2 * width * columns),
        name="gradient",
    )(place, a, b)


def shifted(field, axis, steps, stride=1):
    count = lax.axis_size(axis)
    return lax.ppermute(
        field, axis, [(i, (i + steps * stride) % count) for i in range(count)]
    )


def other_core(field):
    return lax.ppermute(field, "dp", [(i, i ^ 1) for i in range(lax.axis_size("dp"))])


def sum_to_owner(send, keep, pairs, ctxs):
    columns = send.shape[1]
    got = other_core(send).reshape(pairs, -1, columns)
    keep = keep.reshape(pairs, -1, columns)
    total = got[-1].astype(f32) + keep[-1].astype(f32)
    for y in range(1, pairs):
        part = (got[y - 1].astype(f32) + keep[y - 1].astype(f32)).astype(bf16)
        total = total + shifted(part, "dp", y, 2).astype(f32)
    total = total.reshape(ctxs, -1, columns)
    result = total[-1]
    for z in range(1, ctxs):
        result = result + shifted(total[z - 1].astype(bf16), "ctx", z).astype(f32)
    return result


def swapped(field):
    count = lax.axis_size("tp")
    return lax.ppermute(field, "tp", [(i, count - 1 - i) for i in range(count)])


def body(
    tokens,
    cotangent,
    lengths,
    block_order,
    pre_gain,
    query_weight,
    key_weight,
    value_weight,
    output_weight,
    mid_gain,
    gate_weight,
    up_weight,
    down_weight,
):
    ctxs = lax.axis_size("ctx")
    pairs = lax.axis_size("dp") // 2
    ctx = lax.axis_index("ctx")
    order = block_order[0]
    ends = jnp.cumsum(lengths[0]).astype(jnp.int32)
    starts = ends - lengths[0]
    place = jnp.stack([ctx]).astype(jnp.int32)
    q_cols = query_weight.shape[1]
    features = tokens.shape[1]
    hidden = gate_weight.shape[1]

    gain_columns = jnp.pad(jnp.stack([pre_gain, mid_gain], axis=1), ((0, 0), (0, LANES - 2)))
    first = lax.all_gather(
        jnp.concatenate([query_weight, key_weight, value_weight, gain_columns], axis=1),
        ROWS, axis=0, tiled=True,
    )
    second = lax.all_gather(
        jnp.concatenate([gate_weight, up_weight, down_weight, output_weight], axis=1),
        ROWS, axis=0, tiled=True,
    )
    output_column = 3 * hidden // q_cols
    gains = first[:, 2 * q_cols : 2 * q_cols + 8].T.astype(f32)

    cosine, sine = angles(own_places(starts, order, ctx, ctxs))
    queries, kv, normed = project(tokens, gains, cosine, sine, first, q_cols)
    pieces = [kv] + [shifted(kv, "ctx", k) for k in range(1, ctxs)]
    attended_low, att, sums = attend(order, starts, place, queries, pieces)
    branch = output_product(attended_low, second, output_column, features)
    middle, mid_normed, mixed, back_gate, back_up, back_part = feed_forward(
        tokens, branch, swapped(branch), gains, cotangent, second, hidden
    )
    back_other = swapped(back_part)
    gate_parts = gradient(mid_normed, back_gate, pairs, ctxs)
    up_parts = gradient(mid_normed, back_up, pairs, ctxs)
    down_parts = gradient(cotangent, mixed, pairs, ctxs)
    feed = down_product(mixed, second, 2)
    result = (middle + feed.astype(f32) + swapped(feed).astype(f32)).astype(bf16)

    back_middle, back_branch, back_attended, mid_grad = middle_back(
        cotangent, back_part, back_other, middle, gains, second, output_column, q_cols
    )
    output_parts = gradient(back_branch, attended_low, pairs, ctxs)
    back = attend_back(
        order, starts, place, queries, back_attended, att, sums, cosine, sine, pieces
    )
    own_parts = [back[1]] + [shifted(back[1 + k], "ctx", -k) for k in range(1, ctxs)]
    cot, normed_part, pre_grad = inputs_back(tokens, back[0], cosine, sine, first, own_parts)
    normed_other = swapped(normed_part)
    qkv_parts = gradient(normed, cot, pairs, ctxs)
    token_gradient = final_back(back_middle, normed_part, normed_other, tokens, gains)

    tp = lax.axis_index("tp")
    mid_once = jnp.where(tp == 0, mid_grad, 0.0)
    pair = jnp.concatenate([pre_grad, mid_once], axis=0).astype(bf16)
    pair = jnp.pad(pair, ((0, 6), (0, 0))).T
    ordered = relative(pair, pairs, ctxs)
    gain_sums = sum_to_owner(ordered[: features // 2], ordered[features // 2 :], pairs, ctxs)
    gain_sums = gain_sums + swapped(gain_sums)

    gate_gradient = sum_to_owner(*gate_parts, pairs, ctxs)
    up_gradient = sum_to_owner(*up_parts, pairs, ctxs)
    down_gradient = sum_to_owner(*down_parts, pairs, ctxs)
    output_gradient = sum_to_owner(*output_parts, pairs, ctxs)
    qkv_gradient = sum_to_owner(*qkv_parts, pairs, ctxs)
    return (
        result,
        token_gradient,
        gain_sums[:, 0],
        qkv_gradient[:, :q_cols],
        qkv_gradient[:, q_cols : q_cols + q_cols // 2],
        qkv_gradient[:, q_cols + q_cols // 2 :],
        output_gradient,
        gain_sums[:, 1],
        gate_gradient,
        up_gradient,
        down_gradient,
    )


def solution(mesh):
    rows, split = P(ROWS, None), P(ROWS, "tp")
    return jax.shard_map(
        body,
        mesh=mesh,
        in_specs=(rows, rows, P("dp", None), P("dp", None, None), P(ROWS))
        + (split,) * 4
        + (P(ROWS),)
        + (split,) * 3,
        out_specs=(rows, rows, P(ROWS)) + (split,) * 4 + (P(ROWS),) + (split,) * 3,
        check_vma=False,
    )
```

```python
import functools
import math

import jax
import jax.numpy as jnp
from jax import lax
from jax.experimental import pallas as pl
from jax.experimental.pallas import tpu as pltpu
from jax.sharding import PartitionSpec as P

HEAD_SIZE = 96
HALF = HEAD_SIZE // 2
BLOCK = 64
SPAN = 256
TILE = 512
LANES = 128

epsilon = 1e-05
rotary_base = 100000.0
masked_score = -1e30
SCALE = HEAD_SIZE**-0.5
SCALE2 = SCALE / math.log(2.0)

f32 = jnp.float32
bf16 = jnp.bfloat16
ROWS = ("dp", "ctx")
MIB = 2**20


def dot(left, right, contract):
    return lax.dot_general(
        left, right, ((contract[:1], contract[1:]), ((), ())), preferred_element_type=f32
    )


NN, NT, TN = (1, 0), (1, 1), (0, 0)


def cost(flops, moved):
    return pl.CostEstimate(flops=int(flops), bytes_accessed=int(moved), transcendentals=0)


def params(mib):
    return pltpu.CompilerParams(vmem_limit_bytes=mib * MIB)


def whole(shape):
    return pl.BlockSpec(shape, lambda *_: (0,) * len(shape))


SCALARS = pl.BlockSpec(memory_space=pltpu.SMEM)


def angles(place):
    frequency = rotary_base ** (-(jnp.arange(HALF, dtype=f32) * 2.0 / HEAD_SIZE))
    turn = place.astype(f32)[:, None] * frequency[None, :]
    return (jnp.cos(turn), jnp.sin(turn))


def own_places(starts, order, ctx, count):
    rounds = order.shape[0]
    within = jnp.arange(rounds * BLOCK, dtype=jnp.int32)
    owner = jnp.repeat(lax.dynamic_index_in_dim(order, ctx, 1, keepdims=False), BLOCK)
    stream = (owner + (within // BLOCK) * count) * BLOCK + within % BLOCK
    first = jnp.max(jnp.where(starts[None, :] <= stream[:, None], starts[None, :], 0), axis=1)
    return stream - first


def turned(head, cosine, sine, sign):
    first, second = head[:, :HALF], head[:, HALF:]
    along = sine if sign > 0 else -sine
    return jnp.concatenate(
        [first * cosine - second * along, second * cosine + first * along], axis=1
    )


def project_kernel(x_ref, gain_ref, cos_ref, sin_ref, w_ref, q_ref, kv_ref, normed_ref):
    step = pl.program_id(0)
    tile = w_ref.shape[1]

    @pl.when(step == 0)
    def _():
        x = x_ref[...].astype(f32)
        scale = lax.rsqrt(jnp.mean(x * x, axis=1, keepdims=True) + epsilon)
        normed_ref[...] = (x * scale * gain_ref[0:1, :]).astype(bf16)

    out = dot(normed_ref[...], w_ref[...], NN)

    def rotated(ref):
        for h in range(tile // HEAD_SIZE):
            lanes = slice(h * HEAD_SIZE, (h + 1) * HEAD_SIZE)
            ref[:, lanes] = turned(out[:, lanes], cos_ref[...], sin_ref[...], 1).astype(bf16)

    @pl.when(step < 2)
    def _():
        rotated(q_ref)

    @pl.when(step == 2)
    def _():
        rotated(kv_ref)

    @pl.when(step == 3)
    def _():
        kv_ref[...] = out.astype(bf16)


def project(x, gains, cosine, sine, weights, q_cols):
    rows, width = x.shape
    tile = q_cols // 2
    return pl.pallas_call(
        project_kernel,
        grid=(4,),
        in_specs=[
            whole(x.shape),
            whole(gains.shape),
            whole(cosine.shape),
            whole(sine.shape),
            pl.BlockSpec((width, tile), lambda j: (0, j)),
        ],
        out_specs=[
            pl.BlockSpec((rows, tile), lambda j: (0, jnp.minimum(j, 1))),
            pl.BlockSpec((rows, tile), lambda j: (0, jnp.maximum(j - 2, 0))),
            whole((rows, width)),
        ],
        out_shape=[
            jax.ShapeDtypeStruct((rows, q_cols), bf16),
            jax.ShapeDtypeStruct((rows, q_cols), bf16),
            jax.ShapeDtypeStruct((rows, width), bf16),
        ],
        compiler_params=params(40),
        cost_estimate=cost(2 * rows * width * 4 * tile, 2 * width * 4 * tile),
        name="project",
    )(x, gains, cosine, sine, weights)


MESH = pl.DeviceIdType.MESH


def gather_project_kernel(
    shard_ref, x_ref, cos_ref, sin_ref,
    full_ref, q_ref, kv_ref, normed_ref, gain_ref,
    w_ref, z_send, z_recv, y_send, y_recv, c_send, c_recv, k_send, k_recv, local,
):
    ctxs = lax.axis_size("ctx")
    dp, ctx, tp = lax.axis_index("dp"), lax.axis_index("ctx"), lax.axis_index("tp")
    far, core = (lax.rem(dp + 2, 4), ctx, tp), (dp + 1 - 2 * lax.rem(dp, 2), ctx, tp)
    after, before = (dp, lax.rem(ctx + 1, ctxs), tp), (dp, lax.rem(ctx + ctxs - 1, ctxs), tp)
    barrier = pltpu.get_barrier_semaphore()
    for device in (after, before, far, core):
        pl.semaphore_signal(barrier, inc=1, device_id=device, device_id_type=MESH)
    pl.semaphore_wait(barrier, 4)
    piece = shard_ref.shape[0]

    def block(pair, steps):
        owner = pair * ctxs + lax.rem(ctx - steps + ctxs, ctxs)
        return w_ref.at[pl.ds(pl.multiple_of(owner * piece, piece), piece)]

    def send(source, target, device, sent, got):
        copy = pltpu.make_async_remote_copy(source, target, sent, got, device, MESH)
        copy.start()
        return copy

    copies, y_copies, c_copies, z_copies = [], [], [], []
    for s in range(ctxs):
        place = block(dp, s)
        source = place if s else shard_ref
        if s:
            z_copies[s - 1].wait_recv()
        if s < ctxs - 1:
            z_copies.append(send(source, place, after, z_send.at[s], z_recv.at[s]))
        y_copies.append(send(source, place, far, y_send.at[s], y_recv.at[s]))
        c_copies.append(send(source, place, core, c_send.at[s], c_recv.at[s]))
        if s == 0:
            own = pltpu.make_async_copy(shard_ref, place, local.at[0])
            own.start()
            x = x_ref[...].astype(f32)
            unit = x * lax.rsqrt(jnp.mean(x * x, axis=1, keepdims=True) + epsilon)
    for s in range(ctxs):
        y_copies[s].wait_recv()
        place = block(far[0], s)
        c_copies.append(send(place, place, core, c_send.at[ctxs + s], c_recv.at[ctxs + s]))
    own.wait()
    for copy in c_copies:
        copy.wait_recv()
    full = pltpu.make_async_copy(w_ref, full_ref, local.at[1])
    full.start()

    q_cols = q_ref.shape[1]
    tile = q_cols // 2
    gains = w_ref[:, 2 * q_cols : 2 * q_cols + LANES].astype(f32).T[:8]
    gain_ref[...] = gains
    normed_ref[...] = (unit * gains[0:1]).astype(bf16)

    def rotated(out, store):
        for h in range(tile // HEAD_SIZE):
            lanes = slice(h * HEAD_SIZE, (h + 1) * HEAD_SIZE)
            store(lanes, turned(out[:, lanes], cos_ref[...], sin_ref[...], 1).astype(bf16))

    def key_store(lanes, value):
        kv_ref[0, :, lanes] = value

    def product(step):
        return dot(normed_ref[...], w_ref[:, step * tile : (step + 1) * tile], NN)

    rotated(product(2), key_store)
    kv_ref[0, :, tile:] = product(3).astype(bf16)
    k_copies = [send(kv_ref.at[0], kv_ref.at[1], after, k_send.at[0], k_recv.at[0])]

    for step in range(2):

        def query_store(lanes, value):
            q_ref[:, step * tile + lanes.start : step * tile + lanes.stop] = value

        rotated(product(step), query_store)
    for s in range(1, ctxs):
        k_copies[s - 1].wait_recv()
        if s < ctxs - 1:
            k_copies.append(
                send(kv_ref.at[s], kv_ref.at[s + 1], after, k_send.at[s], k_recv.at[s])
            )
    for copy in z_copies + y_copies + c_copies + k_copies:
        copy.wait_send()
    full.wait()


def gather_project(shard, x, cosine, sine, q_cols, ctxs):
    rows, width = x.shape
    columns = shard.shape[1]
    vmem = pl.BlockSpec(memory_space=pltpu.VMEM)
    sems = lambda n: pltpu.SemaphoreType.DMA((n,))
    return pl.pallas_call(
        gather_project_kernel,
        in_specs=[vmem] * 4,
        out_specs=[pl.BlockSpec(memory_space=pl.ANY)] + [vmem] * 4,
        out_shape=[
            jax.ShapeDtypeStruct((width, columns), bf16),
            jax.ShapeDtypeStruct((rows, q_cols), bf16),
            jax.ShapeDtypeStruct((ctxs, rows, q_cols), bf16),
            jax.ShapeDtypeStruct((rows, width), bf16),
            jax.ShapeDtypeStruct((8, width), f32),
        ],
        scratch_shapes=[pltpu.VMEM((width, columns), bf16)]
        + [sems(ctxs - 1)] * 2
        + [sems(ctxs)] * 2
        + [sems(2 * ctxs)] * 2
        + [sems(ctxs - 1)] * 2
        + [sems(2)],
        compiler_params=pltpu.CompilerParams(
            vmem_limit_bytes=48 * MIB, collective_id=0, has_side_effects=True
        ),
        cost_estimate=cost(2 * rows * width * 2 * q_cols, 1e8),
        name="gather_project",
    )(shard, x, cosine, sine)


def gather_stream(order, ctx, pieces, k_ref, v_ref):
    count, groups = len(pieces), k_ref.shape[0]
    width = groups * HEAD_SIZE

    def fill(i, unused):
        source = pl.ds(pl.multiple_of(i * BLOCK, BLOCK), BLOCK)
        for k, piece in enumerate(pieces):
            block = i * count + order[i, lax.rem(ctx - k + count, count)]
            target = pl.ds(pl.multiple_of(block * BLOCK, BLOCK), BLOCK)
            for g in range(groups):
                lanes = slice(g * HEAD_SIZE, (g + 1) * HEAD_SIZE)
                k_ref[g, target, :] = piece[source, lanes]
                v_ref[g, target, :] = piece[
                    source, width + g * HEAD_SIZE : width + (g + 1) * HEAD_SIZE
                ]
        return unused

    lax.fori_loop(0, order.shape[0], fill, 0)


def reach(starts, first):
    low = jnp.int32(0)
    for j in range(starts.shape[0]):
        low = jnp.where(starts[j] <= first, starts[j], low)
    return low


def row_limits(starts, first, lanes):
    row = first + lax.rem(lax.broadcasted_iota(jnp.int32, (1, lanes), 1), BLOCK)
    low = jnp.zeros((1, lanes), jnp.int32)
    for j in range(starts.shape[0]):
        low = jnp.where(row >= starts[j], starts[j], low)
    return row, low


def stacked(ref, rows, group, ratio):
    return jnp.concatenate(
        [
            ref[rows, (group * ratio + h) * HEAD_SIZE : (group * ratio + h + 1) * HEAD_SIZE]
            for h in range(ratio)
        ],
        axis=0,
    )


def attend_kernel(count, order, starts, place, q_ref, *refs):
    pieces = refs[:count]
    low_ref, att_ref, sum_ref, k_ref, v_ref = refs[count:]
    groups = k_ref.shape[0]
    ratio = q_ref.shape[1] // (groups * HEAD_SIZE)
    lanes = ratio * BLOCK
    ctx = place[0]
    gather_stream(order, ctx, pieces, k_ref, v_ref)

    def one(i, unused):
        first = (i * count + order[i, ctx]) * BLOCK
        row, low = row_limits(starts, first, lanes)
        begin = reach(starts, first) // SPAN
        end = (first + BLOCK - 1) // SPAN + 1
        rows = pl.ds(pl.multiple_of(i * BLOCK, BLOCK), BLOCK)
        queries = [stacked(q_ref, rows, g, ratio) for g in range(groups)]

        def chunk(c, carry):
            keys = pl.ds(pl.multiple_of(c * SPAN, SPAN), SPAN)
            index = c * SPAN + lax.broadcasted_iota(jnp.int32, (SPAN, lanes), 0)
            allowed = (index <= row) & (index >= low)
            new = []
            for g in range(groups):
                top, total, out = carry[g]
                raw = dot(k_ref[g, keys, :], queries[g], NT) * SCALE2
                raw = jnp.where(allowed, raw, masked_score)
                new_top = jnp.maximum(top, jnp.max(raw, axis=0, keepdims=True))
                weights = jnp.where(allowed, jnp.exp2(raw - new_top), 0.0)
                back = jnp.exp2(top - new_top)
                total = total * back + jnp.sum(weights, axis=0, keepdims=True)
                out = out * back + dot(v_ref[g, keys, :], weights.astype(bf16), TN)
                new.append((new_top, total, out))
            return tuple(new)

        blank = (
            jnp.full((1, lanes), masked_score, f32),
            jnp.zeros((1, lanes), f32),
            jnp.zeros((HEAD_SIZE, lanes), f32),
        )
        result = lax.fori_loop(begin, end, chunk, (blank,) * groups)
        for g in range(groups):
            top, total, out = result[g]
            out = out / total
            att_ref[i * groups + g] = out
            sum_ref[pl.ds(i * groups + g, 1), :] = top + jnp.log2(total)
            flat = out.T.astype(bf16)
            for h in range(ratio):
                head = g * ratio + h
                low_ref[rows, head * HEAD_SIZE : (head + 1) * HEAD_SIZE] = flat[
                    h * BLOCK : (h + 1) * BLOCK
                ]
        return unused

    lax.fori_loop(0, order.shape[0], one, 0)


def attend(order, starts, place, queries, pieces):
    count, rows = len(pieces), queries.shape[0]
    groups = pieces[0].shape[1] // (2 * HEAD_SIZE)
    ratio = queries.shape[1] // (groups * HEAD_SIZE)
    rounds, lanes = order.shape[0], ratio * BLOCK
    return pl.pallas_call(
        functools.partial(attend_kernel, count),
        in_specs=[SCALARS] * 3 + [pl.BlockSpec(memory_space=pltpu.VMEM)] * (1 + count),
        out_specs=[pl.BlockSpec(memory_space=pltpu.VMEM)] * 3,
        out_shape=[
            jax.ShapeDtypeStruct(queries.shape, bf16),
            jax.ShapeDtypeStruct((rounds * groups, HEAD_SIZE, lanes), f32),
            jax.ShapeDtypeStruct((rounds * groups, lanes), f32),
        ],
        scratch_shapes=[pltpu.VMEM((groups, count * rows, HEAD_SIZE), bf16)] * 2,
        compiler_params=params(40),
        cost_estimate=cost(8e9, 1e7),
        name="attend",
    )(order, starts, place, queries, *pieces)


def attend_back_kernel(count, order, starts, place, q_ref, d_ref, att_ref, sum_ref, cos_ref, sin_ref, *refs):
    pieces = refs[:count]
    qc_ref = refs[count]
    outs = refs[count + 1 : 2 * count + 1]
    k_ref, v_ref, dk_ref, dv_ref = refs[2 * count + 1 :]
    groups = k_ref.shape[0]
    ratio = q_ref.shape[1] // (groups * HEAD_SIZE)
    lanes = ratio * BLOCK
    width = groups * HEAD_SIZE
    ctx = place[0]
    gather_stream(order, ctx, pieces, k_ref, v_ref)
    dk_ref[...] = jnp.zeros_like(dk_ref)
    dv_ref[...] = jnp.zeros_like(dv_ref)

    def one(i, unused):
        first = (i * count + order[i, ctx]) * BLOCK
        row, low = row_limits(starts, first, lanes)
        begin = reach(starts, first) // SPAN
        end = (first + BLOCK - 1) // SPAN + 1
        rows = pl.ds(pl.multiple_of(i * BLOCK, BLOCK), BLOCK)
        queries = [stacked(q_ref, rows, g, ratio) for g in range(groups)]
        slopes = [stacked(d_ref, rows, g, ratio) for g in range(groups)]
        sums, deltas = [], []
        for g in range(groups):
            sums.append(sum_ref[pl.ds(i * groups + g, 1), :])
            across = slopes[g].astype(f32).T
            deltas.append(jnp.sum(across * att_ref[i * groups + g], axis=0, keepdims=True))

        def chunk(c, carry):
            keys = pl.ds(pl.multiple_of(c * SPAN, SPAN), SPAN)
            index = c * SPAN + lax.broadcasted_iota(jnp.int32, (SPAN, lanes), 0)
            allowed = (index <= row) & (index >= low)
            new = []
            for g in range(groups):
                key, value = k_ref[g, keys, :], v_ref[g, keys, :]
                raw = dot(key, queries[g], NT) * SCALE2
                share = jnp.where(allowed, jnp.exp2(jnp.minimum(raw - sums[g], 0.0)), 0.0)
                back_share = dot(value, slopes[g], NT)
                back = (share * (back_share - deltas[g])).astype(bf16)
                dv_ref[g, keys, :] += dot(share.astype(bf16), slopes[g], NN)
                dk_ref[g, keys, :] += dot(back, queries[g], NN)
                new.append(carry[g] + dot(key, back, TN))
            return tuple(new)

        blank = jnp.zeros((HEAD_SIZE, lanes), f32)
        result = lax.fori_loop(begin, end, chunk, (blank,) * groups)
        cosine, sine = cos_ref[rows, :], sin_ref[rows, :]
        for g in range(groups):
            flat = result[g].T * SCALE
            for h in range(ratio):
                head = g * ratio + h
                qc_ref[rows, head * HEAD_SIZE : (head + 1) * HEAD_SIZE] = turned(
                    flat[h * BLOCK : (h + 1) * BLOCK], cosine, sine, -1
                ).astype(bf16)
        return unused

    lax.fori_loop(0, order.shape[0], one, 0)

    def spread(i, unused):
        target = pl.ds(pl.multiple_of(i * BLOCK, BLOCK), BLOCK)
        for k, out in enumerate(outs):
            block = i * count + order[i, lax.rem(ctx - k + count, count)]
            source = pl.ds(pl.multiple_of(block * BLOCK, BLOCK), BLOCK)
            for g in range(groups):
                out[target, g * HEAD_SIZE : (g + 1) * HEAD_SIZE] = (
                    dk_ref[g, source, :] * SCALE
                ).astype(bf16)
                out[target, width + g * HEAD_SIZE : width + (g + 1) * HEAD_SIZE] = dv_ref[
                    g, source, :
                ].astype(bf16)
        return unused

    lax.fori_loop(0, order.shape[0], spread, 0)


def attend_back(order, starts, place, queries, slopes, att, sums, cosine, sine, pieces):
    count, rows = len(pieces), queries.shape[0]
    groups = pieces[0].shape[1] // (2 * HEAD_SIZE)
    keys = (groups, count * rows, HEAD_SIZE)
    return pl.pallas_call(
        functools.partial(attend_back_kernel, count),
        in_specs=[SCALARS] * 3 + [pl.BlockSpec(memory_space=pltpu.VMEM)] * (6 + count),
        out_specs=[pl.BlockSpec(memory_space=pltpu.VMEM)] * (1 + count),
        out_shape=[jax.ShapeDtypeStruct(queries.shape, bf16)]
        + [jax.ShapeDtypeStruct(pieces[0].shape, bf16)] * count,
        scratch_shapes=[pltpu.VMEM(keys, bf16)] * 2 + [pltpu.VMEM(keys, f32)] * 2,
        compiler_params=params(56),
        cost_estimate=cost(16e9, 2e7),
        name="attend_back",
    )(order, starts, place, queries, slopes, att, sums, cosine, sine, *pieces)


def output_kernel(a_ref, w_ref, o_ref):
    o_ref[...] = dot(a_ref[...], w_ref[...], NT).astype(bf16)


def output_product(attended, weights, column, features):
    rows, inner = attended.shape
    return pl.pallas_call(
        output_kernel,
        grid=(2,),
        in_specs=[
            whole(attended.shape),
            pl.BlockSpec((features // 2, inner), lambda j: (j, column)),
        ],
        out_specs=pl.BlockSpec((rows, features // 2), lambda j: (0, j)),
        out_shape=jax.ShapeDtypeStruct((rows, features), bf16),
        compiler_params=params(40),
        cost_estimate=cost(2 * rows * inner * features, 2 * inner * features),
        name="output_product",
    )(attended, weights)


def feed_kernel(
    x_ref, mine_ref, other_ref, gain_ref, cot_ref, gate_ref, up_ref, down_ref,
    middle_ref, normed_ref, mixed_ref, bg_ref, bu_ref, back_ref, total_ref,
):
    step = pl.program_id(0)

    @pl.when(step == 0)
    def _():
        middle = (
            x_ref[...].astype(f32) + mine_ref[...].astype(f32) + other_ref[...].astype(f32)
        )
        middle_ref[...] = middle
        scale = lax.rsqrt(jnp.mean(middle * middle, axis=1, keepdims=True) + epsilon)
        normed_ref[...] = (middle * scale * gain_ref[1:2, :]).astype(bf16)

    gate = dot(normed_ref[...], gate_ref[...], NN)
    upward = dot(normed_ref[...], up_ref[...], NN)
    back_mixed = dot(cot_ref[...], down_ref[...], NN)
    sigmoid = 1.0 / (1.0 + jnp.exp(-gate))
    activated = gate * sigmoid
    mixed_ref[...] = (activated * upward).astype(bf16)
    back_gate = (back_mixed * upward * sigmoid * (1.0 + gate * (1.0 - sigmoid))).astype(bf16)
    back_up = (back_mixed * activated).astype(bf16)
    bg_ref[...] = back_gate
    bu_ref[...] = back_up
    part = dot(back_gate, gate_ref[...], NT) + dot(back_up, up_ref[...], NT)

    @pl.when(step == 0)
    def _():
        total_ref[...] = part

    @pl.when(step > 0)
    def _():
        total_ref[...] += part

    @pl.when(step == pl.num_programs(0) - 1)
    def _():
        back_ref[...] = total_ref[...].astype(bf16)


def feed_forward(x, mine, other, gains, cotangent, weights, hidden):
    rows, width = x.shape
    steps = hidden // TILE
    tile_of = lambda which: pl.BlockSpec((width, TILE), lambda j: (0, which * steps + j))
    rows_of = pl.BlockSpec((rows, TILE), lambda j: (0, j))
    full = whole((rows, width))
    return pl.pallas_call(
        feed_kernel,
        grid=(steps,),
        in_specs=[full, full, full, whole(gains.shape), full]
        + [tile_of(0), tile_of(1), tile_of(2)],
        out_specs=[full, full, rows_of, rows_of, rows_of, full],
        out_shape=[
            jax.ShapeDtypeStruct((rows, width), f32),
            jax.ShapeDtypeStruct((rows, width), bf16),
            jax.ShapeDtypeStruct((rows, hidden), bf16),
            jax.ShapeDtypeStruct((rows, hidden), bf16),
            jax.ShapeDtypeStruct((rows, hidden), bf16),
            jax.ShapeDtypeStruct((rows, width), bf16),
        ],
        scratch_shapes=[pltpu.VMEM((rows, width), f32)],
        compiler_params=params(56),
        cost_estimate=cost(10 * rows * width * hidden, 6 * width * hidden),
        name="feed_forward",
    )(x, mine, other, gains, cotangent, weights, weights, weights)


def down_kernel(mixed_ref, w_ref, o_ref):
    o_ref[...] = dot(mixed_ref[...], w_ref[...], NT).astype(bf16)


def down_product(mixed, weights, column):
    rows, hidden = mixed.shape
    width = weights.shape[0]
    return pl.pallas_call(
        down_kernel,
        grid=(3,),
        in_specs=[
            whole(mixed.shape),
            pl.BlockSpec((width // 3, hidden), lambda j: (j, column)),
        ],
        out_specs=pl.BlockSpec((rows, width // 3), lambda j: (0, j)),
        out_shape=jax.ShapeDtypeStruct((rows, width), bf16),
        compiler_params=params(40),
        cost_estimate=cost(2 * rows * width * hidden, 2 * width * hidden),
        name="down_product",
    )(mixed, weights)


def middle_kernel(cot_ref, mine_ref, other_ref, middle_ref, gain_ref, w_ref, bm_ref, bb_ref, ba_ref, grad_ref):
    middle = middle_ref[...]
    scale = lax.rsqrt(jnp.mean(middle * middle, axis=1, keepdims=True) + epsilon)
    unit = middle * scale
    back = mine_ref[...].astype(f32) + other_ref[...].astype(f32)
    grad_ref[...] = jnp.sum(back * unit, axis=0, keepdims=True)
    inner = back * gain_ref[1:2, :]
    out = cot_ref[...].astype(f32) + scale * (
        inner - unit * jnp.mean(inner * unit, axis=1, keepdims=True)
    )
    bm_ref[...] = out
    low = out.astype(bf16)
    bb_ref[...] = low
    ba_ref[...] = dot(low, w_ref[...], NN).astype(bf16)


def middle_back(cotangent, mine, other, middle, gains, weights, column, inner):
    rows, width = middle.shape
    full = whole((rows, width))
    return pl.pallas_call(
        middle_kernel,
        grid=(1,),
        in_specs=[full, full, full, full, whole(gains.shape)]
        + [pl.BlockSpec((width, inner), lambda j: (0, column))],
        out_specs=[full, full, whole((rows, inner)), whole((1, width))],
        out_shape=[
            jax.ShapeDtypeStruct((rows, width), f32),
            jax.ShapeDtypeStruct((rows, width), bf16),
            jax.ShapeDtypeStruct((rows, inner), bf16),
            jax.ShapeDtypeStruct((1, width), f32),
        ],
        compiler_params=params(56),
        cost_estimate=cost(2 * rows * width * inner, 1.5e7),
        name="middle_back",
    )(cotangent, mine, other, middle, gains, weights)


def inputs_kernel(count, x_ref, qc_ref, cos_ref, sin_ref, w_ref, *refs):
    parts = refs[:count]
    cot_ref, back_ref, grad_ref = refs[count:]
    half = qc_ref.shape[1] // 2
    cot_ref[:, : 2 * half] = qc_ref[...]
    total = parts[0][...].astype(f32)
    for part in parts[1:]:
        total += part[...].astype(f32)
    for h in range(half // HEAD_SIZE):
        lanes = slice(h * HEAD_SIZE, (h + 1) * HEAD_SIZE)
        there = slice(2 * half + h * HEAD_SIZE, 2 * half + (h + 1) * HEAD_SIZE)
        cot_ref[:, there] = turned(total[:, lanes], cos_ref[...], sin_ref[...], -1).astype(bf16)
    cot_ref[:, 3 * half :] = total[:, half:].astype(bf16)
    back = dot(cot_ref[...], w_ref[...], NT)
    back_ref[...] = back.astype(bf16)
    x = x_ref[...].astype(f32)
    unit = x * lax.rsqrt(jnp.mean(x * x, axis=1, keepdims=True) + epsilon)
    grad_ref[...] = jnp.sum(back * unit, axis=0, keepdims=True)


def inputs_back(x, qc, cosine, sine, weights, parts):
    rows, width = x.shape
    inner = 2 * qc.shape[1]
    full = whole((rows, width))
    return pl.pallas_call(
        functools.partial(inputs_kernel, len(parts)),
        grid=(1,),
        in_specs=[full, whole(qc.shape), whole(cosine.shape), whole(sine.shape)]
        + [pl.BlockSpec((width, inner), lambda j: (0, 0))]
        + [whole(parts[0].shape)] * len(parts),
        out_specs=[whole((rows, inner)), full, whole((1, width))],
        out_shape=[
            jax.ShapeDtypeStruct((rows, inner), bf16),
            jax.ShapeDtypeStruct((rows, width), bf16),
            jax.ShapeDtypeStruct((1, width), f32),
        ],
        compiler_params=params(56),
        cost_estimate=cost(2 * rows * width * inner, 1.5e7),
        name="inputs_back",
    )(x, qc, cosine, sine, weights, *parts)


def final_kernel(bm_ref, mine_ref, other_ref, x_ref, gain_ref, o_ref):
    x = x_ref[...].astype(f32)
    scale = lax.rsqrt(jnp.mean(x * x, axis=1, keepdims=True) + epsilon)
    unit = x * scale
    inner = (mine_ref[...].astype(f32) + other_ref[...].astype(f32)) * gain_ref[0:1, :]
    out = bm_ref[...] + scale * (inner - unit * jnp.mean(inner * unit, axis=1, keepdims=True))
    o_ref[...] = out.astype(bf16)


def final_back(back_middle, mine, other, x, gains):
    rows, width = x.shape
    block = pl.BlockSpec((rows // 4, width), lambda j: (j, 0))
    return pl.pallas_call(
        final_kernel,
        grid=(4,),
        in_specs=[block] * 4 + [whole(gains.shape)],
        out_specs=block,
        out_shape=jax.ShapeDtypeStruct((rows, width), bf16),
        compiler_params=params(40),
        cost_estimate=cost(1e6, 1e7),
        name="final_back",
    )(back_middle, mine, other, x, gains)


def relative(field, pairs, ctxs):
    dp, ctx = lax.axis_index("dp"), lax.axis_index("ctx")
    shaped = field.reshape((pairs, 2, ctxs, -1) + field.shape[1:])
    for axis, shift in ((0, dp // 2 + 1), (1, dp % 2 + 1), (2, ctx + 1)):
        shaped = jnp.roll(shaped, -shift, axis)
    return shaped.swapaxes(0, 1).reshape(field.shape)


def gradient_kernel(pairs, ctxs, place, a_ref, b_ref, send_ref, keep_ref):
    width = a_ref.shape[1]
    section = width // (2 * pairs)
    piece = section // ctxs
    for c, out in ((1, send_ref), (0, keep_ref)):
        for y in range(pairs):
            pair = lax.rem(place[0] + y + 1, pairs)
            core = lax.rem(place[1] + c, 2)
            lanes = pl.ds(pl.multiple_of((pair * 2 + core) * section, LANES), section)
            result = dot(a_ref[:, lanes], b_ref[...], TN).astype(bf16)
            for z in range(ctxs):
                far = lax.rem(z + ctxs - place[2] - 1 + ctxs, ctxs)
                rows = pl.ds(pl.multiple_of(y * section + far * piece, piece), piece)
                out[rows, :] = result[z * piece : (z + 1) * piece]


def gradient(a, b, pairs, ctxs):
    rows, width = a.shape
    columns = b.shape[1]
    section = width // (2 * pairs)
    if section % LANES or (section // ctxs) % 32:
        ordered = relative(dot(a, b, TN).astype(bf16), pairs, ctxs)
        return ordered[: width // 2], ordered[width // 2 :]
    dp, ctx = lax.axis_index("dp"), lax.axis_index("ctx")
    place = jnp.stack([dp // 2, dp % 2, ctx]).astype(jnp.int32)
    tile = TILE if columns % TILE == 0 else columns // 2
    block = pl.BlockSpec((width // 2, tile), lambda j: (0, j))
    return pl.pallas_call(
        functools.partial(gradient_kernel, pairs, ctxs),
        grid=(columns // tile,),
        in_specs=[SCALARS, whole(a.shape), pl.BlockSpec((rows, tile), lambda j: (0, j))],
        out_specs=[block, block],
        out_shape=[jax.ShapeDtypeStruct((width // 2, columns), bf16)] * 2,
        compiler_params=params(40),
        cost_estimate=cost(2 * rows * width * columns, 2 * width * columns),
        name="gradient",
    )(place, a, b)


def shifted(field, axis, steps, stride=1):
    count = lax.axis_size(axis)
    return lax.ppermute(
        field, axis, [(i, (i + steps * stride) % count) for i in range(count)]
    )


def other_core(field):
    return lax.ppermute(field, "dp", [(i, i ^ 1) for i in range(lax.axis_size("dp"))])


def sum_to_owner(send, keep, pairs, ctxs):
    columns = send.shape[1]
    got = other_core(send).reshape(pairs, -1, columns)
    keep = keep.reshape(pairs, -1, columns)
    total = got[-1].astype(f32) + keep[-1].astype(f32)
    for y in range(1, pairs):
        part = (got[y - 1].astype(f32) + keep[y - 1].astype(f32)).astype(bf16)
        total = total + shifted(part, "dp", y, 2).astype(f32)
    total = total.reshape(ctxs, -1, columns)
    result = total[-1]
    for z in range(1, ctxs):
        result = result + shifted(total[z - 1].astype(bf16), "ctx", z).astype(f32)
    return result


def swapped(field):
    count = lax.axis_size("tp")
    return lax.ppermute(field, "tp", [(i, count - 1 - i) for i in range(count)])


def body(
    tokens,
    cotangent,
    lengths,
    block_order,
    pre_gain,
    query_weight,
    key_weight,
    value_weight,
    output_weight,
    mid_gain,
    gate_weight,
    up_weight,
    down_weight,
):
    ctxs = lax.axis_size("ctx")
    pairs = lax.axis_size("dp") // 2
    ctx = lax.axis_index("ctx")
    order = block_order[0]
    ends = jnp.cumsum(lengths[0]).astype(jnp.int32)
    starts = ends - lengths[0]
    place = jnp.stack([ctx]).astype(jnp.int32)
    q_cols = query_weight.shape[1]
    features = tokens.shape[1]
    hidden = gate_weight.shape[1]

    gain_columns = jnp.pad(jnp.stack([pre_gain, mid_gain], axis=1), ((0, 0), (0, LANES - 2)))
    shard = jnp.concatenate(
        [query_weight, key_weight, value_weight, gain_columns, output_weight], axis=1
    )
    second = lax.all_gather(
        jnp.concatenate([gate_weight, up_weight, down_weight], axis=1), ROWS, axis=0, tiled=True
    )
    cosine, sine = angles(own_places(starts, order, ctx, ctxs))
    if pairs == 2 and shard.shape[0] % 16 == 0:
        first, queries, kv, normed, gains = gather_project(
            shard, tokens, cosine, sine, q_cols, ctxs
        )
        pieces = [kv[k] for k in range(ctxs)]
    else:
        first = lax.all_gather(shard, ROWS, axis=0, tiled=True)
        gains = first[:, 2 * q_cols : 2 * q_cols + 8].T.astype(f32)
        queries, kv, normed = project(tokens, gains, cosine, sine, first, q_cols)
        pieces = [kv] + [shifted(kv, "ctx", k) for k in range(1, ctxs)]
    output_weights = first[:, 2 * q_cols + LANES :]
    attended_low, att, sums = attend(order, starts, place, queries, pieces)
    branch = output_product(attended_low, output_weights, 0, features)
    middle, mid_normed, mixed, back_gate, back_up, back_part = feed_forward(
        tokens, branch, swapped(branch), gains, cotangent, second, hidden
    )
    back_other = swapped(back_part)
    gate_parts = gradient(mid_normed, back_gate, pairs, ctxs)
    up_parts = gradient(mid_normed, back_up, pairs, ctxs)
    down_parts = gradient(cotangent, mixed, pairs, ctxs)
    feed = down_product(mixed, second, 2)
    result = (middle + feed.astype(f32) + swapped(feed).astype(f32)).astype(bf16)

    back_middle, back_branch, back_attended, mid_grad = middle_back(
        cotangent, back_part, back_other, middle, gains, output_weights, 0, q_cols
    )
    output_parts = gradient(back_branch, attended_low, pairs, ctxs)
    back = attend_back(
        order, starts, place, queries, back_attended, att, sums, cosine, sine, pieces
    )
    own_parts = [back[1]] + [shifted(back[1 + k], "ctx", -k) for k in range(1, ctxs)]
    cot, normed_part, pre_grad = inputs_back(tokens, back[0], cosine, sine, first, own_parts)
    normed_other = swapped(normed_part)
    qkv_parts = gradient(normed, cot, pairs, ctxs)
    token_gradient = final_back(back_middle, normed_part, normed_other, tokens, gains)

    tp = lax.axis_index("tp")
    mid_once = jnp.where(tp == 0, mid_grad, 0.0)
    pair = jnp.concatenate([pre_grad, mid_once], axis=0).astype(bf16)
    pair = jnp.pad(pair, ((0, 6), (0, 0))).T
    ordered = relative(pair, pairs, ctxs)
    gain_sums = sum_to_owner(ordered[: features // 2], ordered[features // 2 :], pairs, ctxs)
    gain_sums = gain_sums + swapped(gain_sums)

    gate_gradient = sum_to_owner(*gate_parts, pairs, ctxs)
    up_gradient = sum_to_owner(*up_parts, pairs, ctxs)
    down_gradient = sum_to_owner(*down_parts, pairs, ctxs)
    output_gradient = sum_to_owner(*output_parts, pairs, ctxs)
    qkv_gradient = sum_to_owner(*qkv_parts, pairs, ctxs)
    return (
        result,
        token_gradient,
        gain_sums[:, 0],
        qkv_gradient[:, :q_cols],
        qkv_gradient[:, q_cols : q_cols + q_cols // 2],
        qkv_gradient[:, q_cols + q_cols // 2 :],
        output_gradient,
        gain_sums[:, 1],
        gate_gradient,
        up_gradient,
        down_gradient,
    )


def solution(mesh):
    rows, split = P(ROWS, None), P(ROWS, "tp")
    return jax.shard_map(
        body,
        mesh=mesh,
        in_specs=(rows, rows, P("dp", None), P("dp", None, None), P(ROWS))
        + (split,) * 4
        + (P(ROWS),)
        + (split,) * 3,
        out_specs=(rows, rows, P(ROWS)) + (split,) * 4 + (P(ROWS),) + (split,) * 3,
        check_vma=False,
    )
```

```python
import functools
import math

import jax
import jax.numpy as jnp
from jax import lax
from jax.experimental import pallas as pl
from jax.experimental.pallas import tpu as pltpu
from jax.sharding import PartitionSpec as P

HEAD_SIZE = 96
HALF = HEAD_SIZE // 2
BLOCK = 64
SPAN = 256
TILE = 512
LANES = 128

epsilon = 1e-05
rotary_base = 100000.0
masked_score = -1e30
SCALE = HEAD_SIZE**-0.5
SCALE2 = SCALE / math.log(2.0)

f32 = jnp.float32
bf16 = jnp.bfloat16
ROWS = ("dp", "ctx")
MIB = 2**20


def dot(left, right, contract):
    return lax.dot_general(
        left, right, ((contract[:1], contract[1:]), ((), ())), preferred_element_type=f32
    )


NN, NT, TN = (1, 0), (1, 1), (0, 0)


def cost(flops, moved):
    return pl.CostEstimate(flops=int(flops), bytes_accessed=int(moved), transcendentals=0)


def params(mib):
    return pltpu.CompilerParams(vmem_limit_bytes=mib * MIB)


def whole(shape):
    return pl.BlockSpec(shape, lambda *_: (0,) * len(shape))


SCALARS = pl.BlockSpec(memory_space=pltpu.SMEM)


def angles(place):
    frequency = rotary_base ** (-(jnp.arange(HALF, dtype=f32) * 2.0 / HEAD_SIZE))
    turn = place.astype(f32)[:, None] * frequency[None, :]
    return (jnp.cos(turn), jnp.sin(turn))


def streams(order, ctx):
    rounds, count = order.shape
    owners = order[:, lax.rem(ctx - jnp.arange(count) + count, count)].T
    blocks = owners + (jnp.arange(rounds, dtype=jnp.int32) * count)[None, :]
    within = jnp.arange(BLOCK, dtype=jnp.int32)
    return (blocks[:, :, None] * BLOCK + within).reshape(count, rounds * BLOCK).astype(jnp.int32)


def turned(head, cosine, sine, sign):
    first, second = head[:, :HALF], head[:, HALF:]
    along = sine if sign > 0 else -sine
    return jnp.concatenate(
        [first * cosine - second * along, second * cosine + first * along], axis=1
    )


def project_kernel(x_ref, gain_ref, cos_ref, sin_ref, w_ref, q_ref, kv_ref, normed_ref):
    step = pl.program_id(0)
    tile = w_ref.shape[1]

    @pl.when(step == 0)
    def _():
        x = x_ref[...].astype(f32)
        scale = lax.rsqrt(jnp.mean(x * x, axis=1, keepdims=True) + epsilon)
        normed_ref[...] = (x * scale * gain_ref[0:1, :]).astype(bf16)

    out = dot(normed_ref[...], w_ref[...], NN)

    def rotated(ref):
        for h in range(tile // HEAD_SIZE):
            lanes = slice(h * HEAD_SIZE, (h + 1) * HEAD_SIZE)
            ref[:, lanes] = turned(out[:, lanes], cos_ref[...], sin_ref[...], 1).astype(bf16)

    @pl.when(step < 2)
    def _():
        rotated(q_ref)

    @pl.when(step == 2)
    def _():
        rotated(kv_ref)

    @pl.when(step == 3)
    def _():
        kv_ref[...] = out.astype(bf16)


def project(x, gains, cosine, sine, weights, q_cols):
    rows, width = x.shape
    tile = q_cols // 2
    return pl.pallas_call(
        project_kernel,
        grid=(4,),
        in_specs=[
            whole(x.shape),
            whole(gains.shape),
            whole(cosine.shape),
            whole(sine.shape),
            pl.BlockSpec((width, tile), lambda j: (0, j)),
        ],
        out_specs=[
            pl.BlockSpec((rows, tile), lambda j: (0, jnp.minimum(j, 1))),
            pl.BlockSpec((rows, tile), lambda j: (0, jnp.maximum(j - 2, 0))),
            whole((rows, width)),
        ],
        out_shape=[
            jax.ShapeDtypeStruct((rows, q_cols), bf16),
            jax.ShapeDtypeStruct((rows, q_cols), bf16),
            jax.ShapeDtypeStruct((rows, width), bf16),
        ],
        compiler_params=params(40),
        cost_estimate=cost(2 * rows * width * 4 * tile, 2 * width * 4 * tile),
        name="project",
    )(x, gains, cosine, sine, weights)


MESH = pl.DeviceIdType.MESH


def gather_project_kernel(
    shard_ref, x_ref, cos_ref, sin_ref,
    full_ref, q_ref, kv_ref, normed_ref, gain_ref,
    w_ref, z_send, z_recv, y_send, y_recv, c_send, c_recv, k_send, k_recv, local,
):
    ctxs = lax.axis_size("ctx")
    dp, ctx, tp = lax.axis_index("dp"), lax.axis_index("ctx"), lax.axis_index("tp")
    far, core = (lax.rem(dp + 2, 4), ctx, tp), (dp + 1 - 2 * lax.rem(dp, 2), ctx, tp)
    after, before = (dp, lax.rem(ctx + 1, ctxs), tp), (dp, lax.rem(ctx + ctxs - 1, ctxs), tp)
    barrier = pltpu.get_barrier_semaphore()
    for device in (after, before, far, core):
        pl.semaphore_signal(barrier, inc=1, device_id=device, device_id_type=MESH)
    pl.semaphore_wait(barrier, 4)
    piece = shard_ref.shape[0]

    def block(pair, steps):
        owner = pair * ctxs + lax.rem(ctx - steps + ctxs, ctxs)
        return w_ref.at[pl.ds(pl.multiple_of(owner * piece, piece), piece)]

    def send(source, target, device, sent, got):
        copy = pltpu.make_async_remote_copy(source, target, sent, got, device, MESH)
        copy.start()
        return copy

    copies, y_copies, c_copies, z_copies = [], [], [], []
    for s in range(ctxs):
        place = block(dp, s)
        source = place if s else shard_ref
        if s:
            z_copies[s - 1].wait_recv()
        if s < ctxs - 1:
            z_copies.append(send(source, place, after, z_send.at[s], z_recv.at[s]))
        y_copies.append(send(source, place, far, y_send.at[s], y_recv.at[s]))
        c_copies.append(send(source, place, core, c_send.at[s], c_recv.at[s]))
        if s == 0:
            own = pltpu.make_async_copy(shard_ref, place, local.at[0])
            own.start()
            x = x_ref[...].astype(f32)
            unit = x * lax.rsqrt(jnp.mean(x * x, axis=1, keepdims=True) + epsilon)
    for s in range(ctxs):
        y_copies[s].wait_recv()
        place = block(far[0], s)
        c_copies.append(send(place, place, core, c_send.at[ctxs + s], c_recv.at[ctxs + s]))
    own.wait()
    for copy in c_copies:
        copy.wait_recv()
    full = pltpu.make_async_copy(w_ref, full_ref, local.at[1])
    full.start()

    q_cols = q_ref.shape[1]
    tile = q_cols // 2
    gains = w_ref[:, 2 * q_cols : 2 * q_cols + LANES].astype(f32).T[:8]
    gain_ref[...] = gains
    normed_ref[...] = (unit * gains[0:1]).astype(bf16)

    def rotated(out, store):
        for h in range(tile // HEAD_SIZE):
            lanes = slice(h * HEAD_SIZE, (h + 1) * HEAD_SIZE)
            store(lanes, turned(out[:, lanes], cos_ref[...], sin_ref[...], 1).astype(bf16))

    def key_store(lanes, value):
        kv_ref[0, :, lanes] = value

    def product(step):
        return dot(normed_ref[...], w_ref[:, step * tile : (step + 1) * tile], NN)

    rotated(product(2), key_store)
    kv_ref[0, :, tile:] = product(3).astype(bf16)
    k_copies = [send(kv_ref.at[0], kv_ref.at[1], after, k_send.at[0], k_recv.at[0])]

    for step in range(2):

        def query_store(lanes, value):
            q_ref[:, step * tile + lanes.start : step * tile + lanes.stop] = value

        rotated(product(step), query_store)
    for s in range(1, ctxs):
        k_copies[s - 1].wait_recv()
        if s < ctxs - 1:
            k_copies.append(
                send(kv_ref.at[s], kv_ref.at[s + 1], after, k_send.at[s], k_recv.at[s])
            )
    for copy in z_copies + y_copies + c_copies + k_copies:
        copy.wait_send()
    full.wait()


def gather_project(shard, x, cosine, sine, q_cols, ctxs):
    rows, width = x.shape
    columns = shard.shape[1]
    vmem = pl.BlockSpec(memory_space=pltpu.VMEM)
    sems = lambda n: pltpu.SemaphoreType.DMA((n,))
    return pl.pallas_call(
        gather_project_kernel,
        in_specs=[vmem] * 4,
        out_specs=[pl.BlockSpec(memory_space=pl.ANY)] + [vmem] * 4,
        out_shape=[
            jax.ShapeDtypeStruct((width, columns), bf16),
            jax.ShapeDtypeStruct((rows, q_cols), bf16),
            jax.ShapeDtypeStruct((ctxs, rows, q_cols), bf16),
            jax.ShapeDtypeStruct((rows, width), bf16),
            jax.ShapeDtypeStruct((8, width), f32),
        ],
        scratch_shapes=[pltpu.VMEM((width, columns), bf16)]
        + [sems(ctxs - 1)] * 2
        + [sems(ctxs)] * 2
        + [sems(2 * ctxs)] * 2
        + [sems(ctxs - 1)] * 2
        + [sems(2)],
        compiler_params=pltpu.CompilerParams(
            vmem_limit_bytes=48 * MIB, collective_id=0, has_side_effects=True
        ),
        cost_estimate=cost(2 * rows * width * 2 * q_cols, 1e8),
        name="gather_project",
    )(shard, x, cosine, sine)


def gather_stream(order, ctx, pieces, k_ref, v_ref):
    count, groups = len(pieces), k_ref.shape[0]
    width = groups * HEAD_SIZE

    def fill(i, unused):
        source = pl.ds(pl.multiple_of(i * BLOCK, BLOCK), BLOCK)
        for k, piece in enumerate(pieces):
            block = i * count + order[i, lax.rem(ctx - k + count, count)]
            target = pl.ds(pl.multiple_of(block * BLOCK, BLOCK), BLOCK)
            for g in range(groups):
                lanes = slice(g * HEAD_SIZE, (g + 1) * HEAD_SIZE)
                k_ref[g, target, :] = piece[source, lanes]
                v_ref[g, target, :] = piece[
                    source, width + g * HEAD_SIZE : width + (g + 1) * HEAD_SIZE
                ]
        return unused

    lax.fori_loop(0, order.shape[0], fill, 0)


def reach(starts, first):
    low = jnp.int32(0)
    for j in range(starts.shape[0]):
        low = jnp.where(starts[j] <= first, starts[j], low)
    return low


def row_limits(starts, first, lanes):
    row = first + lax.rem(lax.broadcasted_iota(jnp.int32, (1, lanes), 1), BLOCK)
    low = jnp.zeros((1, lanes), jnp.int32)
    for j in range(starts.shape[0]):
        low = jnp.where(row >= starts[j], starts[j], low)
    return row, low


def stacked(ref, rows, group, ratio):
    return jnp.concatenate(
        [
            ref[rows, (group * ratio + h) * HEAD_SIZE : (group * ratio + h + 1) * HEAD_SIZE]
            for h in range(ratio)
        ],
        axis=0,
    )


def attend_kernel(count, order, starts, place, q_ref, *refs):
    pieces = refs[:count]
    low_ref, att_ref, sum_ref, k_ref, v_ref = refs[count:]
    groups = k_ref.shape[0]
    ratio = q_ref.shape[1] // (groups * HEAD_SIZE)
    lanes = ratio * BLOCK
    ctx = place[0]
    gather_stream(order, ctx, pieces, k_ref, v_ref)

    def one(i, unused):
        first = (i * count + order[i, ctx]) * BLOCK
        row, low = row_limits(starts, first, lanes)
        begin = reach(starts, first) // SPAN
        end = (first + BLOCK - 1) // SPAN + 1
        rows = pl.ds(pl.multiple_of(i * BLOCK, BLOCK), BLOCK)
        queries = [stacked(q_ref, rows, g, ratio) for g in range(groups)]

        def chunk(c, carry):
            keys = pl.ds(pl.multiple_of(c * SPAN, SPAN), SPAN)
            index = c * SPAN + lax.broadcasted_iota(jnp.int32, (SPAN, lanes), 0)
            allowed = (index <= row) & (index >= low)
            new = []
            for g in range(groups):
                top, total, out = carry[g]
                raw = dot(k_ref[g, keys, :], queries[g], NT) * SCALE2
                raw = jnp.where(allowed, raw, masked_score)
                new_top = jnp.maximum(top, jnp.max(raw, axis=0, keepdims=True))
                weights = jnp.where(allowed, jnp.exp2(raw - new_top), 0.0)
                back = jnp.exp2(top - new_top)
                total = total * back + jnp.sum(weights, axis=0, keepdims=True)
                out = out * back + dot(v_ref[g, keys, :], weights.astype(bf16), TN)
                new.append((new_top, total, out))
            return tuple(new)

        blank = (
            jnp.full((1, lanes), masked_score, f32),
            jnp.zeros((1, lanes), f32),
            jnp.zeros((HEAD_SIZE, lanes), f32),
        )
        result = lax.fori_loop(begin, end, chunk, (blank,) * groups)
        for g in range(groups):
            top, total, out = result[g]
            out = out / total
            att_ref[i * groups + g] = out
            sum_ref[pl.ds(i * groups + g, 1), :] = top + jnp.log2(total)
            flat = out.T.astype(bf16)
            for h in range(ratio):
                head = g * ratio + h
                low_ref[rows, head * HEAD_SIZE : (head + 1) * HEAD_SIZE] = flat[
                    h * BLOCK : (h + 1) * BLOCK
                ]
        return unused

    lax.fori_loop(0, order.shape[0], one, 0)


def attend(order, starts, place, queries, pieces):
    count, rows = len(pieces), queries.shape[0]
    groups = pieces[0].shape[1] // (2 * HEAD_SIZE)
    ratio = queries.shape[1] // (groups * HEAD_SIZE)
    rounds, lanes = order.shape[0], ratio * BLOCK
    return pl.pallas_call(
        functools.partial(attend_kernel, count),
        in_specs=[SCALARS] * 3 + [pl.BlockSpec(memory_space=pltpu.VMEM)] * (1 + count),
        out_specs=[pl.BlockSpec(memory_space=pltpu.VMEM)] * 3,
        out_shape=[
            jax.ShapeDtypeStruct(queries.shape, bf16),
            jax.ShapeDtypeStruct((rounds * groups, HEAD_SIZE, lanes), f32),
            jax.ShapeDtypeStruct((rounds * groups, lanes), f32),
        ],
        scratch_shapes=[pltpu.VMEM((groups, count * rows, HEAD_SIZE), bf16)] * 2,
        compiler_params=params(40),
        cost_estimate=cost(8e9, 1e7),
        name="attend",
    )(order, starts, place, queries, *pieces)


def attend_back_kernel(count, order, starts, place, q_ref, d_ref, att_ref, sum_ref, cos_ref, sin_ref, *refs):
    pieces = refs[:count]
    qc_ref = refs[count]
    outs = refs[count + 1 : 2 * count + 1]
    k_ref, v_ref, dk_ref, dv_ref = refs[2 * count + 1 :]
    groups = k_ref.shape[0]
    ratio = q_ref.shape[1] // (groups * HEAD_SIZE)
    lanes = ratio * BLOCK
    width = groups * HEAD_SIZE
    ctx = place[0]
    gather_stream(order, ctx, pieces, k_ref, v_ref)
    dk_ref[...] = jnp.zeros_like(dk_ref)
    dv_ref[...] = jnp.zeros_like(dv_ref)

    def one(i, unused):
        first = (i * count + order[i, ctx]) * BLOCK
        row, low = row_limits(starts, first, lanes)
        begin = reach(starts, first) // SPAN
        end = (first + BLOCK - 1) // SPAN + 1
        rows = pl.ds(pl.multiple_of(i * BLOCK, BLOCK), BLOCK)
        queries = [stacked(q_ref, rows, g, ratio) for g in range(groups)]
        slopes = [stacked(d_ref, rows, g, ratio) for g in range(groups)]
        sums, deltas = [], []
        for g in range(groups):
            sums.append(sum_ref[pl.ds(i * groups + g, 1), :])
            across = slopes[g].astype(f32).T
            deltas.append(jnp.sum(across * att_ref[i * groups + g], axis=0, keepdims=True))

        def chunk(c, carry):
            keys = pl.ds(pl.multiple_of(c * SPAN, SPAN), SPAN)
            index = c * SPAN + lax.broadcasted_iota(jnp.int32, (SPAN, lanes), 0)
            allowed = (index <= row) & (index >= low)
            new = []
            for g in range(groups):
                key, value = k_ref[g, keys, :], v_ref[g, keys, :]
                raw = dot(key, queries[g], NT) * SCALE2
                share = jnp.where(allowed, jnp.exp2(jnp.minimum(raw - sums[g], 0.0)), 0.0)
                back_share = dot(value, slopes[g], NT)
                back = (share * (back_share - deltas[g])).astype(bf16)
                dv_ref[g, keys, :] += dot(share.astype(bf16), slopes[g], NN)
                dk_ref[g, keys, :] += dot(back, queries[g], NN)
                new.append(carry[g] + dot(key, back, TN))
            return tuple(new)

        blank = jnp.zeros((HEAD_SIZE, lanes), f32)
        result = lax.fori_loop(begin, end, chunk, (blank,) * groups)
        cosine, sine = cos_ref[rows, :], sin_ref[rows, :]
        for g in range(groups):
            flat = result[g].T * SCALE
            for h in range(ratio):
                head = g * ratio + h
                qc_ref[rows, head * HEAD_SIZE : (head + 1) * HEAD_SIZE] = turned(
                    flat[h * BLOCK : (h + 1) * BLOCK], cosine, sine, -1
                ).astype(bf16)
        return unused

    lax.fori_loop(0, order.shape[0], one, 0)

    def spread(i, unused):
        target = pl.ds(pl.multiple_of(i * BLOCK, BLOCK), BLOCK)
        for k, out in enumerate(outs):
            block = i * count + order[i, lax.rem(ctx - k + count, count)]
            source = pl.ds(pl.multiple_of(block * BLOCK, BLOCK), BLOCK)
            for g in range(groups):
                out[target, g * HEAD_SIZE : (g + 1) * HEAD_SIZE] = (
                    dk_ref[g, source, :] * SCALE
                ).astype(bf16)
                out[target, width + g * HEAD_SIZE : width + (g + 1) * HEAD_SIZE] = dv_ref[
                    g, source, :
                ].astype(bf16)
        return unused

    lax.fori_loop(0, order.shape[0], spread, 0)


def attend_back(order, starts, place, queries, slopes, att, sums, cosine, sine, pieces):
    count, rows = len(pieces), queries.shape[0]
    groups = pieces[0].shape[1] // (2 * HEAD_SIZE)
    keys = (groups, count * rows, HEAD_SIZE)
    return pl.pallas_call(
        functools.partial(attend_back_kernel, count),
        in_specs=[SCALARS] * 3 + [pl.BlockSpec(memory_space=pltpu.VMEM)] * (6 + count),
        out_specs=[pl.BlockSpec(memory_space=pltpu.VMEM)] * (1 + count),
        out_shape=[jax.ShapeDtypeStruct(queries.shape, bf16)]
        + [jax.ShapeDtypeStruct(pieces[0].shape, bf16)] * count,
        scratch_shapes=[pltpu.VMEM(keys, bf16)] * 2 + [pltpu.VMEM(keys, f32)] * 2,
        compiler_params=params(56),
        cost_estimate=cost(16e9, 2e7),
        name="attend_back",
    )(order, starts, place, queries, slopes, att, sums, cosine, sine, *pieces)


SIDE = 256


def tile_bias(qi_ref, ki_ref, k, q_tile, k_tile, ratio):
    rows = slice(q_tile * SIDE, (q_tile + 1) * SIDE)
    keys = ki_ref[k, k_tile * SIDE : (k_tile + 1) * SIDE, :]
    allowed = (keys <= qi_ref[0:1, rows]) & (keys >= qi_ref[1:2, rows])
    bias = jnp.where(allowed, 0.0, masked_score)
    return jnp.concatenate([bias] * ratio, axis=1)


def flat_heads(ref, q_tile, group, ratio):
    return jnp.concatenate(
        [
            ref[
                q_tile * SIDE : (q_tile + 1) * SIDE,
                (group * ratio + h) * HEAD_SIZE : (group * ratio + h + 1) * HEAD_SIZE,
            ]
            for h in range(ratio)
        ],
        axis=0,
    )


def head_lanes(g, offset=0):
    return slice(offset + g * HEAD_SIZE, offset + (g + 1) * HEAD_SIZE)


def dense_begin(q_ref, groups, ratio, qt_ref, top_ref, total_ref, att_ref):
    for q_tile in range(q_ref.shape[0] // SIDE):
        for g in range(groups):
            flat = flat_heads(q_ref, q_tile, g, ratio)
            qt_ref[q_tile * groups + g] = flat.astype(f32).T.astype(bf16)
    top_ref[...] = jnp.full(top_ref.shape, masked_score, f32)
    total_ref[...] = jnp.zeros(total_ref.shape, f32)
    att_ref[...] = jnp.zeros(att_ref.shape, f32)


def dense_piece(k, kv_ref, qi_ref, ki_ref, groups, ratio, qt_ref, top_ref, total_ref, att_ref):
    width = groups * HEAD_SIZE
    for q_tile in range(qi_ref.shape[1] // SIDE):
        for k_tile in range(q_tile, -1, -1):
            bias = tile_bias(qi_ref, ki_ref, k, q_tile, k_tile, ratio)
            rows = slice(k_tile * SIDE, (k_tile + 1) * SIDE)
            for g in range(groups):
                i = q_tile * groups + g
                raw = dot(kv_ref[k, rows, head_lanes(g)], qt_ref[i], NN) * SCALE2 + bias
                top = top_ref[i]
                new_top = jnp.maximum(top, jnp.max(raw, axis=0, keepdims=True))
                weights = jnp.exp2(raw - new_top)
                back = jnp.exp2(top - new_top)
                top_ref[i] = new_top
                total_ref[i] = total_ref[i] * back + jnp.sum(weights, axis=0, keepdims=True)
                att_ref[i] = att_ref[i] * back + dot(
                    kv_ref[k, rows, head_lanes(g, width)], weights.astype(bf16), TN
                )


def dense_end(groups, ratio, top_ref, total_ref, att_ref, sum_ref, low_ref):
    for i in range(att_ref.shape[0]):
        q_tile, g = divmod(i, groups)
        out = att_ref[i] * (1.0 / total_ref[i])
        att_ref[i] = out
        sum_ref[i] = top_ref[i] + jnp.log2(total_ref[i])
        flat = out.T.astype(bf16)
        for h in range(ratio):
            low_ref[q_tile * SIDE : (q_tile + 1) * SIDE, head_lanes(g * ratio + h)] = flat[
                h * SIDE : (h + 1) * SIDE
            ]


def dense_kernel(q_ref, kv_ref, qi_ref, ki_ref, low_ref, att_ref, sum_ref, qt_ref, top_ref, total_ref):
    groups = kv_ref.shape[2] // (2 * HEAD_SIZE)
    ratio = q_ref.shape[1] // (groups * HEAD_SIZE)
    dense_begin(q_ref, groups, ratio, qt_ref, top_ref, total_ref, att_ref)

    def piece(k, unused):
        dense_piece(k, kv_ref, qi_ref, ki_ref, groups, ratio, qt_ref, top_ref, total_ref, att_ref)
        return unused

    lax.fori_loop(0, kv_ref.shape[0], piece, 0)
    dense_end(groups, ratio, top_ref, total_ref, att_ref, sum_ref, low_ref)


def dense_shapes(rows, groups, ratio):
    tiles = rows // SIDE * groups
    return tiles, ratio * SIDE


def dense_attend(queries, kv, qi, ki):
    rows = queries.shape[0]
    groups = kv.shape[2] // (2 * HEAD_SIZE)
    tiles, lanes = dense_shapes(rows, groups, queries.shape[1] // (groups * HEAD_SIZE))
    vmem = pl.BlockSpec(memory_space=pltpu.VMEM)
    return pl.pallas_call(
        dense_kernel,
        in_specs=[vmem] * 4,
        out_specs=[vmem] * 3,
        out_shape=[
            jax.ShapeDtypeStruct(queries.shape, bf16),
            jax.ShapeDtypeStruct((tiles, HEAD_SIZE, lanes), f32),
            jax.ShapeDtypeStruct((tiles, 1, lanes), f32),
        ],
        scratch_shapes=[
            pltpu.VMEM((tiles, HEAD_SIZE, lanes), bf16),
            pltpu.VMEM((tiles, 1, lanes), f32),
            pltpu.VMEM((tiles, 1, lanes), f32),
        ],
        compiler_params=params(40),
        cost_estimate=cost(8e9, 1e7),
        name="dense_attend",
    )(queries, kv, qi, ki)


FEED_TILES = 12
TILES = 17


def back_kernel(
    part_hbm, feed_hbm, cot_hbm, middle_hbm, gain_ref, act_hbm, mid_normed_hbm, x_hbm, normed_hbm,
    low_ref, q_ref, kv_ref, att_ref, sum_ref, qi_ref, ki_ref, cos_ref, sin_ref, weight_hbm,
    feed_other, back_middle, part2_out, part2_other, grads_ref, held_hbm, far_hbm,
    lhs, mid, part, part_other, w_out, w_in, rhs, q2, q2t, d2, d2t, delta, bias_ref, dq_ref,
    kv_sent, kv_got, cot, gain_rows, gain_other, gain_columns,
    p_send, p_keep, c_got, s_one, own, y_got, z_got,
    load_sem, act_sem, x_send, x_recv, c_send, c_recv, c_free, held_sem, y_send, y_recv, own_sem,
    z_send, z_recv, k_send, k_recv,
):
    ctxs = lax.axis_size("ctx")
    dp, ctx, tp = lax.axis_index("dp"), lax.axis_index("ctx"), lax.axis_index("tp")
    pair_at, core_at = dp // 2, lax.rem(dp, 2)
    far, core = (lax.rem(dp + 2, 4), ctx, tp), (dp + 1 - 2 * core_at, ctx, tp)
    after, before = (dp, lax.rem(ctx + 1, ctxs), tp), (dp, lax.rem(ctx + ctxs - 1, ctxs), tp)
    across = (dp, ctx, 1 - tp)
    rows, width = mid.shape
    section = width // 4
    piece = section // ctxs
    groups = kv_ref.shape[2] // (2 * HEAD_SIZE)
    kv_width = groups * HEAD_SIZE
    ratio = q_ref.shape[1] // kv_width
    q_cols = q_ref.shape[1]

    barrier = pltpu.get_barrier_semaphore()
    for device in (after, before, far, core, across):
        pl.semaphore_signal(barrier, inc=1, device_id=device, device_id_type=MESH)
    pl.semaphore_wait(barrier, 5)

    def remote(source, target, device, sent, got):
        return pltpu.make_async_remote_copy(source, target, sent, got, device, MESH)

    def load(source, target, index):
        return pltpu.make_async_copy(source, target, load_sem.at[index])


    def product(t, lhs_of, rhs_of):
        slot = lax.rem(t, 2)

        @pl.when(t >= 2)
        def _():
            core_copy(t - 2).wait_send()

        for c, out in ((1, p_send), (0, p_keep)):
            for y in range(2):
                there = lax.rem(pair_at + y + 1, 2) * 2 + lax.rem(core_at + c, 2)
                start = pl.multiple_of(there * section, LANES)
                result = rhs_of(start, lhs_of(pl.ds(start, section)))
                for z in range(ctxs):
                    place = lax.rem(z + 2 * ctxs - ctx - 1, ctxs)
                    target = pl.ds(pl.multiple_of(y * section + place * piece, piece), piece)
                    out[slot, target, :] = result[z * piece : (z + 1) * piece]

        @pl.when(t >= 4)
        def _():
            pl.semaphore_wait(c_free, 1)

        core_copy(t).start()

    def core_copy(t):
        return remote(
            p_send.at[lax.rem(t, 2)], c_got.at[lax.rem(t, 4)], core, c_send.at[t], c_recv.at[t]
        )

    def held_copy(t):
        return pltpu.make_async_copy(s_one.at[lax.rem(t, 2)], held_hbm.at[t], held_sem.at[t])

    def meet_core(t):
        core_copy(t).wait_recv()
        slot, got = lax.rem(t, 2), lax.rem(t, 4)

        def add(i, unused):
            part_rows = pl.ds(pl.multiple_of(i * piece, piece), piece)
            total = p_keep[slot, part_rows, :].astype(f32) + c_got[got, part_rows, :].astype(f32)
            s_one[slot, part_rows, :] = total.astype(bf16)
            return unused

        lax.fori_loop(0, 2 * section // piece, add, 0)

        @pl.when(t + 4 < TILES)
        def _():
            pl.semaphore_signal(c_free, inc=1, device_id=core, device_id_type=MESH)

        held_copy(t).start()

    def far_copy(t):
        return remote(
            held_hbm.at[t, pl.ds(0, section)], far_hbm.at[t], far, y_send.at[t], y_recv.at[t]
        )

    def send_far(t):
        held_copy(t).wait()
        far_copy(t).start()

    def own_copy(t):
        return pltpu.make_async_copy(
            held_hbm.at[t, pl.ds(section, section)], own.at[lax.rem(t, 6)], own_sem.at[t, 0]
        )

    def got_copy(t):
        return pltpu.make_async_copy(far_hbm.at[t], y_got.at[lax.rem(t, 2)], own_sem.at[t, 1])

    def ring_copy(t, step):
        return remote(
            own.at[lax.rem(t, 6), pl.ds((ctxs - 2 - step) * piece, piece)],
            z_got.at[t, step], after, z_send.at[t, step], z_recv.at[t, step],
        )

    def ring_add(t, step):
        ring_copy(t, step).wait_recv()
        ring_copy(t, step).wait_send()
        place = ctxs - 3 - step if step < ctxs - 2 else ctxs - 1
        target = pl.ds(place * piece, piece)
        total = own[lax.rem(t, 6), target, :].astype(f32) + z_got[t, step].astype(f32)
        if step < ctxs - 2:
            own[lax.rem(t, 6), target, :] = total.astype(bf16)
            ring_copy(t, step + 1).start()
        else:
            grads_ref[t] = total

    def tick(n):
        for step in range(ctxs - 2, -1, -1):

            @pl.when((n - 2 - step >= 0) & (n - 2 - step < TILES))
            def _(step=step):
                ring_add(n - 2 - step, step)

        @pl.when((n >= 1) & (n - 1 < TILES))
        def _():
            t = n - 1
            own_copy(t).wait()
            got_copy(t).wait()
            slot, got = lax.rem(t, 6), lax.rem(t, 2)
            for z in range(ctxs):
                target = pl.ds(z * piece, piece)
                total = own[slot, target, :].astype(f32) + y_got[got, target, :].astype(f32)
                own[slot, target, :] = total.astype(bf16)
            ring_copy(t, 0).start()

        @pl.when(n < TILES)
        def _():
            far_copy(n).wait_recv()
            own_copy(n).start()
            got_copy(n).start()


    part_copy = remote(part_hbm, part_other, across, x_send.at[0], x_recv.at[0])
    part_copy.start()
    feed_copy = remote(feed_hbm, feed_other, across, x_send.at[1], x_recv.at[1])
    feed_copy.start()

    def act_copy(t):
        columns = pl.ds(pl.multiple_of(lax.rem(t, 4) * TILE, TILE), TILE)
        return pltpu.make_async_copy(
            act_hbm.at[t // 4, :, columns], rhs.at[lax.rem(t, 2)], act_sem.at[t]
        )

    loads = [
        load(mid_normed_hbm, lhs.at[0], 0),
        load(cot_hbm, lhs.at[1], 1),
        load(part_hbm, part, 2),
        load(middle_hbm, mid, 3),
        load(weight_hbm.at[:, pl.ds(2 * q_cols + LANES, q_cols)], w_out, 4),
        load(weight_hbm.at[:, pl.ds(0, 2 * q_cols)], w_in, 5),
    ]
    act_copy(0).start()
    for copy in loads:
        copy.start()
    loads[0].wait()
    loads[1].wait()

    def plain(t):
        def times(start, left):
            return dot(left, rhs[lax.rem(t, 2)], TN).astype(bf16)

        return times

    def feed_step(t, unused):
        act_copy(t).wait()

        @pl.when(t + 1 < FEED_TILES)
        def _():
            act_copy(t + 1).start()

        product(t, lambda lanes: lhs[t // 8, :, lanes], plain(t))

        @pl.when(t >= 1)
        def _():
            meet_core(t - 1)

        @pl.when(t >= 2)
        def _():
            send_far(t - 2)

        @pl.when((t >= 5) & (lax.rem(t, 3) == 2))
        def _():
            tick((t - 5) // 3)

        return unused

    lax.fori_loop(0, FEED_TILES, feed_step, 0)
    meet_core(FEED_TILES - 1)
    send_far(FEED_TILES - 2)
    send_far(FEED_TILES - 1)

    for q_tile in range(rows // SIDE):
        for g in range(groups):
            flat = flat_heads(q_ref, q_tile, g, ratio)
            q2[q_tile * groups + g] = flat
            q2t[q_tile * groups + g] = flat.astype(f32).T.astype(bf16)
    dq_ref[...] = jnp.zeros(dq_ref.shape, f32)
    kv_got[0] = jnp.zeros(kv_got.shape[1:], bf16)
    gain_rows[...] = jnp.zeros(gain_rows.shape, f32)


    loads[2].wait()
    loads[3].wait()
    part_copy.wait_recv()
    few = 64

    def norm_rows(i, unused):
        here = pl.ds(pl.multiple_of(i * few, few), few)
        field = mid[here, :]
        scale = lax.rsqrt(jnp.mean(field * field, axis=1, keepdims=True) + epsilon)
        unit = field * scale
        back = part[here, :].astype(f32) + part_other[here, :].astype(f32)
        gain_rows[1:2, :] += jnp.sum(back * unit, axis=0, keepdims=True)
        inner = back * gain_ref[1:2, :]
        out = lhs[1, here, :].astype(f32) + scale * (
            inner - unit * jnp.mean(inner * unit, axis=1, keepdims=True)
        )
        mid[here, :] = out
        lhs[0, here, :] = out.astype(bf16)
        return unused

    lax.fori_loop(0, rows // few, norm_rows, 0)
    middle_copy = load(mid, back_middle, 6)
    middle_copy.start()
    normed_copy = load(normed_hbm, lhs.at[1], 7)
    normed_copy.start()
    x_copy = load(x_hbm, part, 8)
    x_copy.start()
    loads[4].wait()
    cot[:, :q_cols] = dot(lhs[0], w_out[...], NN).astype(bf16)
    for q_tile in range(rows // SIDE):
        for g in range(groups):
            i = q_tile * groups + g
            flat = flat_heads(cot, q_tile, g, ratio)
            turned_flat = flat.astype(f32).T
            d2[i] = flat
            d2t[i] = turned_flat.astype(bf16)
            delta[i] = jnp.sum(turned_flat * att_ref[i], axis=0, keepdims=True)
    tick(jnp.int32(3))

    t_out = jnp.int32(FEED_TILES)
    product(
        t_out, lambda lanes: lhs[0, :, lanes], lambda start, left: dot(left, low_ref[:, :TILE], TN).astype(bf16)
    )


    def kv_copy(s):
        return remote(kv_sent.at[s], kv_got.at[s + 1], after, k_send.at[s], k_recv.at[s])

    def back_piece(s, unused):
        k = lax.rem(s + 1, ctxs)
        pairs = [(q, kk) for kk in range(rows // SIDE) for q in range(kk, rows // SIDE)]
        for index, (q_tile, k_tile) in enumerate(pairs):
            bias_ref[index] = tile_bias(qi_ref, ki_ref, k, q_tile, k_tile, ratio)
        sums = []
        for k_tile in range(rows // SIDE):
            here = slice(k_tile * SIDE, (k_tile + 1) * SIDE)
            for g in range(groups):
                key, value = kv_ref[k, here, head_lanes(g)], kv_ref[k, here, head_lanes(g, kv_width)]
                d_key = d_value = None
                for index, (q_tile, which) in enumerate(pairs):
                    if which != k_tile:
                        continue
                    i = q_tile * groups + g
                    raw = dot(key, q2t[i], NN) * SCALE2 + bias_ref[index]
                    share = jnp.exp2(raw - sum_ref[i])
                    back_share = dot(value, d2t[i], NN)
                    back = (share * (back_share - delta[i])).astype(bf16)
                    one_value = dot(share.astype(bf16), d2[i], NN)
                    one_key = dot(back, q2[i], NN)
                    d_value = one_value if d_value is None else d_value + one_value
                    d_key = one_key if d_key is None else d_key + one_key
                    dq_ref[i] += dot(key, back, TN)
                kv_sent[s, here, head_lanes(g)] = (d_key * SCALE).astype(bf16)
                kv_sent[s, here, head_lanes(g, kv_width)] = d_value.astype(bf16)

        @pl.when(s >= 1)
        def _():
            kv_copy(s - 1).wait_recv()

            def add(i, unused):
                here = pl.ds(pl.multiple_of(i * few, few), few)
                total = kv_sent[s, here, :].astype(f32) + kv_got[s, here, :].astype(f32)
                kv_sent[s, here, :] = total.astype(bf16)
                return unused

            lax.fori_loop(0, rows // few, add, 0)

        @pl.when(s < ctxs - 1)
        def _():
            kv_copy(s).start()

        @pl.when(s == 0)
        def _():
            meet_core(t_out)
            send_far(t_out)

        @pl.when(s < ctxs - 1)
        def _():
            tick(4 + 2 * s)
            tick(5 + 2 * s)

        return unused

    lax.fori_loop(0, ctxs, back_piece, 0)


    for i in range(dq_ref.shape[0]):
        q_tile, g = divmod(i, groups)
        here = slice(q_tile * SIDE, (q_tile + 1) * SIDE)
        flat = dq_ref[i].T * SCALE
        for h in range(ratio):
            cot[here, head_lanes(g * ratio + h)] = turned(
                flat[h * SIDE : (h + 1) * SIDE], cos_ref[here, :], sin_ref[here, :], -1
            ).astype(bf16)
    for g in range(groups):
        cot[:, head_lanes(g, q_cols)] = turned(
            kv_sent[ctxs - 1, :, head_lanes(g)].astype(f32), cos_ref[...], sin_ref[...], -1
        ).astype(bf16)
    cot[:, q_cols + kv_width :] = kv_sent[ctxs - 1, :, kv_width:]
    loads[5].wait()
    x_copy.wait()
    x_rows = part[...].astype(f32)
    scale = lax.rsqrt(jnp.mean(x_rows * x_rows, axis=1, keepdims=True) + epsilon)
    for j in range(width // TILE):
        lanes = slice(j * TILE, (j + 1) * TILE)
        back = dot(cot[...], w_in[lanes, :], NT)
        part_other[:, lanes] = back.astype(bf16)
        gain_rows[0:1, lanes] += jnp.sum(back * (part[:, lanes].astype(f32) * scale), axis=0, keepdims=True)
    gain_copy = remote(gain_rows.at[pl.ds(0, 8)], gain_other, across, x_send.at[2], x_recv.at[2])
    gain_copy.start()
    part2_copy = remote(part_other, part2_other, across, x_send.at[3], x_recv.at[3])
    part2_copy.start()
    part2_save = load(part_other, part2_out, 9)
    part2_save.start()
    normed_copy.wait()

    def qkv_step(j, unused):
        t = FEED_TILES + 1 + j

        def times(start, left):
            lanes = pl.ds(pl.multiple_of(j * TILE, TILE), TILE)
            return dot(left, cot[:, lanes], TN).astype(bf16)

        product(t, lambda lanes: lhs[1, :, lanes], times)

        @pl.when(j >= 1)
        def _():
            meet_core(t - 1)

        @pl.when(j >= 2)
        def _():
            send_far(t - 2)

        return unused

    lax.fori_loop(0, 3, qkv_step, 0)
    gain_copy.wait_recv()
    gain_copy.wait_send()
    gain_rows[0:1, :] += gain_other[0:1, :]
    gain_columns[...] = gain_rows[...].T
    last = jnp.int32(TILES - 1)
    tail = q_cols - TILE

    def times_last(start, left):
        some = dot(left, low_ref[:, TILE:], TN)
        gains = gain_columns[pl.ds(start, section), :]
        spare = jnp.zeros((section, TILE - tail - LANES), f32)
        return jnp.concatenate([some, gains, spare], axis=1).astype(bf16)

    product(last, lambda lanes: lhs[0, :, lanes], times_last)
    meet_core(last - 1)
    send_far(last - 2)
    meet_core(last)
    send_far(last - 1)
    send_far(last)

    def drain(n, unused):
        tick(n)
        return unused

    lax.fori_loop(4 + 2 * (ctxs - 1), TILES + ctxs, drain, 0)

    for t in (TILES - 2, TILES - 1):
        core_copy(jnp.int32(t)).wait_send()

    def far_done(t, unused):
        far_copy(t).wait_send()
        return unused

    lax.fori_loop(0, TILES, far_done, 0)
    for s in range(ctxs - 1):
        kv_copy(s).wait_send()
    part_copy.wait_send()
    feed_copy.wait()
    part2_copy.wait()
    part2_save.wait()
    middle_copy.wait()


def back_all(part, feed, cotangent, middle, gains, act, mid_normed, x, normed, low, queries, kv, att, sums, qi, ki, cosine, sine, weights, ctxs):
    rows, width = x.shape
    q_cols = queries.shape[1]
    groups = kv.shape[2] // (2 * HEAD_SIZE)
    ratio = q_cols // (groups * HEAD_SIZE)
    tiles, lanes = dense_shapes(rows, groups, ratio)
    section = width // 4
    piece = section // ctxs
    vmem, hbm = pl.BlockSpec(memory_space=pltpu.VMEM), pl.BlockSpec(memory_space=pl.ANY)
    full = jax.ShapeDtypeStruct((rows, width), bf16)
    sems = lambda *n: pltpu.SemaphoreType.DMA(n)
    space = lambda *shape: pltpu.VMEM(shape, bf16)
    wide = lambda *shape: pltpu.VMEM(shape, f32)
    pairs = (rows // SIDE) * (rows // SIDE + 1) // 2
    return pl.pallas_call(
        back_kernel,
        in_specs=[hbm] * 4 + [vmem] + [hbm] * 4 + [vmem] * 9 + [hbm],
        out_specs=[hbm] * 4 + [vmem] + [hbm] * 2,
        out_shape=[
            full,
            jax.ShapeDtypeStruct((rows, width), f32),
            full,
            full,
            jax.ShapeDtypeStruct((TILES, piece, TILE), f32),
            jax.ShapeDtypeStruct((TILES, 2 * section, TILE), bf16),
            jax.ShapeDtypeStruct((TILES, section, TILE), bf16),
        ],
        scratch_shapes=[
            space(2, rows, width), wide(rows, width), space(rows, width), space(rows, width),
            space(width, q_cols), space(width, 2 * q_cols), space(2, rows, TILE),
            space(tiles, lanes, HEAD_SIZE), space(tiles, HEAD_SIZE, lanes),
            space(tiles, lanes, HEAD_SIZE), space(tiles, HEAD_SIZE, lanes),
            wide(tiles, 1, lanes), wide(pairs, SIDE, lanes), wide(tiles, HEAD_SIZE, lanes),
            space(ctxs, rows, q_cols), space(ctxs, rows, q_cols), space(rows, 2 * q_cols),
            wide(LANES, width), wide(8, width), wide(width, LANES),
            space(2, 2 * section, TILE), space(2, 2 * section, TILE), space(4, 2 * section, TILE),
            space(2, 2 * section, TILE), space(6, section, TILE), space(2, section, TILE),
            space(TILES, ctxs - 1, piece, TILE),
            sems(10), sems(FEED_TILES), sems(4), sems(4), sems(TILES), sems(TILES),
            pltpu.SemaphoreType.REGULAR, sems(TILES), sems(TILES), sems(TILES), sems(TILES, 2),
            sems(TILES, ctxs - 1), sems(TILES, ctxs - 1), sems(ctxs - 1), sems(ctxs - 1),
        ],
        compiler_params=pltpu.CompilerParams(
            vmem_limit_bytes=63 * MIB, collective_id=1, has_side_effects=True
        ),
        cost_estimate=cost(4e10, 1e8),
        name="back_all",
    )(part, feed, cotangent, middle, gains, act, mid_normed, x, normed, low, queries, kv, att, sums, qi, ki, cosine, sine, weights)


def output_kernel(a_ref, w_ref, o_ref):
    o_ref[...] = dot(a_ref[...], w_ref[...], NT).astype(bf16)


def output_product(attended, weights, column, features):
    rows, inner = attended.shape
    return pl.pallas_call(
        output_kernel,
        grid=(2,),
        in_specs=[
            whole(attended.shape),
            pl.BlockSpec((features // 2, inner), lambda j: (j, column)),
        ],
        out_specs=pl.BlockSpec((rows, features // 2), lambda j: (0, j)),
        out_shape=jax.ShapeDtypeStruct((rows, features), bf16),
        compiler_params=params(40),
        cost_estimate=cost(2 * rows * inner * features, 2 * inner * features),
        name="output_product",
    )(attended, weights)


def feed_kernel(
    x_ref, mine_ref, other_ref, gain_ref, cot_ref, gate_ref, up_ref, down_ref,
    middle_ref, normed_ref, act_ref, back_ref, feed_ref, total_ref, feed_total,
):
    step = pl.program_id(0)

    @pl.when(step == 0)
    def _():
        middle = (
            x_ref[...].astype(f32) + mine_ref[...].astype(f32) + other_ref[...].astype(f32)
        )
        middle_ref[...] = middle
        scale = lax.rsqrt(jnp.mean(middle * middle, axis=1, keepdims=True) + epsilon)
        normed_ref[...] = (middle * scale * gain_ref[1:2, :]).astype(bf16)

    gate = dot(normed_ref[...], gate_ref[...], NN)
    upward = dot(normed_ref[...], up_ref[...], NN)
    back_mixed = dot(cot_ref[...], down_ref[...], NN)
    sigmoid = 1.0 / (1.0 + jnp.exp(-gate))
    activated = gate * sigmoid
    mixed = (activated * upward).astype(bf16)
    back_gate = (back_mixed * upward * sigmoid * (1.0 + gate * (1.0 - sigmoid))).astype(bf16)
    back_up = (back_mixed * activated).astype(bf16)
    act_ref[0] = back_gate
    act_ref[1] = back_up
    act_ref[2] = mixed
    part = dot(back_gate, gate_ref[...], NT) + dot(back_up, up_ref[...], NT)
    feed = dot(mixed, down_ref[...], NT)

    @pl.when(step == 0)
    def _():
        total_ref[...] = part
        feed_total[...] = feed

    @pl.when(step > 0)
    def _():
        total_ref[...] += part
        feed_total[...] += feed

    @pl.when(step == pl.num_programs(0) - 1)
    def _():
        back_ref[...] = total_ref[...].astype(bf16)
        feed_ref[...] = feed_total[...].astype(bf16)


def feed_forward(x, mine, other, gains, cotangent, weights, hidden):
    rows, width = x.shape
    steps = hidden // TILE
    tile_of = lambda which: pl.BlockSpec((width, TILE), lambda j: (0, which * steps + j))
    acts_of = pl.BlockSpec((3, rows, TILE), lambda j: (0, 0, j))
    full = whole((rows, width))
    return pl.pallas_call(
        feed_kernel,
        grid=(steps,),
        in_specs=[full, full, full, whole(gains.shape), full]
        + [tile_of(0), tile_of(1), tile_of(2)],
        out_specs=[full, full, acts_of, full, full],
        out_shape=[
            jax.ShapeDtypeStruct((rows, width), f32),
            jax.ShapeDtypeStruct((rows, width), bf16),
            jax.ShapeDtypeStruct((3, rows, hidden), bf16),
            jax.ShapeDtypeStruct((rows, width), bf16),
            jax.ShapeDtypeStruct((rows, width), bf16),
        ],
        scratch_shapes=[pltpu.VMEM((rows, width), f32)] * 2,
        compiler_params=params(56),
        cost_estimate=cost(12 * rows * width * hidden, 6 * width * hidden),
        name="feed_forward",
    )(x, mine, other, gains, cotangent, weights, weights, weights)


def middle_kernel(cot_ref, mine_ref, other_ref, middle_ref, gain_ref, w_ref, bm_ref, bb_ref, ba_ref, grad_ref):
    middle = middle_ref[...]
    scale = lax.rsqrt(jnp.mean(middle * middle, axis=1, keepdims=True) + epsilon)
    unit = middle * scale
    back = mine_ref[...].astype(f32) + other_ref[...].astype(f32)
    grad_ref[...] = jnp.sum(back * unit, axis=0, keepdims=True)
    inner = back * gain_ref[1:2, :]
    out = cot_ref[...].astype(f32) + scale * (
        inner - unit * jnp.mean(inner * unit, axis=1, keepdims=True)
    )
    bm_ref[...] = out
    low = out.astype(bf16)
    bb_ref[...] = low
    ba_ref[...] = dot(low, w_ref[...], NN).astype(bf16)


def middle_back(cotangent, mine, other, middle, gains, weights, column, inner):
    rows, width = middle.shape
    full = whole((rows, width))
    return pl.pallas_call(
        middle_kernel,
        grid=(1,),
        in_specs=[full, full, full, full, whole(gains.shape)]
        + [pl.BlockSpec((width, inner), lambda j: (0, column))],
        out_specs=[full, full, whole((rows, inner)), whole((1, width))],
        out_shape=[
            jax.ShapeDtypeStruct((rows, width), f32),
            jax.ShapeDtypeStruct((rows, width), bf16),
            jax.ShapeDtypeStruct((rows, inner), bf16),
            jax.ShapeDtypeStruct((1, width), f32),
        ],
        compiler_params=params(56),
        cost_estimate=cost(2 * rows * width * inner, 1.5e7),
        name="middle_back",
    )(cotangent, mine, other, middle, gains, weights)


def inputs_kernel(count, x_ref, qc_ref, cos_ref, sin_ref, w_ref, *refs):
    parts = refs[:count]
    cot_ref, back_ref, grad_ref = refs[count:]
    half = qc_ref.shape[1] // 2
    cot_ref[:, : 2 * half] = qc_ref[...]
    total = parts[0][...].astype(f32)
    for part in parts[1:]:
        total += part[...].astype(f32)
    for h in range(half // HEAD_SIZE):
        lanes = slice(h * HEAD_SIZE, (h + 1) * HEAD_SIZE)
        there = slice(2 * half + h * HEAD_SIZE, 2 * half + (h + 1) * HEAD_SIZE)
        cot_ref[:, there] = turned(total[:, lanes], cos_ref[...], sin_ref[...], -1).astype(bf16)
    cot_ref[:, 3 * half :] = total[:, half:].astype(bf16)
    back = dot(cot_ref[...], w_ref[...], NT)
    back_ref[...] = back.astype(bf16)
    x = x_ref[...].astype(f32)
    unit = x * lax.rsqrt(jnp.mean(x * x, axis=1, keepdims=True) + epsilon)
    grad_ref[...] = jnp.sum(back * unit, axis=0, keepdims=True)


def inputs_back(x, qc, cosine, sine, weights, parts):
    rows, width = x.shape
    inner = 2 * qc.shape[1]
    full = whole((rows, width))
    return pl.pallas_call(
        functools.partial(inputs_kernel, len(parts)),
        grid=(1,),
        in_specs=[full, whole(qc.shape), whole(cosine.shape), whole(sine.shape)]
        + [pl.BlockSpec((width, inner), lambda j: (0, 0))]
        + [whole(parts[0].shape)] * len(parts),
        out_specs=[whole((rows, inner)), full, whole((1, width))],
        out_shape=[
            jax.ShapeDtypeStruct((rows, inner), bf16),
            jax.ShapeDtypeStruct((rows, width), bf16),
            jax.ShapeDtypeStruct((1, width), f32),
        ],
        compiler_params=params(56),
        cost_estimate=cost(2 * rows * width * inner, 1.5e7),
        name="inputs_back",
    )(x, qc, cosine, sine, weights, *parts)


def final_kernel(bm_ref, mine_ref, other_ref, x_ref, gain_ref, o_ref):
    x = x_ref[...].astype(f32)
    scale = lax.rsqrt(jnp.mean(x * x, axis=1, keepdims=True) + epsilon)
    unit = x * scale
    inner = (mine_ref[...].astype(f32) + other_ref[...].astype(f32)) * gain_ref[0:1, :]
    out = bm_ref[...] + scale * (inner - unit * jnp.mean(inner * unit, axis=1, keepdims=True))
    o_ref[...] = out.astype(bf16)


def final_back(back_middle, mine, other, x, gains):
    rows, width = x.shape
    block = pl.BlockSpec((rows // 4, width), lambda j: (j, 0))
    return pl.pallas_call(
        final_kernel,
        grid=(4,),
        in_specs=[block] * 4 + [whole(gains.shape)],
        out_specs=block,
        out_shape=jax.ShapeDtypeStruct((rows, width), bf16),
        compiler_params=params(40),
        cost_estimate=cost(1e6, 1e7),
        name="final_back",
    )(back_middle, mine, other, x, gains)


def relative(field, pairs, ctxs):
    dp, ctx = lax.axis_index("dp"), lax.axis_index("ctx")
    shaped = field.reshape((pairs, 2, ctxs, -1) + field.shape[1:])
    for axis, shift in ((0, dp // 2 + 1), (1, dp % 2 + 1), (2, ctx + 1)):
        shaped = jnp.roll(shaped, -shift, axis)
    return shaped.swapaxes(0, 1).reshape(field.shape)


def gradient_kernel(pairs, ctxs, place, a_ref, b_ref, send_ref, keep_ref):
    width = a_ref.shape[1]
    section = width // (2 * pairs)
    piece = section // ctxs
    for c, out in ((1, send_ref), (0, keep_ref)):
        for y in range(pairs):
            pair = lax.rem(place[0] + y + 1, pairs)
            core = lax.rem(place[1] + c, 2)
            lanes = pl.ds(pl.multiple_of((pair * 2 + core) * section, LANES), section)
            result = dot(a_ref[:, lanes], b_ref[...], TN).astype(bf16)
            for z in range(ctxs):
                far = lax.rem(z + ctxs - place[2] - 1 + ctxs, ctxs)
                rows = pl.ds(pl.multiple_of(y * section + far * piece, piece), piece)
                out[rows, :] = result[z * piece : (z + 1) * piece]


def gradient(a, b, pairs, ctxs):
    rows, width = a.shape
    columns = b.shape[1]
    section = width // (2 * pairs)
    if section % LANES or (section // ctxs) % 32:
        ordered = relative(dot(a, b, TN).astype(bf16), pairs, ctxs)
        return ordered[: width // 2], ordered[width // 2 :]
    dp, ctx = lax.axis_index("dp"), lax.axis_index("ctx")
    place = jnp.stack([dp // 2, dp % 2, ctx]).astype(jnp.int32)
    tile = TILE if columns % TILE == 0 else columns // 2
    block = pl.BlockSpec((width // 2, tile), lambda j: (0, j))
    return pl.pallas_call(
        functools.partial(gradient_kernel, pairs, ctxs),
        grid=(columns // tile,),
        in_specs=[SCALARS, whole(a.shape), pl.BlockSpec((rows, tile), lambda j: (0, j))],
        out_specs=[block, block],
        out_shape=[jax.ShapeDtypeStruct((width // 2, columns), bf16)] * 2,
        compiler_params=params(40),
        cost_estimate=cost(2 * rows * width * columns, 2 * width * columns),
        name="gradient",
    )(place, a, b)


def shifted(field, axis, steps, stride=1):
    count = lax.axis_size(axis)
    return lax.ppermute(
        field, axis, [(i, (i + steps * stride) % count) for i in range(count)]
    )


def other_core(field):
    return lax.ppermute(field, "dp", [(i, i ^ 1) for i in range(lax.axis_size("dp"))])


def sum_to_owner(send, keep, pairs, ctxs):
    columns = send.shape[1]
    got = other_core(send).reshape(pairs, -1, columns)
    keep = keep.reshape(pairs, -1, columns)
    total = got[-1].astype(f32) + keep[-1].astype(f32)
    for y in range(1, pairs):
        part = (got[y - 1].astype(f32) + keep[y - 1].astype(f32)).astype(bf16)
        total = total + shifted(part, "dp", y, 2).astype(f32)
    total = total.reshape(ctxs, -1, columns)
    result = total[-1]
    for z in range(1, ctxs):
        result = result + shifted(total[z - 1].astype(bf16), "ctx", z).astype(f32)
    return result


def swapped(field):
    count = lax.axis_size("tp")
    return lax.ppermute(field, "tp", [(i, count - 1 - i) for i in range(count)])


def body(
    tokens,
    cotangent,
    lengths,
    block_order,
    pre_gain,
    query_weight,
    key_weight,
    value_weight,
    output_weight,
    mid_gain,
    gate_weight,
    up_weight,
    down_weight,
):
    ctxs = lax.axis_size("ctx")
    pairs = lax.axis_size("dp") // 2
    ctx = lax.axis_index("ctx")
    order = block_order[0]
    ends = jnp.cumsum(lengths[0]).astype(jnp.int32)
    starts = ends - lengths[0]
    place = jnp.stack([ctx]).astype(jnp.int32)
    q_cols = query_weight.shape[1]
    features = tokens.shape[1]
    hidden = gate_weight.shape[1]

    gain_columns = jnp.pad(jnp.stack([pre_gain, mid_gain], axis=1), ((0, 0), (0, LANES - 2)))
    shard = jnp.concatenate(
        [query_weight, key_weight, value_weight, gain_columns, output_weight], axis=1
    )
    second = lax.all_gather(
        jnp.concatenate([gate_weight, up_weight, down_weight], axis=1), ROWS, axis=0, tiled=True
    )
    stream = streams(order, ctx)
    lows = jnp.max(jnp.where(starts[None, :] <= stream[0][:, None], starts[None, :], 0), axis=1)
    cosine, sine = angles(stream[0] - lows)
    if pairs == 2 and shard.shape[0] % 32 == 0:
        first, queries, kv, normed, gains = gather_project(
            shard, tokens, cosine, sine, q_cols, ctxs
        )
        qi = jnp.pad(jnp.stack([stream[0], lows]), ((0, 6), (0, 0)))
        attended_low, att, sums = dense_attend(queries, kv, qi, stream[:, :, None])
        output_weights = first[:, 2 * q_cols + LANES :]
        branch = output_product(attended_low, output_weights, 0, features)
        middle, mid_normed, act, back_part, feed = feed_forward(
            tokens, branch, swapped(branch), gains, cotangent, second, hidden
        )
        feed_other, back_middle, part, part_other, grads, _, _ = back_all(
            back_part, feed, cotangent, middle, gains, act, mid_normed, tokens, normed,
            attended_low, queries, kv, att, sums, qi, stream[:, :, None], cosine, sine, first, ctxs,
        )
        result = (middle + feed.astype(f32) + feed_other.astype(f32)).astype(bf16)
        token_gradient = final_back(back_middle, part, part_other, tokens, gains)
        wide = lambda *tiles: jnp.concatenate([grads[t] for t in tiles], axis=1)
        qkv_gradient = wide(13, 14, 15)
        output_gradient = jnp.concatenate([grads[12], grads[16][:, : q_cols - TILE]], axis=1)
        gain_sums = grads[16][:, q_cols - TILE :]
        gate_gradient, up_gradient = wide(0, 1, 2, 3), wide(4, 5, 6, 7)
        down_gradient = wide(8, 9, 10, 11)
    else:
        first = lax.all_gather(shard, ROWS, axis=0, tiled=True)
        gains = first[:, 2 * q_cols : 2 * q_cols + 8].T.astype(f32)
        queries, kv, normed = project(tokens, gains, cosine, sine, first, q_cols)
        pieces = [kv] + [shifted(kv, "ctx", k) for k in range(1, ctxs)]
        output_weights = first[:, 2 * q_cols + LANES :]
        attended_low, att, sums = attend(order, starts, place, queries, pieces)
        branch = output_product(attended_low, output_weights, 0, features)
        middle, mid_normed, act, back_part, feed = feed_forward(
            tokens, branch, swapped(branch), gains, cotangent, second, hidden
        )
        back_other = swapped(back_part)
        gate_parts = gradient(mid_normed, act[0], pairs, ctxs)
        up_parts = gradient(mid_normed, act[1], pairs, ctxs)
        down_parts = gradient(cotangent, act[2], pairs, ctxs)
        result = (middle + feed.astype(f32) + swapped(feed).astype(f32)).astype(bf16)

        back_middle, back_branch, back_attended, mid_grad = middle_back(
            cotangent, back_part, back_other, middle, gains, output_weights, 0, q_cols
        )
        output_parts = gradient(back_branch, attended_low, pairs, ctxs)
        back = attend_back(
            order, starts, place, queries, back_attended, att, sums, cosine, sine, pieces
        )
        own_parts = [back[1]] + [shifted(back[1 + k], "ctx", -k) for k in range(1, ctxs)]
        cot, normed_part, pre_grad = inputs_back(
            tokens, back[0], cosine, sine, first, own_parts
        )
        normed_other = swapped(normed_part)
        qkv_parts = gradient(normed, cot, pairs, ctxs)
        token_gradient = final_back(back_middle, normed_part, normed_other, tokens, gains)

        mid_once = jnp.where(lax.axis_index("tp") == 0, mid_grad, 0.0)
        pair = jnp.concatenate([pre_grad, mid_once], axis=0).astype(bf16)
        pair = jnp.pad(pair, ((0, 6), (0, 0))).T
        ordered = relative(pair, pairs, ctxs)
        gain_sums = sum_to_owner(
            ordered[: features // 2], ordered[features // 2 :], pairs, ctxs
        )
        gain_sums = gain_sums + swapped(gain_sums)
        gate_gradient = sum_to_owner(*gate_parts, pairs, ctxs)
        up_gradient = sum_to_owner(*up_parts, pairs, ctxs)
        down_gradient = sum_to_owner(*down_parts, pairs, ctxs)
        output_gradient = sum_to_owner(*output_parts, pairs, ctxs)
        qkv_gradient = sum_to_owner(*qkv_parts, pairs, ctxs)
    return (
        result,
        token_gradient,
        gain_sums[:, 0],
        qkv_gradient[:, :q_cols],
        qkv_gradient[:, q_cols : q_cols + q_cols // 2],
        qkv_gradient[:, q_cols + q_cols // 2 :],
        output_gradient,
        gain_sums[:, 1],
        gate_gradient,
        up_gradient,
        down_gradient,
    )


def solution(mesh):
    rows, split = P(ROWS, None), P(ROWS, "tp")
    return jax.shard_map(
        body,
        mesh=mesh,
        in_specs=(rows, rows, P("dp", None), P("dp", None, None), P(ROWS))
        + (split,) * 4
        + (P(ROWS),)
        + (split,) * 3,
        out_specs=(rows, rows, P(ROWS)) + (split,) * 4 + (P(ROWS),) + (split,) * 3,
        check_vma=False,
    )
```

```python
import functools
import math

import jax
import jax.numpy as jnp
from jax import lax
from jax.experimental import pallas as pl
from jax.experimental.pallas import tpu as pltpu
from jax.sharding import PartitionSpec as P

HEAD_SIZE = 96
HALF = HEAD_SIZE // 2
BLOCK = 64
SPAN = 256
TILE = 512
LANES = 128

epsilon = 1e-05
rotary_base = 100000.0
masked_score = -1e30
SCALE = HEAD_SIZE**-0.5
SCALE2 = SCALE / math.log(2.0)

f32 = jnp.float32
bf16 = jnp.bfloat16
ROWS = ("dp", "ctx")
MIB = 2**20


def dot(left, right, contract):
    return lax.dot_general(
        left, right, ((contract[:1], contract[1:]), ((), ())), preferred_element_type=f32
    )


NN, NT, TN = (1, 0), (1, 1), (0, 0)


def cost(flops, moved):
    return pl.CostEstimate(flops=int(flops), bytes_accessed=int(moved), transcendentals=0)


def params(mib):
    return pltpu.CompilerParams(vmem_limit_bytes=mib * MIB)


def whole(shape):
    return pl.BlockSpec(shape, lambda *_: (0,) * len(shape))


SCALARS = pl.BlockSpec(memory_space=pltpu.SMEM)


def angles(place):
    frequency = rotary_base ** (-(jnp.arange(HALF, dtype=f32) * 2.0 / HEAD_SIZE))
    turn = place.astype(f32)[:, None] * frequency[None, :]
    return (jnp.cos(turn), jnp.sin(turn))


def streams(order, ctx):
    rounds, count = order.shape
    owners = order[:, lax.rem(ctx - jnp.arange(count) + count, count)].T
    blocks = owners + (jnp.arange(rounds, dtype=jnp.int32) * count)[None, :]
    within = jnp.arange(BLOCK, dtype=jnp.int32)
    return (blocks[:, :, None] * BLOCK + within).reshape(count, rounds * BLOCK).astype(jnp.int32)


def turned(head, cosine, sine, sign):
    first, second = head[:, :HALF], head[:, HALF:]
    along = sine if sign > 0 else -sine
    return jnp.concatenate(
        [first * cosine - second * along, second * cosine + first * along], axis=1
    )


def project_kernel(x_ref, gain_ref, cos_ref, sin_ref, w_ref, q_ref, kv_ref, normed_ref):
    step = pl.program_id(0)
    tile = w_ref.shape[1]

    @pl.when(step == 0)
    def _():
        x = x_ref[...].astype(f32)
        scale = lax.rsqrt(jnp.mean(x * x, axis=1, keepdims=True) + epsilon)
        normed_ref[...] = (x * scale * gain_ref[0:1, :]).astype(bf16)

    out = dot(normed_ref[...], w_ref[...], NN)

    def rotated(ref):
        for h in range(tile // HEAD_SIZE):
            lanes = slice(h * HEAD_SIZE, (h + 1) * HEAD_SIZE)
            ref[:, lanes] = turned(out[:, lanes], cos_ref[...], sin_ref[...], 1).astype(bf16)

    @pl.when(step < 2)
    def _():
        rotated(q_ref)

    @pl.when(step == 2)
    def _():
        rotated(kv_ref)

    @pl.when(step == 3)
    def _():
        kv_ref[...] = out.astype(bf16)


def project(x, gains, cosine, sine, weights, q_cols):
    rows, width = x.shape
    tile = q_cols // 2
    return pl.pallas_call(
        project_kernel,
        grid=(4,),
        in_specs=[
            whole(x.shape),
            whole(gains.shape),
            whole(cosine.shape),
            whole(sine.shape),
            pl.BlockSpec((width, tile), lambda j: (0, j)),
        ],
        out_specs=[
            pl.BlockSpec((rows, tile), lambda j: (0, jnp.minimum(j, 1))),
            pl.BlockSpec((rows, tile), lambda j: (0, jnp.maximum(j - 2, 0))),
            whole((rows, width)),
        ],
        out_shape=[
            jax.ShapeDtypeStruct((rows, q_cols), bf16),
            jax.ShapeDtypeStruct((rows, q_cols), bf16),
            jax.ShapeDtypeStruct((rows, width), bf16),
        ],
        compiler_params=params(40),
        cost_estimate=cost(2 * rows * width * 4 * tile, 2 * width * 4 * tile),
        name="project",
    )(x, gains, cosine, sine, weights)


MESH = pl.DeviceIdType.MESH


def forward_kernel(
    shard_ref, gate_shard, up_shard, down_shard, x_ref, cos_ref, sin_ref, qi_ref, ki_ref,
    full_ref, gate_ref, up_ref, down_ref, q_ref, kv_ref, normed_ref, gain_ref, low_ref, att_ref, sum_ref,
    branch_ref, other_ref,
    w_ref, qt_ref, top_ref, total_ref,
    z_send, z_recv, y_send, y_recv, c_send, c_recv, k_send, k_recv, x_send, x_recv, local,
):
    ctxs = lax.axis_size("ctx")
    dp, ctx, tp = lax.axis_index("dp"), lax.axis_index("ctx"), lax.axis_index("tp")
    far, core = (lax.rem(dp + 2, 4), ctx, tp), (dp + 1 - 2 * lax.rem(dp, 2), ctx, tp)
    after, before = (dp, lax.rem(ctx + 1, ctxs), tp), (dp, lax.rem(ctx + ctxs - 1, ctxs), tp)
    across = (dp, ctx, 1 - tp)
    barrier = pltpu.get_barrier_semaphore()
    for device in (after, before, far, core, across):
        pl.semaphore_signal(barrier, inc=1, device_id=device, device_id_type=MESH)
    pl.semaphore_wait(barrier, 5)
    piece = shard_ref.shape[0]
    shards = (shard_ref, gate_shard, up_shard, down_shard)
    wholes = (w_ref, gate_ref, up_ref, down_ref)
    last = ctxs - 1


    def place(group, pair, steps):
        owner = pair * ctxs + lax.rem(ctx - steps + ctxs, ctxs)
        return wholes[group].at[pl.ds(pl.multiple_of(owner * piece, piece), piece)]

    def source(group, steps):
        return place(group, dp, steps) if steps else shards[group]

    def remote(source, target, device, sent, got):
        return pltpu.make_async_remote_copy(source, target, device_id=device, device_id_type=MESH, send_sem=sent, recv_sem=got)

    def ring(group, s):
        return remote(
            source(group, s), place(group, dp, s), after, z_send.at[group, s], z_recv.at[group, s]
        )

    def over(group, s):
        return remote(
            source(group, s), place(group, dp, s), far, y_send.at[group, s], y_recv.at[group, s]
        )

    def aside(group, s):
        return remote(
            source(group, s), place(group, dp, s), core, c_send.at[group, s], c_recv.at[group, s]
        )

    def aside_far(group, s):
        there = place(group, far[0], s)
        return remote(
            there, there, core, c_send.at[group, ctxs + s], c_recv.at[group, ctxs + s]
        )

    def own_copy(group):
        return pltpu.make_async_copy(shards[group], place(group, dp, 0), local.at[group])

    def begin(group):
        over(group, 0).start()
        aside(group, 0).start()
        own_copy(group).start()

    def along(group, s):
        ring(group, s - 1).wait_recv()
        if s < last:
            ring(group, s).start()
        over(group, s).start()
        aside(group, s).start()

    def came_over(group, s):
        over(group, s).wait_recv()
        aside_far(group, s).start()

    def gathered(group):
        own_copy(group).wait()
        for s in range(ctxs):
            aside(group, s).wait_recv()
            aside_far(group, s).wait_recv()

    first, gate, up, down = range(4)
    ring(first, 0).start()
    begin(first)
    x = x_ref[...].astype(f32)
    unit = x * lax.rsqrt(jnp.mean(x * x, axis=1, keepdims=True) + epsilon)
    for s in range(1, ctxs):
        along(first, s)
        came_over(first, s - 1)
    ring(gate, 0).start()
    begin(gate)
    came_over(first, last)
    gathered(first)
    full = pltpu.make_async_copy(w_ref, full_ref, local.at[4])
    full.start()
    along(gate, 1)

    q_cols = q_ref.shape[1]
    tile = q_cols // 2
    groups = kv_ref.shape[2] // (2 * HEAD_SIZE)
    ratio = q_cols // (groups * HEAD_SIZE)
    gains = w_ref[:, 2 * q_cols : 2 * q_cols + LANES].astype(f32).T[:8]
    gain_ref[...] = gains
    normed_ref[...] = (unit * gains[0:1]).astype(bf16)

    def product(step):
        return dot(normed_ref[...], w_ref[:, step * tile : (step + 1) * tile], NN)

    def rotated(out, store):
        for h in range(tile // HEAD_SIZE):
            lanes = slice(h * HEAD_SIZE, (h + 1) * HEAD_SIZE)
            store(lanes, turned(out[:, lanes], cos_ref[...], sin_ref[...], 1).astype(bf16))

    def key_store(lanes, value):
        kv_ref[0, :, lanes] = value

    rotated(product(2), key_store)
    kv_ref[0, :, tile:] = product(3).astype(bf16)

    def kv_copy(s):
        return remote(kv_ref.at[s], kv_ref.at[s + 1], after, k_send.at[s], k_recv.at[s])

    kv_copy(0).start()
    begin(up)
    for step in range(2):

        def query_store(lanes, value):
            q_ref[:, step * tile + lanes.start : step * tile + lanes.stop] = value

        rotated(product(step), query_store)

    def attention(k):
        dense_piece(k, kv_ref, qi_ref, ki_ref, groups, ratio, qt_ref, top_ref, total_ref, att_ref)

    dense_begin(q_ref, groups, ratio, qt_ref, top_ref, total_ref, att_ref)
    waits = [
        [lambda: along(gate, 2), lambda: came_over(gate, 0), lambda: came_over(gate, 1)],
        [lambda: ring(up, 0).start(), lambda: begin(down), lambda: along(gate, last), lambda: came_over(up, 0)],
        [],
    ]

    def attention_step(k, unused):
        for s in range(1, ctxs):

            @pl.when(k == s)
            def _(s=s):
                kv_copy(s - 1).wait_recv()
                if s < last:
                    kv_copy(s).start()
                for step in waits[s - 1] if s - 1 < len(waits) else []:
                    step()

        attention(k)
        return unused

    lax.fori_loop(0, ctxs, attention_step, 0)
    ring(down, 0).start()
    along(up, 1)
    dense_end(groups, ratio, top_ref, total_ref, att_ref, sum_ref, low_ref)
    branch_ref[...] = dot(low_ref[...], w_ref[:, 2 * q_cols + LANES :], NT).astype(bf16)
    exchange = remote(branch_ref, other_ref, across, x_send.at[0], x_recv.at[0])
    exchange.start()

    for s in range(2, ctxs):
        along(up, s)
        came_over(gate, s)
        along(down, s - 1)
        came_over(up, s - 1)
        came_over(down, s - 2)
    along(down, last)
    came_over(up, last)
    came_over(down, last - 1)
    came_over(down, last)
    for group in (gate, up, down):
        gathered(group)
    for group in range(4):
        for s in range(ctxs):
            if s < last:
                ring(group, s).wait_send()
            over(group, s).wait_send()
            aside(group, s).wait_send()
            aside_far(group, s).wait_send()
    for s in range(last):
        kv_copy(s).wait_send()
    exchange.wait()
    full.wait()


def forward_all(shard, gate, up, down, x, cosine, sine, qi, ki, q_cols, ctxs):
    rows, width = x.shape
    columns, hidden = shard.shape[1], gate.shape[1]
    groups = q_cols // 2 // HEAD_SIZE
    tiles, lanes = dense_shapes(rows, groups, 2)
    vmem, hbm = pl.BlockSpec(memory_space=pltpu.VMEM), pl.BlockSpec(memory_space=pl.ANY)
    sems = lambda *n: pltpu.SemaphoreType.DMA(n)
    shape = jax.ShapeDtypeStruct
    full = shape((rows, width), bf16)
    return pl.pallas_call(
        forward_kernel,
        in_specs=[vmem] + [hbm] * 3 + [vmem] * 5,
        out_specs=[hbm] * 4 + [vmem] * 9,
        out_shape=[
            shape((width, columns), bf16),
            shape((width, hidden), bf16),
            shape((width, hidden), bf16),
            shape((width, hidden), bf16),
            shape((rows, q_cols), bf16),
            shape((ctxs, rows, q_cols), bf16),
            full,
            shape((8, width), f32),
            shape((rows, q_cols), bf16),
            shape((tiles, HEAD_SIZE, lanes), f32),
            shape((tiles, 1, lanes), f32),
            full,
            full,
        ],
        scratch_shapes=[
            pltpu.VMEM((width, columns), bf16),
            pltpu.VMEM((tiles, HEAD_SIZE, lanes), bf16),
            pltpu.VMEM((tiles, 1, lanes), f32),
            pltpu.VMEM((tiles, 1, lanes), f32),
        ]
        + [sems(4, ctxs - 1)] * 2
        + [sems(4, ctxs)] * 2
        + [sems(4, 2 * ctxs)] * 2
        + [sems(ctxs - 1)] * 2
        + [sems(1)] * 2
        + [sems(5)],
        compiler_params=pltpu.CompilerParams(
            vmem_limit_bytes=56 * MIB, collective_id=0, has_side_effects=True
        ),
        cost_estimate=cost(1e10, 1e8),
        name="forward_all",
    )(shard, gate, up, down, x, cosine, sine, qi, ki)


def gather_stream(order, ctx, pieces, k_ref, v_ref):
    count, groups = len(pieces), k_ref.shape[0]
    width = groups * HEAD_SIZE

    def fill(i, unused):
        source = pl.ds(pl.multiple_of(i * BLOCK, BLOCK), BLOCK)
        for k, piece in enumerate(pieces):
            block = i * count + order[i, lax.rem(ctx - k + count, count)]
            target = pl.ds(pl.multiple_of(block * BLOCK, BLOCK), BLOCK)
            for g in range(groups):
                lanes = slice(g * HEAD_SIZE, (g + 1) * HEAD_SIZE)
                k_ref[g, target, :] = piece[source, lanes]
                v_ref[g, target, :] = piece[
                    source, width + g * HEAD_SIZE : width + (g + 1) * HEAD_SIZE
                ]
        return unused

    lax.fori_loop(0, order.shape[0], fill, 0)


def reach(starts, first):
    low = jnp.int32(0)
    for j in range(starts.shape[0]):
        low = jnp.where(starts[j] <= first, starts[j], low)
    return low


def row_limits(starts, first, lanes):
    row = first + lax.rem(lax.broadcasted_iota(jnp.int32, (1, lanes), 1), BLOCK)
    low = jnp.zeros((1, lanes), jnp.int32)
    for j in range(starts.shape[0]):
        low = jnp.where(row >= starts[j], starts[j], low)
    return row, low


def stacked(ref, rows, group, ratio):
    return jnp.concatenate(
        [
            ref[rows, (group * ratio + h) * HEAD_SIZE : (group * ratio + h + 1) * HEAD_SIZE]
            for h in range(ratio)
        ],
        axis=0,
    )


def attend_kernel(count, order, starts, place, q_ref, *refs):
    pieces = refs[:count]
    low_ref, att_ref, sum_ref, k_ref, v_ref = refs[count:]
    groups = k_ref.shape[0]
    ratio = q_ref.shape[1] // (groups * HEAD_SIZE)
    lanes = ratio * BLOCK
    ctx = place[0]
    gather_stream(order, ctx, pieces, k_ref, v_ref)

    def one(i, unused):
        first = (i * count + order[i, ctx]) * BLOCK
        row, low = row_limits(starts, first, lanes)
        begin = reach(starts, first) // SPAN
        end = (first + BLOCK - 1) // SPAN + 1
        rows = pl.ds(pl.multiple_of(i * BLOCK, BLOCK), BLOCK)
        queries = [stacked(q_ref, rows, g, ratio) for g in range(groups)]

        def chunk(c, carry):
            keys = pl.ds(pl.multiple_of(c * SPAN, SPAN), SPAN)
            index = c * SPAN + lax.broadcasted_iota(jnp.int32, (SPAN, lanes), 0)
            allowed = (index <= row) & (index >= low)
            new = []
            for g in range(groups):
                top, total, out = carry[g]
                raw = dot(k_ref[g, keys, :], queries[g], NT) * SCALE2
                raw = jnp.where(allowed, raw, masked_score)
                new_top = jnp.maximum(top, jnp.max(raw, axis=0, keepdims=True))
                weights = jnp.where(allowed, jnp.exp2(raw - new_top), 0.0)
                back = jnp.exp2(top - new_top)
                total = total * back + jnp.sum(weights, axis=0, keepdims=True)
                out = out * back + dot(v_ref[g, keys, :], weights.astype(bf16), TN)
                new.append((new_top, total, out))
            return tuple(new)

        blank = (
            jnp.full((1, lanes), masked_score, f32),
            jnp.zeros((1, lanes), f32),
            jnp.zeros((HEAD_SIZE, lanes), f32),
        )
        result = lax.fori_loop(begin, end, chunk, (blank,) * groups)
        for g in range(groups):
            top, total, out = result[g]
            out = out / total
            att_ref[i * groups + g] = out
            sum_ref[pl.ds(i * groups + g, 1), :] = top + jnp.log2(total)
            flat = out.T.astype(bf16)
            for h in range(ratio):
                head = g * ratio + h
                low_ref[rows, head * HEAD_SIZE : (head + 1) * HEAD_SIZE] = flat[
                    h * BLOCK : (h + 1) * BLOCK
                ]
        return unused

    lax.fori_loop(0, order.shape[0], one, 0)


def attend(order, starts, place, queries, pieces):
    count, rows = len(pieces), queries.shape[0]
    groups = pieces[0].shape[1] // (2 * HEAD_SIZE)
    ratio = queries.shape[1] // (groups * HEAD_SIZE)
    rounds, lanes = order.shape[0], ratio * BLOCK
    return pl.pallas_call(
        functools.partial(attend_kernel, count),
        in_specs=[SCALARS] * 3 + [pl.BlockSpec(memory_space=pltpu.VMEM)] * (1 + count),
        out_specs=[pl.BlockSpec(memory_space=pltpu.VMEM)] * 3,
        out_shape=[
            jax.ShapeDtypeStruct(queries.shape, bf16),
            jax.ShapeDtypeStruct((rounds * groups, HEAD_SIZE, lanes), f32),
            jax.ShapeDtypeStruct((rounds * groups, lanes), f32),
        ],
        scratch_shapes=[pltpu.VMEM((groups, count * rows, HEAD_SIZE), bf16)] * 2,
        compiler_params=params(40),
        cost_estimate=cost(8e9, 1e7),
        name="attend",
    )(order, starts, place, queries, *pieces)


def attend_back_kernel(count, order, starts, place, q_ref, d_ref, att_ref, sum_ref, cos_ref, sin_ref, *refs):
    pieces = refs[:count]
    qc_ref = refs[count]
    outs = refs[count + 1 : 2 * count + 1]
    k_ref, v_ref, dk_ref, dv_ref = refs[2 * count + 1 :]
    groups = k_ref.shape[0]
    ratio = q_ref.shape[1] // (groups * HEAD_SIZE)
    lanes = ratio * BLOCK
    width = groups * HEAD_SIZE
    ctx = place[0]
    gather_stream(order, ctx, pieces, k_ref, v_ref)
    dk_ref[...] = jnp.zeros_like(dk_ref)
    dv_ref[...] = jnp.zeros_like(dv_ref)

    def one(i, unused):
        first = (i * count + order[i, ctx]) * BLOCK
        row, low = row_limits(starts, first, lanes)
        begin = reach(starts, first) // SPAN
        end = (first + BLOCK - 1) // SPAN + 1
        rows = pl.ds(pl.multiple_of(i * BLOCK, BLOCK), BLOCK)
        queries = [stacked(q_ref, rows, g, ratio) for g in range(groups)]
        slopes = [stacked(d_ref, rows, g, ratio) for g in range(groups)]
        sums, deltas = [], []
        for g in range(groups):
            sums.append(sum_ref[pl.ds(i * groups + g, 1), :])
            across = slopes[g].astype(f32).T
            deltas.append(jnp.sum(across * att_ref[i * groups + g], axis=0, keepdims=True))

        def chunk(c, carry):
            keys = pl.ds(pl.multiple_of(c * SPAN, SPAN), SPAN)
            index = c * SPAN + lax.broadcasted_iota(jnp.int32, (SPAN, lanes), 0)
            allowed = (index <= row) & (index >= low)
            new = []
            for g in range(groups):
                key, value = k_ref[g, keys, :], v_ref[g, keys, :]
                raw = dot(key, queries[g], NT) * SCALE2
                share = jnp.where(allowed, jnp.exp2(jnp.minimum(raw - sums[g], 0.0)), 0.0)
                back_share = dot(value, slopes[g], NT)
                back = (share * (back_share - deltas[g])).astype(bf16)
                dv_ref[g, keys, :] += dot(share.astype(bf16), slopes[g], NN)
                dk_ref[g, keys, :] += dot(back, queries[g], NN)
                new.append(carry[g] + dot(key, back, TN))
            return tuple(new)

        blank = jnp.zeros((HEAD_SIZE, lanes), f32)
        result = lax.fori_loop(begin, end, chunk, (blank,) * groups)
        cosine, sine = cos_ref[rows, :], sin_ref[rows, :]
        for g in range(groups):
            flat = result[g].T * SCALE
            for h in range(ratio):
                head = g * ratio + h
                qc_ref[rows, head * HEAD_SIZE : (head + 1) * HEAD_SIZE] = turned(
                    flat[h * BLOCK : (h + 1) * BLOCK], cosine, sine, -1
                ).astype(bf16)
        return unused

    lax.fori_loop(0, order.shape[0], one, 0)

    def spread(i, unused):
        target = pl.ds(pl.multiple_of(i * BLOCK, BLOCK), BLOCK)
        for k, out in enumerate(outs):
            block = i * count + order[i, lax.rem(ctx - k + count, count)]
            source = pl.ds(pl.multiple_of(block * BLOCK, BLOCK), BLOCK)
            for g in range(groups):
                out[target, g * HEAD_SIZE : (g + 1) * HEAD_SIZE] = (
                    dk_ref[g, source, :] * SCALE
                ).astype(bf16)
                out[target, width + g * HEAD_SIZE : width + (g + 1) * HEAD_SIZE] = dv_ref[
                    g, source, :
                ].astype(bf16)
        return unused

    lax.fori_loop(0, order.shape[0], spread, 0)


def attend_back(order, starts, place, queries, slopes, att, sums, cosine, sine, pieces):
    count, rows = len(pieces), queries.shape[0]
    groups = pieces[0].shape[1] // (2 * HEAD_SIZE)
    keys = (groups, count * rows, HEAD_SIZE)
    return pl.pallas_call(
        functools.partial(attend_back_kernel, count),
        in_specs=[SCALARS] * 3 + [pl.BlockSpec(memory_space=pltpu.VMEM)] * (6 + count),
        out_specs=[pl.BlockSpec(memory_space=pltpu.VMEM)] * (1 + count),
        out_shape=[jax.ShapeDtypeStruct(queries.shape, bf16)]
        + [jax.ShapeDtypeStruct(pieces[0].shape, bf16)] * count,
        scratch_shapes=[pltpu.VMEM(keys, bf16)] * 2 + [pltpu.VMEM(keys, f32)] * 2,
        compiler_params=params(56),
        cost_estimate=cost(16e9, 2e7),
        name="attend_back",
    )(order, starts, place, queries, slopes, att, sums, cosine, sine, *pieces)


SIDE = 256


def tile_bias(qi_ref, ki_ref, k, q_tile, k_tile, ratio):
    rows = slice(q_tile * SIDE, (q_tile + 1) * SIDE)
    keys = ki_ref[k, k_tile * SIDE : (k_tile + 1) * SIDE, :]
    allowed = (keys <= qi_ref[0:1, rows]) & (keys >= qi_ref[1:2, rows])
    bias = jnp.where(allowed, 0.0, masked_score)
    return jnp.concatenate([bias] * ratio, axis=1)


def flat_heads(ref, q_tile, group, ratio):
    return jnp.concatenate(
        [
            ref[
                q_tile * SIDE : (q_tile + 1) * SIDE,
                (group * ratio + h) * HEAD_SIZE : (group * ratio + h + 1) * HEAD_SIZE,
            ]
            for h in range(ratio)
        ],
        axis=0,
    )


def head_lanes(g, offset=0):
    return slice(offset + g * HEAD_SIZE, offset + (g + 1) * HEAD_SIZE)


def dense_begin(q_ref, groups, ratio, qt_ref, top_ref, total_ref, att_ref):
    for q_tile in range(q_ref.shape[0] // SIDE):
        for g in range(groups):
            flat = flat_heads(q_ref, q_tile, g, ratio)
            qt_ref[q_tile * groups + g] = flat.astype(f32).T.astype(bf16)
    top_ref[...] = jnp.full(top_ref.shape, masked_score, f32)
    total_ref[...] = jnp.zeros(total_ref.shape, f32)
    att_ref[...] = jnp.zeros(att_ref.shape, f32)


def dense_piece(k, kv_ref, qi_ref, ki_ref, groups, ratio, qt_ref, top_ref, total_ref, att_ref):
    width = groups * HEAD_SIZE
    for q_tile in range(qi_ref.shape[1] // SIDE):
        for k_tile in range(q_tile, -1, -1):
            bias = tile_bias(qi_ref, ki_ref, k, q_tile, k_tile, ratio)
            rows = slice(k_tile * SIDE, (k_tile + 1) * SIDE)
            for g in range(groups):
                i = q_tile * groups + g
                raw = dot(kv_ref[k, rows, head_lanes(g)], qt_ref[i], NN) * SCALE2 + bias
                top = top_ref[i]
                new_top = jnp.maximum(top, jnp.max(raw, axis=0, keepdims=True))
                weights = jnp.exp2(raw - new_top)
                back = jnp.exp2(top - new_top)
                top_ref[i] = new_top
                total_ref[i] = total_ref[i] * back + jnp.sum(weights, axis=0, keepdims=True)
                att_ref[i] = att_ref[i] * back + dot(
                    kv_ref[k, rows, head_lanes(g, width)], weights.astype(bf16), TN
                )


def dense_end(groups, ratio, top_ref, total_ref, att_ref, sum_ref, low_ref):
    for i in range(att_ref.shape[0]):
        q_tile, g = divmod(i, groups)
        out = att_ref[i] * (1.0 / total_ref[i])
        att_ref[i] = out
        sum_ref[i] = top_ref[i] + jnp.log2(total_ref[i])
        flat = out.T.astype(bf16)
        for h in range(ratio):
            low_ref[q_tile * SIDE : (q_tile + 1) * SIDE, head_lanes(g * ratio + h)] = flat[
                h * SIDE : (h + 1) * SIDE
            ]


def dense_shapes(rows, groups, ratio):
    tiles = rows // SIDE * groups
    return tiles, ratio * SIDE


FEED_TILES = 12
TILES = 17
SLOTS = 8


def back_kernel(
    part_hbm, feed_hbm, cot_hbm, middle_hbm, gain_ref, act_hbm, mid_normed_hbm, x_hbm, normed_hbm,
    low_ref, q_ref, kv_ref, att_ref, sum_ref, qi_ref, ki_ref, cos_ref, sin_ref, weight_hbm,
    feed_other, back_middle, part2_out, part2_other, grads_ref, held_hbm, far_hbm,
    lhs, mid, part, part_other, w_out, w_in, rhs, q2, q2t, d2, d2t, delta, bias_ref, dq_ref,
    kv_sent, kv_got, cot, gain_rows, gain_other, gain_columns,
    p_send, p_keep, c_got, s_one, own, y_got, z_got,
    load_sem, act_sem, x_send, x_recv, c_send, c_recv, c_free, held_sem, y_send, y_recv, own_sem,
    z_send, z_recv, k_send, k_recv,
):
    ctxs = lax.axis_size("ctx")
    dp, ctx, tp = lax.axis_index("dp"), lax.axis_index("ctx"), lax.axis_index("tp")
    pair_at, core_at = dp // 2, lax.rem(dp, 2)
    far, core = (lax.rem(dp + 2, 4), ctx, tp), (dp + 1 - 2 * core_at, ctx, tp)
    after, before = (dp, lax.rem(ctx + 1, ctxs), tp), (dp, lax.rem(ctx + ctxs - 1, ctxs), tp)
    across = (dp, ctx, 1 - tp)
    rows, width = mid.shape
    section = width // 4
    piece = section // ctxs
    groups = kv_ref.shape[2] // (2 * HEAD_SIZE)
    kv_width = groups * HEAD_SIZE
    ratio = q_ref.shape[1] // kv_width
    q_cols = q_ref.shape[1]

    barrier = pltpu.get_barrier_semaphore()
    for device in (after, before, far, core, across):
        pl.semaphore_signal(barrier, inc=1, device_id=device, device_id_type=MESH)
    pl.semaphore_wait(barrier, 5)

    def remote(source, target, device, sent, got):
        return pltpu.make_async_remote_copy(source, target, sent, got, device, MESH)

    def load(source, target, index):
        return pltpu.make_async_copy(source, target, load_sem.at[index])


    def product(t, lhs_of, rhs_of):
        slot = lax.rem(t, 2)

        @pl.when(t >= 2)
        def _():
            core_copy(t - 2).wait_send()

        for c, out in ((1, p_send), (0, p_keep)):
            for y in range(2):
                there = lax.rem(pair_at + y + 1, 2) * 2 + lax.rem(core_at + c, 2)
                start = pl.multiple_of(there * section, LANES)
                result = rhs_of(start, lhs_of(pl.ds(start, section)))
                for z in range(ctxs):
                    place = lax.rem(z + 2 * ctxs - ctx - 1, ctxs)
                    target = pl.ds(pl.multiple_of(y * section + place * piece, piece), piece)
                    out[slot, target, :] = result[z * piece : (z + 1) * piece]

        @pl.when(t >= 4)
        def _():
            pl.semaphore_wait(c_free, 1)

        core_copy(t).start()

    def core_copy(t):
        return remote(
            p_send.at[lax.rem(t, 2)], c_got.at[lax.rem(t, 4)], core, c_send.at[t], c_recv.at[t]
        )

    def held_copy(t):
        return pltpu.make_async_copy(s_one.at[lax.rem(t, 2)], held_hbm.at[t], held_sem.at[t])

    def meet_core(t):
        core_copy(t).wait_recv()
        slot, got = lax.rem(t, 2), lax.rem(t, 4)

        def add(i, unused):
            part_rows = pl.ds(pl.multiple_of(i * piece, piece), piece)
            total = p_keep[slot, part_rows, :].astype(f32) + c_got[got, part_rows, :].astype(f32)
            s_one[slot, part_rows, :] = total.astype(bf16)
            return unused

        lax.fori_loop(0, 2 * section // piece, add, 0)

        @pl.when(t + 4 < TILES)
        def _():
            pl.semaphore_signal(c_free, inc=1, device_id=core, device_id_type=MESH)

        held_copy(t).start()

    def far_copy(t):
        return remote(
            held_hbm.at[t, pl.ds(0, section)], far_hbm.at[t], far, y_send.at[t], y_recv.at[t]
        )

    def send_far(t):
        held_copy(t).wait()
        far_copy(t).start()

    def own_copy(t):
        return pltpu.make_async_copy(
            held_hbm.at[t, pl.ds(section, section)], own.at[lax.rem(t, SLOTS)], own_sem.at[t, 0]
        )

    def got_copy(t):
        return pltpu.make_async_copy(far_hbm.at[t], y_got.at[lax.rem(t, 2)], own_sem.at[t, 1])

    def ring_copy(t, step):
        return remote(
            own.at[lax.rem(t, SLOTS), pl.ds((ctxs - 2 - step) * piece, piece)],
            z_got.at[t, step], after, z_send.at[t, step], z_recv.at[t, step],
        )

    def ring_add(t, step):
        ring_copy(t, step).wait_recv()
        ring_copy(t, step).wait_send()
        place = ctxs - 3 - step if step < ctxs - 2 else ctxs - 1
        target = pl.ds(place * piece, piece)
        total = own[lax.rem(t, SLOTS), target, :].astype(f32) + z_got[t, step].astype(f32)
        if step < ctxs - 2:
            own[lax.rem(t, SLOTS), target, :] = total.astype(bf16)
            ring_copy(t, step + 1).start()
        else:
            grads_ref[t] = total

    def tick(n):
        for step in range(ctxs - 2, -1, -1):

            t = n - 3 - 2 * step

            @pl.when((t >= 0) & (t < TILES))
            def _(t=t, step=step):
                ring_add(t, step)

        @pl.when((n >= 1) & (n - 1 < TILES))
        def _():
            t = n - 1
            own_copy(t).wait()
            got_copy(t).wait()
            slot, got = lax.rem(t, SLOTS), lax.rem(t, 2)
            for z in range(ctxs):
                target = pl.ds(z * piece, piece)
                total = own[slot, target, :].astype(f32) + y_got[got, target, :].astype(f32)
                own[slot, target, :] = total.astype(bf16)
            ring_copy(t, 0).start()

        @pl.when(n < TILES)
        def _():
            far_copy(n).wait_recv()
            own_copy(n).start()
            got_copy(n).start()


    part_copy = remote(part_hbm, part_other, across, x_send.at[0], x_recv.at[0])
    part_copy.start()
    feed_copy = remote(feed_hbm, feed_other, across, x_send.at[1], x_recv.at[1])
    feed_copy.start()

    def act_copy(t):
        columns = pl.ds(pl.multiple_of(lax.rem(t, 4) * TILE, TILE), TILE)
        return pltpu.make_async_copy(
            act_hbm.at[t // 4, :, columns], rhs.at[lax.rem(t, 2)], act_sem.at[t]
        )

    loads = [
        load(mid_normed_hbm, lhs.at[0], 0),
        load(cot_hbm, lhs.at[1], 1),
        load(part_hbm, part, 2),
        load(middle_hbm, mid, 3),
        load(weight_hbm.at[:, pl.ds(2 * q_cols + LANES, q_cols)], w_out, 4),
        load(weight_hbm.at[:, pl.ds(0, 2 * q_cols)], w_in, 5),
    ]
    act_copy(0).start()
    for copy in loads:
        copy.start()
    loads[0].wait()
    loads[1].wait()

    def plain(t):
        def times(start, left):
            return dot(left, rhs[lax.rem(t, 2)], TN).astype(bf16)

        return times

    def feed_step(t, unused):
        act_copy(t).wait()

        @pl.when(t + 1 < FEED_TILES)
        def _():
            act_copy(t + 1).start()

        product(t, lambda lanes: lhs[t // 8, :, lanes], plain(t))

        @pl.when(t >= 1)
        def _():
            meet_core(t - 1)

        @pl.when(t >= 2)
        def _():
            send_far(t - 2)

        @pl.when((t >= 5) & (lax.rem(t, 3) == 2))
        def _():
            tick((t - 5) // 3)

        return unused

    lax.fori_loop(0, FEED_TILES, feed_step, 0)
    meet_core(FEED_TILES - 1)
    send_far(FEED_TILES - 2)
    send_far(FEED_TILES - 1)

    for q_tile in range(rows // SIDE):
        for g in range(groups):
            flat = flat_heads(q_ref, q_tile, g, ratio)
            q2[q_tile * groups + g] = flat
            q2t[q_tile * groups + g] = flat.astype(f32).T.astype(bf16)
    dq_ref[...] = jnp.zeros(dq_ref.shape, f32)
    kv_got[0] = jnp.zeros(kv_got.shape[1:], bf16)
    gain_rows[...] = jnp.zeros(gain_rows.shape, f32)


    loads[2].wait()
    loads[3].wait()
    part_copy.wait_recv()
    few = 64

    def norm_rows(i, unused):
        here = pl.ds(pl.multiple_of(i * few, few), few)
        field = mid[here, :]
        scale = lax.rsqrt(jnp.mean(field * field, axis=1, keepdims=True) + epsilon)
        unit = field * scale
        back = part[here, :].astype(f32) + part_other[here, :].astype(f32)
        gain_rows[1:2, :] += jnp.sum(back * unit, axis=0, keepdims=True)
        inner = back * gain_ref[1:2, :]
        out = lhs[1, here, :].astype(f32) + scale * (
            inner - unit * jnp.mean(inner * unit, axis=1, keepdims=True)
        )
        mid[here, :] = out
        lhs[0, here, :] = out.astype(bf16)
        return unused

    lax.fori_loop(0, rows // few, norm_rows, 0)
    middle_copy = load(mid, back_middle, 6)
    middle_copy.start()
    normed_copy = load(normed_hbm, lhs.at[1], 7)
    normed_copy.start()
    x_copy = load(x_hbm, part, 8)
    x_copy.start()
    loads[4].wait()
    cot[:, :q_cols] = dot(lhs[0], w_out[...], NN).astype(bf16)
    for q_tile in range(rows // SIDE):
        for g in range(groups):
            i = q_tile * groups + g
            flat = flat_heads(cot, q_tile, g, ratio)
            turned_flat = flat.astype(f32).T
            d2[i] = flat
            d2t[i] = turned_flat.astype(bf16)
            delta[i] = jnp.sum(turned_flat * att_ref[i], axis=0, keepdims=True)
    tick(jnp.int32(3))

    t_out = jnp.int32(FEED_TILES)
    product(
        t_out, lambda lanes: lhs[0, :, lanes], lambda start, left: dot(left, low_ref[:, :TILE], TN).astype(bf16)
    )


    def kv_copy(s):
        return remote(kv_sent.at[s], kv_got.at[s + 1], after, k_send.at[s], k_recv.at[s])

    def back_piece(s, unused):
        k = lax.rem(s + 1, ctxs)
        pairs = [(q, kk) for kk in range(rows // SIDE) for q in range(kk, rows // SIDE)]
        for index, (q_tile, k_tile) in enumerate(pairs):
            bias_ref[index] = tile_bias(qi_ref, ki_ref, k, q_tile, k_tile, ratio)
        sums = []
        for k_tile in range(rows // SIDE):
            here = slice(k_tile * SIDE, (k_tile + 1) * SIDE)
            for g in range(groups):
                key, value = kv_ref[k, here, head_lanes(g)], kv_ref[k, here, head_lanes(g, kv_width)]
                d_key = d_value = None
                for index, (q_tile, which) in enumerate(pairs):
                    if which != k_tile:
                        continue
                    i = q_tile * groups + g
                    raw = dot(key, q2t[i], NN) * SCALE2 + bias_ref[index]
                    share = jnp.exp2(raw - sum_ref[i])
                    back_share = dot(value, d2t[i], NN)
                    back = (share * (back_share - delta[i])).astype(bf16)
                    one_value = dot(share.astype(bf16), d2[i], NN)
                    one_key = dot(back, q2[i], NN)
                    d_value = one_value if d_value is None else d_value + one_value
                    d_key = one_key if d_key is None else d_key + one_key
                    dq_ref[i] += dot(key, back, TN)
                kv_sent[s, here, head_lanes(g)] = (d_key * SCALE).astype(bf16)
                kv_sent[s, here, head_lanes(g, kv_width)] = d_value.astype(bf16)

        @pl.when(s >= 1)
        def _():
            kv_copy(s - 1).wait_recv()

            def add(i, unused):
                here = pl.ds(pl.multiple_of(i * few, few), few)
                total = kv_sent[s, here, :].astype(f32) + kv_got[s, here, :].astype(f32)
                kv_sent[s, here, :] = total.astype(bf16)
                return unused

            lax.fori_loop(0, rows // few, add, 0)

        @pl.when(s < ctxs - 1)
        def _():
            kv_copy(s).start()

        @pl.when(s == 0)
        def _():
            meet_core(t_out)
            send_far(t_out)

        @pl.when(s < ctxs - 1)
        def _():
            tick(5 + s)

        return unused

    tick(jnp.int32(4))
    lax.fori_loop(0, ctxs, back_piece, 0)


    for i in range(dq_ref.shape[0]):
        q_tile, g = divmod(i, groups)
        here = slice(q_tile * SIDE, (q_tile + 1) * SIDE)
        flat = dq_ref[i].T * SCALE
        for h in range(ratio):
            cot[here, head_lanes(g * ratio + h)] = turned(
                flat[h * SIDE : (h + 1) * SIDE], cos_ref[here, :], sin_ref[here, :], -1
            ).astype(bf16)
    for g in range(groups):
        cot[:, head_lanes(g, q_cols)] = turned(
            kv_sent[ctxs - 1, :, head_lanes(g)].astype(f32), cos_ref[...], sin_ref[...], -1
        ).astype(bf16)
    cot[:, q_cols + kv_width :] = kv_sent[ctxs - 1, :, kv_width:]
    loads[5].wait()
    x_copy.wait()
    x_rows = part[...].astype(f32)
    scale = lax.rsqrt(jnp.mean(x_rows * x_rows, axis=1, keepdims=True) + epsilon)
    for j in range(width // TILE):
        lanes = slice(j * TILE, (j + 1) * TILE)
        back = dot(cot[...], w_in[lanes, :], NT)
        part_other[:, lanes] = back.astype(bf16)
        gain_rows[0:1, lanes] += jnp.sum(back * (part[:, lanes].astype(f32) * scale), axis=0, keepdims=True)
    gain_copy = remote(gain_rows.at[pl.ds(0, 8)], gain_other, across, x_send.at[2], x_recv.at[2])
    gain_copy.start()
    part2_copy = remote(part_other, part2_other, across, x_send.at[3], x_recv.at[3])
    part2_copy.start()
    part2_save = load(part_other, part2_out, 9)
    part2_save.start()
    normed_copy.wait()

    def qkv_step(j, unused):
        t = FEED_TILES + 1 + j

        def times(start, left):
            lanes = pl.ds(pl.multiple_of(j * TILE, TILE), TILE)
            return dot(left, cot[:, lanes], TN).astype(bf16)

        product(t, lambda lanes: lhs[1, :, lanes], times)

        @pl.when(j >= 1)
        def _():
            meet_core(t - 1)

        @pl.when(j >= 2)
        def _():
            send_far(t - 2)

        tick(4 + ctxs + j)
        return unused

    lax.fori_loop(0, 3, qkv_step, 0)
    gain_copy.wait_recv()
    gain_copy.wait_send()
    gain_rows[0:1, :] += gain_other[0:1, :]
    gain_columns[...] = gain_rows[...].T
    last = jnp.int32(TILES - 1)
    tail = q_cols - TILE

    def times_last(start, left):
        some = dot(left, low_ref[:, TILE:], TN)
        gains = gain_columns[pl.ds(start, section), :]
        spare = jnp.zeros((section, TILE - tail - LANES), f32)
        return jnp.concatenate([some, gains, spare], axis=1).astype(bf16)

    product(last, lambda lanes: lhs[0, :, lanes], times_last)
    meet_core(last - 1)
    send_far(last - 2)
    meet_core(last)
    send_far(last - 1)
    send_far(last)

    def drain(n, unused):
        tick(n)
        return unused

    lax.fori_loop(7 + ctxs, TILES + 2 * ctxs - 1, drain, 0)

    for t in (TILES - 2, TILES - 1):
        core_copy(jnp.int32(t)).wait_send()

    def far_done(t, unused):
        far_copy(t).wait_send()
        return unused

    lax.fori_loop(0, TILES, far_done, 0)
    for s in range(ctxs - 1):
        kv_copy(s).wait_send()
    part_copy.wait_send()
    feed_copy.wait()
    part2_copy.wait()
    part2_save.wait()
    middle_copy.wait()


def back_all(part, feed, cotangent, middle, gains, act, mid_normed, x, normed, low, queries, kv, att, sums, qi, ki, cosine, sine, weights, ctxs):
    rows, width = x.shape
    q_cols = queries.shape[1]
    groups = kv.shape[2] // (2 * HEAD_SIZE)
    ratio = q_cols // (groups * HEAD_SIZE)
    tiles, lanes = dense_shapes(rows, groups, ratio)
    section = width // 4
    piece = section // ctxs
    vmem, hbm = pl.BlockSpec(memory_space=pltpu.VMEM), pl.BlockSpec(memory_space=pl.ANY)
    full = jax.ShapeDtypeStruct((rows, width), bf16)
    sems = lambda *n: pltpu.SemaphoreType.DMA(n)
    space = lambda *shape: pltpu.VMEM(shape, bf16)
    wide = lambda *shape: pltpu.VMEM(shape, f32)
    pairs = (rows // SIDE) * (rows // SIDE + 1) // 2
    return pl.pallas_call(
        back_kernel,
        in_specs=[hbm] * 4 + [vmem] + [hbm] * 4 + [vmem] * 9 + [hbm],
        out_specs=[hbm] * 4 + [vmem] + [hbm] * 2,
        out_shape=[
            full,
            jax.ShapeDtypeStruct((rows, width), f32),
            full,
            full,
            jax.ShapeDtypeStruct((TILES, piece, TILE), f32),
            jax.ShapeDtypeStruct((TILES, 2 * section, TILE), bf16),
            jax.ShapeDtypeStruct((TILES, section, TILE), bf16),
        ],
        scratch_shapes=[
            space(2, rows, width), wide(rows, width), space(rows, width), space(rows, width),
            space(width, q_cols), space(width, 2 * q_cols), space(2, rows, TILE),
            space(tiles, lanes, HEAD_SIZE), space(tiles, HEAD_SIZE, lanes),
            space(tiles, lanes, HEAD_SIZE), space(tiles, HEAD_SIZE, lanes),
            wide(tiles, 1, lanes), wide(pairs, SIDE, lanes), wide(tiles, HEAD_SIZE, lanes),
            space(ctxs, rows, q_cols), space(ctxs, rows, q_cols), space(rows, 2 * q_cols),
            wide(LANES, width), wide(8, width), wide(width, LANES),
            space(2, 2 * section, TILE), space(2, 2 * section, TILE), space(4, 2 * section, TILE),
            space(2, 2 * section, TILE), space(SLOTS, section, TILE), space(2, section, TILE),
            space(TILES, ctxs - 1, piece, TILE),
            sems(10), sems(FEED_TILES), sems(4), sems(4), sems(TILES), sems(TILES),
            pltpu.SemaphoreType.REGULAR, sems(TILES), sems(TILES), sems(TILES), sems(TILES, 2),
            sems(TILES, ctxs - 1), sems(TILES, ctxs - 1), sems(ctxs - 1), sems(ctxs - 1),
        ],
        compiler_params=pltpu.CompilerParams(
            vmem_limit_bytes=63 * MIB, collective_id=1, has_side_effects=True
        ),
        cost_estimate=cost(4e10, 1e8),
        name="back_all",
    )(part, feed, cotangent, middle, gains, act, mid_normed, x, normed, low, queries, kv, att, sums, qi, ki, cosine, sine, weights)


def output_kernel(a_ref, w_ref, o_ref):
    o_ref[...] = dot(a_ref[...], w_ref[...], NT).astype(bf16)


def output_product(attended, weights, column, features):
    rows, inner = attended.shape
    return pl.pallas_call(
        output_kernel,
        grid=(2,),
        in_specs=[
            whole(attended.shape),
            pl.BlockSpec((features // 2, inner), lambda j: (j, column)),
        ],
        out_specs=pl.BlockSpec((rows, features // 2), lambda j: (0, j)),
        out_shape=jax.ShapeDtypeStruct((rows, features), bf16),
        compiler_params=params(40),
        cost_estimate=cost(2 * rows * inner * features, 2 * inner * features),
        name="output_product",
    )(attended, weights)


def feed_kernel(
    x_ref, mine_ref, other_ref, gain_ref, cot_ref, gate_ref, up_ref, down_ref,
    middle_ref, normed_ref, act_ref, back_ref, feed_ref, total_ref, feed_total,
):
    step = pl.program_id(0)

    @pl.when(step == 0)
    def _():
        middle = (
            x_ref[...].astype(f32) + mine_ref[...].astype(f32) + other_ref[...].astype(f32)
        )
        middle_ref[...] = middle
        scale = lax.rsqrt(jnp.mean(middle * middle, axis=1, keepdims=True) + epsilon)
        normed_ref[...] = (middle * scale * gain_ref[1:2, :]).astype(bf16)

    gate = dot(normed_ref[...], gate_ref[...], NN)
    upward = dot(normed_ref[...], up_ref[...], NN)
    back_mixed = dot(cot_ref[...], down_ref[...], NN)
    sigmoid = 1.0 / (1.0 + jnp.exp(-gate))
    activated = gate * sigmoid
    mixed = (activated * upward).astype(bf16)
    back_gate = (back_mixed * upward * sigmoid * (1.0 + gate * (1.0 - sigmoid))).astype(bf16)
    back_up = (back_mixed * activated).astype(bf16)
    act_ref[0] = back_gate
    act_ref[1] = back_up
    act_ref[2] = mixed
    part = dot(back_gate, gate_ref[...], NT) + dot(back_up, up_ref[...], NT)
    feed = dot(mixed, down_ref[...], NT)

    @pl.when(step == 0)
    def _():
        total_ref[...] = part
        feed_total[...] = feed

    @pl.when(step > 0)
    def _():
        total_ref[...] += part
        feed_total[...] += feed

    @pl.when(step == pl.num_programs(0) - 1)
    def _():
        back_ref[...] = total_ref[...].astype(bf16)
        feed_ref[...] = feed_total[...].astype(bf16)


def feed_forward(x, mine, other, gains, cotangent, gate, up, down):
    rows, width = x.shape
    hidden = gate.shape[1]
    steps = hidden // TILE
    tile_of = pl.BlockSpec((width, TILE), lambda j: (0, j))
    acts_of = pl.BlockSpec((3, rows, TILE), lambda j: (0, 0, j))
    full = whole((rows, width))
    return pl.pallas_call(
        feed_kernel,
        grid=(steps,),
        in_specs=[full, full, full, whole(gains.shape), full]
        + [tile_of] * 3,
        out_specs=[full, full, acts_of, full, full],
        out_shape=[
            jax.ShapeDtypeStruct((rows, width), f32),
            jax.ShapeDtypeStruct((rows, width), bf16),
            jax.ShapeDtypeStruct((3, rows, hidden), bf16),
            jax.ShapeDtypeStruct((rows, width), bf16),
            jax.ShapeDtypeStruct((rows, width), bf16),
        ],
        scratch_shapes=[pltpu.VMEM((rows, width), f32)] * 2,
        compiler_params=params(56),
        cost_estimate=cost(12 * rows * width * hidden, 6 * width * hidden),
        name="feed_forward",
    )(x, mine, other, gains, cotangent, gate, up, down)


def middle_kernel(cot_ref, mine_ref, other_ref, middle_ref, gain_ref, w_ref, bm_ref, bb_ref, ba_ref, grad_ref):
    middle = middle_ref[...]
    scale = lax.rsqrt(jnp.mean(middle * middle, axis=1, keepdims=True) + epsilon)
    unit = middle * scale
    back = mine_ref[...].astype(f32) + other_ref[...].astype(f32)
    grad_ref[...] = jnp.sum(back * unit, axis=0, keepdims=True)
    inner = back * gain_ref[1:2, :]
    out = cot_ref[...].astype(f32) + scale * (
        inner - unit * jnp.mean(inner * unit, axis=1, keepdims=True)
    )
    bm_ref[...] = out
    low = out.astype(bf16)
    bb_ref[...] = low
    ba_ref[...] = dot(low, w_ref[...], NN).astype(bf16)


def middle_back(cotangent, mine, other, middle, gains, weights, column, inner):
    rows, width = middle.shape
    full = whole((rows, width))
    return pl.pallas_call(
        middle_kernel,
        grid=(1,),
        in_specs=[full, full, full, full, whole(gains.shape)]
        + [pl.BlockSpec((width, inner), lambda j: (0, column))],
        out_specs=[full, full, whole((rows, inner)), whole((1, width))],
        out_shape=[
            jax.ShapeDtypeStruct((rows, width), f32),
            jax.ShapeDtypeStruct((rows, width), bf16),
            jax.ShapeDtypeStruct((rows, inner), bf16),
            jax.ShapeDtypeStruct((1, width), f32),
        ],
        compiler_params=params(56),
        cost_estimate=cost(2 * rows * width * inner, 1.5e7),
        name="middle_back",
    )(cotangent, mine, other, middle, gains, weights)


def inputs_kernel(count, x_ref, qc_ref, cos_ref, sin_ref, w_ref, *refs):
    parts = refs[:count]
    cot_ref, back_ref, grad_ref = refs[count:]
    half = qc_ref.shape[1] // 2
    cot_ref[:, : 2 * half] = qc_ref[...]
    total = parts[0][...].astype(f32)
    for part in parts[1:]:
        total += part[...].astype(f32)
    for h in range(half // HEAD_SIZE):
        lanes = slice(h * HEAD_SIZE, (h + 1) * HEAD_SIZE)
        there = slice(2 * half + h * HEAD_SIZE, 2 * half + (h + 1) * HEAD_SIZE)
        cot_ref[:, there] = turned(total[:, lanes], cos_ref[...], sin_ref[...], -1).astype(bf16)
    cot_ref[:, 3 * half :] = total[:, half:].astype(bf16)
    back = dot(cot_ref[...], w_ref[...], NT)
    back_ref[...] = back.astype(bf16)
    x = x_ref[...].astype(f32)
    unit = x * lax.rsqrt(jnp.mean(x * x, axis=1, keepdims=True) + epsilon)
    grad_ref[...] = jnp.sum(back * unit, axis=0, keepdims=True)


def inputs_back(x, qc, cosine, sine, weights, parts):
    rows, width = x.shape
    inner = 2 * qc.shape[1]
    full = whole((rows, width))
    return pl.pallas_call(
        functools.partial(inputs_kernel, len(parts)),
        grid=(1,),
        in_specs=[full, whole(qc.shape), whole(cosine.shape), whole(sine.shape)]
        + [pl.BlockSpec((width, inner), lambda j: (0, 0))]
        + [whole(parts[0].shape)] * len(parts),
        out_specs=[whole((rows, inner)), full, whole((1, width))],
        out_shape=[
            jax.ShapeDtypeStruct((rows, inner), bf16),
            jax.ShapeDtypeStruct((rows, width), bf16),
            jax.ShapeDtypeStruct((1, width), f32),
        ],
        compiler_params=params(56),
        cost_estimate=cost(2 * rows * width * inner, 1.5e7),
        name="inputs_back",
    )(x, qc, cosine, sine, weights, *parts)


def final_kernel(bm_ref, mine_ref, other_ref, x_ref, gain_ref, o_ref):
    x = x_ref[...].astype(f32)
    scale = lax.rsqrt(jnp.mean(x * x, axis=1, keepdims=True) + epsilon)
    unit = x * scale
    inner = (mine_ref[...].astype(f32) + other_ref[...].astype(f32)) * gain_ref[0:1, :]
    out = bm_ref[...] + scale * (inner - unit * jnp.mean(inner * unit, axis=1, keepdims=True))
    o_ref[...] = out.astype(bf16)


def final_back(back_middle, mine, other, x, gains):
    rows, width = x.shape
    block = pl.BlockSpec((rows // 4, width), lambda j: (j, 0))
    return pl.pallas_call(
        final_kernel,
        grid=(4,),
        in_specs=[block] * 4 + [whole(gains.shape)],
        out_specs=block,
        out_shape=jax.ShapeDtypeStruct((rows, width), bf16),
        compiler_params=params(40),
        cost_estimate=cost(1e6, 1e7),
        name="final_back",
    )(back_middle, mine, other, x, gains)


def relative(field, pairs, ctxs):
    dp, ctx = lax.axis_index("dp"), lax.axis_index("ctx")
    shaped = field.reshape((pairs, 2, ctxs, -1) + field.shape[1:])
    for axis, shift in ((0, dp // 2 + 1), (1, dp % 2 + 1), (2, ctx + 1)):
        shaped = jnp.roll(shaped, -shift, axis)
    return shaped.swapaxes(0, 1).reshape(field.shape)


def gradient_kernel(pairs, ctxs, place, a_ref, b_ref, send_ref, keep_ref):
    width = a_ref.shape[1]
    section = width // (2 * pairs)
    piece = section // ctxs
    for c, out in ((1, send_ref), (0, keep_ref)):
        for y in range(pairs):
            pair = lax.rem(place[0] + y + 1, pairs)
            core = lax.rem(place[1] + c, 2)
            lanes = pl.ds(pl.multiple_of((pair * 2 + core) * section, LANES), section)
            result = dot(a_ref[:, lanes], b_ref[...], TN).astype(bf16)
            for z in range(ctxs):
                far = lax.rem(z + ctxs - place[2] - 1 + ctxs, ctxs)
                rows = pl.ds(pl.multiple_of(y * section + far * piece, piece), piece)
                out[rows, :] = result[z * piece : (z + 1) * piece]


def gradient(a, b, pairs, ctxs):
    rows, width = a.shape
    columns = b.shape[1]
    section = width // (2 * pairs)
    if section % LANES or (section // ctxs) % 32:
        ordered = relative(dot(a, b, TN).astype(bf16), pairs, ctxs)
        return ordered[: width // 2], ordered[width // 2 :]
    dp, ctx = lax.axis_index("dp"), lax.axis_index("ctx")
    place = jnp.stack([dp // 2, dp % 2, ctx]).astype(jnp.int32)
    tile = TILE if columns % TILE == 0 else columns // 2
    block = pl.BlockSpec((width // 2, tile), lambda j: (0, j))
    return pl.pallas_call(
        functools.partial(gradient_kernel, pairs, ctxs),
        grid=(columns // tile,),
        in_specs=[SCALARS, whole(a.shape), pl.BlockSpec((rows, tile), lambda j: (0, j))],
        out_specs=[block, block],
        out_shape=[jax.ShapeDtypeStruct((width // 2, columns), bf16)] * 2,
        compiler_params=params(40),
        cost_estimate=cost(2 * rows * width * columns, 2 * width * columns),
        name="gradient",
    )(place, a, b)


def shifted(field, axis, steps, stride=1):
    count = lax.axis_size(axis)
    return lax.ppermute(
        field, axis, [(i, (i + steps * stride) % count) for i in range(count)]
    )


def other_core(field):
    return lax.ppermute(field, "dp", [(i, i ^ 1) for i in range(lax.axis_size("dp"))])


def sum_to_owner(send, keep, pairs, ctxs):
    columns = send.shape[1]
    got = other_core(send).reshape(pairs, -1, columns)
    keep = keep.reshape(pairs, -1, columns)
    total = got[-1].astype(f32) + keep[-1].astype(f32)
    for y in range(1, pairs):
        part = (got[y - 1].astype(f32) + keep[y - 1].astype(f32)).astype(bf16)
        total = total + shifted(part, "dp", y, 2).astype(f32)
    total = total.reshape(ctxs, -1, columns)
    result = total[-1]
    for z in range(1, ctxs):
        result = result + shifted(total[z - 1].astype(bf16), "ctx", z).astype(f32)
    return result


def swapped(field):
    count = lax.axis_size("tp")
    return lax.ppermute(field, "tp", [(i, count - 1 - i) for i in range(count)])


def body(
    tokens,
    cotangent,
    lengths,
    block_order,
    pre_gain,
    query_weight,
    key_weight,
    value_weight,
    output_weight,
    mid_gain,
    gate_weight,
    up_weight,
    down_weight,
):
    ctxs = lax.axis_size("ctx")
    pairs = lax.axis_size("dp") // 2
    ctx = lax.axis_index("ctx")
    order = block_order[0]
    ends = jnp.cumsum(lengths[0]).astype(jnp.int32)
    starts = ends - lengths[0]
    place = jnp.stack([ctx]).astype(jnp.int32)
    q_cols = query_weight.shape[1]
    features = tokens.shape[1]

    gain_columns = jnp.pad(jnp.stack([pre_gain, mid_gain], axis=1), ((0, 0), (0, LANES - 2)))
    shard = jnp.concatenate(
        [query_weight, key_weight, value_weight, gain_columns, output_weight], axis=1
    )
    stream = streams(order, ctx)
    lows = jnp.max(jnp.where(starts[None, :] <= stream[0][:, None], starts[None, :], 0), axis=1)
    cosine, sine = angles(stream[0] - lows)
    if pairs == 2 and ctxs == 4 and shard.shape[0] % 32 == 0:
        qi = jnp.pad(jnp.stack([stream[0], lows]), ((0, 6), (0, 0)))
        ki = stream[:, :, None]
        (
            first, gate_full, up_full, down_full, queries, kv, normed, gains,
            attended_low, att, sums, branch, branch_other,
        ) = forward_all(
            shard, gate_weight, up_weight, down_weight, tokens, cosine, sine, qi, ki, q_cols, ctxs
        )
        middle, mid_normed, act, back_part, feed = feed_forward(
            tokens, branch, branch_other, gains, cotangent, gate_full, up_full, down_full
        )
        feed_other, back_middle, part, part_other, grads, _, _ = back_all(
            back_part, feed, cotangent, middle, gains, act, mid_normed, tokens, normed,
            attended_low, queries, kv, att, sums, qi, ki, cosine, sine, first, ctxs,
        )
        result = (middle + feed.astype(f32) + feed_other.astype(f32)).astype(bf16)
        token_gradient = final_back(back_middle, part, part_other, tokens, gains)
        wide = lambda *tiles: jnp.concatenate([grads[t] for t in tiles], axis=1)
        qkv_gradient = wide(13, 14, 15)
        output_gradient = jnp.concatenate([grads[12], grads[16][:, : q_cols - TILE]], axis=1)
        gain_sums = grads[16][:, q_cols - TILE :]
        gate_gradient, up_gradient = wide(0, 1, 2, 3), wide(4, 5, 6, 7)
        down_gradient = wide(8, 9, 10, 11)
    else:
        first, gate_full, up_full, down_full = (
            lax.all_gather(field, ROWS, axis=0, tiled=True)
            for field in (shard, gate_weight, up_weight, down_weight)
        )
        gains = first[:, 2 * q_cols : 2 * q_cols + 8].T.astype(f32)
        queries, kv, normed = project(tokens, gains, cosine, sine, first, q_cols)
        pieces = [kv] + [shifted(kv, "ctx", k) for k in range(1, ctxs)]
        output_weights = first[:, 2 * q_cols + LANES :]
        attended_low, att, sums = attend(order, starts, place, queries, pieces)
        branch = output_product(attended_low, output_weights, 0, features)
        middle, mid_normed, act, back_part, feed = feed_forward(
            tokens, branch, swapped(branch), gains, cotangent, gate_full, up_full, down_full
        )
        back_other = swapped(back_part)
        gate_parts = gradient(mid_normed, act[0], pairs, ctxs)
        up_parts = gradient(mid_normed, act[1], pairs, ctxs)
        down_parts = gradient(cotangent, act[2], pairs, ctxs)
        result = (middle + feed.astype(f32) + swapped(feed).astype(f32)).astype(bf16)

        back_middle, back_branch, back_attended, mid_grad = middle_back(
            cotangent, back_part, back_other, middle, gains, output_weights, 0, q_cols
        )
        output_parts = gradient(back_branch, attended_low, pairs, ctxs)
        back = attend_back(
            order, starts, place, queries, back_attended, att, sums, cosine, sine, pieces
        )
        own_parts = [back[1]] + [shifted(back[1 + k], "ctx", -k) for k in range(1, ctxs)]
        cot, normed_part, pre_grad = inputs_back(
            tokens, back[0], cosine, sine, first, own_parts
        )
        normed_other = swapped(normed_part)
        qkv_parts = gradient(normed, cot, pairs, ctxs)
        token_gradient = final_back(back_middle, normed_part, normed_other, tokens, gains)

        mid_once = jnp.where(lax.axis_index("tp") == 0, mid_grad, 0.0)
        pair = jnp.concatenate([pre_grad, mid_once], axis=0).astype(bf16)
        pair = jnp.pad(pair, ((0, 6), (0, 0))).T
        ordered = relative(pair, pairs, ctxs)
        gain_sums = sum_to_owner(
            ordered[: features // 2], ordered[features // 2 :], pairs, ctxs
        )
        gain_sums = gain_sums + swapped(gain_sums)
        gate_gradient = sum_to_owner(*gate_parts, pairs, ctxs)
        up_gradient = sum_to_owner(*up_parts, pairs, ctxs)
        down_gradient = sum_to_owner(*down_parts, pairs, ctxs)
        output_gradient = sum_to_owner(*output_parts, pairs, ctxs)
        qkv_gradient = sum_to_owner(*qkv_parts, pairs, ctxs)
    return (
        result,
        token_gradient,
        gain_sums[:, 0],
        qkv_gradient[:, :q_cols],
        qkv_gradient[:, q_cols : q_cols + q_cols // 2],
        qkv_gradient[:, q_cols + q_cols // 2 :],
        output_gradient,
        gain_sums[:, 1],
        gate_gradient,
        up_gradient,
        down_gradient,
    )


def solution(mesh):
    rows, split = P(ROWS, None), P(ROWS, "tp")
    return jax.shard_map(
        body,
        mesh=mesh,
        in_specs=(rows, rows, P("dp", None), P("dp", None, None), P(ROWS))
        + (split,) * 4
        + (P(ROWS),)
        + (split,) * 3,
        out_specs=(rows, rows, P(ROWS)) + (split,) * 4 + (P(ROWS),) + (split,) * 3,
        check_vma=False,
    )
```

```python
import functools
import math

import jax
import jax.numpy as jnp
from jax import lax
from jax.experimental import pallas as pl
from jax.experimental.pallas import tpu as pltpu
from jax.sharding import PartitionSpec as P

HEAD_SIZE = 96
HALF = HEAD_SIZE // 2
BLOCK = 64
SPAN = 256
TILE = 512
LANES = 128

epsilon = 1e-05
rotary_base = 100000.0
masked_score = -1e30
SCALE = HEAD_SIZE**-0.5
SCALE2 = SCALE / math.log(2.0)

f32 = jnp.float32
bf16 = jnp.bfloat16
ROWS = ("dp", "ctx")
MIB = 2**20


def dot(left, right, contract):
    return lax.dot_general(
        left, right, ((contract[:1], contract[1:]), ((), ())), preferred_element_type=f32
    )


NN, NT, TN = (1, 0), (1, 1), (0, 0)


def cost(flops, moved):
    return pl.CostEstimate(flops=int(flops), bytes_accessed=int(moved), transcendentals=0)


def params(mib):
    return pltpu.CompilerParams(vmem_limit_bytes=mib * MIB)


def whole(shape):
    return pl.BlockSpec(shape, lambda *_: (0,) * len(shape))


SCALARS = pl.BlockSpec(memory_space=pltpu.SMEM)


def angles(place):
    frequency = rotary_base ** (-(jnp.arange(HALF, dtype=f32) * 2.0 / HEAD_SIZE))
    turn = place.astype(f32)[:, None] * frequency[None, :]
    return (jnp.cos(turn), jnp.sin(turn))


def streams(order, ctx):
    rounds, count = order.shape
    owners = order[:, lax.rem(ctx - jnp.arange(count) + count, count)].T
    blocks = owners + (jnp.arange(rounds, dtype=jnp.int32) * count)[None, :]
    within = jnp.arange(BLOCK, dtype=jnp.int32)
    return (blocks[:, :, None] * BLOCK + within).reshape(count, rounds * BLOCK).astype(jnp.int32)


def turned(head, cosine, sine, sign):
    first, second = head[:, :HALF], head[:, HALF:]
    along = sine if sign > 0 else -sine
    return jnp.concatenate(
        [first * cosine - second * along, second * cosine + first * along], axis=1
    )


def project_kernel(x_ref, gain_ref, cos_ref, sin_ref, w_ref, q_ref, kv_ref, normed_ref):
    step = pl.program_id(0)
    tile = w_ref.shape[1]

    @pl.when(step == 0)
    def _():
        x = x_ref[...].astype(f32)
        scale = lax.rsqrt(jnp.mean(x * x, axis=1, keepdims=True) + epsilon)
        normed_ref[...] = (x * scale * gain_ref[0:1, :]).astype(bf16)

    out = dot(normed_ref[...], w_ref[...], NN)

    def rotated(ref):
        for h in range(tile // HEAD_SIZE):
            lanes = slice(h * HEAD_SIZE, (h + 1) * HEAD_SIZE)
            ref[:, lanes] = turned(out[:, lanes], cos_ref[...], sin_ref[...], 1).astype(bf16)

    @pl.when(step < 2)
    def _():
        rotated(q_ref)

    @pl.when(step == 2)
    def _():
        rotated(kv_ref)

    @pl.when(step == 3)
    def _():
        kv_ref[...] = out.astype(bf16)


def project(x, gains, cosine, sine, weights, q_cols):
    rows, width = x.shape
    tile = q_cols // 2
    return pl.pallas_call(
        project_kernel,
        grid=(4,),
        in_specs=[
            whole(x.shape),
            whole(gains.shape),
            whole(cosine.shape),
            whole(sine.shape),
            pl.BlockSpec((width, tile), lambda j: (0, j)),
        ],
        out_specs=[
            pl.BlockSpec((rows, tile), lambda j: (0, jnp.minimum(j, 1))),
            pl.BlockSpec((rows, tile), lambda j: (0, jnp.maximum(j - 2, 0))),
            whole((rows, width)),
        ],
        out_shape=[
            jax.ShapeDtypeStruct((rows, q_cols), bf16),
            jax.ShapeDtypeStruct((rows, q_cols), bf16),
            jax.ShapeDtypeStruct((rows, width), bf16),
        ],
        compiler_params=params(40),
        cost_estimate=cost(2 * rows * width * 4 * tile, 2 * width * 4 * tile),
        name="project",
    )(x, gains, cosine, sine, weights)


MESH = pl.DeviceIdType.MESH


def forward_kernel(
    query_shard, key_shard, value_shard, gain_shard, out_shard, gate_shard, up_shard, down_shard,
    x_ref, cos_ref, sin_ref, qi_ref, ki_ref,
    full_ref, gate_ref, up_ref, down_ref, q_ref, kv_ref, normed_ref, gain_ref, low_ref, att_ref, sum_ref,
    branch_ref, other_ref,
    w_ref, qt_ref, top_ref, total_ref,
    z_send, z_recv, y_send, y_recv, c_send, c_recv, k_send, k_recv, x_send, x_recv, local,
):
    ctxs = lax.axis_size("ctx")
    dp, ctx, tp = lax.axis_index("dp"), lax.axis_index("ctx"), lax.axis_index("tp")
    far, core = (lax.rem(dp + 2, 4), ctx, tp), (dp + 1 - 2 * lax.rem(dp, 2), ctx, tp)
    after, before = (dp, lax.rem(ctx + 1, ctxs), tp), (dp, lax.rem(ctx + ctxs - 1, ctxs), tp)
    across = (dp, ctx, 1 - tp)
    piece = query_shard.shape[0]
    mine = pl.ds(pl.multiple_of((dp * ctxs + ctx) * piece, piece), piece)
    packs, column = [], 0
    for j, part in enumerate((query_shard, key_shard, value_shard, gain_shard, out_shard)):
        target = w_ref.at[mine, pl.ds(column, part.shape[1])]
        packs.append(pltpu.make_async_copy(part, target, local.at[5 + j]))
        packs[-1].start()
        column += part.shape[1]
    barrier = pltpu.get_barrier_semaphore()
    for device in (after, before, far, core, across):
        pl.semaphore_signal(barrier, inc=1, device_id=device, device_id_type=MESH)
    pl.semaphore_wait(barrier, 5)
    shards = (w_ref.at[mine], gate_shard, up_shard, down_shard)
    wholes = (w_ref, gate_ref, up_ref, down_ref)
    last = ctxs - 1


    def place(group, pair, steps):
        owner = pair * ctxs + lax.rem(ctx - steps + ctxs, ctxs)
        return wholes[group].at[pl.ds(pl.multiple_of(owner * piece, piece), piece)]

    def source(group, steps):
        return place(group, dp, steps) if steps else shards[group]

    def remote(source, target, device, sent, got):
        return pltpu.make_async_remote_copy(source, target, device_id=device, device_id_type=MESH, send_sem=sent, recv_sem=got)

    def ring(group, s):
        return remote(
            source(group, s), place(group, dp, s), after, z_send.at[group, s], z_recv.at[group, s]
        )

    def over(group, s):
        return remote(
            source(group, s), place(group, dp, s), far, y_send.at[group, s], y_recv.at[group, s]
        )

    def aside(group, s):
        return remote(
            source(group, s), place(group, dp, s), core, c_send.at[group, s], c_recv.at[group, s]
        )

    def aside_far(group, s):
        there = place(group, far[0], s)
        return remote(
            there, there, core, c_send.at[group, ctxs + s], c_recv.at[group, ctxs + s]
        )

    def own_copy(group):
        return pltpu.make_async_copy(shards[group], place(group, dp, 0), local.at[group])

    def begin(group):
        over(group, 0).start()
        aside(group, 0).start()
        if group:
            own_copy(group).start()

    def along(group, s):
        ring(group, s - 1).wait_recv()
        if s < last:
            ring(group, s).start()
        over(group, s).start()
        aside(group, s).start()

    def came_over(group, s):
        over(group, s).wait_recv()
        aside_far(group, s).start()

    def gathered(group):
        if group:
            own_copy(group).wait()
        for s in range(ctxs):
            aside(group, s).wait_recv()
            aside_far(group, s).wait_recv()

    first, gate, up, down = range(4)
    for copy in packs:
        copy.wait()
    ring(first, 0).start()
    begin(first)
    x = x_ref[...].astype(f32)
    unit = x * lax.rsqrt(jnp.mean(x * x, axis=1, keepdims=True) + epsilon)
    for s in range(1, ctxs):
        along(first, s)
        came_over(first, s - 1)
    ring(gate, 0).start()
    begin(gate)
    ring(up, 0).start()
    came_over(first, last)
    begin(up)
    gathered(first)
    full = pltpu.make_async_copy(w_ref, full_ref, local.at[4])
    full.start()
    along(gate, 1)

    q_cols = q_ref.shape[1]
    tile = q_cols // 2
    groups = kv_ref.shape[2] // (2 * HEAD_SIZE)
    ratio = q_cols // (groups * HEAD_SIZE)
    gains = w_ref[:, 2 * q_cols : 2 * q_cols + LANES].astype(f32).T[:8]
    gain_ref[...] = gains
    normed_ref[...] = (unit * gains[0:1]).astype(bf16)

    def product(step):
        return dot(normed_ref[...], w_ref[:, step * tile : (step + 1) * tile], NN)

    def rotated(out, store):
        for h in range(tile // HEAD_SIZE):
            lanes = slice(h * HEAD_SIZE, (h + 1) * HEAD_SIZE)
            store(lanes, turned(out[:, lanes], cos_ref[...], sin_ref[...], 1).astype(bf16))

    def key_store(lanes, value):
        kv_ref[0, :, lanes] = value

    rotated(product(2), key_store)
    kv_ref[0, :, tile:] = product(3).astype(bf16)

    def kv_copy(s):
        return remote(kv_ref.at[s], kv_ref.at[s + 1], after, k_send.at[s], k_recv.at[s])

    kv_copy(0).start()
    begin(down)
    for step in range(2):

        def query_store(lanes, value):
            q_ref[:, step * tile + lanes.start : step * tile + lanes.stop] = value

        rotated(product(step), query_store)

    def attention(k):
        dense_piece(k, kv_ref, qi_ref, ki_ref, groups, ratio, qt_ref, top_ref, total_ref, att_ref)

    dense_begin(q_ref, groups, ratio, qt_ref, top_ref, total_ref, att_ref)
    along(gate, 2)
    came_over(gate, 0)
    waits = [
        [lambda: along(up, 1), lambda: along(gate, last), lambda: came_over(gate, 1), lambda: came_over(up, 0)],
        [lambda: ring(down, 0).start(), lambda: came_over(down, 0), lambda: came_over(gate, 2)],
        [lambda: along(up, 2)],
    ]

    def attention_step(k, unused):
        for s in range(1, ctxs):

            @pl.when(k == s)
            def _(s=s):
                kv_copy(s - 1).wait_recv()
                if s < last:
                    kv_copy(s).start()
                for step in waits[s - 1] if s - 1 < len(waits) else []:
                    step()

        attention(k)
        return unused

    lax.fori_loop(0, ctxs, attention_step, 0)
    dense_end(groups, ratio, top_ref, total_ref, att_ref, sum_ref, low_ref)
    branch_ref[...] = dot(low_ref[...], w_ref[:, 2 * q_cols + LANES :], NT).astype(bf16)
    exchange = remote(branch_ref, other_ref, across, x_send.at[0], x_recv.at[0])
    exchange.start()

    along(down, 1)
    came_over(gate, last)
    came_over(up, 1)
    along(up, last)
    came_over(up, 2)
    along(down, 2)
    came_over(down, 1)
    came_over(up, last)
    along(down, last)
    came_over(down, 2)
    came_over(down, last)
    for group in (gate, up, down):
        gathered(group)
    for group in range(4):
        for s in range(ctxs):
            if s < last:
                ring(group, s).wait_send()
            over(group, s).wait_send()
            aside(group, s).wait_send()
            aside_far(group, s).wait_send()
    for s in range(last):
        kv_copy(s).wait_send()
    exchange.wait()
    full.wait()


def forward_all(packed, gate, up, down, x, cosine, sine, qi, ki, q_cols, ctxs):
    rows, width = x.shape
    columns, hidden = sum(part.shape[1] for part in packed), gate.shape[1]
    groups = q_cols // 2 // HEAD_SIZE
    tiles, lanes = dense_shapes(rows, groups, 2)
    vmem, hbm = pl.BlockSpec(memory_space=pltpu.VMEM), pl.BlockSpec(memory_space=pl.ANY)
    sems = lambda *n: pltpu.SemaphoreType.DMA(n)
    shape = jax.ShapeDtypeStruct
    full = shape((rows, width), bf16)
    return pl.pallas_call(
        forward_kernel,
        in_specs=[hbm] * (len(packed) + 3) + [vmem] * 5,
        out_specs=[hbm] * 4 + [vmem] * 9,
        out_shape=[
            shape((width, columns), bf16),
            shape((width, hidden), bf16),
            shape((width, hidden), bf16),
            shape((width, hidden), bf16),
            shape((rows, q_cols), bf16),
            shape((ctxs, rows, q_cols), bf16),
            full,
            shape((8, width), f32),
            shape((rows, q_cols), bf16),
            shape((tiles, HEAD_SIZE, lanes), f32),
            shape((tiles, 1, lanes), f32),
            full,
            full,
        ],
        scratch_shapes=[
            pltpu.VMEM((width, columns), bf16),
            pltpu.VMEM((tiles, HEAD_SIZE, lanes), bf16),
            pltpu.VMEM((tiles, 1, lanes), f32),
            pltpu.VMEM((tiles, 1, lanes), f32),
        ]
        + [sems(4, ctxs - 1)] * 2
        + [sems(4, ctxs)] * 2
        + [sems(4, 2 * ctxs)] * 2
        + [sems(ctxs - 1)] * 2
        + [sems(1)] * 2
        + [sems(5 + len(packed))],
        compiler_params=pltpu.CompilerParams(
            vmem_limit_bytes=56 * MIB, collective_id=0, has_side_effects=True
        ),
        cost_estimate=cost(1e10, 1e8),
        name="forward_all",
    )(*packed, gate, up, down, x, cosine, sine, qi, ki)


def gather_stream(order, ctx, pieces, k_ref, v_ref):
    count, groups = len(pieces), k_ref.shape[0]
    width = groups * HEAD_SIZE

    def fill(i, unused):
        source = pl.ds(pl.multiple_of(i * BLOCK, BLOCK), BLOCK)
        for k, piece in enumerate(pieces):
            block = i * count + order[i, lax.rem(ctx - k + count, count)]
            target = pl.ds(pl.multiple_of(block * BLOCK, BLOCK), BLOCK)
            for g in range(groups):
                lanes = slice(g * HEAD_SIZE, (g + 1) * HEAD_SIZE)
                k_ref[g, target, :] = piece[source, lanes]
                v_ref[g, target, :] = piece[
                    source, width + g * HEAD_SIZE : width + (g + 1) * HEAD_SIZE
                ]
        return unused

    lax.fori_loop(0, order.shape[0], fill, 0)


def reach(starts, first):
    low = jnp.int32(0)
    for j in range(starts.shape[0]):
        low = jnp.where(starts[j] <= first, starts[j], low)
    return low


def row_limits(starts, first, lanes):
    row = first + lax.rem(lax.broadcasted_iota(jnp.int32, (1, lanes), 1), BLOCK)
    low = jnp.zeros((1, lanes), jnp.int32)
    for j in range(starts.shape[0]):
        low = jnp.where(row >= starts[j], starts[j], low)
    return row, low


def stacked(ref, rows, group, ratio):
    return jnp.concatenate(
        [
            ref[rows, (group * ratio + h) * HEAD_SIZE : (group * ratio + h + 1) * HEAD_SIZE]
            for h in range(ratio)
        ],
        axis=0,
    )


def attend_kernel(count, order, starts, place, q_ref, *refs):
    pieces = refs[:count]
    low_ref, att_ref, sum_ref, k_ref, v_ref = refs[count:]
    groups = k_ref.shape[0]
    ratio = q_ref.shape[1] // (groups * HEAD_SIZE)
    lanes = ratio * BLOCK
    ctx = place[0]
    gather_stream(order, ctx, pieces, k_ref, v_ref)

    def one(i, unused):
        first = (i * count + order[i, ctx]) * BLOCK
        row, low = row_limits(starts, first, lanes)
        begin = reach(starts, first) // SPAN
        end = (first + BLOCK - 1) // SPAN + 1
        rows = pl.ds(pl.multiple_of(i * BLOCK, BLOCK), BLOCK)
        queries = [stacked(q_ref, rows, g, ratio) for g in range(groups)]

        def chunk(c, carry):
            keys = pl.ds(pl.multiple_of(c * SPAN, SPAN), SPAN)
            index = c * SPAN + lax.broadcasted_iota(jnp.int32, (SPAN, lanes), 0)
            allowed = (index <= row) & (index >= low)
            new = []
            for g in range(groups):
                top, total, out = carry[g]
                raw = dot(k_ref[g, keys, :], queries[g], NT) * SCALE2
                raw = jnp.where(allowed, raw, masked_score)
                new_top = jnp.maximum(top, jnp.max(raw, axis=0, keepdims=True))
                weights = jnp.where(allowed, jnp.exp2(raw - new_top), 0.0)
                back = jnp.exp2(top - new_top)
                total = total * back + jnp.sum(weights, axis=0, keepdims=True)
                out = out * back + dot(v_ref[g, keys, :], weights.astype(bf16), TN)
                new.append((new_top, total, out))
            return tuple(new)

        blank = (
            jnp.full((1, lanes), masked_score, f32),
            jnp.zeros((1, lanes), f32),
            jnp.zeros((HEAD_SIZE, lanes), f32),
        )
        result = lax.fori_loop(begin, end, chunk, (blank,) * groups)
        for g in range(groups):
            top, total, out = result[g]
            out = out / total
            att_ref[i * groups + g] = out
            sum_ref[pl.ds(i * groups + g, 1), :] = top + jnp.log2(total)
            flat = out.T.astype(bf16)
            for h in range(ratio):
                head = g * ratio + h
                low_ref[rows, head * HEAD_SIZE : (head + 1) * HEAD_SIZE] = flat[
                    h * BLOCK : (h + 1) * BLOCK
                ]
        return unused

    lax.fori_loop(0, order.shape[0], one, 0)


def attend(order, starts, place, queries, pieces):
    count, rows = len(pieces), queries.shape[0]
    groups = pieces[0].shape[1] // (2 * HEAD_SIZE)
    ratio = queries.shape[1] // (groups * HEAD_SIZE)
    rounds, lanes = order.shape[0], ratio * BLOCK
    return pl.pallas_call(
        functools.partial(attend_kernel, count),
        in_specs=[SCALARS] * 3 + [pl.BlockSpec(memory_space=pltpu.VMEM)] * (1 + count),
        out_specs=[pl.BlockSpec(memory_space=pltpu.VMEM)] * 3,
        out_shape=[
            jax.ShapeDtypeStruct(queries.shape, bf16),
            jax.ShapeDtypeStruct((rounds * groups, HEAD_SIZE, lanes), f32),
            jax.ShapeDtypeStruct((rounds * groups, lanes), f32),
        ],
        scratch_shapes=[pltpu.VMEM((groups, count * rows, HEAD_SIZE), bf16)] * 2,
        compiler_params=params(40),
        cost_estimate=cost(8e9, 1e7),
        name="attend",
    )(order, starts, place, queries, *pieces)


def attend_back_kernel(count, order, starts, place, q_ref, d_ref, att_ref, sum_ref, cos_ref, sin_ref, *refs):
    pieces = refs[:count]
    qc_ref = refs[count]
    outs = refs[count + 1 : 2 * count + 1]
    k_ref, v_ref, dk_ref, dv_ref = refs[2 * count + 1 :]
    groups = k_ref.shape[0]
    ratio = q_ref.shape[1] // (groups * HEAD_SIZE)
    lanes = ratio * BLOCK
    width = groups * HEAD_SIZE
    ctx = place[0]
    gather_stream(order, ctx, pieces, k_ref, v_ref)
    dk_ref[...] = jnp.zeros_like(dk_ref)
    dv_ref[...] = jnp.zeros_like(dv_ref)

    def one(i, unused):
        first = (i * count + order[i, ctx]) * BLOCK
        row, low = row_limits(starts, first, lanes)
        begin = reach(starts, first) // SPAN
        end = (first + BLOCK - 1) // SPAN + 1
        rows = pl.ds(pl.multiple_of(i * BLOCK, BLOCK), BLOCK)
        queries = [stacked(q_ref, rows, g, ratio) for g in range(groups)]
        slopes = [stacked(d_ref, rows, g, ratio) for g in range(groups)]
        sums, deltas = [], []
        for g in range(groups):
            sums.append(sum_ref[pl.ds(i * groups + g, 1), :])
            across = slopes[g].astype(f32).T
            deltas.append(jnp.sum(across * att_ref[i * groups + g], axis=0, keepdims=True))

        def chunk(c, carry):
            keys = pl.ds(pl.multiple_of(c * SPAN, SPAN), SPAN)
            index = c * SPAN + lax.broadcasted_iota(jnp.int32, (SPAN, lanes), 0)
            allowed = (index <= row) & (index >= low)
            new = []
            for g in range(groups):
                key, value = k_ref[g, keys, :], v_ref[g, keys, :]
                raw = dot(key, queries[g], NT) * SCALE2
                share = jnp.where(allowed, jnp.exp2(jnp.minimum(raw - sums[g], 0.0)), 0.0)
                back_share = dot(value, slopes[g], NT)
                back = (share * (back_share - deltas[g])).astype(bf16)
                dv_ref[g, keys, :] += dot(share.astype(bf16), slopes[g], NN)
                dk_ref[g, keys, :] += dot(back, queries[g], NN)
                new.append(carry[g] + dot(key, back, TN))
            return tuple(new)

        blank = jnp.zeros((HEAD_SIZE, lanes), f32)
        result = lax.fori_loop(begin, end, chunk, (blank,) * groups)
        cosine, sine = cos_ref[rows, :], sin_ref[rows, :]
        for g in range(groups):
            flat = result[g].T * SCALE
            for h in range(ratio):
                head = g * ratio + h
                qc_ref[rows, head * HEAD_SIZE : (head + 1) * HEAD_SIZE] = turned(
                    flat[h * BLOCK : (h + 1) * BLOCK], cosine, sine, -1
                ).astype(bf16)
        return unused

    lax.fori_loop(0, order.shape[0], one, 0)

    def spread(i, unused):
        target = pl.ds(pl.multiple_of(i * BLOCK, BLOCK), BLOCK)
        for k, out in enumerate(outs):
            block = i * count + order[i, lax.rem(ctx - k + count, count)]
            source = pl.ds(pl.multiple_of(block * BLOCK, BLOCK), BLOCK)
            for g in range(groups):
                out[target, g * HEAD_SIZE : (g + 1) * HEAD_SIZE] = (
                    dk_ref[g, source, :] * SCALE
                ).astype(bf16)
                out[target, width + g * HEAD_SIZE : width + (g + 1) * HEAD_SIZE] = dv_ref[
                    g, source, :
                ].astype(bf16)
        return unused

    lax.fori_loop(0, order.shape[0], spread, 0)


def attend_back(order, starts, place, queries, slopes, att, sums, cosine, sine, pieces):
    count, rows = len(pieces), queries.shape[0]
    groups = pieces[0].shape[1] // (2 * HEAD_SIZE)
    keys = (groups, count * rows, HEAD_SIZE)
    return pl.pallas_call(
        functools.partial(attend_back_kernel, count),
        in_specs=[SCALARS] * 3 + [pl.BlockSpec(memory_space=pltpu.VMEM)] * (6 + count),
        out_specs=[pl.BlockSpec(memory_space=pltpu.VMEM)] * (1 + count),
        out_shape=[jax.ShapeDtypeStruct(queries.shape, bf16)]
        + [jax.ShapeDtypeStruct(pieces[0].shape, bf16)] * count,
        scratch_shapes=[pltpu.VMEM(keys, bf16)] * 2 + [pltpu.VMEM(keys, f32)] * 2,
        compiler_params=params(56),
        cost_estimate=cost(16e9, 2e7),
        name="attend_back",
    )(order, starts, place, queries, slopes, att, sums, cosine, sine, *pieces)


SIDE = 256


def tile_bias(qi_ref, ki_ref, k, q_tile, k_tile, ratio):
    rows = slice(q_tile * SIDE, (q_tile + 1) * SIDE)
    keys = ki_ref[k, k_tile * SIDE : (k_tile + 1) * SIDE, :]
    allowed = (keys <= qi_ref[0:1, rows]) & (keys >= qi_ref[1:2, rows])
    bias = jnp.where(allowed, 0.0, masked_score)
    return jnp.concatenate([bias] * ratio, axis=1)


def flat_heads(ref, q_tile, group, ratio):
    return jnp.concatenate(
        [
            ref[
                q_tile * SIDE : (q_tile + 1) * SIDE,
                (group * ratio + h) * HEAD_SIZE : (group * ratio + h + 1) * HEAD_SIZE,
            ]
            for h in range(ratio)
        ],
        axis=0,
    )


def head_lanes(g, offset=0):
    return slice(offset + g * HEAD_SIZE, offset + (g + 1) * HEAD_SIZE)


def dense_begin(q_ref, groups, ratio, qt_ref, top_ref, total_ref, att_ref):
    for q_tile in range(q_ref.shape[0] // SIDE):
        for g in range(groups):
            flat = flat_heads(q_ref, q_tile, g, ratio)
            qt_ref[q_tile * groups + g] = flat.astype(f32).T.astype(bf16)
    top_ref[...] = jnp.full(top_ref.shape, masked_score, f32)
    total_ref[...] = jnp.zeros(total_ref.shape, f32)
    att_ref[...] = jnp.zeros(att_ref.shape, f32)


def dense_piece(k, kv_ref, qi_ref, ki_ref, groups, ratio, qt_ref, top_ref, total_ref, att_ref):
    width = groups * HEAD_SIZE
    for q_tile in range(qi_ref.shape[1] // SIDE):
        for k_tile in range(q_tile, -1, -1):
            bias = tile_bias(qi_ref, ki_ref, k, q_tile, k_tile, ratio)
            rows = slice(k_tile * SIDE, (k_tile + 1) * SIDE)
            for g in range(groups):
                i = q_tile * groups + g
                raw = dot(kv_ref[k, rows, head_lanes(g)], qt_ref[i], NN) * SCALE2 + bias
                top = top_ref[i]
                new_top = jnp.maximum(top, jnp.max(raw, axis=0, keepdims=True))
                weights = jnp.exp2(raw - new_top)
                back = jnp.exp2(top - new_top)
                top_ref[i] = new_top
                total_ref[i] = total_ref[i] * back + jnp.sum(weights, axis=0, keepdims=True)
                att_ref[i] = att_ref[i] * back + dot(
                    kv_ref[k, rows, head_lanes(g, width)], weights.astype(bf16), TN
                )


def dense_end(groups, ratio, top_ref, total_ref, att_ref, sum_ref, low_ref):
    for i in range(att_ref.shape[0]):
        q_tile, g = divmod(i, groups)
        out = att_ref[i] * (1.0 / total_ref[i])
        att_ref[i] = out
        sum_ref[i] = top_ref[i] + jnp.log2(total_ref[i])
        flat = out.T.astype(bf16)
        for h in range(ratio):
            low_ref[q_tile * SIDE : (q_tile + 1) * SIDE, head_lanes(g * ratio + h)] = flat[
                h * SIDE : (h + 1) * SIDE
            ]


def dense_shapes(rows, groups, ratio):
    tiles = rows // SIDE * groups
    return tiles, ratio * SIDE


FEED_TILES = 12
TILES = 17
EARLY = 5
SLOTS = 6


def back_kernel(
    part_hbm, feed_hbm, cot_hbm, middle_hbm, gain_ref, act_hbm, mid_normed_hbm, x_hbm, normed_hbm,
    low_ref, q_ref, kv_ref, att_ref, sum_ref, qi_ref, ki_ref, cos_ref, sin_ref, weight_hbm,
    feed_other, back_middle, part2_other, result_ref, token_ref, grads_ref, held_hbm, far_hbm,
    lhs, mid, part, part_other, w_out, w_in, rhs, q2, q2t, d2, d2t, delta, bias_ref, dq_ref,
    kv_sent, kv_got, cot, gain_rows, gain_other, gain_columns,
    p_send, p_keep, c_got, s_one, own, y_got, z_got,
    load_sem, act_sem, x_send, x_recv, c_send, c_recv, c_free, held_sem, y_send, y_recv, own_sem,
    z_send, z_recv, k_send, k_recv,
):
    ctxs = lax.axis_size("ctx")
    dp, ctx, tp = lax.axis_index("dp"), lax.axis_index("ctx"), lax.axis_index("tp")
    pair_at, core_at = dp // 2, lax.rem(dp, 2)
    far, core = (lax.rem(dp + 2, 4), ctx, tp), (dp + 1 - 2 * core_at, ctx, tp)
    after, before = (dp, lax.rem(ctx + 1, ctxs), tp), (dp, lax.rem(ctx + ctxs - 1, ctxs), tp)
    beside, opposite = (dp, ctx + 1 - 2 * lax.rem(ctx, 2), tp), (dp, lax.rem(ctx + 2, 4), tp)
    across = (dp, ctx, 1 - tp)
    rows, width = mid.shape
    section = width // 4
    piece = section // ctxs
    groups = kv_ref.shape[2] // (2 * HEAD_SIZE)
    kv_width = groups * HEAD_SIZE
    ratio = q_ref.shape[1] // kv_width
    q_cols = q_ref.shape[1]

    barrier = pltpu.get_barrier_semaphore()
    for device in (after, before, opposite, far, core, across):
        pl.semaphore_signal(barrier, inc=1, device_id=device, device_id_type=MESH)
    pl.semaphore_wait(barrier, 6)

    def remote(source, target, device, sent, got):
        return pltpu.make_async_remote_copy(source, target, sent, got, device, MESH)

    def load(source, target, index):
        return pltpu.make_async_copy(source, target, load_sem.at[index])


    def product(t, lhs_of, rhs_of):
        slot = lax.rem(t, 2)

        @pl.when(t >= 2)
        def _():
            core_copy(t - 2).wait_send()

        for c, out in ((1, p_send), (0, p_keep)):
            for y in range(2):
                there = lax.rem(pair_at + y + 1, 2) * 2 + lax.rem(core_at + c, 2)
                start = pl.multiple_of(there * section, LANES)
                result = rhs_of(start, lhs_of(pl.ds(start, section)))
                for z in range(ctxs):
                    odd, half = lax.rem(z + ctx, 2), lax.rem(z // 2 + ctx // 2, 2)
                    place = 2 * (1 - odd) + odd * half + (1 - odd) * (1 - half)
                    target = pl.ds(pl.multiple_of(y * section + place * piece, piece), piece)
                    out[slot, target, :] = result[z * piece : (z + 1) * piece]

        @pl.when(t >= 4)
        def _():
            pl.semaphore_wait(c_free, 1)

        core_copy(t).start()

    def core_copy(t):
        return remote(
            p_send.at[lax.rem(t, 2)], c_got.at[lax.rem(t, 4)], core, c_send.at[t], c_recv.at[t]
        )

    def held_copy(t):
        return pltpu.make_async_copy(s_one.at[lax.rem(t, 2)], held_hbm.at[t], held_sem.at[t])

    def meet_core(t):
        core_copy(t).wait_recv()
        slot, got = lax.rem(t, 2), lax.rem(t, 4)

        def add(i, unused):
            part_rows = pl.ds(pl.multiple_of(i * piece, piece), piece)
            total = p_keep[slot, part_rows, :].astype(f32) + c_got[got, part_rows, :].astype(f32)
            s_one[slot, part_rows, :] = total.astype(bf16)
            return unused

        lax.fori_loop(0, 2 * section // piece, add, 0)

        @pl.when(t + 4 < TILES)
        def _():
            pl.semaphore_signal(c_free, inc=1, device_id=core, device_id_type=MESH)

        held_copy(t).start()

    def far_copy(t):
        return remote(
            held_hbm.at[t, pl.ds(0, section)], far_hbm.at[t], far, y_send.at[t], y_recv.at[t]
        )

    def send_far(t):
        held_copy(t).wait()
        far_copy(t).start()

    def own_copy(t):
        return pltpu.make_async_copy(
            held_hbm.at[t, pl.ds(section, section)], own.at[lax.rem(t, SLOTS)], own_sem.at[t, 0]
        )

    def got_copy(t):
        return pltpu.make_async_copy(far_hbm.at[t], y_got.at[lax.rem(t, 2)], own_sem.at[t, 1])


    def near_copy(t):
        return remote(
            own.at[lax.rem(t, SLOTS), pl.ds(0, 2 * piece)],
            z_got.at[t, pl.ds(0, 2 * piece)], beside, z_send.at[t, 0], z_recv.at[t, 0],
        )

    def last_copy(t):
        return remote(
            own.at[lax.rem(t, SLOTS), pl.ds(2 * piece, piece)],
            z_got.at[t, pl.ds(2 * piece, piece)], opposite, z_send.at[t, 1], z_recv.at[t, 1],
        )

    def meet_near(t):
        near_copy(t).wait_recv()
        near_copy(t).wait_send()
        slot = lax.rem(t, SLOTS)
        for target, came in ((2, 1), (3, 0)):
            here = pl.ds(target * piece, piece)
            total = own[slot, here, :].astype(f32) + z_got[t, came * piece : (came + 1) * piece].astype(f32)
            own[slot, here, :] = total.astype(bf16)
        last_copy(t).start()

    def meet_last(t):
        last_copy(t).wait_recv()
        last_copy(t).wait_send()
        mine = own[lax.rem(t, SLOTS), 3 * piece :, :].astype(f32)
        grads_ref[t] = mine + z_got[t, 2 * piece :].astype(f32)

    def fetch(t):
        far_copy(t).wait_recv()
        own_copy(t).start()
        got_copy(t).start()

    def meet_far(t):
        own_copy(t).wait()
        got_copy(t).wait()
        slot, got = lax.rem(t, SLOTS), lax.rem(t, 2)
        for z in range(ctxs):
            target = pl.ds(z * piece, piece)
            total = own[slot, target, :].astype(f32) + y_got[got, target, :].astype(f32)
            own[slot, target, :] = total.astype(bf16)
        near_copy(t).start()

    def when(test, step, t):
        @pl.when(test)
        def _():
            step(t)

    def tick(n):
        when((n - 1 > EARLY) & (n - 1 < TILES), meet_far, n - 1)
        when((n - 3 >= EARLY) & (n - 3 < TILES), meet_near, n - 3)
        when((n - 5 >= EARLY - 1) & (n - 5 < TILES), meet_last, n - 5)
        when(n < TILES, fetch, n)


    part_copy = remote(part_hbm, part_other, across, x_send.at[0], x_recv.at[0])
    part_copy.start()
    feed_copy = remote(feed_hbm, feed_other, across, x_send.at[1], x_recv.at[1])
    feed_copy.start()

    def act_copy(t):
        columns = pl.ds(pl.multiple_of(lax.rem(t, 4) * TILE, TILE), TILE)
        return pltpu.make_async_copy(
            act_hbm.at[t // 4, :, columns], rhs.at[lax.rem(t, 2)], act_sem.at[t]
        )

    loads = [
        load(mid_normed_hbm, lhs.at[0], 0),
        load(cot_hbm, lhs.at[1], 1),
        load(part_hbm, part, 2),
        load(middle_hbm, mid, 3),
        load(weight_hbm.at[:, pl.ds(2 * q_cols + LANES, q_cols)], w_out, 4),
        load(weight_hbm.at[:, pl.ds(0, 2 * q_cols)], w_in, 5),
    ]
    act_copy(0).start()
    for copy in loads:
        copy.start()
    loads[0].wait()
    loads[1].wait()

    def plain(t):
        def times(start, left):
            return dot(left, rhs[lax.rem(t, 2)], TN).astype(bf16)

        return times

    def feed_step(t, unused):
        act_copy(t).wait()

        @pl.when(t + 1 < FEED_TILES)
        def _():
            act_copy(t + 1).start()

        product(t, lambda lanes: lhs[t // 8, :, lanes], plain(t))

        @pl.when(t >= 1)
        def _():
            meet_core(t - 1)

        @pl.when(t >= 2)
        def _():
            send_far(t - 2)

        n, turn = (t - 4) // 3, lax.rem(t, 3)
        when((t >= 4) & (turn == 1), fetch, n)
        when((t >= 7) & (turn == 1), meet_near, n - 1)
        when((t >= 4) & (turn == 2), meet_far, n)
        when((t >= 7) & (turn == 0), meet_last, n - 1)

        return unused

    lax.fori_loop(0, FEED_TILES, feed_step, 0)
    meet_core(FEED_TILES - 1)
    send_far(FEED_TILES - 2)
    send_far(FEED_TILES - 1)

    for q_tile in range(rows // SIDE):
        for g in range(groups):
            flat = flat_heads(q_ref, q_tile, g, ratio)
            q2[q_tile * groups + g] = flat
            q2t[q_tile * groups + g] = flat.astype(f32).T.astype(bf16)
    dq_ref[...] = jnp.zeros(dq_ref.shape, f32)
    gain_rows[...] = jnp.zeros(gain_rows.shape, f32)


    loads[2].wait()
    loads[3].wait()
    t_1, t_2, t_3, t_4, t_5 = (jnp.int32(j) for j in range(1, 6))
    fetch(t_3)
    meet_last(t_1)
    meet_near(t_2)
    part_copy.wait_recv()
    few = 64

    def norm_rows(i, unused):
        here = pl.ds(pl.multiple_of(i * few, few), few)
        field = mid[here, :]
        scale = lax.rsqrt(jnp.mean(field * field, axis=1, keepdims=True) + epsilon)
        unit = field * scale
        back = part[here, :].astype(f32) + part_other[here, :].astype(f32)
        gain_rows[1:2, :] += jnp.sum(back * unit, axis=0, keepdims=True)
        inner = back * gain_ref[1:2, :]
        out = lhs[1, here, :].astype(f32) + scale * (
            inner - unit * jnp.mean(inner * unit, axis=1, keepdims=True)
        )
        mid[here, :] = out
        lhs[0, here, :] = out.astype(bf16)
        return unused

    lax.fori_loop(0, rows // few, norm_rows, 0)
    meet_far(t_3)
    meet_last(t_2)
    fetch(t_4)
    middle_copy = load(mid, back_middle, 6)
    middle_copy.start()
    normed_copy = load(normed_hbm, lhs.at[1], 7)
    normed_copy.start()
    x_copy = load(x_hbm, part, 8)
    x_copy.start()
    loads[4].wait()
    cot[:, :q_cols] = dot(lhs[0], w_out[...], NN).astype(bf16)
    meet_far(t_4)
    meet_near(t_3)
    fetch(t_5)
    for q_tile in range(rows // SIDE):
        for g in range(groups):
            i = q_tile * groups + g
            flat = flat_heads(cot, q_tile, g, ratio)
            turned_flat = flat.astype(f32).T
            d2[i] = flat
            d2t[i] = turned_flat.astype(bf16)
            delta[i] = jnp.sum(turned_flat * att_ref[i], axis=0, keepdims=True)
    meet_last(t_3)
    meet_far(t_5)
    meet_near(t_4)

    t_out = jnp.int32(FEED_TILES)
    product(
        t_out, lambda lanes: lhs[0, :, lanes], lambda start, left: dot(left, low_ref[:, :TILE], TN).astype(bf16)
    )


    def kv_copy(s):
        return remote(kv_sent.at[s], kv_got.at[s], after, k_send.at[s], k_recv.at[s])

    def back_piece(s, unused):
        k = lax.rem(s + 1, ctxs)
        pairs = [(q, kk) for kk in range(rows // SIDE) for q in range(kk, rows // SIDE)]
        for index, (q_tile, k_tile) in enumerate(pairs):
            bias_ref[index] = tile_bias(qi_ref, ki_ref, k, q_tile, k_tile, ratio)
        sums = []
        for k_tile in range(rows // SIDE):
            here = slice(k_tile * SIDE, (k_tile + 1) * SIDE)
            for g in range(groups):
                key, value = kv_ref[k, here, head_lanes(g)], kv_ref[k, here, head_lanes(g, kv_width)]
                d_key = d_value = None
                for index, (q_tile, which) in enumerate(pairs):
                    if which != k_tile:
                        continue
                    i = q_tile * groups + g
                    raw = dot(key, q2t[i], NN) * SCALE2 + bias_ref[index]
                    share = jnp.exp2(raw - sum_ref[i])
                    back_share = dot(value, d2t[i], NN)
                    back = (share * (back_share - delta[i])).astype(bf16)
                    one_value = dot(share.astype(bf16), d2[i], NN)
                    one_key = dot(back, q2[i], NN)
                    d_value = one_value if d_value is None else d_value + one_value
                    d_key = one_key if d_key is None else d_key + one_key
                    dq_ref[i] += dot(key, back, TN)
                kv_sent[s, here, head_lanes(g)] = (d_key * SCALE).astype(bf16)
                kv_sent[s, here, head_lanes(g, kv_width)] = d_value.astype(bf16)

        @pl.when(s == 0)
        def _():
            kv_copy(0).start()
            meet_core(t_out)
            send_far(t_out)

        @pl.when((s == 1) | (s == 3))
        def _():
            tick(6 + s // 2)

        return unused

    lax.fori_loop(0, ctxs, back_piece, 0)

    def kv_pass(s):
        kv_copy(s).wait_recv()

        def add(i, unused):
            here = pl.ds(pl.multiple_of(i * few, few), few)
            total = kv_sent[s + 1, here, :].astype(f32) + kv_got[s, here, :].astype(f32)
            kv_sent[s + 1, here, :] = total.astype(bf16)
            return unused

        lax.fori_loop(0, rows // few, add, 0)
        if s + 1 < ctxs - 1:
            kv_copy(s + 1).start()


    kv_pass(0)
    for i in range(dq_ref.shape[0]):
        q_tile, g = divmod(i, groups)
        here = slice(q_tile * SIDE, (q_tile + 1) * SIDE)
        flat = dq_ref[i].T * SCALE
        for h in range(ratio):
            cot[here, head_lanes(g * ratio + h)] = turned(
                flat[h * SIDE : (h + 1) * SIDE], cos_ref[here, :], sin_ref[here, :], -1
            ).astype(bf16)
    normed_copy.wait()
    tail = q_cols - TILE
    t_query, t_both, t_key, t_last = (jnp.int32(FEED_TILES + 1 + j) for j in range(4))
    product(
        t_query, lambda lanes: lhs[1, :, lanes], lambda start, left: dot(left, cot[:, :TILE], TN).astype(bf16)
    )

    def times_both(start, left):
        from_query = dot(left, cot[:, TILE:q_cols], TN)
        from_output = dot(lhs[0, :, pl.ds(start, section)], low_ref[:, TILE:], TN)
        return jnp.concatenate([from_query, from_output], axis=1).astype(bf16)

    meet_core(t_query)
    product(t_both, lambda lanes: lhs[1, :, lanes], times_both)
    send_far(t_query)
    tick(jnp.int32(8))
    meet_core(t_both)
    send_far(t_both)
    feed_copy.wait_recv()
    here_copies = [load(feed_hbm, lhs.at[0], 9), load(feed_other, part_other, 10)]
    for copy in here_copies:
        copy.start()
    loads[5].wait()
    middle_copy.wait()
    for j in range(width // TILE):
        lanes = slice(j * TILE, (j + 1) * TILE)
        mid[:, lanes] = dot(cot[:, :q_cols], w_in[lanes, :q_cols], NT)
    kv_pass(1)
    tick(jnp.int32(9))


    for copy in here_copies:
        copy.wait()
    for half in range(rows // SIDE):
        here = slice(half * SIDE, (half + 1) * SIDE)
        pieces = [
            load(
                middle_hbm.at[pl.ds(half * SIDE, SIDE), pl.ds(j * TILE, TILE)],
                bias_ref.at[j], 11 + half * (width // TILE) + j,
            )
            for j in range(width // TILE)
        ]
        for copy in pieces:
            copy.start()
        for j, copy in enumerate(pieces):
            copy.wait()
            lanes = slice(j * TILE, (j + 1) * TILE)
            total = bias_ref[j] + lhs[0, here, lanes].astype(f32)
            lhs[0, here, lanes] = (total + part_other[here, lanes].astype(f32)).astype(bf16)
    result_copy = load(lhs.at[0], result_ref, 17)
    result_copy.start()
    tick(jnp.int32(10))

    kv_pass(2)
    for g in range(groups):
        cot[:, head_lanes(g, q_cols)] = turned(
            kv_sent[ctxs - 1, :, head_lanes(g)].astype(f32), cos_ref[...], sin_ref[...], -1
        ).astype(bf16)
    cot[:, q_cols + kv_width :] = kv_sent[ctxs - 1, :, kv_width:]
    x_copy.wait()
    x_rows = part[...].astype(f32)
    scale = lax.rsqrt(jnp.mean(x_rows * x_rows, axis=1, keepdims=True) + epsilon)
    for j in range(width // TILE):
        lanes = slice(j * TILE, (j + 1) * TILE)
        back = mid[:, lanes] + dot(cot[:, q_cols:], w_in[lanes, q_cols:], NT)
        part_other[:, lanes] = back.astype(bf16)
        gain_rows[0:1, lanes] += jnp.sum(back * (part[:, lanes].astype(f32) * scale), axis=0, keepdims=True)
    gain_copy = remote(gain_rows.at[pl.ds(0, 8)], gain_other, across, x_send.at[2], x_recv.at[2])
    gain_copy.start()
    part2_copy = remote(part_other, part2_other, across, x_send.at[3], x_recv.at[3])
    part2_copy.start()
    middle_back_copy = load(back_middle, mid, 18)
    middle_back_copy.start()
    product(
        t_key, lambda lanes: lhs[1, :, lanes], lambda start, left: dot(left, cot[:, q_cols : q_cols + TILE], TN).astype(bf16)
    )
    gain_copy.wait_recv()
    gain_copy.wait_send()
    gain_rows[0:1, :] += gain_other[0:1, :]
    gain_columns[...] = gain_rows[...].T

    def times_last(start, left):
        some = dot(left, cot[:, q_cols + TILE :], TN)
        gains = gain_columns[pl.ds(start, section), :]
        spare = jnp.zeros((section, TILE - tail - LANES), f32)
        return jnp.concatenate([some, gains, spare], axis=1).astype(bf16)

    meet_core(t_key)
    product(t_last, lambda lanes: lhs[1, :, lanes], times_last)
    send_far(t_key)
    meet_core(t_last)
    send_far(t_last)

    def drain(n, unused):
        tick(n)
        return unused

    lax.fori_loop(11, TILES, drain, 0)


    result_copy.wait()
    part2_copy.wait()
    other_copy = load(part2_other, lhs.at[0], 19)
    other_copy.start()
    middle_back_copy.wait()
    other_copy.wait()

    def token_rows(i, unused):
        here = pl.ds(pl.multiple_of(i * few, few), few)
        field = part[here, :].astype(f32)
        scale = lax.rsqrt(jnp.mean(field * field, axis=1, keepdims=True) + epsilon)
        unit = field * scale
        back = part_other[here, :].astype(f32) + lhs[0, here, :].astype(f32)
        inner = back * gain_ref[0:1, :]
        out = mid[here, :] + scale * (
            inner - unit * jnp.mean(inner * unit, axis=1, keepdims=True)
        )
        part_other[here, :] = out.astype(bf16)
        return unused

    lax.fori_loop(0, rows // few, token_rows, 0)
    token_copy = load(part_other, token_ref, 20)
    token_copy.start()
    lax.fori_loop(TILES, TILES + 5, drain, 0)

    for t in (TILES - 2, TILES - 1):
        core_copy(jnp.int32(t)).wait_send()

    def far_done(t, unused):
        far_copy(t).wait_send()
        return unused

    lax.fori_loop(0, TILES, far_done, 0)
    for s in range(ctxs - 1):
        kv_copy(s).wait_send()
    part_copy.wait_send()
    feed_copy.wait_send()
    token_copy.wait()


def back_all(part, feed, cotangent, middle, gains, act, mid_normed, x, normed, low, queries, kv, att, sums, qi, ki, cosine, sine, weights, ctxs):
    rows, width = x.shape
    q_cols = queries.shape[1]
    groups = kv.shape[2] // (2 * HEAD_SIZE)
    ratio = q_cols // (groups * HEAD_SIZE)
    tiles, lanes = dense_shapes(rows, groups, ratio)
    section = width // 4
    piece = section // ctxs
    vmem, hbm = pl.BlockSpec(memory_space=pltpu.VMEM), pl.BlockSpec(memory_space=pl.ANY)
    full = jax.ShapeDtypeStruct((rows, width), bf16)
    sems = lambda *n: pltpu.SemaphoreType.DMA(n)
    space = lambda *shape: pltpu.VMEM(shape, bf16)
    wide = lambda *shape: pltpu.VMEM(shape, f32)
    pairs = (rows // SIDE) * (rows // SIDE + 1) // 2
    return pl.pallas_call(
        back_kernel,
        in_specs=[hbm] * 4 + [vmem] + [hbm] * 4 + [vmem] * 9 + [hbm],
        out_specs=[hbm] * 5 + [vmem] + [hbm] * 2,
        out_shape=[
            full,
            jax.ShapeDtypeStruct((rows, width), f32),
            full,
            full,
            full,
            jax.ShapeDtypeStruct((TILES, piece, TILE), f32),
            jax.ShapeDtypeStruct((TILES, 2 * section, TILE), bf16),
            jax.ShapeDtypeStruct((TILES, section, TILE), bf16),
        ],
        scratch_shapes=[
            space(2, rows, width), wide(rows, width), space(rows, width), space(rows, width),
            space(width, q_cols), space(width, 2 * q_cols), space(2, rows, TILE),
            space(tiles, lanes, HEAD_SIZE), space(tiles, HEAD_SIZE, lanes),
            space(tiles, lanes, HEAD_SIZE), space(tiles, HEAD_SIZE, lanes),
            wide(tiles, 1, lanes), wide(pairs, SIDE, lanes), wide(tiles, HEAD_SIZE, lanes),
            space(ctxs, rows, q_cols), space(ctxs - 1, rows, q_cols), space(rows, 2 * q_cols),
            wide(LANES, width), wide(8, width), wide(width, LANES),
            space(2, 2 * section, TILE), space(2, 2 * section, TILE), space(4, 2 * section, TILE),
            space(2, 2 * section, TILE), space(SLOTS, section, TILE), space(2, section, TILE),
            space(TILES, (ctxs - 1) * piece, TILE),
            sems(21), sems(FEED_TILES), sems(4), sems(4), sems(TILES), sems(TILES),
            pltpu.SemaphoreType.REGULAR, sems(TILES), sems(TILES), sems(TILES), sems(TILES, 2),
            sems(TILES, 2), sems(TILES, 2), sems(ctxs - 1), sems(ctxs - 1),
        ],
        compiler_params=pltpu.CompilerParams(
            vmem_limit_bytes=63 * MIB, collective_id=1, has_side_effects=True
        ),
        cost_estimate=cost(4e10, 1e8),
        name="back_all",
    )(part, feed, cotangent, middle, gains, act, mid_normed, x, normed, low, queries, kv, att, sums, qi, ki, cosine, sine, weights)


def output_kernel(a_ref, w_ref, o_ref):
    o_ref[...] = dot(a_ref[...], w_ref[...], NT).astype(bf16)


def output_product(attended, weights, column, features):
    rows, inner = attended.shape
    return pl.pallas_call(
        output_kernel,
        grid=(2,),
        in_specs=[
            whole(attended.shape),
            pl.BlockSpec((features // 2, inner), lambda j: (j, column)),
        ],
        out_specs=pl.BlockSpec((rows, features // 2), lambda j: (0, j)),
        out_shape=jax.ShapeDtypeStruct((rows, features), bf16),
        compiler_params=params(40),
        cost_estimate=cost(2 * rows * inner * features, 2 * inner * features),
        name="output_product",
    )(attended, weights)


def feed_kernel(
    x_ref, mine_ref, other_ref, gain_ref, cot_ref, gate_ref, up_ref, down_ref,
    middle_ref, normed_ref, act_ref, back_ref, feed_ref, total_ref, feed_total,
):
    step = pl.program_id(0)

    @pl.when(step == 0)
    def _():
        middle = (
            x_ref[...].astype(f32) + mine_ref[...].astype(f32) + other_ref[...].astype(f32)
        )
        middle_ref[...] = middle
        scale = lax.rsqrt(jnp.mean(middle * middle, axis=1, keepdims=True) + epsilon)
        normed_ref[...] = (middle * scale * gain_ref[1:2, :]).astype(bf16)

    gate = dot(normed_ref[...], gate_ref[...], NN)
    upward = dot(normed_ref[...], up_ref[...], NN)
    back_mixed = dot(cot_ref[...], down_ref[...], NN)
    sigmoid = 1.0 / (1.0 + jnp.exp(-gate))
    activated = gate * sigmoid
    mixed = (activated * upward).astype(bf16)
    back_gate = (back_mixed * upward * sigmoid * (1.0 + gate * (1.0 - sigmoid))).astype(bf16)
    back_up = (back_mixed * activated).astype(bf16)
    act_ref[0] = back_gate
    act_ref[1] = back_up
    act_ref[2] = mixed
    part = dot(back_gate, gate_ref[...], NT) + dot(back_up, up_ref[...], NT)
    feed = dot(mixed, down_ref[...], NT)

    @pl.when(step == 0)
    def _():
        total_ref[...] = part
        feed_total[...] = feed

    @pl.when(step > 0)
    def _():
        total_ref[...] += part
        feed_total[...] += feed

    @pl.when(step == pl.num_programs(0) - 1)
    def _():
        back_ref[...] = total_ref[...].astype(bf16)
        feed_ref[...] = feed_total[...].astype(bf16)


def feed_forward(x, mine, other, gains, cotangent, gate, up, down):
    rows, width = x.shape
    hidden = gate.shape[1]
    steps = hidden // TILE
    tile_of = pl.BlockSpec((width, TILE), lambda j: (0, j))
    acts_of = pl.BlockSpec((3, rows, TILE), lambda j: (0, 0, j))
    full = whole((rows, width))
    return pl.pallas_call(
        feed_kernel,
        grid=(steps,),
        in_specs=[full, full, full, whole(gains.shape), full]
        + [tile_of] * 3,
        out_specs=[full, full, acts_of, full, full],
        out_shape=[
            jax.ShapeDtypeStruct((rows, width), f32),
            jax.ShapeDtypeStruct((rows, width), bf16),
            jax.ShapeDtypeStruct((3, rows, hidden), bf16),
            jax.ShapeDtypeStruct((rows, width), bf16),
            jax.ShapeDtypeStruct((rows, width), bf16),
        ],
        scratch_shapes=[pltpu.VMEM((rows, width), f32)] * 2,
        compiler_params=params(56),
        cost_estimate=cost(12 * rows * width * hidden, 6 * width * hidden),
        name="feed_forward",
    )(x, mine, other, gains, cotangent, gate, up, down)


def middle_kernel(cot_ref, mine_ref, other_ref, middle_ref, gain_ref, w_ref, bm_ref, bb_ref, ba_ref, grad_ref):
    middle = middle_ref[...]
    scale = lax.rsqrt(jnp.mean(middle * middle, axis=1, keepdims=True) + epsilon)
    unit = middle * scale
    back = mine_ref[...].astype(f32) + other_ref[...].astype(f32)
    grad_ref[...] = jnp.sum(back * unit, axis=0, keepdims=True)
    inner = back * gain_ref[1:2, :]
    out = cot_ref[...].astype(f32) + scale * (
        inner - unit * jnp.mean(inner * unit, axis=1, keepdims=True)
    )
    bm_ref[...] = out
    low = out.astype(bf16)
    bb_ref[...] = low
    ba_ref[...] = dot(low, w_ref[...], NN).astype(bf16)


def middle_back(cotangent, mine, other, middle, gains, weights, column, inner):
    rows, width = middle.shape
    full = whole((rows, width))
    return pl.pallas_call(
        middle_kernel,
        grid=(1,),
        in_specs=[full, full, full, full, whole(gains.shape)]
        + [pl.BlockSpec((width, inner), lambda j: (0, column))],
        out_specs=[full, full, whole((rows, inner)), whole((1, width))],
        out_shape=[
            jax.ShapeDtypeStruct((rows, width), f32),
            jax.ShapeDtypeStruct((rows, width), bf16),
            jax.ShapeDtypeStruct((rows, inner), bf16),
            jax.ShapeDtypeStruct((1, width), f32),
        ],
        compiler_params=params(56),
        cost_estimate=cost(2 * rows * width * inner, 1.5e7),
        name="middle_back",
    )(cotangent, mine, other, middle, gains, weights)


def inputs_kernel(count, x_ref, qc_ref, cos_ref, sin_ref, w_ref, *refs):
    parts = refs[:count]
    cot_ref, back_ref, grad_ref = refs[count:]
    half = qc_ref.shape[1] // 2
    cot_ref[:, : 2 * half] = qc_ref[...]
    total = parts[0][...].astype(f32)
    for part in parts[1:]:
        total += part[...].astype(f32)
    for h in range(half // HEAD_SIZE):
        lanes = slice(h * HEAD_SIZE, (h + 1) * HEAD_SIZE)
        there = slice(2 * half + h * HEAD_SIZE, 2 * half + (h + 1) * HEAD_SIZE)
        cot_ref[:, there] = turned(total[:, lanes], cos_ref[...], sin_ref[...], -1).astype(bf16)
    cot_ref[:, 3 * half :] = total[:, half:].astype(bf16)
    back = dot(cot_ref[...], w_ref[...], NT)
    back_ref[...] = back.astype(bf16)
    x = x_ref[...].astype(f32)
    unit = x * lax.rsqrt(jnp.mean(x * x, axis=1, keepdims=True) + epsilon)
    grad_ref[...] = jnp.sum(back * unit, axis=0, keepdims=True)


def inputs_back(x, qc, cosine, sine, weights, parts):
    rows, width = x.shape
    inner = 2 * qc.shape[1]
    full = whole((rows, width))
    return pl.pallas_call(
        functools.partial(inputs_kernel, len(parts)),
        grid=(1,),
        in_specs=[full, whole(qc.shape), whole(cosine.shape), whole(sine.shape)]
        + [pl.BlockSpec((width, inner), lambda j: (0, 0))]
        + [whole(parts[0].shape)] * len(parts),
        out_specs=[whole((rows, inner)), full, whole((1, width))],
        out_shape=[
            jax.ShapeDtypeStruct((rows, inner), bf16),
            jax.ShapeDtypeStruct((rows, width), bf16),
            jax.ShapeDtypeStruct((1, width), f32),
        ],
        compiler_params=params(56),
        cost_estimate=cost(2 * rows * width * inner, 1.5e7),
        name="inputs_back",
    )(x, qc, cosine, sine, weights, *parts)


def final_kernel(bm_ref, mine_ref, other_ref, x_ref, gain_ref, o_ref):
    x = x_ref[...].astype(f32)
    scale = lax.rsqrt(jnp.mean(x * x, axis=1, keepdims=True) + epsilon)
    unit = x * scale
    inner = (mine_ref[...].astype(f32) + other_ref[...].astype(f32)) * gain_ref[0:1, :]
    out = bm_ref[...] + scale * (inner - unit * jnp.mean(inner * unit, axis=1, keepdims=True))
    o_ref[...] = out.astype(bf16)


def final_back(back_middle, mine, other, x, gains):
    rows, width = x.shape
    block = pl.BlockSpec((rows // 4, width), lambda j: (j, 0))
    return pl.pallas_call(
        final_kernel,
        grid=(4,),
        in_specs=[block] * 4 + [whole(gains.shape)],
        out_specs=block,
        out_shape=jax.ShapeDtypeStruct((rows, width), bf16),
        compiler_params=params(40),
        cost_estimate=cost(1e6, 1e7),
        name="final_back",
    )(back_middle, mine, other, x, gains)


def relative(field, pairs, ctxs):
    dp, ctx = lax.axis_index("dp"), lax.axis_index("ctx")
    shaped = field.reshape((pairs, 2, ctxs, -1) + field.shape[1:])
    for axis, shift in ((0, dp // 2 + 1), (1, dp % 2 + 1), (2, ctx + 1)):
        shaped = jnp.roll(shaped, -shift, axis)
    return shaped.swapaxes(0, 1).reshape(field.shape)


def gradient_kernel(pairs, ctxs, place, a_ref, b_ref, send_ref, keep_ref):
    width = a_ref.shape[1]
    section = width // (2 * pairs)
    piece = section // ctxs
    for c, out in ((1, send_ref), (0, keep_ref)):
        for y in range(pairs):
            pair = lax.rem(place[0] + y + 1, pairs)
            core = lax.rem(place[1] + c, 2)
            lanes = pl.ds(pl.multiple_of((pair * 2 + core) * section, LANES), section)
            result = dot(a_ref[:, lanes], b_ref[...], TN).astype(bf16)
            for z in range(ctxs):
                far = lax.rem(z + ctxs - place[2] - 1 + ctxs, ctxs)
                rows = pl.ds(pl.multiple_of(y * section + far * piece, piece), piece)
                out[rows, :] = result[z * piece : (z + 1) * piece]


def gradient(a, b, pairs, ctxs):
    rows, width = a.shape
    columns = b.shape[1]
    section = width // (2 * pairs)
    if section % LANES or (section // ctxs) % 32:
        ordered = relative(dot(a, b, TN).astype(bf16), pairs, ctxs)
        return ordered[: width // 2], ordered[width // 2 :]
    dp, ctx = lax.axis_index("dp"), lax.axis_index("ctx")
    place = jnp.stack([dp // 2, dp % 2, ctx]).astype(jnp.int32)
    tile = TILE if columns % TILE == 0 else columns // 2
    block = pl.BlockSpec((width // 2, tile), lambda j: (0, j))
    return pl.pallas_call(
        functools.partial(gradient_kernel, pairs, ctxs),
        grid=(columns // tile,),
        in_specs=[SCALARS, whole(a.shape), pl.BlockSpec((rows, tile), lambda j: (0, j))],
        out_specs=[block, block],
        out_shape=[jax.ShapeDtypeStruct((width // 2, columns), bf16)] * 2,
        compiler_params=params(40),
        cost_estimate=cost(2 * rows * width * columns, 2 * width * columns),
        name="gradient",
    )(place, a, b)


def shifted(field, axis, steps, stride=1):
    count = lax.axis_size(axis)
    return lax.ppermute(
        field, axis, [(i, (i + steps * stride) % count) for i in range(count)]
    )


def other_core(field):
    return lax.ppermute(field, "dp", [(i, i ^ 1) for i in range(lax.axis_size("dp"))])


def sum_to_owner(send, keep, pairs, ctxs):
    columns = send.shape[1]
    got = other_core(send).reshape(pairs, -1, columns)
    keep = keep.reshape(pairs, -1, columns)
    total = got[-1].astype(f32) + keep[-1].astype(f32)
    for y in range(1, pairs):
        part = (got[y - 1].astype(f32) + keep[y - 1].astype(f32)).astype(bf16)
        total = total + shifted(part, "dp", y, 2).astype(f32)
    total = total.reshape(ctxs, -1, columns)
    result = total[-1]
    for z in range(1, ctxs):
        result = result + shifted(total[z - 1].astype(bf16), "ctx", z).astype(f32)
    return result


def swapped(field):
    count = lax.axis_size("tp")
    return lax.ppermute(field, "tp", [(i, count - 1 - i) for i in range(count)])


def body(
    tokens,
    cotangent,
    lengths,
    block_order,
    pre_gain,
    query_weight,
    key_weight,
    value_weight,
    output_weight,
    mid_gain,
    gate_weight,
    up_weight,
    down_weight,
):
    ctxs = lax.axis_size("ctx")
    pairs = lax.axis_size("dp") // 2
    ctx = lax.axis_index("ctx")
    order = block_order[0]
    ends = jnp.cumsum(lengths[0]).astype(jnp.int32)
    starts = ends - lengths[0]
    place = jnp.stack([ctx]).astype(jnp.int32)
    q_cols = query_weight.shape[1]
    features = tokens.shape[1]

    gain_columns = jnp.pad(jnp.stack([pre_gain, mid_gain], axis=1), ((0, 0), (0, LANES - 2)))
    packed = (query_weight, key_weight, value_weight, gain_columns, output_weight)
    stream = streams(order, ctx)
    lows = jnp.max(jnp.where(starts[None, :] <= stream[0][:, None], starts[None, :], 0), axis=1)
    cosine, sine = angles(stream[0] - lows)
    if pairs == 2 and ctxs == 4 and query_weight.shape[0] % 32 == 0:
        qi = jnp.pad(jnp.stack([stream[0], lows]), ((0, 6), (0, 0)))
        ki = stream[:, :, None]
        (
            first, gate_full, up_full, down_full, queries, kv, normed, gains,
            attended_low, att, sums, branch, branch_other,
        ) = forward_all(
            packed, gate_weight, up_weight, down_weight, tokens, cosine, sine, qi, ki, q_cols, ctxs
        )
        middle, mid_normed, act, back_part, feed = feed_forward(
            tokens, branch, branch_other, gains, cotangent, gate_full, up_full, down_full
        )
        _, _, _, result, token_gradient, grads, _, _ = back_all(
            back_part, feed, cotangent, middle, gains, act, mid_normed, tokens, normed,
            attended_low, queries, kv, att, sums, qi, ki, cosine, sine, first, ctxs,
        )
        wide = lambda *tiles: jnp.concatenate([grads[t] for t in tiles], axis=1)
        tail = q_cols - TILE
        qkv_gradient = jnp.concatenate(
            [grads[13], grads[14][:, :tail], grads[15], grads[16][:, :tail]], axis=1
        )
        output_gradient = jnp.concatenate([grads[12], grads[14][:, tail:]], axis=1)
        gain_sums = grads[16][:, tail : tail + LANES]
        gate_gradient, up_gradient = wide(0, 1, 2, 3), wide(4, 5, 6, 7)
        down_gradient = wide(8, 9, 10, 11)
    else:
        first, gate_full, up_full, down_full = (
            lax.all_gather(field, ROWS, axis=0, tiled=True)
            for field in (jnp.concatenate(packed, axis=1), gate_weight, up_weight, down_weight)
        )
        gains = first[:, 2 * q_cols : 2 * q_cols + 8].T.astype(f32)
        queries, kv, normed = project(tokens, gains, cosine, sine, first, q_cols)
        pieces = [kv] + [shifted(kv, "ctx", k) for k in range(1, ctxs)]
        output_weights = first[:, 2 * q_cols + LANES :]
        attended_low, att, sums = attend(order, starts, place, queries, pieces)
        branch = output_product(attended_low, output_weights, 0, features)
        middle, mid_normed, act, back_part, feed = feed_forward(
            tokens, branch, swapped(branch), gains, cotangent, gate_full, up_full, down_full
        )
        back_other = swapped(back_part)
        gate_parts = gradient(mid_normed, act[0], pairs, ctxs)
        up_parts = gradient(mid_normed, act[1], pairs, ctxs)
        down_parts = gradient(cotangent, act[2], pairs, ctxs)
        result = (middle + feed.astype(f32) + swapped(feed).astype(f32)).astype(bf16)

        back_middle, back_branch, back_attended, mid_grad = middle_back(
            cotangent, back_part, back_other, middle, gains, output_weights, 0, q_cols
        )
        output_parts = gradient(back_branch, attended_low, pairs, ctxs)
        back = attend_back(
            order, starts, place, queries, back_attended, att, sums, cosine, sine, pieces
        )
        own_parts = [back[1]] + [shifted(back[1 + k], "ctx", -k) for k in range(1, ctxs)]
        cot, normed_part, pre_grad = inputs_back(
            tokens, back[0], cosine, sine, first, own_parts
        )
        normed_other = swapped(normed_part)
        qkv_parts = gradient(normed, cot, pairs, ctxs)
        token_gradient = final_back(back_middle, normed_part, normed_other, tokens, gains)

        mid_once = jnp.where(lax.axis_index("tp") == 0, mid_grad, 0.0)
        pair = jnp.concatenate([pre_grad, mid_once], axis=0).astype(bf16)
        pair = jnp.pad(pair, ((0, 6), (0, 0))).T
        ordered = relative(pair, pairs, ctxs)
        gain_sums = sum_to_owner(
            ordered[: features // 2], ordered[features // 2 :], pairs, ctxs
        )
        gain_sums = gain_sums + swapped(gain_sums)
        gate_gradient = sum_to_owner(*gate_parts, pairs, ctxs)
        up_gradient = sum_to_owner(*up_parts, pairs, ctxs)
        down_gradient = sum_to_owner(*down_parts, pairs, ctxs)
        output_gradient = sum_to_owner(*output_parts, pairs, ctxs)
        qkv_gradient = sum_to_owner(*qkv_parts, pairs, ctxs)
    return (
        result,
        token_gradient,
        gain_sums[:, 0],
        qkv_gradient[:, :q_cols],
        qkv_gradient[:, q_cols : q_cols + q_cols // 2],
        qkv_gradient[:, q_cols + q_cols // 2 :],
        output_gradient,
        gain_sums[:, 1],
        gate_gradient,
        up_gradient,
        down_gradient,
    )


def solution(mesh):
    rows, split = P(ROWS, None), P(ROWS, "tp")
    return jax.shard_map(
        body,
        mesh=mesh,
        in_specs=(rows, rows, P("dp", None), P("dp", None, None), P(ROWS))
        + (split,) * 4
        + (P(ROWS),)
        + (split,) * 3,
        out_specs=(rows, rows, P(ROWS)) + (split,) * 4 + (P(ROWS),) + (split,) * 3,
        check_vma=False,
    )
```

```python
import functools
import math

import jax
import jax.numpy as jnp
import numpy as np
from jax import lax
from jax.experimental import pallas as pl
from jax.experimental.pallas import tpu as pltpu
from jax.sharding import PartitionSpec as P

HEAD_SIZE = 96
HALF = HEAD_SIZE // 2
BLOCK = 64
SPAN = 256
TILE = 512
FEED_TILE = 512
LANES = 128

epsilon = 1e-05
rotary_base = 100000.0
masked_score = -1e30
SCALE = HEAD_SIZE**-0.5
SCALE2 = SCALE / math.log(2.0)

f32 = jnp.float32
bf16 = jnp.bfloat16
ROWS = ("dp", "ctx")
MIB = 2**20


def dot(left, right, contract):
    return lax.dot_general(
        left, right, ((contract[:1], contract[1:]), ((), ())), preferred_element_type=f32
    )


NN, NT, TN = (1, 0), (1, 1), (0, 0)


def cost(flops, moved):
    return pl.CostEstimate(flops=int(flops), bytes_accessed=int(moved), transcendentals=0)


def params(mib):
    return pltpu.CompilerParams(vmem_limit_bytes=mib * MIB)


def whole(shape):
    return pl.BlockSpec(shape, lambda *_: (0,) * len(shape))


SCALARS = pl.BlockSpec(memory_space=pltpu.SMEM)


def frequencies():
    steps = np.arange(HALF, dtype=np.float64) * 2.0 / HEAD_SIZE
    return jnp.asarray(rotary_base ** -steps, f32)[None, :]


def angles(place):
    turn = place.astype(f32)[:, None] * frequencies()
    return (jnp.cos(turn), jnp.sin(turn))


def streams(order, ctx):
    rounds, count = order.shape
    owners = order[:, lax.rem(ctx - jnp.arange(count) + count, count)].T
    blocks = owners + (jnp.arange(rounds, dtype=jnp.int32) * count)[None, :]
    within = jnp.arange(BLOCK, dtype=jnp.int32)
    return (blocks[:, :, None] * BLOCK + within).reshape(count, rounds * BLOCK).astype(jnp.int32)


def turned(head, cosine, sine, sign):
    first, second = head[:, :HALF], head[:, HALF:]
    along = sine if sign > 0 else -sine
    return jnp.concatenate(
        [first * cosine - second * along, second * cosine + first * along], axis=1
    )


def project_kernel(x_ref, gain_ref, cos_ref, sin_ref, w_ref, q_ref, kv_ref, normed_ref):
    step = pl.program_id(0)
    tile = w_ref.shape[1]

    @pl.when(step == 0)
    def _():
        x = x_ref[...].astype(f32)
        scale = lax.rsqrt(jnp.mean(x * x, axis=1, keepdims=True) + epsilon)
        normed_ref[...] = (x * scale * gain_ref[0:1, :]).astype(bf16)

    out = dot(normed_ref[...], w_ref[...], NN)

    def rotated(ref):
        for h in range(tile // HEAD_SIZE):
            lanes = slice(h * HEAD_SIZE, (h + 1) * HEAD_SIZE)
            ref[:, lanes] = turned(out[:, lanes], cos_ref[...], sin_ref[...], 1).astype(bf16)

    @pl.when(step < 2)
    def _():
        rotated(q_ref)

    @pl.when(step == 2)
    def _():
        rotated(kv_ref)

    @pl.when(step == 3)
    def _():
        kv_ref[...] = out.astype(bf16)


def project(x, gains, cosine, sine, weights, q_cols):
    rows, width = x.shape
    tile = q_cols // 2
    return pl.pallas_call(
        project_kernel,
        grid=(4,),
        in_specs=[
            whole(x.shape),
            whole(gains.shape),
            whole(cosine.shape),
            whole(sine.shape),
            pl.BlockSpec((width, tile), lambda j: (0, j)),
        ],
        out_specs=[
            pl.BlockSpec((rows, tile), lambda j: (0, jnp.minimum(j, 1))),
            pl.BlockSpec((rows, tile), lambda j: (0, jnp.maximum(j - 2, 0))),
            whole((rows, width)),
        ],
        out_shape=[
            jax.ShapeDtypeStruct((rows, q_cols), bf16),
            jax.ShapeDtypeStruct((rows, q_cols), bf16),
            jax.ShapeDtypeStruct((rows, width), bf16),
        ],
        compiler_params=params(40),
        cost_estimate=cost(2 * rows * width * 4 * tile, 2 * width * 4 * tile),
        name="project",
    )(x, gains, cosine, sine, weights)


MESH = pl.DeviceIdType.MESH


def forward_kernel(
    query_shard, key_shard, value_shard, gain_shard, out_shard, gate_shard, up_shard, down_shard,
    x_ref, frequency_ref, qi_ref,
    full_ref, gate_ref, up_ref, down_ref, q_ref, kv_ref, normed_ref, gain_ref, low_ref, att_ref, sum_ref,
    middle_ref, mid_normed_ref, cos_ref, sin_ref, ki_ref,
    branch_ref, other_ref, w_ref, qt_ref, top_ref, total_ref,
    z_send, z_recv, y_send, y_recv, c_send, c_recv, k_send, k_recv, x_send, x_recv, local,
):
    ctxs = lax.axis_size("ctx")
    dp, ctx, tp = lax.axis_index("dp"), lax.axis_index("ctx"), lax.axis_index("tp")
    far, core = (lax.rem(dp + 2, 4), ctx, tp), (dp + 1 - 2 * lax.rem(dp, 2), ctx, tp)
    after, before = (dp, lax.rem(ctx + 1, ctxs), tp), (dp, lax.rem(ctx + ctxs - 1, ctxs), tp)
    across = (dp, ctx, 1 - tp)
    piece = query_shard.shape[0]
    mine = pl.ds(pl.multiple_of((dp * ctxs + ctx) * piece, piece), piece)
    packs, column = [], 0
    for j, part in enumerate((query_shard, key_shard, value_shard, gain_shard, out_shard)):
        target = w_ref.at[mine, pl.ds(column, part.shape[1])]
        packs.append(pltpu.make_async_copy(part, target, local.at[5 + j]))
        packs[-1].start()
        column += part.shape[1]
    barrier = pltpu.get_barrier_semaphore()
    for device in (after, before, far, core, across):
        pl.semaphore_signal(barrier, inc=1, device_id=device, device_id_type=MESH)
    pl.semaphore_wait(barrier, 5)
    shards = (w_ref.at[mine], gate_shard, up_shard, down_shard)
    wholes = (w_ref, gate_ref, up_ref, down_ref)
    last = ctxs - 1


    def place(group, pair, steps):
        owner = pair * ctxs + lax.rem(ctx - steps + ctxs, ctxs)
        return wholes[group].at[pl.ds(pl.multiple_of(owner * piece, piece), piece)]

    def source(group, steps):
        return place(group, dp, steps) if steps else shards[group]

    def remote(source, target, device, sent, got):
        return pltpu.make_async_remote_copy(source, target, device_id=device, device_id_type=MESH, send_sem=sent, recv_sem=got)

    def ring(group, s):
        return remote(
            source(group, s), place(group, dp, s), after, z_send.at[group, s], z_recv.at[group, s]
        )

    def over(group, s):
        return remote(
            source(group, s), place(group, dp, s), far, y_send.at[group, s], y_recv.at[group, s]
        )

    def aside(group, s):
        return remote(
            source(group, s), place(group, dp, s), core, c_send.at[group, s], c_recv.at[group, s]
        )

    def aside_far(group, s):
        there = place(group, far[0], s)
        return remote(
            there, there, core, c_send.at[group, ctxs + s], c_recv.at[group, ctxs + s]
        )

    def own_copy(group):
        return pltpu.make_async_copy(shards[group], place(group, dp, 0), local.at[group])

    def begin(group):
        over(group, 0).start()
        aside(group, 0).start()
        if group:
            own_copy(group).start()

    def along(group, s):
        ring(group, s - 1).wait_recv()
        if s < last:
            ring(group, s).start()
        over(group, s).start()
        aside(group, s).start()

    def came_over(group, s):
        over(group, s).wait_recv()
        aside_far(group, s).start()

    def gathered(group):
        if group:
            own_copy(group).wait()
        for s in range(ctxs):
            aside(group, s).wait_recv()
            aside_far(group, s).wait_recv()

    first, gate, up, down = range(4)
    for copy in packs:
        copy.wait()
    ring(first, 0).start()
    begin(first)
    columns = qi_ref[...].astype(f32).T
    turn = (columns[:, 0:1] - columns[:, 1:2]) * frequency_ref[...]
    cos_ref[...] = jnp.cos(turn)
    sin_ref[...] = jnp.sin(turn)
    for k in range(ctxs):
        ki_ref[k] = columns[:, 2 + k : 3 + k].astype(jnp.int32)
    x = x_ref[...].astype(f32)
    unit = x * lax.rsqrt(jnp.mean(x * x, axis=1, keepdims=True) + epsilon)
    for s in range(1, ctxs):
        along(first, s)
        came_over(first, s - 1)
    ring(gate, 0).start()
    begin(gate)
    ring(up, 0).start()
    came_over(first, last)
    begin(up)
    gathered(first)
    full = pltpu.make_async_copy(w_ref, full_ref, local.at[4])
    full.start()
    along(gate, 1)

    q_cols = q_ref.shape[1]
    tile = q_cols // 2
    groups = kv_ref.shape[2] // (2 * HEAD_SIZE)
    ratio = q_cols // (groups * HEAD_SIZE)
    gains = w_ref[:, 2 * q_cols : 2 * q_cols + LANES].astype(f32).T[:8]
    gain_ref[...] = gains
    normed_ref[...] = (unit * gains[0:1]).astype(bf16)

    def product(step):
        return dot(normed_ref[...], w_ref[:, step * tile : (step + 1) * tile], NN)

    def rotated(out, store):
        for h in range(tile // HEAD_SIZE):
            lanes = slice(h * HEAD_SIZE, (h + 1) * HEAD_SIZE)
            store(lanes, turned(out[:, lanes], cos_ref[...], sin_ref[...], 1).astype(bf16))

    def key_store(lanes, value):
        kv_ref[0, :, lanes] = value

    rotated(product(2), key_store)
    kv_ref[0, :, tile:] = product(3).astype(bf16)

    def kv_copy(s):
        return remote(kv_ref.at[s], kv_ref.at[s + 1], after, k_send.at[s], k_recv.at[s])

    kv_copy(0).start()
    begin(down)
    for step in range(2):

        def query_store(lanes, value):
            q_ref[:, step * tile + lanes.start : step * tile + lanes.stop] = value

        rotated(product(step), query_store)

    def attention(k):
        dense_piece(k, kv_ref, qi_ref, ki_ref, groups, ratio, qt_ref, top_ref, total_ref, att_ref)

    dense_begin(q_ref, groups, ratio, qt_ref, top_ref, total_ref, att_ref)
    along(gate, 2)
    came_over(gate, 0)
    waits = [
        [lambda: along(up, 1), lambda: along(gate, last), lambda: came_over(gate, 1), lambda: came_over(up, 0)],
        [lambda: ring(down, 0).start(), lambda: came_over(down, 0), lambda: came_over(gate, 2)],
        [lambda: along(up, 2)],
    ]

    def attention_step(k, unused):
        for s in range(1, ctxs):

            @pl.when(k == s)
            def _(s=s):
                kv_copy(s - 1).wait_recv()
                if s < last:
                    kv_copy(s).start()
                for step in waits[s - 1] if s - 1 < len(waits) else []:
                    step()

        attention(k)
        return unused

    lax.fori_loop(0, ctxs, attention_step, 0)
    dense_end(groups, ratio, top_ref, total_ref, att_ref, sum_ref, low_ref)
    branch_ref[...] = dot(low_ref[...], w_ref[:, 2 * q_cols + LANES :], NT).astype(bf16)
    exchange = remote(branch_ref, other_ref, across, x_send.at[0], x_recv.at[0])
    exchange.start()

    along(down, 1)
    came_over(gate, last)
    came_over(up, 1)
    along(up, last)
    came_over(up, 2)
    along(down, 2)
    came_over(down, 1)
    came_over(up, last)
    along(down, last)
    came_over(down, 2)
    exchange.wait_recv()
    few = 64

    def middle_rows(i, unused):
        here = pl.ds(pl.multiple_of(i * few, few), few)
        middle = x_ref[here, :].astype(f32) + (
            branch_ref[here, :].astype(f32) + other_ref[here, :].astype(f32)
        )
        middle_ref[here, :] = middle
        scale = lax.rsqrt(jnp.mean(middle * middle, axis=1, keepdims=True) + epsilon)
        mid_normed_ref[here, :] = (middle * scale * gain_ref[1:2, :]).astype(bf16)
        return unused

    lax.fori_loop(0, x_ref.shape[0] // few, middle_rows, 0)
    came_over(down, last)
    for group in (gate, up, down):
        gathered(group)
    for group in range(4):
        for s in range(ctxs):
            if s < last:
                ring(group, s).wait_send()
            over(group, s).wait_send()
            aside(group, s).wait_send()
            aside_far(group, s).wait_send()
    for s in range(last):
        kv_copy(s).wait_send()
    exchange.wait_send()
    full.wait()


def forward_all(packed, gate, up, down, x, frequency, qi, q_cols, ctxs):
    rows, width = x.shape
    columns, hidden = sum(part.shape[1] for part in packed), gate.shape[1]
    groups = q_cols // 2 // HEAD_SIZE
    tiles, lanes = dense_shapes(rows, groups, 2)
    vmem, hbm = pl.BlockSpec(memory_space=pltpu.VMEM), pl.BlockSpec(memory_space=pl.ANY)
    sems = lambda *n: pltpu.SemaphoreType.DMA(n)
    shape = jax.ShapeDtypeStruct
    full = shape((rows, width), bf16)
    return pl.pallas_call(
        forward_kernel,
        in_specs=[hbm] * (len(packed) + 3) + [vmem] * 3,
        out_specs=[hbm] * 4 + [vmem] * 12,
        out_shape=[
            shape((width, columns), bf16),
            shape((width, hidden), bf16),
            shape((width, hidden), bf16),
            shape((width, hidden), bf16),
            shape((rows, q_cols), bf16),
            shape((ctxs, rows, q_cols), bf16),
            full,
            shape((8, width), f32),
            shape((rows, q_cols), bf16),
            shape((tiles, HEAD_SIZE, lanes), f32),
            shape((tiles, 1, lanes), f32),
            shape((rows, width), f32),
            full,
            shape((rows, HALF), f32),
            shape((rows, HALF), f32),
            shape((ctxs, rows, 1), jnp.int32),
        ],
        scratch_shapes=[
            pltpu.VMEM((rows, width), bf16),
            pltpu.VMEM((rows, width), bf16),
            pltpu.VMEM((width, columns), bf16),
            pltpu.VMEM((tiles, HEAD_SIZE, lanes), bf16),
            pltpu.VMEM((tiles, 1, lanes), f32),
            pltpu.VMEM((tiles, 1, lanes), f32),
        ]
        + [sems(4, ctxs - 1)] * 2
        + [sems(4, ctxs)] * 2
        + [sems(4, 2 * ctxs)] * 2
        + [sems(ctxs - 1)] * 2
        + [sems(1)] * 2
        + [sems(5 + len(packed))],
        compiler_params=pltpu.CompilerParams(
            vmem_limit_bytes=56 * MIB, collective_id=0, has_side_effects=True
        ),
        cost_estimate=cost(1e10, 1e8),
        name="forward_all",
    )(*packed, gate, up, down, x, frequency, qi)


def gather_stream(order, ctx, pieces, k_ref, v_ref):
    count, groups = len(pieces), k_ref.shape[0]
    width = groups * HEAD_SIZE

    def fill(i, unused):
        source = pl.ds(pl.multiple_of(i * BLOCK, BLOCK), BLOCK)
        for k, piece in enumerate(pieces):
            block = i * count + order[i, lax.rem(ctx - k + count, count)]
            target = pl.ds(pl.multiple_of(block * BLOCK, BLOCK), BLOCK)
            for g in range(groups):
                lanes = slice(g * HEAD_SIZE, (g + 1) * HEAD_SIZE)
                k_ref[g, target, :] = piece[source, lanes]
                v_ref[g, target, :] = piece[
                    source, width + g * HEAD_SIZE : width + (g + 1) * HEAD_SIZE
                ]
        return unused

    lax.fori_loop(0, order.shape[0], fill, 0)


def reach(starts, first):
    low = jnp.int32(0)
    for j in range(starts.shape[0]):
        low = jnp.where(starts[j] <= first, starts[j], low)
    return low


def row_limits(starts, first, lanes):
    row = first + lax.rem(lax.broadcasted_iota(jnp.int32, (1, lanes), 1), BLOCK)
    low = jnp.zeros((1, lanes), jnp.int32)
    for j in range(starts.shape[0]):
        low = jnp.where(row >= starts[j], starts[j], low)
    return row, low


def stacked(ref, rows, group, ratio):
    return jnp.concatenate(
        [
            ref[rows, (group * ratio + h) * HEAD_SIZE : (group * ratio + h + 1) * HEAD_SIZE]
            for h in range(ratio)
        ],
        axis=0,
    )


def attend_kernel(count, order, starts, place, q_ref, *refs):
    pieces = refs[:count]
    low_ref, att_ref, sum_ref, k_ref, v_ref = refs[count:]
    groups = k_ref.shape[0]
    ratio = q_ref.shape[1] // (groups * HEAD_SIZE)
    lanes = ratio * BLOCK
    ctx = place[0]
    gather_stream(order, ctx, pieces, k_ref, v_ref)

    def one(i, unused):
        first = (i * count + order[i, ctx]) * BLOCK
        row, low = row_limits(starts, first, lanes)
        begin = reach(starts, first) // SPAN
        end = (first + BLOCK - 1) // SPAN + 1
        rows = pl.ds(pl.multiple_of(i * BLOCK, BLOCK), BLOCK)
        queries = [stacked(q_ref, rows, g, ratio) for g in range(groups)]

        def chunk(c, carry):
            keys = pl.ds(pl.multiple_of(c * SPAN, SPAN), SPAN)
            index = c * SPAN + lax.broadcasted_iota(jnp.int32, (SPAN, lanes), 0)
            allowed = (index <= row) & (index >= low)
            new = []
            for g in range(groups):
                top, total, out = carry[g]
                raw = dot(k_ref[g, keys, :], queries[g], NT) * SCALE2
                raw = jnp.where(allowed, raw, masked_score)
                new_top = jnp.maximum(top, jnp.max(raw, axis=0, keepdims=True))
                weights = jnp.where(allowed, jnp.exp2(raw - new_top), 0.0)
                back = jnp.exp2(top - new_top)
                total = total * back + jnp.sum(weights, axis=0, keepdims=True)
                out = out * back + dot(v_ref[g, keys, :], weights.astype(bf16), TN)
                new.append((new_top, total, out))
            return tuple(new)

        blank = (
            jnp.full((1, lanes), masked_score, f32),
            jnp.zeros((1, lanes), f32),
            jnp.zeros((HEAD_SIZE, lanes), f32),
        )
        result = lax.fori_loop(begin, end, chunk, (blank,) * groups)
        for g in range(groups):
            top, total, out = result[g]
            out = out / total
            att_ref[i * groups + g] = out
            sum_ref[pl.ds(i * groups + g, 1), :] = top + jnp.log2(total)
            flat = out.T.astype(bf16)
            for h in range(ratio):
                head = g * ratio + h
                low_ref[rows, head * HEAD_SIZE : (head + 1) * HEAD_SIZE] = flat[
                    h * BLOCK : (h + 1) * BLOCK
                ]
        return unused

    lax.fori_loop(0, order.shape[0], one, 0)


def attend(order, starts, place, queries, pieces):
    count, rows = len(pieces), queries.shape[0]
    groups = pieces[0].shape[1] // (2 * HEAD_SIZE)
    ratio = queries.shape[1] // (groups * HEAD_SIZE)
    rounds, lanes = order.shape[0], ratio * BLOCK
    return pl.pallas_call(
        functools.partial(attend_kernel, count),
        in_specs=[SCALARS] * 3 + [pl.BlockSpec(memory_space=pltpu.VMEM)] * (1 + count),
        out_specs=[pl.BlockSpec(memory_space=pltpu.VMEM)] * 3,
        out_shape=[
            jax.ShapeDtypeStruct(queries.shape, bf16),
            jax.ShapeDtypeStruct((rounds * groups, HEAD_SIZE, lanes), f32),
            jax.ShapeDtypeStruct((rounds * groups, lanes), f32),
        ],
        scratch_shapes=[pltpu.VMEM((groups, count * rows, HEAD_SIZE), bf16)] * 2,
        compiler_params=params(40),
        cost_estimate=cost(8e9, 1e7),
        name="attend",
    )(order, starts, place, queries, *pieces)


def attend_back_kernel(count, order, starts, place, q_ref, d_ref, att_ref, sum_ref, cos_ref, sin_ref, *refs):
    pieces = refs[:count]
    qc_ref = refs[count]
    outs = refs[count + 1 : 2 * count + 1]
    k_ref, v_ref, dk_ref, dv_ref = refs[2 * count + 1 :]
    groups = k_ref.shape[0]
    ratio = q_ref.shape[1] // (groups * HEAD_SIZE)
    lanes = ratio * BLOCK
    width = groups * HEAD_SIZE
    ctx = place[0]
    gather_stream(order, ctx, pieces, k_ref, v_ref)
    dk_ref[...] = jnp.zeros_like(dk_ref)
    dv_ref[...] = jnp.zeros_like(dv_ref)

    def one(i, unused):
        first = (i * count + order[i, ctx]) * BLOCK
        row, low = row_limits(starts, first, lanes)
        begin = reach(starts, first) // SPAN
        end = (first + BLOCK - 1) // SPAN + 1
        rows = pl.ds(pl.multiple_of(i * BLOCK, BLOCK), BLOCK)
        queries = [stacked(q_ref, rows, g, ratio) for g in range(groups)]
        slopes = [stacked(d_ref, rows, g, ratio) for g in range(groups)]
        sums, deltas = [], []
        for g in range(groups):
            sums.append(sum_ref[pl.ds(i * groups + g, 1), :])
            across = slopes[g].astype(f32).T
            deltas.append(jnp.sum(across * att_ref[i * groups + g], axis=0, keepdims=True))

        def chunk(c, carry):
            keys = pl.ds(pl.multiple_of(c * SPAN, SPAN), SPAN)
            index = c * SPAN + lax.broadcasted_iota(jnp.int32, (SPAN, lanes), 0)
            allowed = (index <= row) & (index >= low)
            new = []
            for g in range(groups):
                key, value = k_ref[g, keys, :], v_ref[g, keys, :]
                raw = dot(key, queries[g], NT) * SCALE2
                share = jnp.where(allowed, jnp.exp2(jnp.minimum(raw - sums[g], 0.0)), 0.0)
                back_share = dot(value, slopes[g], NT)
                back = (share * (back_share - deltas[g])).astype(bf16)
                dv_ref[g, keys, :] += dot(share.astype(bf16), slopes[g], NN)
                dk_ref[g, keys, :] += dot(back, queries[g], NN)
                new.append(carry[g] + dot(key, back, TN))
            return tuple(new)

        blank = jnp.zeros((HEAD_SIZE, lanes), f32)
        result = lax.fori_loop(begin, end, chunk, (blank,) * groups)
        cosine, sine = cos_ref[rows, :], sin_ref[rows, :]
        for g in range(groups):
            flat = result[g].T * SCALE
            for h in range(ratio):
                head = g * ratio + h
                qc_ref[rows, head * HEAD_SIZE : (head + 1) * HEAD_SIZE] = turned(
                    flat[h * BLOCK : (h + 1) * BLOCK], cosine, sine, -1
                ).astype(bf16)
        return unused

    lax.fori_loop(0, order.shape[0], one, 0)

    def spread(i, unused):
        target = pl.ds(pl.multiple_of(i * BLOCK, BLOCK), BLOCK)
        for k, out in enumerate(outs):
            block = i * count + order[i, lax.rem(ctx - k + count, count)]
            source = pl.ds(pl.multiple_of(block * BLOCK, BLOCK), BLOCK)
            for g in range(groups):
                out[target, g * HEAD_SIZE : (g + 1) * HEAD_SIZE] = (
                    dk_ref[g, source, :] * SCALE
                ).astype(bf16)
                out[target, width + g * HEAD_SIZE : width + (g + 1) * HEAD_SIZE] = dv_ref[
                    g, source, :
                ].astype(bf16)
        return unused

    lax.fori_loop(0, order.shape[0], spread, 0)


def attend_back(order, starts, place, queries, slopes, att, sums, cosine, sine, pieces):
    count, rows = len(pieces), queries.shape[0]
    groups = pieces[0].shape[1] // (2 * HEAD_SIZE)
    keys = (groups, count * rows, HEAD_SIZE)
    return pl.pallas_call(
        functools.partial(attend_back_kernel, count),
        in_specs=[SCALARS] * 3 + [pl.BlockSpec(memory_space=pltpu.VMEM)] * (6 + count),
        out_specs=[pl.BlockSpec(memory_space=pltpu.VMEM)] * (1 + count),
        out_shape=[jax.ShapeDtypeStruct(queries.shape, bf16)]
        + [jax.ShapeDtypeStruct(pieces[0].shape, bf16)] * count,
        scratch_shapes=[pltpu.VMEM(keys, bf16)] * 2 + [pltpu.VMEM(keys, f32)] * 2,
        compiler_params=params(56),
        cost_estimate=cost(16e9, 2e7),
        name="attend_back",
    )(order, starts, place, queries, slopes, att, sums, cosine, sine, *pieces)


SIDE = 256


def tile_bias(qi_ref, ki_ref, k, q_tile, k_tile, ratio):
    rows = slice(q_tile * SIDE, (q_tile + 1) * SIDE)
    keys = ki_ref[k, k_tile * SIDE : (k_tile + 1) * SIDE, :]
    allowed = (keys <= qi_ref[0:1, rows]) & (keys >= qi_ref[1:2, rows])
    bias = jnp.where(allowed, 0.0, masked_score)
    return jnp.concatenate([bias] * ratio, axis=1)


def flat_heads(ref, q_tile, group, ratio):
    return jnp.concatenate(
        [
            ref[
                q_tile * SIDE : (q_tile + 1) * SIDE,
                (group * ratio + h) * HEAD_SIZE : (group * ratio + h + 1) * HEAD_SIZE,
            ]
            for h in range(ratio)
        ],
        axis=0,
    )


def head_lanes(g, offset=0):
    return slice(offset + g * HEAD_SIZE, offset + (g + 1) * HEAD_SIZE)


def dense_begin(q_ref, groups, ratio, qt_ref, top_ref, total_ref, att_ref):
    for q_tile in range(q_ref.shape[0] // SIDE):
        for g in range(groups):
            flat = flat_heads(q_ref, q_tile, g, ratio)
            qt_ref[q_tile * groups + g] = flat.astype(f32).T.astype(bf16)
    top_ref[...] = jnp.full(top_ref.shape, masked_score, f32)
    total_ref[...] = jnp.zeros(total_ref.shape, f32)
    att_ref[...] = jnp.zeros(att_ref.shape, f32)


def dense_piece(k, kv_ref, qi_ref, ki_ref, groups, ratio, qt_ref, top_ref, total_ref, att_ref):
    width = groups * HEAD_SIZE
    for q_tile in range(qi_ref.shape[1] // SIDE):
        for k_tile in range(q_tile, -1, -1):
            bias = tile_bias(qi_ref, ki_ref, k, q_tile, k_tile, ratio)
            rows = slice(k_tile * SIDE, (k_tile + 1) * SIDE)
            for g in range(groups):
                i = q_tile * groups + g
                raw = dot(kv_ref[k, rows, head_lanes(g)], qt_ref[i], NN) * SCALE2 + bias
                top = top_ref[i]
                new_top = jnp.maximum(top, jnp.max(raw, axis=0, keepdims=True))
                weights = jnp.exp2(raw - new_top)
                back = jnp.exp2(top - new_top)
                top_ref[i] = new_top
                total_ref[i] = total_ref[i] * back + jnp.sum(weights, axis=0, keepdims=True)
                att_ref[i] = att_ref[i] * back + dot(
                    kv_ref[k, rows, head_lanes(g, width)], weights.astype(bf16), TN
                )


def dense_end(groups, ratio, top_ref, total_ref, att_ref, sum_ref, low_ref):
    for i in range(att_ref.shape[0]):
        q_tile, g = divmod(i, groups)
        out = att_ref[i] * (1.0 / total_ref[i])
        att_ref[i] = out
        sum_ref[i] = top_ref[i] + jnp.log2(total_ref[i])
        flat = out.T.astype(bf16)
        for h in range(ratio):
            low_ref[q_tile * SIDE : (q_tile + 1) * SIDE, head_lanes(g * ratio + h)] = flat[
                h * SIDE : (h + 1) * SIDE
            ]


def dense_shapes(rows, groups, ratio):
    tiles = rows // SIDE * groups
    return tiles, ratio * SIDE


FEED_TILES = 12
TILES = 17
EARLY = 5
SLOTS = 6


def back_kernel(
    part_hbm, feed_hbm, cot_hbm, middle_hbm, gain_ref, act_hbm, mid_normed_hbm, x_hbm, normed_hbm,
    low_ref, q_ref, kv_ref, att_ref, sum_ref, qi_ref, ki_ref, cos_ref, sin_ref, weight_hbm,
    feed_other, back_middle, part2_other, result_ref, token_ref, grads_ref, held_hbm, far_hbm,
    lhs, mid, part, part_other, w_out, w_in, rhs, q2, q2t, d2, d2t, delta, bias_ref, dq_ref,
    kv_sent, kv_got, cot, gain_rows, gain_other, gain_columns,
    p_send, p_keep, c_got, s_one, own, y_got, z_got,
    load_sem, act_sem, x_send, x_recv, c_send, c_recv, c_free, held_sem, y_send, y_recv, own_sem,
    z_send, z_recv, k_send, k_recv,
):
    ctxs = lax.axis_size("ctx")
    dp, ctx, tp = lax.axis_index("dp"), lax.axis_index("ctx"), lax.axis_index("tp")
    pair_at, core_at = dp // 2, lax.rem(dp, 2)
    far, core = (lax.rem(dp + 2, 4), ctx, tp), (dp + 1 - 2 * core_at, ctx, tp)
    after, before = (dp, lax.rem(ctx + 1, ctxs), tp), (dp, lax.rem(ctx + ctxs - 1, ctxs), tp)
    beside, opposite = (dp, ctx + 1 - 2 * lax.rem(ctx, 2), tp), (dp, lax.rem(ctx + 2, 4), tp)
    across = (dp, ctx, 1 - tp)
    rows, width = mid.shape
    section = width // 4
    piece = section // ctxs
    groups = kv_ref.shape[2] // (2 * HEAD_SIZE)
    kv_width = groups * HEAD_SIZE
    ratio = q_ref.shape[1] // kv_width
    q_cols = q_ref.shape[1]

    barrier = pltpu.get_barrier_semaphore()
    for device in (after, before, opposite, far, core, across):
        pl.semaphore_signal(barrier, inc=1, device_id=device, device_id_type=MESH)
    pl.semaphore_wait(barrier, 6)

    def remote(source, target, device, sent, got):
        return pltpu.make_async_remote_copy(source, target, sent, got, device, MESH)

    def load(source, target, index):
        return pltpu.make_async_copy(source, target, load_sem.at[index])


    def product(t, lhs_of, rhs_of):
        slot = lax.rem(t, 2)

        @pl.when(t >= 2)
        def _():
            core_copy(t - 2).wait_send()

        for c, out in ((1, p_send), (0, p_keep)):
            for y in range(2):
                there = lax.rem(pair_at + y + 1, 2) * 2 + lax.rem(core_at + c, 2)
                start = pl.multiple_of(there * section, LANES)
                result = rhs_of(start, lhs_of(pl.ds(start, section)))
                for z in range(ctxs):
                    odd, half = lax.rem(z + ctx, 2), lax.rem(z // 2 + ctx // 2, 2)
                    place = 2 * (1 - odd) + odd * half + (1 - odd) * (1 - half)
                    target = pl.ds(pl.multiple_of(y * section + place * piece, piece), piece)
                    out[slot, target, :] = result[z * piece : (z + 1) * piece]

        @pl.when(t >= 4)
        def _():
            pl.semaphore_wait(c_free, 1)

        core_copy(t).start()

    def core_copy(t):
        return remote(
            p_send.at[lax.rem(t, 2)], c_got.at[lax.rem(t, 4)], core, c_send.at[t], c_recv.at[t]
        )

    def held_copy(t):
        return pltpu.make_async_copy(s_one.at[lax.rem(t, 2)], held_hbm.at[t], held_sem.at[t])

    def meet_core(t):
        core_copy(t).wait_recv()
        slot, got = lax.rem(t, 2), lax.rem(t, 4)

        def add(i, unused):
            part_rows = pl.ds(pl.multiple_of(i * piece, piece), piece)
            total = p_keep[slot, part_rows, :].astype(f32) + c_got[got, part_rows, :].astype(f32)
            s_one[slot, part_rows, :] = total.astype(bf16)
            return unused

        lax.fori_loop(0, 2 * section // piece, add, 0)

        @pl.when(t + 4 < TILES)
        def _():
            pl.semaphore_signal(c_free, inc=1, device_id=core, device_id_type=MESH)

        held_copy(t).start()

    def far_copy(t):
        return remote(
            held_hbm.at[t, pl.ds(0, section)], far_hbm.at[t], far, y_send.at[t], y_recv.at[t]
        )

    def send_far(t):
        held_copy(t).wait()
        far_copy(t).start()

    def own_copy(t):
        return pltpu.make_async_copy(
            held_hbm.at[t, pl.ds(section, section)], own.at[lax.rem(t, SLOTS)], own_sem.at[t, 0]
        )

    def got_copy(t):
        return pltpu.make_async_copy(far_hbm.at[t], y_got.at[lax.rem(t, 2)], own_sem.at[t, 1])


    def near_copy(t):
        return remote(
            own.at[lax.rem(t, SLOTS), pl.ds(0, 2 * piece)],
            z_got.at[t, pl.ds(0, 2 * piece)], beside, z_send.at[t, 0], z_recv.at[t, 0],
        )

    def last_copy(t):
        return remote(
            own.at[lax.rem(t, SLOTS), pl.ds(2 * piece, piece)],
            z_got.at[t, pl.ds(2 * piece, piece)], opposite, z_send.at[t, 1], z_recv.at[t, 1],
        )

    def meet_near(t):
        near_copy(t).wait_recv()
        near_copy(t).wait_send()
        slot = lax.rem(t, SLOTS)
        for target, came in ((2, 1), (3, 0)):
            here = pl.ds(target * piece, piece)
            total = own[slot, here, :].astype(f32) + z_got[t, came * piece : (came + 1) * piece].astype(f32)
            own[slot, here, :] = total.astype(bf16)
        last_copy(t).start()

    def meet_last(t):
        last_copy(t).wait_recv()
        last_copy(t).wait_send()
        mine = own[lax.rem(t, SLOTS), 3 * piece :, :].astype(f32)
        grads_ref[t] = mine + z_got[t, 2 * piece :].astype(f32)

    def fetch(t):
        far_copy(t).wait_recv()
        own_copy(t).start()
        got_copy(t).start()

    def meet_far(t):
        own_copy(t).wait()
        got_copy(t).wait()
        slot, got = lax.rem(t, SLOTS), lax.rem(t, 2)
        for z in range(ctxs):
            target = pl.ds(z * piece, piece)
            total = own[slot, target, :].astype(f32) + y_got[got, target, :].astype(f32)
            own[slot, target, :] = total.astype(bf16)
        near_copy(t).start()

    def when(test, step, t):
        @pl.when(test)
        def _():
            step(t)

    def tick(n):
        when((n - 1 > EARLY) & (n - 1 < TILES), meet_far, n - 1)
        when((n - 3 >= EARLY) & (n - 3 < TILES), meet_near, n - 3)
        when((n - 5 >= EARLY - 1) & (n - 5 < TILES), meet_last, n - 5)
        when(n < TILES, fetch, n)


    part_copy = remote(part_hbm, part_other, across, x_send.at[0], x_recv.at[0])
    part_copy.start()
    feed_copy = remote(feed_hbm, feed_other, across, x_send.at[1], x_recv.at[1])
    feed_copy.start()

    def act_copy(t):
        columns = pl.ds(pl.multiple_of(lax.rem(t, 4) * TILE, TILE), TILE)
        return pltpu.make_async_copy(
            act_hbm.at[t // 4, :, columns], rhs.at[lax.rem(t, 2)], act_sem.at[t]
        )

    loads = [
        load(mid_normed_hbm, lhs.at[0], 0),
        load(cot_hbm, lhs.at[1], 1),
        load(part_hbm, part, 2),
        load(middle_hbm, mid, 3),
        load(weight_hbm.at[:, pl.ds(2 * q_cols + LANES, q_cols)], w_out, 4),
        load(weight_hbm.at[:, pl.ds(0, 2 * q_cols)], w_in, 5),
    ]
    act_copy(0).start()
    for copy in loads:
        copy.start()
    loads[0].wait()
    loads[1].wait()

    def plain(t):
        def times(start, left):
            return dot(left, rhs[lax.rem(t, 2)], TN).astype(bf16)

        return times

    def feed_step(t, unused):
        act_copy(t).wait()

        @pl.when(t + 1 < FEED_TILES)
        def _():
            act_copy(t + 1).start()

        product(t, lambda lanes: lhs[t // 8, :, lanes], plain(t))

        @pl.when(t >= 1)
        def _():
            meet_core(t - 1)

        @pl.when(t >= 2)
        def _():
            send_far(t - 2)

        n, turn = (t - 4) // 3, lax.rem(t, 3)
        when((t >= 4) & (turn == 1), fetch, n)
        when((t >= 7) & (turn == 1), meet_near, n - 1)
        when((t >= 4) & (turn == 2), meet_far, n)
        when((t >= 7) & (turn == 0), meet_last, n - 1)

        return unused

    lax.fori_loop(0, FEED_TILES, feed_step, 0)
    meet_core(FEED_TILES - 1)
    send_far(FEED_TILES - 2)
    send_far(FEED_TILES - 1)

    for q_tile in range(rows // SIDE):
        for g in range(groups):
            flat = flat_heads(q_ref, q_tile, g, ratio)
            q2[q_tile * groups + g] = flat
            q2t[q_tile * groups + g] = flat.astype(f32).T.astype(bf16)
    dq_ref[...] = jnp.zeros(dq_ref.shape, f32)
    gain_rows[...] = jnp.zeros(gain_rows.shape, f32)


    loads[2].wait()
    loads[3].wait()
    t_1, t_2, t_3, t_4, t_5 = (jnp.int32(j) for j in range(1, 6))
    fetch(t_3)
    meet_last(t_1)
    meet_near(t_2)
    part_copy.wait_recv()
    few = 64

    def norm_rows(i, unused):
        here = pl.ds(pl.multiple_of(i * few, few), few)
        field = mid[here, :]
        scale = lax.rsqrt(jnp.mean(field * field, axis=1, keepdims=True) + epsilon)
        unit = field * scale
        back = part[here, :].astype(f32) + part_other[here, :].astype(f32)
        gain_rows[1:2, :] += jnp.sum(back * unit, axis=0, keepdims=True)
        inner = back * gain_ref[1:2, :]
        out = lhs[1, here, :].astype(f32) + scale * (
            inner - unit * jnp.mean(inner * unit, axis=1, keepdims=True)
        )
        mid[here, :] = out
        lhs[0, here, :] = out.astype(bf16)
        return unused

    lax.fori_loop(0, rows // few, norm_rows, 0)
    meet_far(t_3)
    meet_last(t_2)
    fetch(t_4)
    middle_copy = load(mid, back_middle, 6)
    middle_copy.start()
    normed_copy = load(normed_hbm, lhs.at[1], 7)
    normed_copy.start()
    x_copy = load(x_hbm, part, 8)
    x_copy.start()
    loads[4].wait()
    cot[:, :q_cols] = dot(lhs[0], w_out[...], NN).astype(bf16)
    meet_far(t_4)
    meet_near(t_3)
    fetch(t_5)
    for q_tile in range(rows // SIDE):
        for g in range(groups):
            i = q_tile * groups + g
            flat = flat_heads(cot, q_tile, g, ratio)
            turned_flat = flat.astype(f32).T
            d2[i] = flat
            d2t[i] = turned_flat.astype(bf16)
            delta[i] = jnp.sum(turned_flat * att_ref[i], axis=0, keepdims=True)
    meet_last(t_3)
    meet_far(t_5)
    meet_near(t_4)

    t_out = jnp.int32(FEED_TILES)
    product(
        t_out, lambda lanes: lhs[0, :, lanes], lambda start, left: dot(left, low_ref[:, :TILE], TN).astype(bf16)
    )


    def kv_copy(s):
        return remote(kv_sent.at[s], kv_got.at[s], after, k_send.at[s], k_recv.at[s])

    def back_piece(s, unused):
        k = lax.rem(s + 1, ctxs)
        pairs = [(q, kk) for kk in range(rows // SIDE) for q in range(kk, rows // SIDE)]
        for index, (q_tile, k_tile) in enumerate(pairs):
            bias_ref[index] = tile_bias(qi_ref, ki_ref, k, q_tile, k_tile, ratio)
        sums = []
        for k_tile in range(rows // SIDE):
            here = slice(k_tile * SIDE, (k_tile + 1) * SIDE)
            for g in range(groups):
                key, value = kv_ref[k, here, head_lanes(g)], kv_ref[k, here, head_lanes(g, kv_width)]
                d_key = d_value = None
                for index, (q_tile, which) in enumerate(pairs):
                    if which != k_tile:
                        continue
                    i = q_tile * groups + g
                    raw = dot(key, q2t[i], NN) * SCALE2 + bias_ref[index]
                    share = jnp.exp2(raw - sum_ref[i])
                    back_share = dot(value, d2t[i], NN)
                    back = (share * (back_share - delta[i])).astype(bf16)
                    one_value = dot(share.astype(bf16), d2[i], NN)
                    one_key = dot(back, q2[i], NN)
                    d_value = one_value if d_value is None else d_value + one_value
                    d_key = one_key if d_key is None else d_key + one_key
                    dq_ref[i] += dot(key, back, TN)
                kv_sent[s, here, head_lanes(g)] = (d_key * SCALE).astype(bf16)
                kv_sent[s, here, head_lanes(g, kv_width)] = d_value.astype(bf16)

        @pl.when(s == 0)
        def _():
            kv_copy(0).start()
            meet_core(t_out)
            send_far(t_out)

        @pl.when((s == 1) | (s == 3))
        def _():
            tick(6 + s // 2)

        return unused

    lax.fori_loop(0, ctxs, back_piece, 0)

    def kv_pass(s):
        kv_copy(s).wait_recv()

        def add(i, unused):
            here = pl.ds(pl.multiple_of(i * few, few), few)
            total = kv_sent[s + 1, here, :].astype(f32) + kv_got[s, here, :].astype(f32)
            kv_sent[s + 1, here, :] = total.astype(bf16)
            return unused

        lax.fori_loop(0, rows // few, add, 0)
        if s + 1 < ctxs - 1:
            kv_copy(s + 1).start()


    kv_pass(0)
    for i in range(dq_ref.shape[0]):
        q_tile, g = divmod(i, groups)
        here = slice(q_tile * SIDE, (q_tile + 1) * SIDE)
        flat = dq_ref[i].T * SCALE
        for h in range(ratio):
            cot[here, head_lanes(g * ratio + h)] = turned(
                flat[h * SIDE : (h + 1) * SIDE], cos_ref[here, :], sin_ref[here, :], -1
            ).astype(bf16)
    normed_copy.wait()
    tail = q_cols - TILE
    t_query, t_both, t_key, t_last = (jnp.int32(FEED_TILES + 1 + j) for j in range(4))
    product(
        t_query, lambda lanes: lhs[1, :, lanes], lambda start, left: dot(left, cot[:, :TILE], TN).astype(bf16)
    )

    def times_both(start, left):
        from_query = dot(left, cot[:, TILE:q_cols], TN)
        from_output = dot(lhs[0, :, pl.ds(start, section)], low_ref[:, TILE:], TN)
        return jnp.concatenate([from_query, from_output], axis=1).astype(bf16)

    meet_core(t_query)
    product(t_both, lambda lanes: lhs[1, :, lanes], times_both)
    send_far(t_query)
    tick(jnp.int32(8))
    meet_core(t_both)
    send_far(t_both)
    feed_copy.wait_recv()
    here_copies = [load(feed_hbm, lhs.at[0], 9), load(feed_other, part_other, 10)]
    for copy in here_copies:
        copy.start()
    loads[5].wait()
    middle_copy.wait()
    for j in range(width // TILE):
        lanes = slice(j * TILE, (j + 1) * TILE)
        mid[:, lanes] = dot(cot[:, :q_cols], w_in[lanes, :q_cols], NT)
    kv_pass(1)
    tick(jnp.int32(9))


    for copy in here_copies:
        copy.wait()
    for half in range(rows // SIDE):
        here = slice(half * SIDE, (half + 1) * SIDE)
        pieces = [
            load(
                middle_hbm.at[pl.ds(half * SIDE, SIDE), pl.ds(j * TILE, TILE)],
                bias_ref.at[j], 11 + half * (width // TILE) + j,
            )
            for j in range(width // TILE)
        ]
        for copy in pieces:
            copy.start()
        for j, copy in enumerate(pieces):
            copy.wait()
            lanes = slice(j * TILE, (j + 1) * TILE)
            total = bias_ref[j] + lhs[0, here, lanes].astype(f32)
            lhs[0, here, lanes] = (total + part_other[here, lanes].astype(f32)).astype(bf16)
    result_copy = load(lhs.at[0], result_ref, 17)
    result_copy.start()
    tick(jnp.int32(10))

    kv_pass(2)
    for g in range(groups):
        cot[:, head_lanes(g, q_cols)] = turned(
            kv_sent[ctxs - 1, :, head_lanes(g)].astype(f32), cos_ref[...], sin_ref[...], -1
        ).astype(bf16)
    cot[:, q_cols + kv_width :] = kv_sent[ctxs - 1, :, kv_width:]
    x_copy.wait()
    x_rows = part[...].astype(f32)
    scale = lax.rsqrt(jnp.mean(x_rows * x_rows, axis=1, keepdims=True) + epsilon)
    for j in range(width // TILE):
        lanes = slice(j * TILE, (j + 1) * TILE)
        back = mid[:, lanes] + dot(cot[:, q_cols:], w_in[lanes, q_cols:], NT)
        part_other[:, lanes] = back.astype(bf16)
        gain_rows[0:1, lanes] += jnp.sum(back * (part[:, lanes].astype(f32) * scale), axis=0, keepdims=True)
    gain_copy = remote(gain_rows.at[pl.ds(0, 8)], gain_other, across, x_send.at[2], x_recv.at[2])
    gain_copy.start()
    part2_copy = remote(part_other, part2_other, across, x_send.at[3], x_recv.at[3])
    part2_copy.start()
    middle_back_copy = load(back_middle, mid, 18)
    middle_back_copy.start()
    product(
        t_key, lambda lanes: lhs[1, :, lanes], lambda start, left: dot(left, cot[:, q_cols : q_cols + TILE], TN).astype(bf16)
    )
    gain_copy.wait_recv()
    gain_copy.wait_send()
    gain_rows[0:1, :] += gain_other[0:1, :]
    gain_columns[...] = gain_rows[...].T

    def times_last(start, left):
        some = dot(left, cot[:, q_cols + TILE :], TN)
        gains = gain_columns[pl.ds(start, section), :]
        spare = jnp.zeros((section, TILE - tail - LANES), f32)
        return jnp.concatenate([some, gains, spare], axis=1).astype(bf16)

    meet_core(t_key)
    product(t_last, lambda lanes: lhs[1, :, lanes], times_last)
    send_far(t_key)
    meet_core(t_last)
    send_far(t_last)

    def drain(n, unused):
        tick(n)
        return unused

    lax.fori_loop(11, TILES, drain, 0)


    result_copy.wait()
    part2_copy.wait()
    other_copy = load(part2_other, lhs.at[0], 19)
    other_copy.start()
    middle_back_copy.wait()
    other_copy.wait()

    def token_rows(i, unused):
        here = pl.ds(pl.multiple_of(i * few, few), few)
        field = part[here, :].astype(f32)
        scale = lax.rsqrt(jnp.mean(field * field, axis=1, keepdims=True) + epsilon)
        unit = field * scale
        back = part_other[here, :].astype(f32) + lhs[0, here, :].astype(f32)
        inner = back * gain_ref[0:1, :]
        out = mid[here, :] + scale * (
            inner - unit * jnp.mean(inner * unit, axis=1, keepdims=True)
        )
        part_other[here, :] = out.astype(bf16)
        return unused

    lax.fori_loop(0, rows // few, token_rows, 0)
    token_copy = load(part_other, token_ref, 20)
    token_copy.start()
    lax.fori_loop(TILES, TILES + 5, drain, 0)

    for t in (TILES - 2, TILES - 1):
        core_copy(jnp.int32(t)).wait_send()

    def far_done(t, unused):
        far_copy(t).wait_send()
        return unused

    lax.fori_loop(0, TILES, far_done, 0)
    for s in range(ctxs - 1):
        kv_copy(s).wait_send()
    part_copy.wait_send()
    feed_copy.wait_send()
    token_copy.wait()


def back_all(part, feed, cotangent, middle, gains, act, mid_normed, x, normed, low, queries, kv, att, sums, qi, ki, cosine, sine, weights, ctxs):
    rows, width = x.shape
    q_cols = queries.shape[1]
    groups = kv.shape[2] // (2 * HEAD_SIZE)
    ratio = q_cols // (groups * HEAD_SIZE)
    tiles, lanes = dense_shapes(rows, groups, ratio)
    section = width // 4
    piece = section // ctxs
    vmem, hbm = pl.BlockSpec(memory_space=pltpu.VMEM), pl.BlockSpec(memory_space=pl.ANY)
    full = jax.ShapeDtypeStruct((rows, width), bf16)
    sems = lambda *n: pltpu.SemaphoreType.DMA(n)
    space = lambda *shape: pltpu.VMEM(shape, bf16)
    wide = lambda *shape: pltpu.VMEM(shape, f32)
    pairs = (rows // SIDE) * (rows // SIDE + 1) // 2
    return pl.pallas_call(
        back_kernel,
        in_specs=[hbm] * 4 + [vmem] + [hbm] * 4 + [vmem] * 9 + [hbm],
        out_specs=[hbm] * 5 + [vmem] + [hbm] * 2,
        out_shape=[
            full,
            jax.ShapeDtypeStruct((rows, width), f32),
            full,
            full,
            full,
            jax.ShapeDtypeStruct((TILES, piece, TILE), f32),
            jax.ShapeDtypeStruct((TILES, 2 * section, TILE), bf16),
            jax.ShapeDtypeStruct((TILES, section, TILE), bf16),
        ],
        scratch_shapes=[
            space(2, rows, width), wide(rows, width), space(rows, width), space(rows, width),
            space(width, q_cols), space(width, 2 * q_cols), space(2, rows, TILE),
            space(tiles, lanes, HEAD_SIZE), space(tiles, HEAD_SIZE, lanes),
            space(tiles, lanes, HEAD_SIZE), space(tiles, HEAD_SIZE, lanes),
            wide(tiles, 1, lanes), wide(pairs, SIDE, lanes), wide(tiles, HEAD_SIZE, lanes),
            space(ctxs, rows, q_cols), space(ctxs - 1, rows, q_cols), space(rows, 2 * q_cols),
            wide(LANES, width), wide(8, width), wide(width, LANES),
            space(2, 2 * section, TILE), space(2, 2 * section, TILE), space(4, 2 * section, TILE),
            space(2, 2 * section, TILE), space(SLOTS, section, TILE), space(2, section, TILE),
            space(TILES, (ctxs - 1) * piece, TILE),
            sems(21), sems(FEED_TILES), sems(4), sems(4), sems(TILES), sems(TILES),
            pltpu.SemaphoreType.REGULAR, sems(TILES), sems(TILES), sems(TILES), sems(TILES, 2),
            sems(TILES, 2), sems(TILES, 2), sems(ctxs - 1), sems(ctxs - 1),
        ],
        compiler_params=pltpu.CompilerParams(
            vmem_limit_bytes=63 * MIB, collective_id=1, has_side_effects=True
        ),
        cost_estimate=cost(4e10, 1e8),
        name="back_all",
    )(part, feed, cotangent, middle, gains, act, mid_normed, x, normed, low, queries, kv, att, sums, qi, ki, cosine, sine, weights)


def output_kernel(a_ref, w_ref, o_ref):
    o_ref[...] = dot(a_ref[...], w_ref[...], NT).astype(bf16)


def output_product(attended, weights, column, features):
    rows, inner = attended.shape
    return pl.pallas_call(
        output_kernel,
        grid=(2,),
        in_specs=[
            whole(attended.shape),
            pl.BlockSpec((features // 2, inner), lambda j: (j, column)),
        ],
        out_specs=pl.BlockSpec((rows, features // 2), lambda j: (0, j)),
        out_shape=jax.ShapeDtypeStruct((rows, features), bf16),
        compiler_params=params(40),
        cost_estimate=cost(2 * rows * inner * features, 2 * inner * features),
        name="output_product",
    )(attended, weights)


def feed_kernel(
    normed_ref, cot_ref, gate_ref, up_ref, down_ref,
    act_ref, back_ref, feed_ref, total_ref, feed_total,
):
    step = pl.program_id(0)
    gate = dot(normed_ref[...], gate_ref[...], NN)
    upward = dot(normed_ref[...], up_ref[...], NN)
    back_mixed = dot(cot_ref[...], down_ref[...], NN)
    sigmoid = 1.0 / (1.0 + jnp.exp(-gate))
    activated = gate * sigmoid
    mixed = (activated * upward).astype(bf16)
    back_gate = (back_mixed * upward * sigmoid * (1.0 + gate * (1.0 - sigmoid))).astype(bf16)
    back_up = (back_mixed * activated).astype(bf16)
    act_ref[0] = back_gate
    act_ref[1] = back_up
    act_ref[2] = mixed
    part = dot(back_gate, gate_ref[...], NT) + dot(back_up, up_ref[...], NT)
    feed = dot(mixed, down_ref[...], NT)

    @pl.when(step == 0)
    def _():
        total_ref[...] = part
        feed_total[...] = feed

    @pl.when(step > 0)
    def _():
        total_ref[...] += part
        feed_total[...] += feed

    @pl.when(step == pl.num_programs(0) - 1)
    def _():
        back_ref[...] = total_ref[...].astype(bf16)
        feed_ref[...] = feed_total[...].astype(bf16)


def feed_forward(normed, cotangent, gate, up, down):
    rows, width = normed.shape
    hidden = gate.shape[1]
    steps = hidden // FEED_TILE
    tile_of = pl.BlockSpec((width, FEED_TILE), lambda j: (0, j))
    acts_of = pl.BlockSpec((3, rows, FEED_TILE), lambda j: (0, 0, j))
    full = whole((rows, width))
    return pl.pallas_call(
        feed_kernel,
        grid=(steps,),
        in_specs=[full, full] + [tile_of] * 3,
        out_specs=[acts_of, full, full],
        out_shape=[
            jax.ShapeDtypeStruct((3, rows, hidden), bf16),
            jax.ShapeDtypeStruct((rows, width), bf16),
            jax.ShapeDtypeStruct((rows, width), bf16),
        ],
        scratch_shapes=[pltpu.VMEM((rows, width), f32)] * 2,
        compiler_params=params(56),
        cost_estimate=cost(12 * rows * width * hidden, 6 * width * hidden),
        name="feed_forward",
    )(normed, cotangent, gate, up, down)


def middle_kernel(cot_ref, mine_ref, other_ref, middle_ref, gain_ref, w_ref, bm_ref, bb_ref, ba_ref, grad_ref):
    middle = middle_ref[...]
    scale = lax.rsqrt(jnp.mean(middle * middle, axis=1, keepdims=True) + epsilon)
    unit = middle * scale
    back = mine_ref[...].astype(f32) + other_ref[...].astype(f32)
    grad_ref[...] = jnp.sum(back * unit, axis=0, keepdims=True)
    inner = back * gain_ref[1:2, :]
    out = cot_ref[...].astype(f32) + scale * (
        inner - unit * jnp.mean(inner * unit, axis=1, keepdims=True)
    )
    bm_ref[...] = out
    low = out.astype(bf16)
    bb_ref[...] = low
    ba_ref[...] = dot(low, w_ref[...], NN).astype(bf16)


def middle_back(cotangent, mine, other, middle, gains, weights, column, inner):
    rows, width = middle.shape
    full = whole((rows, width))
    return pl.pallas_call(
        middle_kernel,
        grid=(1,),
        in_specs=[full, full, full, full, whole(gains.shape)]
        + [pl.BlockSpec((width, inner), lambda j: (0, column))],
        out_specs=[full, full, whole((rows, inner)), whole((1, width))],
        out_shape=[
            jax.ShapeDtypeStruct((rows, width), f32),
            jax.ShapeDtypeStruct((rows, width), bf16),
            jax.ShapeDtypeStruct((rows, inner), bf16),
            jax.ShapeDtypeStruct((1, width), f32),
        ],
        compiler_params=params(56),
        cost_estimate=cost(2 * rows * width * inner, 1.5e7),
        name="middle_back",
    )(cotangent, mine, other, middle, gains, weights)


def inputs_kernel(count, x_ref, qc_ref, cos_ref, sin_ref, w_ref, *refs):
    parts = refs[:count]
    cot_ref, back_ref, grad_ref = refs[count:]
    half = qc_ref.shape[1] // 2
    cot_ref[:, : 2 * half] = qc_ref[...]
    total = parts[0][...].astype(f32)
    for part in parts[1:]:
        total += part[...].astype(f32)
    for h in range(half // HEAD_SIZE):
        lanes = slice(h * HEAD_SIZE, (h + 1) * HEAD_SIZE)
        there = slice(2 * half + h * HEAD_SIZE, 2 * half + (h + 1) * HEAD_SIZE)
        cot_ref[:, there] = turned(total[:, lanes], cos_ref[...], sin_ref[...], -1).astype(bf16)
    cot_ref[:, 3 * half :] = total[:, half:].astype(bf16)
    back = dot(cot_ref[...], w_ref[...], NT)
    back_ref[...] = back.astype(bf16)
    x = x_ref[...].astype(f32)
    unit = x * lax.rsqrt(jnp.mean(x * x, axis=1, keepdims=True) + epsilon)
    grad_ref[...] = jnp.sum(back * unit, axis=0, keepdims=True)


def inputs_back(x, qc, cosine, sine, weights, parts):
    rows, width = x.shape
    inner = 2 * qc.shape[1]
    full = whole((rows, width))
    return pl.pallas_call(
        functools.partial(inputs_kernel, len(parts)),
        grid=(1,),
        in_specs=[full, whole(qc.shape), whole(cosine.shape), whole(sine.shape)]
        + [pl.BlockSpec((width, inner), lambda j: (0, 0))]
        + [whole(parts[0].shape)] * len(parts),
        out_specs=[whole((rows, inner)), full, whole((1, width))],
        out_shape=[
            jax.ShapeDtypeStruct((rows, inner), bf16),
            jax.ShapeDtypeStruct((rows, width), bf16),
            jax.ShapeDtypeStruct((1, width), f32),
        ],
        compiler_params=params(56),
        cost_estimate=cost(2 * rows * width * inner, 1.5e7),
        name="inputs_back",
    )(x, qc, cosine, sine, weights, *parts)


def final_kernel(bm_ref, mine_ref, other_ref, x_ref, gain_ref, o_ref):
    x = x_ref[...].astype(f32)
    scale = lax.rsqrt(jnp.mean(x * x, axis=1, keepdims=True) + epsilon)
    unit = x * scale
    inner = (mine_ref[...].astype(f32) + other_ref[...].astype(f32)) * gain_ref[0:1, :]
    out = bm_ref[...] + scale * (inner - unit * jnp.mean(inner * unit, axis=1, keepdims=True))
    o_ref[...] = out.astype(bf16)


def final_back(back_middle, mine, other, x, gains):
    rows, width = x.shape
    block = pl.BlockSpec((rows // 4, width), lambda j: (j, 0))
    return pl.pallas_call(
        final_kernel,
        grid=(4,),
        in_specs=[block] * 4 + [whole(gains.shape)],
        out_specs=block,
        out_shape=jax.ShapeDtypeStruct((rows, width), bf16),
        compiler_params=params(40),
        cost_estimate=cost(1e6, 1e7),
        name="final_back",
    )(back_middle, mine, other, x, gains)


def relative(field, pairs, ctxs):
    dp, ctx = lax.axis_index("dp"), lax.axis_index("ctx")
    shaped = field.reshape((pairs, 2, ctxs, -1) + field.shape[1:])
    for axis, shift in ((0, dp // 2 + 1), (1, dp % 2 + 1), (2, ctx + 1)):
        shaped = jnp.roll(shaped, -shift, axis)
    return shaped.swapaxes(0, 1).reshape(field.shape)


def gradient_kernel(pairs, ctxs, place, a_ref, b_ref, send_ref, keep_ref):
    width = a_ref.shape[1]
    section = width // (2 * pairs)
    piece = section // ctxs
    for c, out in ((1, send_ref), (0, keep_ref)):
        for y in range(pairs):
            pair = lax.rem(place[0] + y + 1, pairs)
            core = lax.rem(place[1] + c, 2)
            lanes = pl.ds(pl.multiple_of((pair * 2 + core) * section, LANES), section)
            result = dot(a_ref[:, lanes], b_ref[...], TN).astype(bf16)
            for z in range(ctxs):
                far = lax.rem(z + ctxs - place[2] - 1 + ctxs, ctxs)
                rows = pl.ds(pl.multiple_of(y * section + far * piece, piece), piece)
                out[rows, :] = result[z * piece : (z + 1) * piece]


def gradient(a, b, pairs, ctxs):
    rows, width = a.shape
    columns = b.shape[1]
    section = width // (2 * pairs)
    if section % LANES or (section // ctxs) % 32:
        ordered = relative(dot(a, b, TN).astype(bf16), pairs, ctxs)
        return ordered[: width // 2], ordered[width // 2 :]
    dp, ctx = lax.axis_index("dp"), lax.axis_index("ctx")
    place = jnp.stack([dp // 2, dp % 2, ctx]).astype(jnp.int32)
    tile = TILE if columns % TILE == 0 else columns // 2
    block = pl.BlockSpec((width // 2, tile), lambda j: (0, j))
    return pl.pallas_call(
        functools.partial(gradient_kernel, pairs, ctxs),
        grid=(columns // tile,),
        in_specs=[SCALARS, whole(a.shape), pl.BlockSpec((rows, tile), lambda j: (0, j))],
        out_specs=[block, block],
        out_shape=[jax.ShapeDtypeStruct((width // 2, columns), bf16)] * 2,
        compiler_params=params(40),
        cost_estimate=cost(2 * rows * width * columns, 2 * width * columns),
        name="gradient",
    )(place, a, b)


def shifted(field, axis, steps, stride=1):
    count = lax.axis_size(axis)
    return lax.ppermute(
        field, axis, [(i, (i + steps * stride) % count) for i in range(count)]
    )


def other_core(field):
    return lax.ppermute(field, "dp", [(i, i ^ 1) for i in range(lax.axis_size("dp"))])


def sum_to_owner(send, keep, pairs, ctxs):
    columns = send.shape[1]
    got = other_core(send).reshape(pairs, -1, columns)
    keep = keep.reshape(pairs, -1, columns)
    total = got[-1].astype(f32) + keep[-1].astype(f32)
    for y in range(1, pairs):
        part = (got[y - 1].astype(f32) + keep[y - 1].astype(f32)).astype(bf16)
        total = total + shifted(part, "dp", y, 2).astype(f32)
    total = total.reshape(ctxs, -1, columns)
    result = total[-1]
    for z in range(1, ctxs):
        result = result + shifted(total[z - 1].astype(bf16), "ctx", z).astype(f32)
    return result


def swapped(field):
    count = lax.axis_size("tp")
    return lax.ppermute(field, "tp", [(i, count - 1 - i) for i in range(count)])


def body(
    tokens,
    cotangent,
    lengths,
    block_order,
    pre_gain,
    query_weight,
    key_weight,
    value_weight,
    output_weight,
    mid_gain,
    gate_weight,
    up_weight,
    down_weight,
):
    ctxs = lax.axis_size("ctx")
    pairs = lax.axis_size("dp") // 2
    ctx = lax.axis_index("ctx")
    order = block_order[0]
    ends = jnp.cumsum(lengths[0]).astype(jnp.int32)
    starts = ends - lengths[0]
    place = jnp.stack([ctx]).astype(jnp.int32)
    q_cols = query_weight.shape[1]
    features = tokens.shape[1]

    gain_columns = jnp.pad(jnp.stack([pre_gain, mid_gain], axis=1), ((0, 0), (0, LANES - 2)))
    packed = (query_weight, key_weight, value_weight, gain_columns, output_weight)
    stream = streams(order, ctx)
    lows = jnp.max(jnp.where(starts[None, :] <= stream[0][:, None], starts[None, :], 0), axis=1)
    if pairs == 2 and ctxs == 4 and query_weight.shape[0] % 32 == 0:
        own = jnp.stack([stream[0], lows])
        qi = jnp.concatenate([own, stream, jnp.zeros_like(own)], axis=0)
        (
            first, gate_full, up_full, down_full, queries, kv, normed, gains,
            attended_low, att, sums, middle, mid_normed, cosine, sine, ki,
        ) = forward_all(
            packed, gate_weight, up_weight, down_weight, tokens, frequencies(), qi, q_cols, ctxs
        )
        act, back_part, feed = feed_forward(mid_normed, cotangent, gate_full, up_full, down_full)
        _, _, _, result, token_gradient, grads, _, _ = back_all(
            back_part, feed, cotangent, middle, gains, act, mid_normed, tokens, normed,
            attended_low, queries, kv, att, sums, qi, ki, cosine, sine, first, ctxs,
        )
        wide = lambda *tiles: jnp.concatenate([grads[t] for t in tiles], axis=1)
        tail = q_cols - TILE
        qkv_gradient = jnp.concatenate(
            [grads[13], grads[14][:, :tail], grads[15], grads[16][:, :tail]], axis=1
        )
        output_gradient = jnp.concatenate([grads[12], grads[14][:, tail:]], axis=1)
        gain_sums = grads[16][:, tail : tail + LANES]
        gate_gradient, up_gradient = wide(0, 1, 2, 3), wide(4, 5, 6, 7)
        down_gradient = wide(8, 9, 10, 11)
    else:
        first, gate_full, up_full, down_full = (
            lax.all_gather(field, ROWS, axis=0, tiled=True)
            for field in (jnp.concatenate(packed, axis=1), gate_weight, up_weight, down_weight)
        )
        cosine, sine = angles(stream[0] - lows)
        gains = first[:, 2 * q_cols : 2 * q_cols + 8].T.astype(f32)
        queries, kv, normed = project(tokens, gains, cosine, sine, first, q_cols)
        pieces = [kv] + [shifted(kv, "ctx", k) for k in range(1, ctxs)]
        output_weights = first[:, 2 * q_cols + LANES :]
        attended_low, att, sums = attend(order, starts, place, queries, pieces)
        branch = output_product(attended_low, output_weights, 0, features)
        middle = tokens.astype(f32) + (branch.astype(f32) + swapped(branch).astype(f32))
        mid_scale = lax.rsqrt(jnp.mean(middle * middle, axis=1, keepdims=True) + epsilon)
        mid_normed = (middle * mid_scale * gains[1:2]).astype(bf16)
        act, back_part, feed = feed_forward(mid_normed, cotangent, gate_full, up_full, down_full)
        back_other = swapped(back_part)
        gate_parts = gradient(mid_normed, act[0], pairs, ctxs)
        up_parts = gradient(mid_normed, act[1], pairs, ctxs)
        down_parts = gradient(cotangent, act[2], pairs, ctxs)
        result = (middle + feed.astype(f32) + swapped(feed).astype(f32)).astype(bf16)

        back_middle, back_branch, back_attended, mid_grad = middle_back(
            cotangent, back_part, back_other, middle, gains, output_weights, 0, q_cols
        )
        output_parts = gradient(back_branch, attended_low, pairs, ctxs)
        back = attend_back(
            order, starts, place, queries, back_attended, att, sums, cosine, sine, pieces
        )
        own_parts = [back[1]] + [shifted(back[1 + k], "ctx", -k) for k in range(1, ctxs)]
        cot, normed_part, pre_grad = inputs_back(
            tokens, back[0], cosine, sine, first, own_parts
        )
        normed_other = swapped(normed_part)
        qkv_parts = gradient(normed, cot, pairs, ctxs)
        token_gradient = final_back(back_middle, normed_part, normed_other, tokens, gains)

        mid_once = jnp.where(lax.axis_index("tp") == 0, mid_grad, 0.0)
        pair = jnp.concatenate([pre_grad, mid_once], axis=0).astype(bf16)
        pair = jnp.pad(pair, ((0, 6), (0, 0))).T
        ordered = relative(pair, pairs, ctxs)
        gain_sums = sum_to_owner(
            ordered[: features // 2], ordered[features // 2 :], pairs, ctxs
        )
        gain_sums = gain_sums + swapped(gain_sums)
        gate_gradient = sum_to_owner(*gate_parts, pairs, ctxs)
        up_gradient = sum_to_owner(*up_parts, pairs, ctxs)
        down_gradient = sum_to_owner(*down_parts, pairs, ctxs)
        output_gradient = sum_to_owner(*output_parts, pairs, ctxs)
        qkv_gradient = sum_to_owner(*qkv_parts, pairs, ctxs)
    return (
        result,
        token_gradient,
        gain_sums[:, 0],
        qkv_gradient[:, :q_cols],
        qkv_gradient[:, q_cols : q_cols + q_cols // 2],
        qkv_gradient[:, q_cols + q_cols // 2 :],
        output_gradient,
        gain_sums[:, 1],
        gate_gradient,
        up_gradient,
        down_gradient,
    )


def solution(mesh):
    rows, split = P(ROWS, None), P(ROWS, "tp")
    return jax.shard_map(
        body,
        mesh=mesh,
        in_specs=(rows, rows, P("dp", None), P("dp", None, None), P(ROWS))
        + (split,) * 4
        + (P(ROWS),)
        + (split,) * 3,
        out_specs=(rows, rows, P(ROWS)) + (split,) * 4 + (P(ROWS),) + (split,) * 3,
        check_vma=False,
    )
```

```python
import functools
import math

import jax
import jax.numpy as jnp
import numpy as np
from jax import lax
from jax.experimental import pallas as pl
from jax.experimental.pallas import tpu as pltpu
from jax.sharding import PartitionSpec as P

HEAD_SIZE = 96
HALF = HEAD_SIZE // 2
BLOCK = 64
SPAN = 256
TILE = 512
FEED_TILE = 512
LANES = 128

epsilon = 1e-05
rotary_base = 100000.0
masked_score = -1e30
SCALE = HEAD_SIZE**-0.5
SCALE2 = SCALE / math.log(2.0)

f32 = jnp.float32
bf16 = jnp.bfloat16
ROWS = ("dp", "ctx")
MIB = 2**20


def dot(left, right, contract):
    return lax.dot_general(
        left, right, ((contract[:1], contract[1:]), ((), ())), preferred_element_type=f32
    )


NN, NT, TN = (1, 0), (1, 1), (0, 0)


def cost(flops, moved):
    return pl.CostEstimate(flops=int(flops), bytes_accessed=int(moved), transcendentals=0)


def params(mib):
    return pltpu.CompilerParams(vmem_limit_bytes=mib * MIB)


def whole(shape):
    return pl.BlockSpec(shape, lambda *_: (0,) * len(shape))


SCALARS = pl.BlockSpec(memory_space=pltpu.SMEM)


def frequencies():
    steps = np.arange(HALF, dtype=np.float64) * 2.0 / HEAD_SIZE
    return jnp.asarray(rotary_base ** -steps, f32)[None, :]


def angles(place):
    turn = place.astype(f32)[:, None] * frequencies()
    return (jnp.cos(turn), jnp.sin(turn))


def streams(order, ctx):
    rounds, count = order.shape
    owners = order[:, lax.rem(ctx - jnp.arange(count) + count, count)].T
    blocks = owners + (jnp.arange(rounds, dtype=jnp.int32) * count)[None, :]
    within = jnp.arange(BLOCK, dtype=jnp.int32)
    return (blocks[:, :, None] * BLOCK + within).reshape(count, rounds * BLOCK).astype(jnp.int32)


def turned(head, cosine, sine, sign):
    first, second = head[:, :HALF], head[:, HALF:]
    along = sine if sign > 0 else -sine
    return jnp.concatenate(
        [first * cosine - second * along, second * cosine + first * along], axis=1
    )


def project_kernel(x_ref, gain_ref, cos_ref, sin_ref, w_ref, q_ref, kv_ref, normed_ref):
    step = pl.program_id(0)
    tile = w_ref.shape[1]

    @pl.when(step == 0)
    def _():
        x = x_ref[...].astype(f32)
        scale = lax.rsqrt(jnp.mean(x * x, axis=1, keepdims=True) + epsilon)
        normed_ref[...] = (x * scale * gain_ref[0:1, :]).astype(bf16)

    out = dot(normed_ref[...], w_ref[...], NN)

    def rotated(ref):
        for h in range(tile // HEAD_SIZE):
            lanes = slice(h * HEAD_SIZE, (h + 1) * HEAD_SIZE)
            ref[:, lanes] = turned(out[:, lanes], cos_ref[...], sin_ref[...], 1).astype(bf16)

    @pl.when(step < 2)
    def _():
        rotated(q_ref)

    @pl.when(step == 2)
    def _():
        rotated(kv_ref)

    @pl.when(step == 3)
    def _():
        kv_ref[...] = out.astype(bf16)


def project(x, gains, cosine, sine, weights, q_cols):
    rows, width = x.shape
    tile = q_cols // 2
    return pl.pallas_call(
        project_kernel,
        grid=(4,),
        in_specs=[
            whole(x.shape),
            whole(gains.shape),
            whole(cosine.shape),
            whole(sine.shape),
            pl.BlockSpec((width, tile), lambda j: (0, j)),
        ],
        out_specs=[
            pl.BlockSpec((rows, tile), lambda j: (0, jnp.minimum(j, 1))),
            pl.BlockSpec((rows, tile), lambda j: (0, jnp.maximum(j - 2, 0))),
            whole((rows, width)),
        ],
        out_shape=[
            jax.ShapeDtypeStruct((rows, q_cols), bf16),
            jax.ShapeDtypeStruct((rows, q_cols), bf16),
            jax.ShapeDtypeStruct((rows, width), bf16),
        ],
        compiler_params=params(40),
        cost_estimate=cost(2 * rows * width * 4 * tile, 2 * width * 4 * tile),
        name="project",
    )(x, gains, cosine, sine, weights)


MESH = pl.DeviceIdType.MESH


def forward_kernel(
    query_shard, key_shard, value_shard, gain_shard, out_shard, gate_shard, up_shard, down_shard,
    x_ref, frequency_ref, qi_ref,
    full_ref, gate_ref, up_ref, down_ref, q_out, kv_out, normed_out, gain_out, low_out, att_out, sum_out,
    middle_out, mid_normed_out, cos_out, sin_out, ki_out,
    q_ref, kv_ref, normed_ref, gain_ref, low_ref, att_ref, sum_ref,
    middle_ref, mid_normed_ref, cos_ref, sin_ref, ki_ref,
    branch_ref, other_ref, w_ref, qt_ref, top_ref, total_ref,
    z_send, z_recv, y_send, y_recv, c_send, c_recv, k_send, k_recv, x_send, x_recv, local, save_sem,
):
    ctxs = lax.axis_size("ctx")
    dp, ctx, tp = lax.axis_index("dp"), lax.axis_index("ctx"), lax.axis_index("tp")
    far, core = (lax.rem(dp + 2, 4), ctx, tp), (dp + 1 - 2 * lax.rem(dp, 2), ctx, tp)
    after, before = (dp, lax.rem(ctx + 1, ctxs), tp), (dp, lax.rem(ctx + ctxs - 1, ctxs), tp)
    across = (dp, ctx, 1 - tp)
    piece = query_shard.shape[0]
    mine = pl.ds(pl.multiple_of((dp * ctxs + ctx) * piece, piece), piece)
    packs, column = [], 0
    for j, part in enumerate((query_shard, key_shard, value_shard, gain_shard, out_shard)):
        target = w_ref.at[mine, pl.ds(column, part.shape[1])]
        packs.append(pltpu.make_async_copy(part, target, local.at[5 + j]))
        packs[-1].start()
        column += part.shape[1]
    barrier = pltpu.get_barrier_semaphore()
    for device in (after, before, far, core, across):
        pl.semaphore_signal(barrier, inc=1, device_id=device, device_id_type=MESH)
    pl.semaphore_wait(barrier, 5)
    shards = (w_ref.at[mine], gate_shard, up_shard, down_shard)
    wholes = (w_ref, gate_ref, up_ref, down_ref)
    last = ctxs - 1


    def place(group, pair, steps):
        owner = pair * ctxs + lax.rem(ctx - steps + ctxs, ctxs)
        return wholes[group].at[pl.ds(pl.multiple_of(owner * piece, piece), piece)]

    def source(group, steps):
        return place(group, dp, steps) if steps else shards[group]

    def remote(source, target, device, sent, got):
        return pltpu.make_async_remote_copy(source, target, device_id=device, device_id_type=MESH, send_sem=sent, recv_sem=got)

    def ring(group, s):
        return remote(
            source(group, s), place(group, dp, s), after, z_send.at[group, s], z_recv.at[group, s]
        )

    def over(group, s):
        return remote(
            source(group, s), place(group, dp, s), far, y_send.at[group, s], y_recv.at[group, s]
        )

    def aside(group, s):
        return remote(
            source(group, s), place(group, dp, s), core, c_send.at[group, s], c_recv.at[group, s]
        )

    def aside_far(group, s):
        there = place(group, far[0], s)
        return remote(
            there, there, core, c_send.at[group, ctxs + s], c_recv.at[group, ctxs + s]
        )

    def own_copy(group):
        return pltpu.make_async_copy(shards[group], place(group, dp, 0), local.at[group])

    def begin(group):
        over(group, 0).start()
        aside(group, 0).start()
        if group:
            own_copy(group).start()

    def along(group, s):
        ring(group, s - 1).wait_recv()
        if s < last:
            ring(group, s).start()
        over(group, s).start()
        aside(group, s).start()

    def came_over(group, s):
        over(group, s).wait_recv()
        aside_far(group, s).start()

    def gathered(group):
        if group:
            own_copy(group).wait()
        for s in range(ctxs):
            aside(group, s).wait_recv()
            aside_far(group, s).wait_recv()

    saves = []

    def save(*pairs):
        for have, out in pairs:
            saves.append(pltpu.make_async_copy(have, out, save_sem.at[len(saves)]))
            saves[-1].start()

    first, gate, up, down = range(4)
    for copy in packs:
        copy.wait()
    ring(first, 0).start()
    begin(first)
    columns = qi_ref[...].astype(f32).T
    turn = (columns[:, 0:1] - columns[:, 1:2]) * frequency_ref[...]
    cos_ref[...] = jnp.cos(turn)
    sin_ref[...] = jnp.sin(turn)
    for k in range(ctxs):
        ki_ref[k] = columns[:, 2 + k : 3 + k].astype(jnp.int32)
    x = x_ref[...].astype(f32)
    unit = x * lax.rsqrt(jnp.mean(x * x, axis=1, keepdims=True) + epsilon)
    for s in range(1, ctxs):
        along(first, s)
        came_over(first, s - 1)
    ring(gate, 0).start()
    begin(gate)
    ring(up, 0).start()
    came_over(first, last)
    begin(up)
    gathered(first)
    full = pltpu.make_async_copy(w_ref, full_ref, local.at[4])
    full.start()
    along(gate, 1)

    q_cols = q_ref.shape[1]
    tile = q_cols // 2
    groups = kv_ref.shape[2] // (2 * HEAD_SIZE)
    ratio = q_cols // (groups * HEAD_SIZE)
    gains = w_ref[:, 2 * q_cols : 2 * q_cols + LANES].astype(f32).T[:8]
    gain_ref[...] = gains
    normed_ref[...] = (unit * gains[0:1]).astype(bf16)
    save((gain_ref, gain_out), (normed_ref, normed_out), (cos_ref, cos_out), (sin_ref, sin_out), (ki_ref, ki_out))

    def product(step):
        return dot(normed_ref[...], w_ref[:, step * tile : (step + 1) * tile], NN)

    def rotated(out, store):
        for h in range(tile // HEAD_SIZE):
            lanes = slice(h * HEAD_SIZE, (h + 1) * HEAD_SIZE)
            store(lanes, turned(out[:, lanes], cos_ref[...], sin_ref[...], 1).astype(bf16))

    def key_store(lanes, value):
        kv_ref[0, :, lanes] = value

    rotated(product(2), key_store)
    kv_ref[0, :, tile:] = product(3).astype(bf16)

    def kv_copy(s):
        return remote(kv_ref.at[s], kv_ref.at[s + 1], after, k_send.at[s], k_recv.at[s])

    kv_copy(0).start()
    begin(down)
    for step in range(2):

        def query_store(lanes, value):
            q_ref[:, step * tile + lanes.start : step * tile + lanes.stop] = value

        rotated(product(step), query_store)

    def attention(k):
        dense_piece(k, kv_ref, qi_ref, ki_ref, groups, ratio, qt_ref, top_ref, total_ref, att_ref)

    dense_begin(q_ref, groups, ratio, qt_ref, top_ref, total_ref, att_ref)
    along(gate, 2)
    came_over(gate, 0)
    waits = [
        [lambda: along(up, 1), lambda: along(gate, last), lambda: came_over(gate, 1), lambda: came_over(up, 0)],
        [lambda: ring(down, 0).start(), lambda: came_over(down, 0), lambda: came_over(gate, 2)],
        [lambda: along(up, 2)],
    ]

    def attention_step(k, unused):
        for s in range(1, ctxs):

            @pl.when(k == s)
            def _(s=s):
                kv_copy(s - 1).wait_recv()
                if s < last:
                    kv_copy(s).start()
                for step in waits[s - 1] if s - 1 < len(waits) else []:
                    step()

        attention(k)
        return unused

    lax.fori_loop(0, ctxs, attention_step, 0)
    save((q_ref, q_out), (kv_ref, kv_out))
    dense_end(groups, ratio, top_ref, total_ref, att_ref, sum_ref, low_ref)
    save((low_ref, low_out), (att_ref, att_out), (sum_ref, sum_out))
    branch_ref[...] = dot(low_ref[...], w_ref[:, 2 * q_cols + LANES :], NT).astype(bf16)
    exchange = remote(branch_ref, other_ref, across, x_send.at[0], x_recv.at[0])
    exchange.start()

    along(down, 1)
    came_over(gate, last)
    came_over(up, 1)
    along(up, last)
    came_over(up, 2)
    along(down, 2)
    came_over(down, 1)
    came_over(up, last)
    along(down, last)
    came_over(down, 2)
    exchange.wait_recv()
    few = 64

    def middle_rows(i, unused):
        here = pl.ds(pl.multiple_of(i * few, few), few)
        middle = x_ref[here, :].astype(f32) + (
            branch_ref[here, :].astype(f32) + other_ref[here, :].astype(f32)
        )
        middle_ref[here, :] = middle
        scale = lax.rsqrt(jnp.mean(middle * middle, axis=1, keepdims=True) + epsilon)
        mid_normed_ref[here, :] = (middle * scale * gain_ref[1:2, :]).astype(bf16)
        return unused

    lax.fori_loop(0, x_ref.shape[0] // few, middle_rows, 0)
    save((middle_ref, middle_out), (mid_normed_ref, mid_normed_out))
    came_over(down, last)
    for group in (gate, up, down):
        gathered(group)
    for group in range(4):
        for s in range(ctxs):
            if s < last:
                ring(group, s).wait_send()
            over(group, s).wait_send()
            aside(group, s).wait_send()
            aside_far(group, s).wait_send()
    for s in range(last):
        kv_copy(s).wait_send()
    exchange.wait_send()
    full.wait()
    for copy in saves:
        copy.wait()


def forward_all(packed, gate, up, down, x, frequency, qi, q_cols, ctxs):
    rows, width = x.shape
    columns, hidden = sum(part.shape[1] for part in packed), gate.shape[1]
    groups = q_cols // 2 // HEAD_SIZE
    tiles, lanes = dense_shapes(rows, groups, 2)
    vmem, hbm = pl.BlockSpec(memory_space=pltpu.VMEM), pl.BlockSpec(memory_space=pl.ANY)
    sems = lambda *n: pltpu.SemaphoreType.DMA(n)
    shape = jax.ShapeDtypeStruct
    full = shape((rows, width), bf16)
    kept = [
        shape((rows, q_cols), bf16),
        shape((ctxs, rows, q_cols), bf16),
        full,
        shape((8, width), f32),
        shape((rows, q_cols), bf16),
        shape((tiles, HEAD_SIZE, lanes), f32),
        shape((tiles, 1, lanes), f32),
        shape((rows, width), f32),
        full,
        shape((rows, HALF), f32),
        shape((rows, HALF), f32),
        shape((ctxs, rows, 1), jnp.int32),
    ]
    return pl.pallas_call(
        forward_kernel,
        in_specs=[hbm] * (len(packed) + 3) + [vmem] * 3,
        out_specs=[hbm] * 16,
        out_shape=[
            shape((width, columns), bf16),
            shape((width, hidden), bf16),
            shape((width, hidden), bf16),
            shape((width, hidden), bf16),
        ]
        + kept,
        scratch_shapes=[pltpu.VMEM(part.shape, part.dtype) for part in kept]
        + [
            pltpu.VMEM((rows, width), bf16),
            pltpu.VMEM((rows, width), bf16),
            pltpu.VMEM((width, columns), bf16),
            pltpu.VMEM((tiles, HEAD_SIZE, lanes), bf16),
            pltpu.VMEM((tiles, 1, lanes), f32),
            pltpu.VMEM((tiles, 1, lanes), f32),
        ]
        + [sems(4, ctxs - 1)] * 2
        + [sems(4, ctxs)] * 2
        + [sems(4, 2 * ctxs)] * 2
        + [sems(ctxs - 1)] * 2
        + [sems(1)] * 2
        + [sems(5 + len(packed)), sems(len(kept))],
        compiler_params=pltpu.CompilerParams(
            vmem_limit_bytes=56 * MIB, collective_id=0, has_side_effects=True
        ),
        cost_estimate=cost(1e10, 1e8),
        name="forward_all",
    )(*packed, gate, up, down, x, frequency, qi)


def gather_stream(order, ctx, pieces, k_ref, v_ref):
    count, groups = len(pieces), k_ref.shape[0]
    width = groups * HEAD_SIZE

    def fill(i, unused):
        source = pl.ds(pl.multiple_of(i * BLOCK, BLOCK), BLOCK)
        for k, piece in enumerate(pieces):
            block = i * count + order[i, lax.rem(ctx - k + count, count)]
            target = pl.ds(pl.multiple_of(block * BLOCK, BLOCK), BLOCK)
            for g in range(groups):
                lanes = slice(g * HEAD_SIZE, (g + 1) * HEAD_SIZE)
                k_ref[g, target, :] = piece[source, lanes]
                v_ref[g, target, :] = piece[
                    source, width + g * HEAD_SIZE : width + (g + 1) * HEAD_SIZE
                ]
        return unused

    lax.fori_loop(0, order.shape[0], fill, 0)


def reach(starts, first):
    low = jnp.int32(0)
    for j in range(starts.shape[0]):
        low = jnp.where(starts[j] <= first, starts[j], low)
    return low


def row_limits(starts, first, lanes):
    row = first + lax.rem(lax.broadcasted_iota(jnp.int32, (1, lanes), 1), BLOCK)
    low = jnp.zeros((1, lanes), jnp.int32)
    for j in range(starts.shape[0]):
        low = jnp.where(row >= starts[j], starts[j], low)
    return row, low


def stacked(ref, rows, group, ratio):
    return jnp.concatenate(
        [
            ref[rows, (group * ratio + h) * HEAD_SIZE : (group * ratio + h + 1) * HEAD_SIZE]
            for h in range(ratio)
        ],
        axis=0,
    )


def attend_kernel(count, order, starts, place, q_ref, *refs):
    pieces = refs[:count]
    low_ref, att_ref, sum_ref, k_ref, v_ref = refs[count:]
    groups = k_ref.shape[0]
    ratio = q_ref.shape[1] // (groups * HEAD_SIZE)
    lanes = ratio * BLOCK
    ctx = place[0]
    gather_stream(order, ctx, pieces, k_ref, v_ref)

    def one(i, unused):
        first = (i * count + order[i, ctx]) * BLOCK
        row, low = row_limits(starts, first, lanes)
        begin = reach(starts, first) // SPAN
        end = (first + BLOCK - 1) // SPAN + 1
        rows = pl.ds(pl.multiple_of(i * BLOCK, BLOCK), BLOCK)
        queries = [stacked(q_ref, rows, g, ratio) for g in range(groups)]

        def chunk(c, carry):
            keys = pl.ds(pl.multiple_of(c * SPAN, SPAN), SPAN)
            index = c * SPAN + lax.broadcasted_iota(jnp.int32, (SPAN, lanes), 0)
            allowed = (index <= row) & (index >= low)
            new = []
            for g in range(groups):
                top, total, out = carry[g]
                raw = dot(k_ref[g, keys, :], queries[g], NT) * SCALE2
                raw = jnp.where(allowed, raw, masked_score)
                new_top = jnp.maximum(top, jnp.max(raw, axis=0, keepdims=True))
                weights = jnp.where(allowed, jnp.exp2(raw - new_top), 0.0)
                back = jnp.exp2(top - new_top)
                total = total * back + jnp.sum(weights, axis=0, keepdims=True)
                out = out * back + dot(v_ref[g, keys, :], weights.astype(bf16), TN)
                new.append((new_top, total, out))
            return tuple(new)

        blank = (
            jnp.full((1, lanes), masked_score, f32),
            jnp.zeros((1, lanes), f32),
            jnp.zeros((HEAD_SIZE, lanes), f32),
        )
        result = lax.fori_loop(begin, end, chunk, (blank,) * groups)
        for g in range(groups):
            top, total, out = result[g]
            out = out / total
            att_ref[i * groups + g] = out
            sum_ref[pl.ds(i * groups + g, 1), :] = top + jnp.log2(total)
            flat = out.T.astype(bf16)
            for h in range(ratio):
                head = g * ratio + h
                low_ref[rows, head * HEAD_SIZE : (head + 1) * HEAD_SIZE] = flat[
                    h * BLOCK : (h + 1) * BLOCK
                ]
        return unused

    lax.fori_loop(0, order.shape[0], one, 0)


def attend(order, starts, place, queries, pieces):
    count, rows = len(pieces), queries.shape[0]
    groups = pieces[0].shape[1] // (2 * HEAD_SIZE)
    ratio = queries.shape[1] // (groups * HEAD_SIZE)
    rounds, lanes = order.shape[0], ratio * BLOCK
    return pl.pallas_call(
        functools.partial(attend_kernel, count),
        in_specs=[SCALARS] * 3 + [pl.BlockSpec(memory_space=pltpu.VMEM)] * (1 + count),
        out_specs=[pl.BlockSpec(memory_space=pltpu.VMEM)] * 3,
        out_shape=[
            jax.ShapeDtypeStruct(queries.shape, bf16),
            jax.ShapeDtypeStruct((rounds * groups, HEAD_SIZE, lanes), f32),
            jax.ShapeDtypeStruct((rounds * groups, lanes), f32),
        ],
        scratch_shapes=[pltpu.VMEM((groups, count * rows, HEAD_SIZE), bf16)] * 2,
        compiler_params=params(40),
        cost_estimate=cost(8e9, 1e7),
        name="attend",
    )(order, starts, place, queries, *pieces)


def attend_back_kernel(count, order, starts, place, q_ref, d_ref, att_ref, sum_ref, cos_ref, sin_ref, *refs):
    pieces = refs[:count]
    qc_ref = refs[count]
    outs = refs[count + 1 : 2 * count + 1]
    k_ref, v_ref, dk_ref, dv_ref = refs[2 * count + 1 :]
    groups = k_ref.shape[0]
    ratio = q_ref.shape[1] // (groups * HEAD_SIZE)
    lanes = ratio * BLOCK
    width = groups * HEAD_SIZE
    ctx = place[0]
    gather_stream(order, ctx, pieces, k_ref, v_ref)
    dk_ref[...] = jnp.zeros_like(dk_ref)
    dv_ref[...] = jnp.zeros_like(dv_ref)

    def one(i, unused):
        first = (i * count + order[i, ctx]) * BLOCK
        row, low = row_limits(starts, first, lanes)
        begin = reach(starts, first) // SPAN
        end = (first + BLOCK - 1) // SPAN + 1
        rows = pl.ds(pl.multiple_of(i * BLOCK, BLOCK), BLOCK)
        queries = [stacked(q_ref, rows, g, ratio) for g in range(groups)]
        slopes = [stacked(d_ref, rows, g, ratio) for g in range(groups)]
        sums, deltas = [], []
        for g in range(groups):
            sums.append(sum_ref[pl.ds(i * groups + g, 1), :])
            across = slopes[g].astype(f32).T
            deltas.append(jnp.sum(across * att_ref[i * groups + g], axis=0, keepdims=True))

        def chunk(c, carry):
            keys = pl.ds(pl.multiple_of(c * SPAN, SPAN), SPAN)
            index = c * SPAN + lax.broadcasted_iota(jnp.int32, (SPAN, lanes), 0)
            allowed = (index <= row) & (index >= low)
            new = []
            for g in range(groups):
                key, value = k_ref[g, keys, :], v_ref[g, keys, :]
                raw = dot(key, queries[g], NT) * SCALE2
                share = jnp.where(allowed, jnp.exp2(jnp.minimum(raw - sums[g], 0.0)), 0.0)
                back_share = dot(value, slopes[g], NT)
                back = (share * (back_share - deltas[g])).astype(bf16)
                dv_ref[g, keys, :] += dot(share.astype(bf16), slopes[g], NN)
                dk_ref[g, keys, :] += dot(back, queries[g], NN)
                new.append(carry[g] + dot(key, back, TN))
            return tuple(new)

        blank = jnp.zeros((HEAD_SIZE, lanes), f32)
        result = lax.fori_loop(begin, end, chunk, (blank,) * groups)
        cosine, sine = cos_ref[rows, :], sin_ref[rows, :]
        for g in range(groups):
            flat = result[g].T * SCALE
            for h in range(ratio):
                head = g * ratio + h
                qc_ref[rows, head * HEAD_SIZE : (head + 1) * HEAD_SIZE] = turned(
                    flat[h * BLOCK : (h + 1) * BLOCK], cosine, sine, -1
                ).astype(bf16)
        return unused

    lax.fori_loop(0, order.shape[0], one, 0)

    def spread(i, unused):
        target = pl.ds(pl.multiple_of(i * BLOCK, BLOCK), BLOCK)
        for k, out in enumerate(outs):
            block = i * count + order[i, lax.rem(ctx - k + count, count)]
            source = pl.ds(pl.multiple_of(block * BLOCK, BLOCK), BLOCK)
            for g in range(groups):
                out[target, g * HEAD_SIZE : (g + 1) * HEAD_SIZE] = (
                    dk_ref[g, source, :] * SCALE
                ).astype(bf16)
                out[target, width + g * HEAD_SIZE : width + (g + 1) * HEAD_SIZE] = dv_ref[
                    g, source, :
                ].astype(bf16)
        return unused

    lax.fori_loop(0, order.shape[0], spread, 0)


def attend_back(order, starts, place, queries, slopes, att, sums, cosine, sine, pieces):
    count, rows = len(pieces), queries.shape[0]
    groups = pieces[0].shape[1] // (2 * HEAD_SIZE)
    keys = (groups, count * rows, HEAD_SIZE)
    return pl.pallas_call(
        functools.partial(attend_back_kernel, count),
        in_specs=[SCALARS] * 3 + [pl.BlockSpec(memory_space=pltpu.VMEM)] * (6 + count),
        out_specs=[pl.BlockSpec(memory_space=pltpu.VMEM)] * (1 + count),
        out_shape=[jax.ShapeDtypeStruct(queries.shape, bf16)]
        + [jax.ShapeDtypeStruct(pieces[0].shape, bf16)] * count,
        scratch_shapes=[pltpu.VMEM(keys, bf16)] * 2 + [pltpu.VMEM(keys, f32)] * 2,
        compiler_params=params(56),
        cost_estimate=cost(16e9, 2e7),
        name="attend_back",
    )(order, starts, place, queries, slopes, att, sums, cosine, sine, *pieces)


SIDE = 256


def tile_bias(qi_ref, ki_ref, k, q_tile, k_tile, ratio):
    rows = slice(q_tile * SIDE, (q_tile + 1) * SIDE)
    keys = ki_ref[k, k_tile * SIDE : (k_tile + 1) * SIDE, :]
    allowed = (keys <= qi_ref[0:1, rows]) & (keys >= qi_ref[1:2, rows])
    bias = jnp.where(allowed, 0.0, masked_score)
    return jnp.concatenate([bias] * ratio, axis=1)


def flat_heads(ref, q_tile, group, ratio):
    return jnp.concatenate(
        [
            ref[
                q_tile * SIDE : (q_tile + 1) * SIDE,
                (group * ratio + h) * HEAD_SIZE : (group * ratio + h + 1) * HEAD_SIZE,
            ]
            for h in range(ratio)
        ],
        axis=0,
    )


def head_lanes(g, offset=0):
    return slice(offset + g * HEAD_SIZE, offset + (g + 1) * HEAD_SIZE)


def dense_begin(q_ref, groups, ratio, qt_ref, top_ref, total_ref, att_ref):
    for q_tile in range(q_ref.shape[0] // SIDE):
        for g in range(groups):
            flat = flat_heads(q_ref, q_tile, g, ratio)
            qt_ref[q_tile * groups + g] = flat.astype(f32).T.astype(bf16)
    top_ref[...] = jnp.full(top_ref.shape, masked_score, f32)
    total_ref[...] = jnp.zeros(total_ref.shape, f32)
    att_ref[...] = jnp.zeros(att_ref.shape, f32)


def dense_piece(k, kv_ref, qi_ref, ki_ref, groups, ratio, qt_ref, top_ref, total_ref, att_ref):
    width = groups * HEAD_SIZE
    for q_tile in range(qi_ref.shape[1] // SIDE):
        for k_tile in range(q_tile, -1, -1):
            bias = tile_bias(qi_ref, ki_ref, k, q_tile, k_tile, ratio)
            rows = slice(k_tile * SIDE, (k_tile + 1) * SIDE)
            for g in range(groups):
                i = q_tile * groups + g
                raw = dot(kv_ref[k, rows, head_lanes(g)], qt_ref[i], NN) * SCALE2 + bias
                top = top_ref[i]
                new_top = jnp.maximum(top, jnp.max(raw, axis=0, keepdims=True))
                weights = jnp.exp2(raw - new_top)
                back = jnp.exp2(top - new_top)
                top_ref[i] = new_top
                total_ref[i] = total_ref[i] * back + jnp.sum(weights, axis=0, keepdims=True)
                att_ref[i] = att_ref[i] * back + dot(
                    kv_ref[k, rows, head_lanes(g, width)], weights.astype(bf16), TN
                )


def dense_end(groups, ratio, top_ref, total_ref, att_ref, sum_ref, low_ref):
    for i in range(att_ref.shape[0]):
        q_tile, g = divmod(i, groups)
        out = att_ref[i] * (1.0 / total_ref[i])
        att_ref[i] = out
        sum_ref[i] = top_ref[i] + jnp.log2(total_ref[i])
        flat = out.T.astype(bf16)
        for h in range(ratio):
            low_ref[q_tile * SIDE : (q_tile + 1) * SIDE, head_lanes(g * ratio + h)] = flat[
                h * SIDE : (h + 1) * SIDE
            ]


def dense_shapes(rows, groups, ratio):
    tiles = rows // SIDE * groups
    return tiles, ratio * SIDE


FEED_TILES = 12
TILES = 17
EARLY = 5
SLOTS = 6


def back_kernel(
    part_hbm, feed_hbm, cot_hbm, middle_hbm, gain_ref, act_hbm, mid_normed_hbm, x_hbm, normed_hbm,
    low_hbm, q_hbm, kv_hbm, att_hbm, sum_hbm, qi_hbm, ki_hbm, cos_hbm, sin_hbm, weight_hbm,
    feed_other, back_middle, part2_other, result_ref, token_ref, grads_ref, held_hbm, far_hbm,
    low_ref, q_ref, kv_ref, att_ref, sum_ref, qi_ref, ki_ref, cos_ref, sin_ref,
    lhs, mid, part, part_other, w_out, w_in, rhs, q2, q2t, d2, d2t, delta, bias_ref, dq_ref,
    kv_sent, kv_got, cot, gain_rows, gain_other, gain_columns,
    p_send, p_keep, c_got, s_one, own, y_got, z_got,
    load_sem, act_sem, x_send, x_recv, c_send, c_recv, c_free, held_sem, y_send, y_recv, own_sem,
    z_send, z_recv, k_send, k_recv,
):
    ctxs = lax.axis_size("ctx")
    dp, ctx, tp = lax.axis_index("dp"), lax.axis_index("ctx"), lax.axis_index("tp")
    pair_at, core_at = dp // 2, lax.rem(dp, 2)
    far, core = (lax.rem(dp + 2, 4), ctx, tp), (dp + 1 - 2 * core_at, ctx, tp)
    after, before = (dp, lax.rem(ctx + 1, ctxs), tp), (dp, lax.rem(ctx + ctxs - 1, ctxs), tp)
    beside, opposite = (dp, ctx + 1 - 2 * lax.rem(ctx, 2), tp), (dp, lax.rem(ctx + 2, 4), tp)
    across = (dp, ctx, 1 - tp)
    rows, width = mid.shape
    section = width // 4
    piece = section // ctxs
    groups = kv_ref.shape[2] // (2 * HEAD_SIZE)
    kv_width = groups * HEAD_SIZE
    ratio = q_ref.shape[1] // kv_width
    q_cols = q_ref.shape[1]

    barrier = pltpu.get_barrier_semaphore()
    for device in (after, before, opposite, far, core, across):
        pl.semaphore_signal(barrier, inc=1, device_id=device, device_id_type=MESH)
    pl.semaphore_wait(barrier, 6)

    def remote(source, target, device, sent, got):
        return pltpu.make_async_remote_copy(source, target, sent, got, device, MESH)

    def load(source, target, index):
        return pltpu.make_async_copy(source, target, load_sem.at[index])


    def product(t, lhs_of, rhs_of):
        slot = lax.rem(t, 2)

        @pl.when(t >= 2)
        def _():
            core_copy(t - 2).wait_send()

        for c, out in ((1, p_send), (0, p_keep)):
            for y in range(2):
                there = lax.rem(pair_at + y + 1, 2) * 2 + lax.rem(core_at + c, 2)
                start = pl.multiple_of(there * section, LANES)
                result = rhs_of(start, lhs_of(pl.ds(start, section)))
                for z in range(ctxs):
                    odd, half = lax.rem(z + ctx, 2), lax.rem(z // 2 + ctx // 2, 2)
                    place = 2 * (1 - odd) + odd * half + (1 - odd) * (1 - half)
                    target = pl.ds(pl.multiple_of(y * section + place * piece, piece), piece)
                    out[slot, target, :] = result[z * piece : (z + 1) * piece]

        @pl.when(t >= 4)
        def _():
            pl.semaphore_wait(c_free, 1)

        core_copy(t).start()

    def core_copy(t):
        return remote(
            p_send.at[lax.rem(t, 2)], c_got.at[lax.rem(t, 4)], core, c_send.at[t], c_recv.at[t]
        )

    def held_copy(t):
        return pltpu.make_async_copy(s_one.at[lax.rem(t, 2)], held_hbm.at[t], held_sem.at[t])

    def meet_core(t):
        core_copy(t).wait_recv()
        slot, got = lax.rem(t, 2), lax.rem(t, 4)

        def add(i, unused):
            part_rows = pl.ds(pl.multiple_of(i * piece, piece), piece)
            total = p_keep[slot, part_rows, :].astype(f32) + c_got[got, part_rows, :].astype(f32)
            s_one[slot, part_rows, :] = total.astype(bf16)
            return unused

        lax.fori_loop(0, 2 * section // piece, add, 0)

        @pl.when(t + 4 < TILES)
        def _():
            pl.semaphore_signal(c_free, inc=1, device_id=core, device_id_type=MESH)

        held_copy(t).start()

    def far_copy(t):
        return remote(
            held_hbm.at[t, pl.ds(0, section)], far_hbm.at[t], far, y_send.at[t], y_recv.at[t]
        )

    def send_far(t):
        held_copy(t).wait()
        far_copy(t).start()

    def own_copy(t):
        return pltpu.make_async_copy(
            held_hbm.at[t, pl.ds(section, section)], own.at[lax.rem(t, SLOTS)], own_sem.at[t, 0]
        )

    def got_copy(t):
        return pltpu.make_async_copy(far_hbm.at[t], y_got.at[lax.rem(t, 2)], own_sem.at[t, 1])


    def near_copy(t):
        return remote(
            own.at[lax.rem(t, SLOTS), pl.ds(0, 2 * piece)],
            z_got.at[t, pl.ds(0, 2 * piece)], beside, z_send.at[t, 0], z_recv.at[t, 0],
        )

    def last_copy(t):
        return remote(
            own.at[lax.rem(t, SLOTS), pl.ds(2 * piece, piece)],
            z_got.at[t, pl.ds(2 * piece, piece)], opposite, z_send.at[t, 1], z_recv.at[t, 1],
        )

    def meet_near(t):
        near_copy(t).wait_recv()
        near_copy(t).wait_send()
        slot = lax.rem(t, SLOTS)
        for target, came in ((2, 1), (3, 0)):
            here = pl.ds(target * piece, piece)
            total = own[slot, here, :].astype(f32) + z_got[t, came * piece : (came + 1) * piece].astype(f32)
            own[slot, here, :] = total.astype(bf16)
        last_copy(t).start()

    def meet_last(t):
        last_copy(t).wait_recv()
        last_copy(t).wait_send()
        mine = own[lax.rem(t, SLOTS), 3 * piece :, :].astype(f32)
        grads_ref[t] = mine + z_got[t, 2 * piece :].astype(f32)

    def fetch(t):
        far_copy(t).wait_recv()
        own_copy(t).start()
        got_copy(t).start()

    def meet_far(t):
        own_copy(t).wait()
        got_copy(t).wait()
        slot, got = lax.rem(t, SLOTS), lax.rem(t, 2)
        for z in range(ctxs):
            target = pl.ds(z * piece, piece)
            total = own[slot, target, :].astype(f32) + y_got[got, target, :].astype(f32)
            own[slot, target, :] = total.astype(bf16)
        near_copy(t).start()

    def when(test, step, t):
        @pl.when(test)
        def _():
            step(t)

    def tick(n):
        when((n - 1 > EARLY) & (n - 1 < TILES), meet_far, n - 1)
        when((n - 3 >= EARLY) & (n - 3 < TILES), meet_near, n - 3)
        when((n - 5 >= EARLY - 1) & (n - 5 < TILES), meet_last, n - 5)
        when(n < TILES, fetch, n)


    part_copy = remote(part_hbm, part_other, across, x_send.at[0], x_recv.at[0])
    part_copy.start()
    feed_copy = remote(feed_hbm, feed_other, across, x_send.at[1], x_recv.at[1])
    feed_copy.start()

    def act_copy(t):
        columns = pl.ds(pl.multiple_of(lax.rem(t, 4) * TILE, TILE), TILE)
        return pltpu.make_async_copy(
            act_hbm.at[t // 4, :, columns], rhs.at[lax.rem(t, 2)], act_sem.at[t]
        )

    loads = [
        load(mid_normed_hbm, lhs.at[0], 0),
        load(cot_hbm, lhs.at[1], 1),
        load(part_hbm, part, 2),
        load(middle_hbm, mid, 3),
        load(weight_hbm.at[:, pl.ds(2 * q_cols + LANES, q_cols)], w_out, 4),
        load(weight_hbm.at[:, pl.ds(0, 2 * q_cols)], w_in, 5),
    ]
    later = (
        (low_hbm, low_ref), (q_hbm, q_ref), (kv_hbm, kv_ref), (att_hbm, att_ref), (sum_hbm, sum_ref),
        (qi_hbm, qi_ref), (ki_hbm, ki_ref), (cos_hbm, cos_ref), (sin_hbm, sin_ref),
    )
    later = [load(have, into, 21 + j) for j, (have, into) in enumerate(later)]
    act_copy(0).start()
    for copy in loads + later:
        copy.start()
    loads[0].wait()
    loads[1].wait()

    def plain(t):
        def times(start, left):
            return dot(left, rhs[lax.rem(t, 2)], TN).astype(bf16)

        return times

    def feed_step(t, unused):
        act_copy(t).wait()

        @pl.when(t + 1 < FEED_TILES)
        def _():
            act_copy(t + 1).start()

        product(t, lambda lanes: lhs[t // 8, :, lanes], plain(t))

        @pl.when(t >= 1)
        def _():
            meet_core(t - 1)

        @pl.when(t >= 2)
        def _():
            send_far(t - 2)

        n, turn = (t - 4) // 3, lax.rem(t, 3)
        when((t >= 4) & (turn == 1), fetch, n)
        when((t >= 7) & (turn == 1), meet_near, n - 1)
        when((t >= 4) & (turn == 2), meet_far, n)
        when((t >= 7) & (turn == 0), meet_last, n - 1)

        return unused

    lax.fori_loop(0, FEED_TILES, feed_step, 0)
    meet_core(FEED_TILES - 1)
    send_far(FEED_TILES - 2)
    send_far(FEED_TILES - 1)
    for copy in later:
        copy.wait()

    for q_tile in range(rows // SIDE):
        for g in range(groups):
            flat = flat_heads(q_ref, q_tile, g, ratio)
            q2[q_tile * groups + g] = flat
            q2t[q_tile * groups + g] = flat.astype(f32).T.astype(bf16)
    dq_ref[...] = jnp.zeros(dq_ref.shape, f32)
    gain_rows[...] = jnp.zeros(gain_rows.shape, f32)


    loads[2].wait()
    loads[3].wait()
    t_1, t_2, t_3, t_4, t_5 = (jnp.int32(j) for j in range(1, 6))
    fetch(t_3)
    meet_last(t_1)
    meet_near(t_2)
    part_copy.wait_recv()
    few = 64

    def norm_rows(i, unused):
        here = pl.ds(pl.multiple_of(i * few, few), few)
        field = mid[here, :]
        scale = lax.rsqrt(jnp.mean(field * field, axis=1, keepdims=True) + epsilon)
        unit = field * scale
        back = part[here, :].astype(f32) + part_other[here, :].astype(f32)
        gain_rows[1:2, :] += jnp.sum(back * unit, axis=0, keepdims=True)
        inner = back * gain_ref[1:2, :]
        out = lhs[1, here, :].astype(f32) + scale * (
            inner - unit * jnp.mean(inner * unit, axis=1, keepdims=True)
        )
        mid[here, :] = out
        lhs[0, here, :] = out.astype(bf16)
        return unused

    lax.fori_loop(0, rows // few, norm_rows, 0)
    meet_far(t_3)
    meet_last(t_2)
    fetch(t_4)
    middle_copy = load(mid, back_middle, 6)
    middle_copy.start()
    normed_copy = load(normed_hbm, lhs.at[1], 7)
    normed_copy.start()
    x_copy = load(x_hbm, part, 8)
    x_copy.start()
    loads[4].wait()
    cot[:, :q_cols] = dot(lhs[0], w_out[...], NN).astype(bf16)
    meet_far(t_4)
    meet_near(t_3)
    fetch(t_5)
    for q_tile in range(rows // SIDE):
        for g in range(groups):
            i = q_tile * groups + g
            flat = flat_heads(cot, q_tile, g, ratio)
            turned_flat = flat.astype(f32).T
            d2[i] = flat
            d2t[i] = turned_flat.astype(bf16)
            delta[i] = jnp.sum(turned_flat * att_ref[i], axis=0, keepdims=True)
    meet_last(t_3)
    meet_far(t_5)
    meet_near(t_4)

    t_out = jnp.int32(FEED_TILES)
    product(
        t_out, lambda lanes: lhs[0, :, lanes], lambda start, left: dot(left, low_ref[:, :TILE], TN).astype(bf16)
    )


    def kv_copy(s):
        return remote(kv_sent.at[s], kv_got.at[s], after, k_send.at[s], k_recv.at[s])

    def back_piece(s, unused):
        k = lax.rem(s + 1, ctxs)
        pairs = [(q, kk) for kk in range(rows // SIDE) for q in range(kk, rows // SIDE)]
        for index, (q_tile, k_tile) in enumerate(pairs):
            bias_ref[index] = tile_bias(qi_ref, ki_ref, k, q_tile, k_tile, ratio)
        sums = []
        for k_tile in range(rows // SIDE):
            here = slice(k_tile * SIDE, (k_tile + 1) * SIDE)
            for g in range(groups):
                key, value = kv_ref[k, here, head_lanes(g)], kv_ref[k, here, head_lanes(g, kv_width)]
                d_key = d_value = None
                for index, (q_tile, which) in enumerate(pairs):
                    if which != k_tile:
                        continue
                    i = q_tile * groups + g
                    raw = dot(key, q2t[i], NN) * SCALE2 + bias_ref[index]
                    share = jnp.exp2(raw - sum_ref[i])
                    back_share = dot(value, d2t[i], NN)
                    back = (share * (back_share - delta[i])).astype(bf16)
                    one_value = dot(share.astype(bf16), d2[i], NN)
                    one_key = dot(back, q2[i], NN)
                    d_value = one_value if d_value is None else d_value + one_value
                    d_key = one_key if d_key is None else d_key + one_key
                    dq_ref[i] += dot(key, back, TN)
                kv_sent[s, here, head_lanes(g)] = (d_key * SCALE).astype(bf16)
                kv_sent[s, here, head_lanes(g, kv_width)] = d_value.astype(bf16)

        @pl.when(s == 0)
        def _():
            kv_copy(0).start()
            meet_core(t_out)
            send_far(t_out)

        @pl.when((s == 1) | (s == 3))
        def _():
            tick(6 + s // 2)

        return unused

    lax.fori_loop(0, ctxs, back_piece, 0)

    def kv_pass(s):
        kv_copy(s).wait_recv()

        def add(i, unused):
            here = pl.ds(pl.multiple_of(i * few, few), few)
            total = kv_sent[s + 1, here, :].astype(f32) + kv_got[s, here, :].astype(f32)
            kv_sent[s + 1, here, :] = total.astype(bf16)
            return unused

        lax.fori_loop(0, rows // few, add, 0)
        if s + 1 < ctxs - 1:
            kv_copy(s + 1).start()


    kv_pass(0)
    for i in range(dq_ref.shape[0]):
        q_tile, g = divmod(i, groups)
        here = slice(q_tile * SIDE, (q_tile + 1) * SIDE)
        flat = dq_ref[i].T * SCALE
        for h in range(ratio):
            cot[here, head_lanes(g * ratio + h)] = turned(
                flat[h * SIDE : (h + 1) * SIDE], cos_ref[here, :], sin_ref[here, :], -1
            ).astype(bf16)
    normed_copy.wait()
    tail = q_cols - TILE
    t_query, t_both, t_key, t_last = (jnp.int32(FEED_TILES + 1 + j) for j in range(4))
    product(
        t_query, lambda lanes: lhs[1, :, lanes], lambda start, left: dot(left, cot[:, :TILE], TN).astype(bf16)
    )

    def times_both(start, left):
        from_query = dot(left, cot[:, TILE:q_cols], TN)
        from_output = dot(lhs[0, :, pl.ds(start, section)], low_ref[:, TILE:], TN)
        return jnp.concatenate([from_query, from_output], axis=1).astype(bf16)

    meet_core(t_query)
    product(t_both, lambda lanes: lhs[1, :, lanes], times_both)
    send_far(t_query)
    tick(jnp.int32(8))
    meet_core(t_both)
    send_far(t_both)
    feed_copy.wait_recv()
    here_copies = [load(feed_hbm, lhs.at[0], 9), load(feed_other, part_other, 10)]
    for copy in here_copies:
        copy.start()
    loads[5].wait()
    middle_copy.wait()
    for j in range(width // TILE):
        lanes = slice(j * TILE, (j + 1) * TILE)
        mid[:, lanes] = dot(cot[:, :q_cols], w_in[lanes, :q_cols], NT)
    kv_pass(1)
    tick(jnp.int32(9))


    for copy in here_copies:
        copy.wait()
    for half in range(rows // SIDE):
        here = slice(half * SIDE, (half + 1) * SIDE)
        pieces = [
            load(
                middle_hbm.at[pl.ds(half * SIDE, SIDE), pl.ds(j * TILE, TILE)],
                bias_ref.at[j], 11 + half * (width // TILE) + j,
            )
            for j in range(width // TILE)
        ]
        for copy in pieces:
            copy.start()
        for j, copy in enumerate(pieces):
            copy.wait()
            lanes = slice(j * TILE, (j + 1) * TILE)
            total = bias_ref[j] + lhs[0, here, lanes].astype(f32)
            lhs[0, here, lanes] = (total + part_other[here, lanes].astype(f32)).astype(bf16)
    result_copy = load(lhs.at[0], result_ref, 17)
    result_copy.start()
    tick(jnp.int32(10))

    kv_pass(2)
    for g in range(groups):
        cot[:, head_lanes(g, q_cols)] = turned(
            kv_sent[ctxs - 1, :, head_lanes(g)].astype(f32), cos_ref[...], sin_ref[...], -1
        ).astype(bf16)
    cot[:, q_cols + kv_width :] = kv_sent[ctxs - 1, :, kv_width:]
    x_copy.wait()
    x_rows = part[...].astype(f32)
    scale = lax.rsqrt(jnp.mean(x_rows * x_rows, axis=1, keepdims=True) + epsilon)
    for j in range(width // TILE):
        lanes = slice(j * TILE, (j + 1) * TILE)
        back = mid[:, lanes] + dot(cot[:, q_cols:], w_in[lanes, q_cols:], NT)
        part_other[:, lanes] = back.astype(bf16)
        gain_rows[0:1, lanes] += jnp.sum(back * (part[:, lanes].astype(f32) * scale), axis=0, keepdims=True)
    gain_copy = remote(gain_rows.at[pl.ds(0, 8)], gain_other, across, x_send.at[2], x_recv.at[2])
    gain_copy.start()
    part2_copy = remote(part_other, part2_other, across, x_send.at[3], x_recv.at[3])
    part2_copy.start()
    middle_back_copy = load(back_middle, mid, 18)
    middle_back_copy.start()
    product(
        t_key, lambda lanes: lhs[1, :, lanes], lambda start, left: dot(left, cot[:, q_cols : q_cols + TILE], TN).astype(bf16)
    )
    gain_copy.wait_recv()
    gain_copy.wait_send()
    gain_rows[0:1, :] += gain_other[0:1, :]
    gain_columns[...] = gain_rows[...].T

    def times_last(start, left):
        some = dot(left, cot[:, q_cols + TILE :], TN)
        gains = gain_columns[pl.ds(start, section), :]
        spare = jnp.zeros((section, TILE - tail - LANES), f32)
        return jnp.concatenate([some, gains, spare], axis=1).astype(bf16)

    meet_core(t_key)
    product(t_last, lambda lanes: lhs[1, :, lanes], times_last)
    send_far(t_key)
    meet_core(t_last)
    send_far(t_last)

    def drain(n, unused):
        tick(n)
        return unused

    lax.fori_loop(11, TILES, drain, 0)


    result_copy.wait()
    part2_copy.wait()
    other_copy = load(part2_other, lhs.at[0], 19)
    other_copy.start()
    middle_back_copy.wait()
    other_copy.wait()

    def token_rows(i, unused):
        here = pl.ds(pl.multiple_of(i * few, few), few)
        field = part[here, :].astype(f32)
        scale = lax.rsqrt(jnp.mean(field * field, axis=1, keepdims=True) + epsilon)
        unit = field * scale
        back = part_other[here, :].astype(f32) + lhs[0, here, :].astype(f32)
        inner = back * gain_ref[0:1, :]
        out = mid[here, :] + scale * (
            inner - unit * jnp.mean(inner * unit, axis=1, keepdims=True)
        )
        part_other[here, :] = out.astype(bf16)
        return unused

    lax.fori_loop(0, rows // few, token_rows, 0)
    token_copy = load(part_other, token_ref, 20)
    token_copy.start()
    lax.fori_loop(TILES, TILES + 5, drain, 0)

    for t in (TILES - 2, TILES - 1):
        core_copy(jnp.int32(t)).wait_send()

    def far_done(t, unused):
        far_copy(t).wait_send()
        return unused

    lax.fori_loop(0, TILES, far_done, 0)
    for s in range(ctxs - 1):
        kv_copy(s).wait_send()
    part_copy.wait_send()
    feed_copy.wait_send()
    token_copy.wait()


def back_all(part, feed, cotangent, middle, gains, act, mid_normed, x, normed, low, queries, kv, att, sums, qi, ki, cosine, sine, weights, ctxs):
    rows, width = x.shape
    q_cols = queries.shape[1]
    groups = kv.shape[2] // (2 * HEAD_SIZE)
    ratio = q_cols // (groups * HEAD_SIZE)
    tiles, lanes = dense_shapes(rows, groups, ratio)
    section = width // 4
    piece = section // ctxs
    vmem, hbm = pl.BlockSpec(memory_space=pltpu.VMEM), pl.BlockSpec(memory_space=pl.ANY)
    full = jax.ShapeDtypeStruct((rows, width), bf16)
    sems = lambda *n: pltpu.SemaphoreType.DMA(n)
    space = lambda *shape: pltpu.VMEM(shape, bf16)
    wide = lambda *shape: pltpu.VMEM(shape, f32)
    pairs = (rows // SIDE) * (rows // SIDE + 1) // 2
    return pl.pallas_call(
        back_kernel,
        in_specs=[hbm] * 4 + [vmem] + [hbm] * 14,
        out_specs=[hbm] * 5 + [vmem] + [hbm] * 2,
        out_shape=[
            full,
            jax.ShapeDtypeStruct((rows, width), f32),
            full,
            full,
            full,
            jax.ShapeDtypeStruct((TILES, piece, TILE), f32),
            jax.ShapeDtypeStruct((TILES, 2 * section, TILE), bf16),
            jax.ShapeDtypeStruct((TILES, section, TILE), bf16),
        ],
        scratch_shapes=[pltpu.VMEM(part_in.shape, part_in.dtype) for part_in in (low, queries, kv, att, sums, qi, ki, cosine, sine)]
        + [
            space(2, rows, width), wide(rows, width), space(rows, width), space(rows, width),
            space(width, q_cols), space(width, 2 * q_cols), space(2, rows, TILE),
            space(tiles, lanes, HEAD_SIZE), space(tiles, HEAD_SIZE, lanes),
            space(tiles, lanes, HEAD_SIZE), space(tiles, HEAD_SIZE, lanes),
            wide(tiles, 1, lanes), wide(pairs, SIDE, lanes), wide(tiles, HEAD_SIZE, lanes),
            space(ctxs, rows, q_cols), space(ctxs - 1, rows, q_cols), space(rows, 2 * q_cols),
            wide(LANES, width), wide(8, width), wide(width, LANES),
            space(2, 2 * section, TILE), space(2, 2 * section, TILE), space(4, 2 * section, TILE),
            space(2, 2 * section, TILE), space(SLOTS, section, TILE), space(2, section, TILE),
            space(TILES, (ctxs - 1) * piece, TILE),
            sems(30), sems(FEED_TILES), sems(4), sems(4), sems(TILES), sems(TILES),
            pltpu.SemaphoreType.REGULAR, sems(TILES), sems(TILES), sems(TILES), sems(TILES, 2),
            sems(TILES, 2), sems(TILES, 2), sems(ctxs - 1), sems(ctxs - 1),
        ],
        compiler_params=pltpu.CompilerParams(
            vmem_limit_bytes=63 * MIB, collective_id=1, has_side_effects=True
        ),
        cost_estimate=cost(4e10, 1e8),
        name="back_all",
    )(part, feed, cotangent, middle, gains, act, mid_normed, x, normed, low, queries, kv, att, sums, qi, ki, cosine, sine, weights)


def output_kernel(a_ref, w_ref, o_ref):
    o_ref[...] = dot(a_ref[...], w_ref[...], NT).astype(bf16)


def output_product(attended, weights, column, features):
    rows, inner = attended.shape
    return pl.pallas_call(
        output_kernel,
        grid=(2,),
        in_specs=[
            whole(attended.shape),
            pl.BlockSpec((features // 2, inner), lambda j: (j, column)),
        ],
        out_specs=pl.BlockSpec((rows, features // 2), lambda j: (0, j)),
        out_shape=jax.ShapeDtypeStruct((rows, features), bf16),
        compiler_params=params(40),
        cost_estimate=cost(2 * rows * inner * features, 2 * inner * features),
        name="output_product",
    )(attended, weights)


def feed_kernel(
    normed_ref, cot_ref, gate_ref, up_ref, down_ref,
    act_ref, back_ref, feed_ref, total_ref, feed_total,
):
    step = pl.program_id(0)
    gate = dot(normed_ref[...], gate_ref[...], NN)
    upward = dot(normed_ref[...], up_ref[...], NN)
    back_mixed = dot(cot_ref[...], down_ref[...], NN)
    sigmoid = 1.0 / (1.0 + jnp.exp(-gate))
    activated = gate * sigmoid
    mixed = (activated * upward).astype(bf16)
    back_gate = (back_mixed * upward * sigmoid * (1.0 + gate * (1.0 - sigmoid))).astype(bf16)
    back_up = (back_mixed * activated).astype(bf16)
    act_ref[0] = back_gate
    act_ref[1] = back_up
    act_ref[2] = mixed
    part = dot(back_gate, gate_ref[...], NT) + dot(back_up, up_ref[...], NT)
    feed = dot(mixed, down_ref[...], NT)

    @pl.when(step == 0)
    def _():
        total_ref[...] = part
        feed_total[...] = feed

    @pl.when(step > 0)
    def _():
        total_ref[...] += part
        feed_total[...] += feed

    @pl.when(step == pl.num_programs(0) - 1)
    def _():
        back_ref[...] = total_ref[...].astype(bf16)
        feed_ref[...] = feed_total[...].astype(bf16)


def feed_forward(normed, cotangent, gate, up, down):
    rows, width = normed.shape
    hidden = gate.shape[1]
    steps = hidden // FEED_TILE
    tile_of = pl.BlockSpec((width, FEED_TILE), lambda j: (0, j))
    acts_of = pl.BlockSpec((3, rows, FEED_TILE), lambda j: (0, 0, j))
    full = whole((rows, width))
    return pl.pallas_call(
        feed_kernel,
        grid=(steps,),
        in_specs=[full, full] + [tile_of] * 3,
        out_specs=[acts_of, full, full],
        out_shape=[
            jax.ShapeDtypeStruct((3, rows, hidden), bf16),
            jax.ShapeDtypeStruct((rows, width), bf16),
            jax.ShapeDtypeStruct((rows, width), bf16),
        ],
        scratch_shapes=[pltpu.VMEM((rows, width), f32)] * 2,
        compiler_params=params(56),
        cost_estimate=cost(12 * rows * width * hidden, 6 * width * hidden),
        name="feed_forward",
    )(normed, cotangent, gate, up, down)


def middle_kernel(cot_ref, mine_ref, other_ref, middle_ref, gain_ref, w_ref, bm_ref, bb_ref, ba_ref, grad_ref):
    middle = middle_ref[...]
    scale = lax.rsqrt(jnp.mean(middle * middle, axis=1, keepdims=True) + epsilon)
    unit = middle * scale
    back = mine_ref[...].astype(f32) + other_ref[...].astype(f32)
    grad_ref[...] = jnp.sum(back * unit, axis=0, keepdims=True)
    inner = back * gain_ref[1:2, :]
    out = cot_ref[...].astype(f32) + scale * (
        inner - unit * jnp.mean(inner * unit, axis=1, keepdims=True)
    )
    bm_ref[...] = out
    low = out.astype(bf16)
    bb_ref[...] = low
    ba_ref[...] = dot(low, w_ref[...], NN).astype(bf16)


def middle_back(cotangent, mine, other, middle, gains, weights, column, inner):
    rows, width = middle.shape
    full = whole((rows, width))
    return pl.pallas_call(
        middle_kernel,
        grid=(1,),
        in_specs=[full, full, full, full, whole(gains.shape)]
        + [pl.BlockSpec((width, inner), lambda j: (0, column))],
        out_specs=[full, full, whole((rows, inner)), whole((1, width))],
        out_shape=[
            jax.ShapeDtypeStruct((rows, width), f32),
            jax.ShapeDtypeStruct((rows, width), bf16),
            jax.ShapeDtypeStruct((rows, inner), bf16),
            jax.ShapeDtypeStruct((1, width), f32),
        ],
        compiler_params=params(56),
        cost_estimate=cost(2 * rows * width * inner, 1.5e7),
        name="middle_back",
    )(cotangent, mine, other, middle, gains, weights)


def inputs_kernel(count, x_ref, qc_ref, cos_ref, sin_ref, w_ref, *refs):
    parts = refs[:count]
    cot_ref, back_ref, grad_ref = refs[count:]
    half = qc_ref.shape[1] // 2
    cot_ref[:, : 2 * half] = qc_ref[...]
    total = parts[0][...].astype(f32)
    for part in parts[1:]:
        total += part[...].astype(f32)
    for h in range(half // HEAD_SIZE):
        lanes = slice(h * HEAD_SIZE, (h + 1) * HEAD_SIZE)
        there = slice(2 * half + h * HEAD_SIZE, 2 * half + (h + 1) * HEAD_SIZE)
        cot_ref[:, there] = turned(total[:, lanes], cos_ref[...], sin_ref[...], -1).astype(bf16)
    cot_ref[:, 3 * half :] = total[:, half:].astype(bf16)
    back = dot(cot_ref[...], w_ref[...], NT)
    back_ref[...] = back.astype(bf16)
    x = x_ref[...].astype(f32)
    unit = x * lax.rsqrt(jnp.mean(x * x, axis=1, keepdims=True) + epsilon)
    grad_ref[...] = jnp.sum(back * unit, axis=0, keepdims=True)


def inputs_back(x, qc, cosine, sine, weights, parts):
    rows, width = x.shape
    inner = 2 * qc.shape[1]
    full = whole((rows, width))
    return pl.pallas_call(
        functools.partial(inputs_kernel, len(parts)),
        grid=(1,),
        in_specs=[full, whole(qc.shape), whole(cosine.shape), whole(sine.shape)]
        + [pl.BlockSpec((width, inner), lambda j: (0, 0))]
        + [whole(parts[0].shape)] * len(parts),
        out_specs=[whole((rows, inner)), full, whole((1, width))],
        out_shape=[
            jax.ShapeDtypeStruct((rows, inner), bf16),
            jax.ShapeDtypeStruct((rows, width), bf16),
            jax.ShapeDtypeStruct((1, width), f32),
        ],
        compiler_params=params(56),
        cost_estimate=cost(2 * rows * width * inner, 1.5e7),
        name="inputs_back",
    )(x, qc, cosine, sine, weights, *parts)


def final_kernel(bm_ref, mine_ref, other_ref, x_ref, gain_ref, o_ref):
    x = x_ref[...].astype(f32)
    scale = lax.rsqrt(jnp.mean(x * x, axis=1, keepdims=True) + epsilon)
    unit = x * scale
    inner = (mine_ref[...].astype(f32) + other_ref[...].astype(f32)) * gain_ref[0:1, :]
    out = bm_ref[...] + scale * (inner - unit * jnp.mean(inner * unit, axis=1, keepdims=True))
    o_ref[...] = out.astype(bf16)


def final_back(back_middle, mine, other, x, gains):
    rows, width = x.shape
    block = pl.BlockSpec((rows // 4, width), lambda j: (j, 0))
    return pl.pallas_call(
        final_kernel,
        grid=(4,),
        in_specs=[block] * 4 + [whole(gains.shape)],
        out_specs=block,
        out_shape=jax.ShapeDtypeStruct((rows, width), bf16),
        compiler_params=params(40),
        cost_estimate=cost(1e6, 1e7),
        name="final_back",
    )(back_middle, mine, other, x, gains)


def relative(field, pairs, ctxs):
    dp, ctx = lax.axis_index("dp"), lax.axis_index("ctx")
    shaped = field.reshape((pairs, 2, ctxs, -1) + field.shape[1:])
    for axis, shift in ((0, dp // 2 + 1), (1, dp % 2 + 1), (2, ctx + 1)):
        shaped = jnp.roll(shaped, -shift, axis)
    return shaped.swapaxes(0, 1).reshape(field.shape)


def gradient_kernel(pairs, ctxs, place, a_ref, b_ref, send_ref, keep_ref):
    width = a_ref.shape[1]
    section = width // (2 * pairs)
    piece = section // ctxs
    for c, out in ((1, send_ref), (0, keep_ref)):
        for y in range(pairs):
            pair = lax.rem(place[0] + y + 1, pairs)
            core = lax.rem(place[1] + c, 2)
            lanes = pl.ds(pl.multiple_of((pair * 2 + core) * section, LANES), section)
            result = dot(a_ref[:, lanes], b_ref[...], TN).astype(bf16)
            for z in range(ctxs):
                far = lax.rem(z + ctxs - place[2] - 1 + ctxs, ctxs)
                rows = pl.ds(pl.multiple_of(y * section + far * piece, piece), piece)
                out[rows, :] = result[z * piece : (z + 1) * piece]


def gradient(a, b, pairs, ctxs):
    rows, width = a.shape
    columns = b.shape[1]
    section = width // (2 * pairs)
    if section % LANES or (section // ctxs) % 32:
        ordered = relative(dot(a, b, TN).astype(bf16), pairs, ctxs)
        return ordered[: width // 2], ordered[width // 2 :]
    dp, ctx = lax.axis_index("dp"), lax.axis_index("ctx")
    place = jnp.stack([dp // 2, dp % 2, ctx]).astype(jnp.int32)
    tile = TILE if columns % TILE == 0 else columns // 2
    block = pl.BlockSpec((width // 2, tile), lambda j: (0, j))
    return pl.pallas_call(
        functools.partial(gradient_kernel, pairs, ctxs),
        grid=(columns // tile,),
        in_specs=[SCALARS, whole(a.shape), pl.BlockSpec((rows, tile), lambda j: (0, j))],
        out_specs=[block, block],
        out_shape=[jax.ShapeDtypeStruct((width // 2, columns), bf16)] * 2,
        compiler_params=params(40),
        cost_estimate=cost(2 * rows * width * columns, 2 * width * columns),
        name="gradient",
    )(place, a, b)


def shifted(field, axis, steps, stride=1):
    count = lax.axis_size(axis)
    return lax.ppermute(
        field, axis, [(i, (i + steps * stride) % count) for i in range(count)]
    )


def other_core(field):
    return lax.ppermute(field, "dp", [(i, i ^ 1) for i in range(lax.axis_size("dp"))])


def sum_to_owner(send, keep, pairs, ctxs):
    columns = send.shape[1]
    got = other_core(send).reshape(pairs, -1, columns)
    keep = keep.reshape(pairs, -1, columns)
    total = got[-1].astype(f32) + keep[-1].astype(f32)
    for y in range(1, pairs):
        part = (got[y - 1].astype(f32) + keep[y - 1].astype(f32)).astype(bf16)
        total = total + shifted(part, "dp", y, 2).astype(f32)
    total = total.reshape(ctxs, -1, columns)
    result = total[-1]
    for z in range(1, ctxs):
        result = result + shifted(total[z - 1].astype(bf16), "ctx", z).astype(f32)
    return result


def swapped(field):
    count = lax.axis_size("tp")
    return lax.ppermute(field, "tp", [(i, count - 1 - i) for i in range(count)])


def body(
    tokens,
    cotangent,
    lengths,
    block_order,
    pre_gain,
    query_weight,
    key_weight,
    value_weight,
    output_weight,
    mid_gain,
    gate_weight,
    up_weight,
    down_weight,
):
    ctxs = lax.axis_size("ctx")
    pairs = lax.axis_size("dp") // 2
    ctx = lax.axis_index("ctx")
    order = block_order[0]
    ends = jnp.cumsum(lengths[0]).astype(jnp.int32)
    starts = ends - lengths[0]
    place = jnp.stack([ctx]).astype(jnp.int32)
    q_cols = query_weight.shape[1]
    features = tokens.shape[1]

    gain_columns = jnp.pad(jnp.stack([pre_gain, mid_gain], axis=1), ((0, 0), (0, LANES - 2)))
    packed = (query_weight, key_weight, value_weight, gain_columns, output_weight)
    stream = streams(order, ctx)
    lows = jnp.max(jnp.where(starts[None, :] <= stream[0][:, None], starts[None, :], 0), axis=1)
    if pairs == 2 and ctxs == 4 and query_weight.shape[0] % 32 == 0:
        own = jnp.stack([stream[0], lows])
        qi = jnp.concatenate([own, stream, jnp.zeros_like(own)], axis=0)
        (
            first, gate_full, up_full, down_full, queries, kv, normed, gains,
            attended_low, att, sums, middle, mid_normed, cosine, sine, ki,
        ) = forward_all(
            packed, gate_weight, up_weight, down_weight, tokens, frequencies(), qi, q_cols, ctxs
        )
        act, back_part, feed = feed_forward(mid_normed, cotangent, gate_full, up_full, down_full)
        _, _, _, result, token_gradient, grads, _, _ = back_all(
            back_part, feed, cotangent, middle, gains, act, mid_normed, tokens, normed,
            attended_low, queries, kv, att, sums, qi, ki, cosine, sine, first, ctxs,
        )
        wide = lambda *tiles: jnp.concatenate([grads[t] for t in tiles], axis=1)
        tail = q_cols - TILE
        qkv_gradient = jnp.concatenate(
            [grads[13], grads[14][:, :tail], grads[15], grads[16][:, :tail]], axis=1
        )
        output_gradient = jnp.concatenate([grads[12], grads[14][:, tail:]], axis=1)
        gain_sums = grads[16][:, tail : tail + LANES]
        gate_gradient, up_gradient = wide(0, 1, 2, 3), wide(4, 5, 6, 7)
        down_gradient = wide(8, 9, 10, 11)
    else:
        first, gate_full, up_full, down_full = (
            lax.all_gather(field, ROWS, axis=0, tiled=True)
            for field in (jnp.concatenate(packed, axis=1), gate_weight, up_weight, down_weight)
        )
        cosine, sine = angles(stream[0] - lows)
        gains = first[:, 2 * q_cols : 2 * q_cols + 8].T.astype(f32)
        queries, kv, normed = project(tokens, gains, cosine, sine, first, q_cols)
        pieces = [kv] + [shifted(kv, "ctx", k) for k in range(1, ctxs)]
        output_weights = first[:, 2 * q_cols + LANES :]
        attended_low, att, sums = attend(order, starts, place, queries, pieces)
        branch = output_product(attended_low, output_weights, 0, features)
        middle = tokens.astype(f32) + (branch.astype(f32) + swapped(branch).astype(f32))
        mid_scale = lax.rsqrt(jnp.mean(middle * middle, axis=1, keepdims=True) + epsilon)
        mid_normed = (middle * mid_scale * gains[1:2]).astype(bf16)
        act, back_part, feed = feed_forward(mid_normed, cotangent, gate_full, up_full, down_full)
        back_other = swapped(back_part)
        gate_parts = gradient(mid_normed, act[0], pairs, ctxs)
        up_parts = gradient(mid_normed, act[1], pairs, ctxs)
        down_parts = gradient(cotangent, act[2], pairs, ctxs)
        result = (middle + feed.astype(f32) + swapped(feed).astype(f32)).astype(bf16)

        back_middle, back_branch, back_attended, mid_grad = middle_back(
            cotangent, back_part, back_other, middle, gains, output_weights, 0, q_cols
        )
        output_parts = gradient(back_branch, attended_low, pairs, ctxs)
        back = attend_back(
            order, starts, place, queries, back_attended, att, sums, cosine, sine, pieces
        )
        own_parts = [back[1]] + [shifted(back[1 + k], "ctx", -k) for k in range(1, ctxs)]
        cot, normed_part, pre_grad = inputs_back(
            tokens, back[0], cosine, sine, first, own_parts
        )
        normed_other = swapped(normed_part)
        qkv_parts = gradient(normed, cot, pairs, ctxs)
        token_gradient = final_back(back_middle, normed_part, normed_other, tokens, gains)

        mid_once = jnp.where(lax.axis_index("tp") == 0, mid_grad, 0.0)
        pair = jnp.concatenate([pre_grad, mid_once], axis=0).astype(bf16)
        pair = jnp.pad(pair, ((0, 6), (0, 0))).T
        ordered = relative(pair, pairs, ctxs)
        gain_sums = sum_to_owner(
            ordered[: features // 2], ordered[features // 2 :], pairs, ctxs
        )
        gain_sums = gain_sums + swapped(gain_sums)
        gate_gradient = sum_to_owner(*gate_parts, pairs, ctxs)
        up_gradient = sum_to_owner(*up_parts, pairs, ctxs)
        down_gradient = sum_to_owner(*down_parts, pairs, ctxs)
        output_gradient = sum_to_owner(*output_parts, pairs, ctxs)
        qkv_gradient = sum_to_owner(*qkv_parts, pairs, ctxs)
    return (
        result,
        token_gradient,
        gain_sums[:, 0],
        qkv_gradient[:, :q_cols],
        qkv_gradient[:, q_cols : q_cols + q_cols // 2],
        qkv_gradient[:, q_cols + q_cols // 2 :],
        output_gradient,
        gain_sums[:, 1],
        gate_gradient,
        up_gradient,
        down_gradient,
    )


def solution(mesh):
    rows, split = P(ROWS, None), P(ROWS, "tp")
    return jax.shard_map(
        body,
        mesh=mesh,
        in_specs=(rows, rows, P("dp", None), P("dp", None, None), P(ROWS))
        + (split,) * 4
        + (P(ROWS),)
        + (split,) * 3,
        out_specs=(rows, rows, P(ROWS)) + (split,) * 4 + (P(ROWS),) + (split,) * 3,
        check_vma=False,
    )
```

```python
import functools
import math

import jax
import jax.numpy as jnp
import numpy as np
from jax import lax
from jax.experimental import pallas as pl
from jax.experimental.pallas import tpu as pltpu
from jax.sharding import PartitionSpec as P

HEAD_SIZE = 96
HALF = HEAD_SIZE // 2
BLOCK = 64
SPAN = 256
TILE = 512
FEED_TILE = 512
LANES = 128

epsilon = 1e-05
rotary_base = 100000.0
masked_score = -1e30
SCALE = HEAD_SIZE**-0.5
SCALE2 = SCALE / math.log(2.0)

f32 = jnp.float32
bf16 = jnp.bfloat16
ROWS = ("dp", "ctx")
MIB = 2**20


def dot(left, right, contract):
    return lax.dot_general(
        left, right, ((contract[:1], contract[1:]), ((), ())), preferred_element_type=f32
    )


NN, NT, TN = (1, 0), (1, 1), (0, 0)


def cost(flops, moved):
    return pl.CostEstimate(flops=int(flops), bytes_accessed=int(moved), transcendentals=0)


def params(mib):
    return pltpu.CompilerParams(vmem_limit_bytes=mib * MIB)


def whole(shape):
    return pl.BlockSpec(shape, lambda *_: (0,) * len(shape))


SCALARS = pl.BlockSpec(memory_space=pltpu.SMEM)


def frequencies():
    steps = np.arange(HALF, dtype=np.float64) * 2.0 / HEAD_SIZE
    return jnp.asarray(rotary_base ** -steps, f32)[None, :]


def angles(place):
    turn = place.astype(f32)[:, None] * frequencies()
    return (jnp.cos(turn), jnp.sin(turn))


def streams(order, ctx):
    rounds, count = order.shape
    owners = order[:, lax.rem(ctx - jnp.arange(count) + count, count)].T
    blocks = owners + (jnp.arange(rounds, dtype=jnp.int32) * count)[None, :]
    within = jnp.arange(BLOCK, dtype=jnp.int32)
    return (blocks[:, :, None] * BLOCK + within).reshape(count, rounds * BLOCK).astype(jnp.int32)


def turned(head, cosine, sine, sign):
    first, second = head[:, :HALF], head[:, HALF:]
    along = sine if sign > 0 else -sine
    return jnp.concatenate(
        [first * cosine - second * along, second * cosine + first * along], axis=1
    )


def project_kernel(x_ref, gain_ref, cos_ref, sin_ref, w_ref, q_ref, kv_ref, normed_ref):
    step = pl.program_id(0)
    tile = w_ref.shape[1]

    @pl.when(step == 0)
    def _():
        x = x_ref[...].astype(f32)
        scale = lax.rsqrt(jnp.mean(x * x, axis=1, keepdims=True) + epsilon)
        normed_ref[...] = (x * scale * gain_ref[0:1, :]).astype(bf16)

    out = dot(normed_ref[...], w_ref[...], NN)

    def rotated(ref):
        for h in range(tile // HEAD_SIZE):
            lanes = slice(h * HEAD_SIZE, (h + 1) * HEAD_SIZE)
            ref[:, lanes] = turned(out[:, lanes], cos_ref[...], sin_ref[...], 1).astype(bf16)

    @pl.when(step < 2)
    def _():
        rotated(q_ref)

    @pl.when(step == 2)
    def _():
        rotated(kv_ref)

    @pl.when(step == 3)
    def _():
        kv_ref[...] = out.astype(bf16)


def project(x, gains, cosine, sine, weights, q_cols):
    rows, width = x.shape
    tile = q_cols // 2
    return pl.pallas_call(
        project_kernel,
        grid=(4,),
        in_specs=[
            whole(x.shape),
            whole(gains.shape),
            whole(cosine.shape),
            whole(sine.shape),
            pl.BlockSpec((width, tile), lambda j: (0, j)),
        ],
        out_specs=[
            pl.BlockSpec((rows, tile), lambda j: (0, jnp.minimum(j, 1))),
            pl.BlockSpec((rows, tile), lambda j: (0, jnp.maximum(j - 2, 0))),
            whole((rows, width)),
        ],
        out_shape=[
            jax.ShapeDtypeStruct((rows, q_cols), bf16),
            jax.ShapeDtypeStruct((rows, q_cols), bf16),
            jax.ShapeDtypeStruct((rows, width), bf16),
        ],
        compiler_params=params(40),
        cost_estimate=cost(2 * rows * width * 4 * tile, 2 * width * 4 * tile),
        name="project",
    )(x, gains, cosine, sine, weights)


MESH = pl.DeviceIdType.MESH


def forward_kernel(
    query_shard, key_shard, value_shard, gain_shard, out_shard, gate_shard, up_shard, down_shard,
    x_ref, frequency_ref, qi_ref,
    full_ref, gate_ref, up_ref, down_ref, q_out, kv_out, normed_out, gain_out, low_out, att_out, sum_out,
    middle_out, mid_normed_out, cos_out, sin_out, ki_out,
    q_ref, kv_ref, normed_ref, gain_ref, low_ref, att_ref, sum_ref,
    middle_ref, mid_normed_ref, cos_ref, sin_ref, ki_ref,
    branch_ref, other_ref, w_ref, qt_ref, top_ref, total_ref,
    z_send, z_recv, y_send, y_recv, c_send, c_recv, k_send, k_recv, x_send, x_recv, local, save_sem,
):
    ctxs = lax.axis_size("ctx")
    dp, ctx, tp = lax.axis_index("dp"), lax.axis_index("ctx"), lax.axis_index("tp")
    far, core = (lax.rem(dp + 2, 4), ctx, tp), (dp + 1 - 2 * lax.rem(dp, 2), ctx, tp)
    after, before = (dp, lax.rem(ctx + 1, ctxs), tp), (dp, lax.rem(ctx + ctxs - 1, ctxs), tp)
    across = (dp, ctx, 1 - tp)
    piece = query_shard.shape[0]
    mine = pl.ds(pl.multiple_of((dp * ctxs + ctx) * piece, piece), piece)
    packs, column = [], 0
    for j, part in enumerate((query_shard, key_shard, value_shard, gain_shard, out_shard)):
        target = w_ref.at[mine, pl.ds(column, part.shape[1])]
        packs.append(pltpu.make_async_copy(part, target, local.at[5 + j]))
        packs[-1].start()
        column += part.shape[1]
    barrier = pltpu.get_barrier_semaphore()
    for device in (after, before, far, core, across):
        pl.semaphore_signal(barrier, inc=1, device_id=device, device_id_type=MESH)
    pl.semaphore_wait(barrier, 5)
    shards = (w_ref.at[mine], gate_shard, up_shard, down_shard)
    wholes = (w_ref, gate_ref, up_ref, down_ref)
    last = ctxs - 1


    def place(group, pair, steps):
        owner = pair * ctxs + lax.rem(ctx - steps + ctxs, ctxs)
        return wholes[group].at[pl.ds(pl.multiple_of(owner * piece, piece), piece)]

    def source(group, steps):
        return place(group, dp, steps) if steps else shards[group]

    def remote(source, target, device, sent, got):
        return pltpu.make_async_remote_copy(source, target, device_id=device, device_id_type=MESH, send_sem=sent, recv_sem=got)

    def ring(group, s):
        return remote(
            source(group, s), place(group, dp, s), after, z_send.at[group, s], z_recv.at[group, s]
        )

    def over(group, s):
        return remote(
            source(group, s), place(group, dp, s), far, y_send.at[group, s], y_recv.at[group, s]
        )

    def aside(group, s):
        return remote(
            source(group, s), place(group, dp, s), core, c_send.at[group, s], c_recv.at[group, s]
        )

    def aside_far(group, s):
        there = place(group, far[0], s)
        return remote(
            there, there, core, c_send.at[group, ctxs + s], c_recv.at[group, ctxs + s]
        )

    def own_copy(group):
        return pltpu.make_async_copy(shards[group], place(group, dp, 0), local.at[group])

    def begin(group):
        over(group, 0).start()
        aside(group, 0).start()
        if group:
            own_copy(group).start()

    def along(group, s):
        ring(group, s - 1).wait_recv()
        if s < last:
            ring(group, s).start()
        over(group, s).start()
        aside(group, s).start()

    def came_over(group, s):
        over(group, s).wait_recv()
        aside_far(group, s).start()

    def gathered(group):
        if group:
            own_copy(group).wait()
        for s in range(ctxs):
            aside(group, s).wait_recv()
            aside_far(group, s).wait_recv()

    saves = []

    def save(*pairs):
        for have, out in pairs:
            saves.append(pltpu.make_async_copy(have, out, save_sem.at[len(saves)]))
            saves[-1].start()

    first, gate, up, down = range(4)
    for copy in packs:
        copy.wait()
    ring(first, 0).start()
    begin(first)
    columns = qi_ref[...].astype(f32).T
    turn = (columns[:, 0:1] - columns[:, 1:2]) * frequency_ref[...]
    cos_ref[...] = jnp.cos(turn)
    sin_ref[...] = jnp.sin(turn)
    for k in range(ctxs):
        ki_ref[k] = columns[:, 2 + k : 3 + k].astype(jnp.int32)
    x = x_ref[...].astype(f32)
    unit = x * lax.rsqrt(jnp.mean(x * x, axis=1, keepdims=True) + epsilon)
    for s in range(1, ctxs):
        along(first, s)
        came_over(first, s - 1)
    ring(gate, 0).start()
    begin(gate)
    ring(up, 0).start()
    came_over(first, last)
    begin(up)
    gathered(first)
    full = pltpu.make_async_copy(w_ref, full_ref, local.at[4])
    full.start()
    along(gate, 1)

    q_cols = q_ref.shape[1]
    tile = q_cols // 2
    groups = kv_ref.shape[2] // (2 * HEAD_SIZE)
    ratio = q_cols // (groups * HEAD_SIZE)
    gains = w_ref[:, 2 * q_cols : 2 * q_cols + LANES].astype(f32).T[:8]
    gain_ref[...] = gains
    normed_ref[...] = (unit * gains[0:1]).astype(bf16)
    save((gain_ref, gain_out), (normed_ref, normed_out), (cos_ref, cos_out), (sin_ref, sin_out), (ki_ref, ki_out))

    def product(step):
        return dot(normed_ref[...], w_ref[:, step * tile : (step + 1) * tile], NN)

    def rotated(out, store):
        for h in range(tile // HEAD_SIZE):
            lanes = slice(h * HEAD_SIZE, (h + 1) * HEAD_SIZE)
            store(lanes, turned(out[:, lanes], cos_ref[...], sin_ref[...], 1).astype(bf16))

    def key_store(lanes, value):
        kv_ref[0, :, lanes] = value

    rotated(product(2), key_store)
    kv_ref[0, :, tile:] = product(3).astype(bf16)

    def kv_copy(s):
        return remote(kv_ref.at[s], kv_ref.at[s + 1], after, k_send.at[s], k_recv.at[s])

    kv_copy(0).start()
    begin(down)
    for step in range(2):

        def query_store(lanes, value):
            q_ref[:, step * tile + lanes.start : step * tile + lanes.stop] = value

        rotated(product(step), query_store)

    def attention(k):
        dense_piece(k, kv_ref, qi_ref, ki_ref, groups, ratio, qt_ref, top_ref, total_ref, att_ref)

    dense_begin(q_ref, groups, ratio, qt_ref, top_ref, total_ref, att_ref)
    along(gate, 2)
    came_over(gate, 0)
    waits = [
        [lambda: along(up, 1), lambda: along(gate, last), lambda: came_over(gate, 1), lambda: came_over(up, 0)],
        [lambda: ring(down, 0).start(), lambda: came_over(down, 0), lambda: came_over(gate, 2)],
        [lambda: along(up, 2)],
    ]

    def attention_step(k, unused):
        for s in range(1, ctxs):

            @pl.when(k == s)
            def _(s=s):
                kv_copy(s - 1).wait_recv()
                if s < last:
                    kv_copy(s).start()
                for step in waits[s - 1] if s - 1 < len(waits) else []:
                    step()

        attention(k)
        return unused

    lax.fori_loop(0, ctxs, attention_step, 0)
    save((q_ref, q_out), (kv_ref, kv_out))
    dense_end(groups, ratio, top_ref, total_ref, att_ref, sum_ref, low_ref)
    save((low_ref, low_out), (att_ref, att_out), (sum_ref, sum_out))
    branch_ref[...] = dot(low_ref[...], w_ref[:, 2 * q_cols + LANES :], NT).astype(bf16)
    exchange = remote(branch_ref, other_ref, across, x_send.at[0], x_recv.at[0])
    exchange.start()

    along(down, 1)
    came_over(gate, last)
    came_over(up, 1)
    along(up, last)
    came_over(up, 2)
    along(down, 2)
    came_over(down, 1)
    came_over(up, last)
    along(down, last)
    came_over(down, 2)
    exchange.wait_recv()
    few = 64

    def middle_rows(i, unused):
        here = pl.ds(pl.multiple_of(i * few, few), few)
        middle = x_ref[here, :].astype(f32) + (
            branch_ref[here, :].astype(f32) + other_ref[here, :].astype(f32)
        )
        middle_ref[here, :] = middle
        scale = lax.rsqrt(jnp.mean(middle * middle, axis=1, keepdims=True) + epsilon)
        mid_normed_ref[here, :] = (middle * scale * gain_ref[1:2, :]).astype(bf16)
        return unused

    lax.fori_loop(0, x_ref.shape[0] // few, middle_rows, 0)
    save((middle_ref, middle_out), (mid_normed_ref, mid_normed_out))
    came_over(down, last)
    for group in (gate, up, down):
        gathered(group)
    for group in range(4):
        for s in range(ctxs):
            if s < last:
                ring(group, s).wait_send()
            over(group, s).wait_send()
            aside(group, s).wait_send()
            aside_far(group, s).wait_send()
    for s in range(last):
        kv_copy(s).wait_send()
    exchange.wait_send()
    full.wait()
    for copy in saves:
        copy.wait()


def forward_all(packed, gate, up, down, x, frequency, qi, q_cols, ctxs):
    rows, width = x.shape
    columns, hidden = sum(part.shape[1] for part in packed), gate.shape[1]
    groups = q_cols // 2 // HEAD_SIZE
    tiles, lanes = dense_shapes(rows, groups, 2)
    vmem, hbm = pl.BlockSpec(memory_space=pltpu.VMEM), pl.BlockSpec(memory_space=pl.ANY)
    sems = lambda *n: pltpu.SemaphoreType.DMA(n)
    shape = jax.ShapeDtypeStruct
    full = shape((rows, width), bf16)
    kept = [
        shape((rows, q_cols), bf16),
        shape((ctxs, rows, q_cols), bf16),
        full,
        shape((8, width), f32),
        shape((rows, q_cols), bf16),
        shape((tiles, HEAD_SIZE, lanes), f32),
        shape((tiles, 1, lanes), f32),
        shape((rows, width), f32),
        full,
        shape((rows, HALF), f32),
        shape((rows, HALF), f32),
        shape((ctxs, rows, 1), jnp.int32),
    ]
    return pl.pallas_call(
        forward_kernel,
        in_specs=[hbm] * (len(packed) + 3) + [vmem] * 3,
        out_specs=[hbm] * 16,
        out_shape=[
            shape((width, columns), bf16),
            shape((width, hidden), bf16),
            shape((width, hidden), bf16),
            shape((width, hidden), bf16),
        ]
        + kept,
        scratch_shapes=[pltpu.VMEM(part.shape, part.dtype) for part in kept]
        + [
            pltpu.VMEM((rows, width), bf16),
            pltpu.VMEM((rows, width), bf16),
            pltpu.VMEM((width, columns), bf16),
            pltpu.VMEM((tiles, HEAD_SIZE, lanes), bf16),
            pltpu.VMEM((tiles, 1, lanes), f32),
            pltpu.VMEM((tiles, 1, lanes), f32),
        ]
        + [sems(4, ctxs - 1)] * 2
        + [sems(4, ctxs)] * 2
        + [sems(4, 2 * ctxs)] * 2
        + [sems(ctxs - 1)] * 2
        + [sems(1)] * 2
        + [sems(5 + len(packed)), sems(len(kept))],
        compiler_params=pltpu.CompilerParams(
            vmem_limit_bytes=56 * MIB, collective_id=0, has_side_effects=True
        ),
        cost_estimate=cost(1e10, 1e8),
        name="forward_all",
    )(*packed, gate, up, down, x, frequency, qi)


def gather_stream(order, ctx, pieces, k_ref, v_ref):
    count, groups = len(pieces), k_ref.shape[0]
    width = groups * HEAD_SIZE

    def fill(i, unused):
        source = pl.ds(pl.multiple_of(i * BLOCK, BLOCK), BLOCK)
        for k, piece in enumerate(pieces):
            block = i * count + order[i, lax.rem(ctx - k + count, count)]
            target = pl.ds(pl.multiple_of(block * BLOCK, BLOCK), BLOCK)
            for g in range(groups):
                lanes = slice(g * HEAD_SIZE, (g + 1) * HEAD_SIZE)
                k_ref[g, target, :] = piece[source, lanes]
                v_ref[g, target, :] = piece[
                    source, width + g * HEAD_SIZE : width + (g + 1) * HEAD_SIZE
                ]
        return unused

    lax.fori_loop(0, order.shape[0], fill, 0)


def reach(starts, first):
    low = jnp.int32(0)
    for j in range(starts.shape[0]):
        low = jnp.where(starts[j] <= first, starts[j], low)
    return low


def row_limits(starts, first, lanes):
    row = first + lax.rem(lax.broadcasted_iota(jnp.int32, (1, lanes), 1), BLOCK)
    low = jnp.zeros((1, lanes), jnp.int32)
    for j in range(starts.shape[0]):
        low = jnp.where(row >= starts[j], starts[j], low)
    return row, low


def stacked(ref, rows, group, ratio):
    return jnp.concatenate(
        [
            ref[rows, (group * ratio + h) * HEAD_SIZE : (group * ratio + h + 1) * HEAD_SIZE]
            for h in range(ratio)
        ],
        axis=0,
    )


def attend_kernel(count, order, starts, place, q_ref, *refs):
    pieces = refs[:count]
    low_ref, att_ref, sum_ref, k_ref, v_ref = refs[count:]
    groups = k_ref.shape[0]
    ratio = q_ref.shape[1] // (groups * HEAD_SIZE)
    lanes = ratio * BLOCK
    ctx = place[0]
    gather_stream(order, ctx, pieces, k_ref, v_ref)

    def one(i, unused):
        first = (i * count + order[i, ctx]) * BLOCK
        row, low = row_limits(starts, first, lanes)
        begin = reach(starts, first) // SPAN
        end = (first + BLOCK - 1) // SPAN + 1
        rows = pl.ds(pl.multiple_of(i * BLOCK, BLOCK), BLOCK)
        queries = [stacked(q_ref, rows, g, ratio) for g in range(groups)]

        def chunk(c, carry):
            keys = pl.ds(pl.multiple_of(c * SPAN, SPAN), SPAN)
            index = c * SPAN + lax.broadcasted_iota(jnp.int32, (SPAN, lanes), 0)
            allowed = (index <= row) & (index >= low)
            new = []
            for g in range(groups):
                top, total, out = carry[g]
                raw = dot(k_ref[g, keys, :], queries[g], NT) * SCALE2
                raw = jnp.where(allowed, raw, masked_score)
                new_top = jnp.maximum(top, jnp.max(raw, axis=0, keepdims=True))
                weights = jnp.where(allowed, jnp.exp2(raw - new_top), 0.0)
                back = jnp.exp2(top - new_top)
                total = total * back + jnp.sum(weights, axis=0, keepdims=True)
                out = out * back + dot(v_ref[g, keys, :], weights.astype(bf16), TN)
                new.append((new_top, total, out))
            return tuple(new)

        blank = (
            jnp.full((1, lanes), masked_score, f32),
            jnp.zeros((1, lanes), f32),
            jnp.zeros((HEAD_SIZE, lanes), f32),
        )
        result = lax.fori_loop(begin, end, chunk, (blank,) * groups)
        for g in range(groups):
            top, total, out = result[g]
            out = out / total
            att_ref[i * groups + g] = out
            sum_ref[pl.ds(i * groups + g, 1), :] = top + jnp.log2(total)
            flat = out.T.astype(bf16)
            for h in range(ratio):
                head = g * ratio + h
                low_ref[rows, head * HEAD_SIZE : (head + 1) * HEAD_SIZE] = flat[
                    h * BLOCK : (h + 1) * BLOCK
                ]
        return unused

    lax.fori_loop(0, order.shape[0], one, 0)


def attend(order, starts, place, queries, pieces):
    count, rows = len(pieces), queries.shape[0]
    groups = pieces[0].shape[1] // (2 * HEAD_SIZE)
    ratio = queries.shape[1] // (groups * HEAD_SIZE)
    rounds, lanes = order.shape[0], ratio * BLOCK
    return pl.pallas_call(
        functools.partial(attend_kernel, count),
        in_specs=[SCALARS] * 3 + [pl.BlockSpec(memory_space=pltpu.VMEM)] * (1 + count),
        out_specs=[pl.BlockSpec(memory_space=pltpu.VMEM)] * 3,
        out_shape=[
            jax.ShapeDtypeStruct(queries.shape, bf16),
            jax.ShapeDtypeStruct((rounds * groups, HEAD_SIZE, lanes), f32),
            jax.ShapeDtypeStruct((rounds * groups, lanes), f32),
        ],
        scratch_shapes=[pltpu.VMEM((groups, count * rows, HEAD_SIZE), bf16)] * 2,
        compiler_params=params(40),
        cost_estimate=cost(8e9, 1e7),
        name="attend",
    )(order, starts, place, queries, *pieces)


def attend_back_kernel(count, order, starts, place, q_ref, d_ref, att_ref, sum_ref, cos_ref, sin_ref, *refs):
    pieces = refs[:count]
    qc_ref = refs[count]
    outs = refs[count + 1 : 2 * count + 1]
    k_ref, v_ref, dk_ref, dv_ref = refs[2 * count + 1 :]
    groups = k_ref.shape[0]
    ratio = q_ref.shape[1] // (groups * HEAD_SIZE)
    lanes = ratio * BLOCK
    width = groups * HEAD_SIZE
    ctx = place[0]
    gather_stream(order, ctx, pieces, k_ref, v_ref)
    dk_ref[...] = jnp.zeros_like(dk_ref)
    dv_ref[...] = jnp.zeros_like(dv_ref)

    def one(i, unused):
        first = (i * count + order[i, ctx]) * BLOCK
        row, low = row_limits(starts, first, lanes)
        begin = reach(starts, first) // SPAN
        end = (first + BLOCK - 1) // SPAN + 1
        rows = pl.ds(pl.multiple_of(i * BLOCK, BLOCK), BLOCK)
        queries = [stacked(q_ref, rows, g, ratio) for g in range(groups)]
        slopes = [stacked(d_ref, rows, g, ratio) for g in range(groups)]
        sums, deltas = [], []
        for g in range(groups):
            sums.append(sum_ref[pl.ds(i * groups + g, 1), :])
            across = slopes[g].astype(f32).T
            deltas.append(jnp.sum(across * att_ref[i * groups + g], axis=0, keepdims=True))

        def chunk(c, carry):
            keys = pl.ds(pl.multiple_of(c * SPAN, SPAN), SPAN)
            index = c * SPAN + lax.broadcasted_iota(jnp.int32, (SPAN, lanes), 0)
            allowed = (index <= row) & (index >= low)
            new = []
            for g in range(groups):
                key, value = k_ref[g, keys, :], v_ref[g, keys, :]
                raw = dot(key, queries[g], NT) * SCALE2
                share = jnp.where(allowed, jnp.exp2(jnp.minimum(raw - sums[g], 0.0)), 0.0)
                back_share = dot(value, slopes[g], NT)
                back = (share * (back_share - deltas[g])).astype(bf16)
                dv_ref[g, keys, :] += dot(share.astype(bf16), slopes[g], NN)
                dk_ref[g, keys, :] += dot(back, queries[g], NN)
                new.append(carry[g] + dot(key, back, TN))
            return tuple(new)

        blank = jnp.zeros((HEAD_SIZE, lanes), f32)
        result = lax.fori_loop(begin, end, chunk, (blank,) * groups)
        cosine, sine = cos_ref[rows, :], sin_ref[rows, :]
        for g in range(groups):
            flat = result[g].T * SCALE
            for h in range(ratio):
                head = g * ratio + h
                qc_ref[rows, head * HEAD_SIZE : (head + 1) * HEAD_SIZE] = turned(
                    flat[h * BLOCK : (h + 1) * BLOCK], cosine, sine, -1
                ).astype(bf16)
        return unused

    lax.fori_loop(0, order.shape[0], one, 0)

    def spread(i, unused):
        target = pl.ds(pl.multiple_of(i * BLOCK, BLOCK), BLOCK)
        for k, out in enumerate(outs):
            block = i * count + order[i, lax.rem(ctx - k + count, count)]
            source = pl.ds(pl.multiple_of(block * BLOCK, BLOCK), BLOCK)
            for g in range(groups):
                out[target, g * HEAD_SIZE : (g + 1) * HEAD_SIZE] = (
                    dk_ref[g, source, :] * SCALE
                ).astype(bf16)
                out[target, width + g * HEAD_SIZE : width + (g + 1) * HEAD_SIZE] = dv_ref[
                    g, source, :
                ].astype(bf16)
        return unused

    lax.fori_loop(0, order.shape[0], spread, 0)


def attend_back(order, starts, place, queries, slopes, att, sums, cosine, sine, pieces):
    count, rows = len(pieces), queries.shape[0]
    groups = pieces[0].shape[1] // (2 * HEAD_SIZE)
    keys = (groups, count * rows, HEAD_SIZE)
    return pl.pallas_call(
        functools.partial(attend_back_kernel, count),
        in_specs=[SCALARS] * 3 + [pl.BlockSpec(memory_space=pltpu.VMEM)] * (6 + count),
        out_specs=[pl.BlockSpec(memory_space=pltpu.VMEM)] * (1 + count),
        out_shape=[jax.ShapeDtypeStruct(queries.shape, bf16)]
        + [jax.ShapeDtypeStruct(pieces[0].shape, bf16)] * count,
        scratch_shapes=[pltpu.VMEM(keys, bf16)] * 2 + [pltpu.VMEM(keys, f32)] * 2,
        compiler_params=params(56),
        cost_estimate=cost(16e9, 2e7),
        name="attend_back",
    )(order, starts, place, queries, slopes, att, sums, cosine, sine, *pieces)


SIDE = 256


def tile_bias(qi_ref, ki_ref, k, q_tile, k_tile, ratio):
    rows = slice(q_tile * SIDE, (q_tile + 1) * SIDE)
    keys = ki_ref[k, k_tile * SIDE : (k_tile + 1) * SIDE, :]
    allowed = (keys <= qi_ref[0:1, rows]) & (keys >= qi_ref[1:2, rows])
    bias = jnp.where(allowed, 0.0, masked_score)
    return jnp.concatenate([bias] * ratio, axis=1)


def flat_heads(ref, q_tile, group, ratio):
    return jnp.concatenate(
        [
            ref[
                q_tile * SIDE : (q_tile + 1) * SIDE,
                (group * ratio + h) * HEAD_SIZE : (group * ratio + h + 1) * HEAD_SIZE,
            ]
            for h in range(ratio)
        ],
        axis=0,
    )


def head_lanes(g, offset=0):
    return slice(offset + g * HEAD_SIZE, offset + (g + 1) * HEAD_SIZE)


def dense_begin(q_ref, groups, ratio, qt_ref, top_ref, total_ref, att_ref):
    for q_tile in range(q_ref.shape[0] // SIDE):
        for g in range(groups):
            flat = flat_heads(q_ref, q_tile, g, ratio)
            qt_ref[q_tile * groups + g] = flat.astype(f32).T.astype(bf16)
    top_ref[...] = jnp.full(top_ref.shape, masked_score, f32)
    total_ref[...] = jnp.zeros(total_ref.shape, f32)
    att_ref[...] = jnp.zeros(att_ref.shape, f32)


def dense_piece(k, kv_ref, qi_ref, ki_ref, groups, ratio, qt_ref, top_ref, total_ref, att_ref):
    width = groups * HEAD_SIZE
    for q_tile in range(qi_ref.shape[1] // SIDE):
        for k_tile in range(q_tile, -1, -1):
            bias = tile_bias(qi_ref, ki_ref, k, q_tile, k_tile, ratio)
            rows = slice(k_tile * SIDE, (k_tile + 1) * SIDE)
            for g in range(groups):
                i = q_tile * groups + g
                raw = dot(kv_ref[k, rows, head_lanes(g)], qt_ref[i], NN) * SCALE2 + bias
                top = top_ref[i]
                new_top = jnp.maximum(top, jnp.max(raw, axis=0, keepdims=True))
                weights = jnp.exp2(raw - new_top)
                back = jnp.exp2(top - new_top)
                top_ref[i] = new_top
                total_ref[i] = total_ref[i] * back + jnp.sum(weights, axis=0, keepdims=True)
                att_ref[i] = att_ref[i] * back + dot(
                    kv_ref[k, rows, head_lanes(g, width)], weights.astype(bf16), TN
                )


def dense_end(groups, ratio, top_ref, total_ref, att_ref, sum_ref, low_ref):
    for i in range(att_ref.shape[0]):
        q_tile, g = divmod(i, groups)
        out = att_ref[i] * (1.0 / total_ref[i])
        att_ref[i] = out
        sum_ref[i] = top_ref[i] + jnp.log2(total_ref[i])
        flat = out.T.astype(bf16)
        for h in range(ratio):
            low_ref[q_tile * SIDE : (q_tile + 1) * SIDE, head_lanes(g * ratio + h)] = flat[
                h * SIDE : (h + 1) * SIDE
            ]


def dense_shapes(rows, groups, ratio):
    tiles = rows // SIDE * groups
    return tiles, ratio * SIDE


FEED_TILES = 12
TILES = 17
EARLY = 4
SLOTS = 6


def back_kernel(
    part_hbm, feed_hbm, cot_hbm, middle_hbm, gain_ref, act_hbm, mid_normed_hbm, x_hbm, normed_hbm,
    low_hbm, q_hbm, kv_hbm, att_hbm, sum_hbm, qi_hbm, ki_hbm, cos_hbm, sin_hbm, weight_hbm,
    feed_other, back_middle, part2_other, result_ref, token_ref, grads_ref, held_hbm, far_hbm,
    low_ref, q_ref, kv_ref, att_ref, sum_ref, qi_ref, ki_ref, cos_ref, sin_ref,
    lhs, mid, part, part_other, w_out, w_in, rhs, q2, q2t, d2, d2t, delta, bias_ref, dq_ref,
    kv_sent, kv_got, cot, gain_rows, gain_other, gain_columns,
    p_send, p_keep, c_got, s_one, own, y_got, z_got,
    load_sem, act_sem, x_send, x_recv, c_send, c_recv, c_free, held_sem, y_send, y_recv, own_sem,
    z_send, z_recv, k_send, k_recv,
):
    ctxs = lax.axis_size("ctx")
    dp, ctx, tp = lax.axis_index("dp"), lax.axis_index("ctx"), lax.axis_index("tp")
    pair_at, core_at = dp // 2, lax.rem(dp, 2)
    far, core = (lax.rem(dp + 2, 4), ctx, tp), (dp + 1 - 2 * core_at, ctx, tp)
    after, before = (dp, lax.rem(ctx + 1, ctxs), tp), (dp, lax.rem(ctx + ctxs - 1, ctxs), tp)
    beside, opposite = (dp, ctx + 1 - 2 * lax.rem(ctx, 2), tp), (dp, lax.rem(ctx + 2, 4), tp)
    across = (dp, ctx, 1 - tp)
    rows, width = mid.shape
    section = width // 4
    piece = section // ctxs
    groups = kv_ref.shape[2] // (2 * HEAD_SIZE)
    kv_width = groups * HEAD_SIZE
    ratio = q_ref.shape[1] // kv_width
    q_cols = q_ref.shape[1]

    barrier = pltpu.get_barrier_semaphore()
    for device in (after, before, opposite, far, core, across):
        pl.semaphore_signal(barrier, inc=1, device_id=device, device_id_type=MESH)
    pl.semaphore_wait(barrier, 6)

    def remote(source, target, device, sent, got):
        return pltpu.make_async_remote_copy(source, target, sent, got, device, MESH)

    def load(source, target, index):
        return pltpu.make_async_copy(source, target, load_sem.at[index])


    def product(t, lhs_of, rhs_of):
        slot = lax.rem(t, 2)

        @pl.when(t >= 2)
        def _():
            core_copy(t - 2).wait_send()

        for c, out in ((1, p_send), (0, p_keep)):
            for y in range(2):
                there = lax.rem(pair_at + y + 1, 2) * 2 + lax.rem(core_at + c, 2)
                start = pl.multiple_of(there * section, LANES)
                result = rhs_of(start, lhs_of(pl.ds(start, section)))
                for z in range(ctxs):
                    odd, half = lax.rem(z + ctx, 2), lax.rem(z // 2 + ctx // 2, 2)
                    place = 2 * (1 - odd) + odd * half + (1 - odd) * (1 - half)
                    target = pl.ds(pl.multiple_of(y * section + place * piece, piece), piece)
                    out[slot, target, :] = result[z * piece : (z + 1) * piece]

        @pl.when(t >= 4)
        def _():
            pl.semaphore_wait(c_free, 1)

        core_copy(t).start()

    def core_copy(t):
        return remote(
            p_send.at[lax.rem(t, 2)], c_got.at[lax.rem(t, 4)], core, c_send.at[t], c_recv.at[t]
        )

    def held_copy(t):
        return pltpu.make_async_copy(s_one.at[lax.rem(t, 2)], held_hbm.at[t], held_sem.at[t])

    def meet_core(t):
        core_copy(t).wait_recv()
        slot, got = lax.rem(t, 2), lax.rem(t, 4)

        def add(i, unused):
            part_rows = pl.ds(pl.multiple_of(i * piece, piece), piece)
            total = p_keep[slot, part_rows, :].astype(f32) + c_got[got, part_rows, :].astype(f32)
            s_one[slot, part_rows, :] = total.astype(bf16)
            return unused

        lax.fori_loop(0, 2 * section // piece, add, 0)

        @pl.when(t + 4 < TILES)
        def _():
            pl.semaphore_signal(c_free, inc=1, device_id=core, device_id_type=MESH)

        held_copy(t).start()

    def far_copy(t):
        return remote(
            held_hbm.at[t, pl.ds(0, section)], far_hbm.at[t], far, y_send.at[t], y_recv.at[t]
        )

    def send_far(t):
        held_copy(t).wait()
        far_copy(t).start()

    def own_copy(t):
        return pltpu.make_async_copy(
            held_hbm.at[t, pl.ds(section, section)], own.at[lax.rem(t, SLOTS)], own_sem.at[t, 0]
        )

    def got_copy(t):
        return pltpu.make_async_copy(far_hbm.at[t], y_got.at[lax.rem(t, 2)], own_sem.at[t, 1])


    def near_copy(t):
        return remote(
            own.at[lax.rem(t, SLOTS), pl.ds(0, 2 * piece)],
            z_got.at[t, pl.ds(0, 2 * piece)], beside, z_send.at[t, 0], z_recv.at[t, 0],
        )

    def last_copy(t):
        return remote(
            own.at[lax.rem(t, SLOTS), pl.ds(2 * piece, piece)],
            z_got.at[t, pl.ds(2 * piece, piece)], opposite, z_send.at[t, 1], z_recv.at[t, 1],
        )

    def meet_near(t):
        near_copy(t).wait_recv()
        near_copy(t).wait_send()
        slot = lax.rem(t, SLOTS)
        for target, came in ((2, 1), (3, 0)):
            here = pl.ds(target * piece, piece)
            total = own[slot, here, :].astype(f32) + z_got[t, came * piece : (came + 1) * piece].astype(f32)
            own[slot, here, :] = total.astype(bf16)
        last_copy(t).start()

    def meet_last(t):
        last_copy(t).wait_recv()
        last_copy(t).wait_send()
        mine = own[lax.rem(t, SLOTS), 3 * piece :, :].astype(f32)
        grads_ref[t] = mine + z_got[t, 2 * piece :].astype(f32)

    def fetch(t):
        far_copy(t).wait_recv()
        own_copy(t).start()
        got_copy(t).start()

    def meet_far(t):
        own_copy(t).wait()
        got_copy(t).wait()
        slot, got = lax.rem(t, SLOTS), lax.rem(t, 2)
        for z in range(ctxs):
            target = pl.ds(z * piece, piece)
            total = own[slot, target, :].astype(f32) + y_got[got, target, :].astype(f32)
            own[slot, target, :] = total.astype(bf16)
        near_copy(t).start()

    def when(test, step, t):
        @pl.when(test)
        def _():
            step(t)

    def tick(n):
        when((n - 1 > EARLY) & (n - 1 < TILES), meet_far, n - 1)
        when((n - 3 >= EARLY) & (n - 3 < TILES), meet_near, n - 3)
        when((n - 5 >= EARLY - 1) & (n - 5 < TILES), meet_last, n - 5)
        when(n < TILES, fetch, n)


    part_copy = remote(part_hbm, part_other, across, x_send.at[0], x_recv.at[0])
    part_copy.start()
    feed_copy = remote(feed_hbm, feed_other, across, x_send.at[1], x_recv.at[1])
    feed_copy.start()

    def act_copy(t):
        columns = pl.ds(pl.multiple_of(lax.rem(t, 4) * TILE, TILE), TILE)
        return pltpu.make_async_copy(
            act_hbm.at[t // 4, :, columns], rhs.at[lax.rem(t, 2)], act_sem.at[t]
        )

    loads = [
        load(mid_normed_hbm, lhs.at[0], 0),
        load(cot_hbm, lhs.at[1], 1),
        load(part_hbm, part, 2),
        load(middle_hbm, mid, 3),
        load(weight_hbm.at[:, pl.ds(2 * q_cols + LANES, q_cols)], w_out, 4),
        load(weight_hbm.at[:, pl.ds(0, 2 * q_cols)], w_in, 5),
    ]
    later = (
        (low_hbm, low_ref), (q_hbm, q_ref), (kv_hbm, kv_ref), (att_hbm, att_ref), (sum_hbm, sum_ref),
        (qi_hbm, qi_ref), (ki_hbm, ki_ref), (cos_hbm, cos_ref), (sin_hbm, sin_ref),
    )
    later = [load(have, into, 21 + j) for j, (have, into) in enumerate(later)]
    act_copy(0).start()
    for copy in loads + later:
        copy.start()
    loads[0].wait()
    loads[1].wait()

    def plain(t):
        def times(start, left):
            return dot(left, rhs[lax.rem(t, 2)], TN).astype(bf16)

        return times

    def feed_step(t, unused):
        act_copy(t).wait()

        @pl.when(t + 1 < FEED_TILES)
        def _():
            act_copy(t + 1).start()

        product(t, lambda lanes: lhs[t // 8, :, lanes], plain(t))

        @pl.when(t == 0)
        def _():
            meet_core(t)
            send_far(t)

        @pl.when(t >= 2)
        def _():
            meet_core(t - 1)

        @pl.when(t >= 3)
        def _():
            send_far(t - 2)

        n, turn = (t - 4) // 3, lax.rem(t, 3)
        when((t >= 4) & (turn == 1), fetch, n)
        when((t >= 7) & (turn == 1), meet_near, n - 1)
        when((t >= 4) & (turn == 2), meet_far, n)
        when((t >= 7) & (turn == 0), meet_last, n - 1)

        return unused

    lax.fori_loop(0, FEED_TILES, feed_step, 0)
    meet_core(FEED_TILES - 1)
    send_far(FEED_TILES - 2)
    send_far(FEED_TILES - 1)
    for copy in later:
        copy.wait()

    for q_tile in range(rows // SIDE):
        for g in range(groups):
            flat = flat_heads(q_ref, q_tile, g, ratio)
            q2[q_tile * groups + g] = flat
            q2t[q_tile * groups + g] = flat.astype(f32).T.astype(bf16)
    dq_ref[...] = jnp.zeros(dq_ref.shape, f32)
    gain_rows[...] = jnp.zeros(gain_rows.shape, f32)


    loads[2].wait()
    loads[3].wait()
    t_1, t_2, t_3, t_4 = (jnp.int32(j) for j in range(1, 5))
    fetch(t_3)
    meet_last(t_1)
    meet_near(t_2)
    part_copy.wait_recv()
    few = 64

    def norm_rows(i, unused):
        here = pl.ds(pl.multiple_of(i * few, few), few)
        field = mid[here, :]
        scale = lax.rsqrt(jnp.mean(field * field, axis=1, keepdims=True) + epsilon)
        unit = field * scale
        back = part[here, :].astype(f32) + part_other[here, :].astype(f32)
        gain_rows[1:2, :] += jnp.sum(back * unit, axis=0, keepdims=True)
        inner = back * gain_ref[1:2, :]
        out = lhs[1, here, :].astype(f32) + scale * (
            inner - unit * jnp.mean(inner * unit, axis=1, keepdims=True)
        )
        mid[here, :] = out
        lhs[0, here, :] = out.astype(bf16)
        return unused

    lax.fori_loop(0, rows // few, norm_rows, 0)
    meet_far(t_3)
    meet_last(t_2)
    fetch(t_4)
    middle_copy = load(mid, back_middle, 6)
    middle_copy.start()
    normed_copy = load(normed_hbm, lhs.at[1], 7)
    normed_copy.start()
    x_copy = load(x_hbm, part, 8)
    x_copy.start()
    loads[4].wait()
    cot[:, :q_cols] = dot(lhs[0], w_out[...], NN).astype(bf16)
    meet_far(t_4)
    meet_near(t_3)
    for q_tile in range(rows // SIDE):
        for g in range(groups):
            i = q_tile * groups + g
            flat = flat_heads(cot, q_tile, g, ratio)
            turned_flat = flat.astype(f32).T
            d2[i] = flat
            d2t[i] = turned_flat.astype(bf16)
            delta[i] = jnp.sum(turned_flat * att_ref[i], axis=0, keepdims=True)

    t_out = jnp.int32(FEED_TILES)
    product(
        t_out, lambda lanes: lhs[0, :, lanes], lambda start, left: dot(left, low_ref[:, :TILE], TN).astype(bf16)
    )


    def kv_copy(s):
        return remote(kv_sent.at[s], kv_got.at[s], after, k_send.at[s], k_recv.at[s])

    def back_piece(s, unused):
        k = lax.rem(s + 1, ctxs)
        pairs = [(q, kk) for kk in range(rows // SIDE) for q in range(kk, rows // SIDE)]
        for index, (q_tile, k_tile) in enumerate(pairs):
            bias_ref[index] = tile_bias(qi_ref, ki_ref, k, q_tile, k_tile, ratio)
        sums = []
        for k_tile in range(rows // SIDE):
            here = slice(k_tile * SIDE, (k_tile + 1) * SIDE)
            for g in range(groups):
                key, value = kv_ref[k, here, head_lanes(g)], kv_ref[k, here, head_lanes(g, kv_width)]
                d_key = d_value = None
                for index, (q_tile, which) in enumerate(pairs):
                    if which != k_tile:
                        continue
                    i = q_tile * groups + g
                    raw = dot(key, q2t[i], NN) * SCALE2 + bias_ref[index]
                    share = jnp.exp2(raw - sum_ref[i])
                    back_share = dot(value, d2t[i], NN)
                    back = (share * (back_share - delta[i])).astype(bf16)
                    one_value = dot(share.astype(bf16), d2[i], NN)
                    one_key = dot(back, q2[i], NN)
                    d_value = one_value if d_value is None else d_value + one_value
                    d_key = one_key if d_key is None else d_key + one_key
                    dq_ref[i] += dot(key, back, TN)
                kv_sent[s, here, head_lanes(g)] = (d_key * SCALE).astype(bf16)
                kv_sent[s, here, head_lanes(g, kv_width)] = d_value.astype(bf16)

        @pl.when(s == 0)
        def _():
            kv_copy(0).start()
            meet_core(t_out)
            send_far(t_out)

        @pl.when((s == 0) | (s == 2))
        def _():
            tick(5 + s // 2)

        return unused

    lax.fori_loop(0, ctxs, back_piece, 0)

    def kv_pass(s):
        kv_copy(s).wait_recv()

        def add(i, unused):
            here = pl.ds(pl.multiple_of(i * few, few), few)
            total = kv_sent[s + 1, here, :].astype(f32) + kv_got[s, here, :].astype(f32)
            kv_sent[s + 1, here, :] = total.astype(bf16)
            return unused

        lax.fori_loop(0, rows // few, add, 0)
        if s + 1 < ctxs - 1:
            kv_copy(s + 1).start()


    kv_pass(0)
    tick(jnp.int32(7))
    for i in range(dq_ref.shape[0]):
        q_tile, g = divmod(i, groups)
        here = slice(q_tile * SIDE, (q_tile + 1) * SIDE)
        flat = dq_ref[i].T * SCALE
        for h in range(ratio):
            cot[here, head_lanes(g * ratio + h)] = turned(
                flat[h * SIDE : (h + 1) * SIDE], cos_ref[here, :], sin_ref[here, :], -1
            ).astype(bf16)
    normed_copy.wait()
    tail = q_cols - TILE
    t_query, t_both, t_key, t_last = (jnp.int32(FEED_TILES + 1 + j) for j in range(4))
    product(
        t_query, lambda lanes: lhs[1, :, lanes], lambda start, left: dot(left, cot[:, :TILE], TN).astype(bf16)
    )

    def times_both(start, left):
        from_query = dot(left, cot[:, TILE:q_cols], TN)
        from_output = dot(lhs[0, :, pl.ds(start, section)], low_ref[:, TILE:], TN)
        return jnp.concatenate([from_query, from_output], axis=1).astype(bf16)

    meet_core(t_query)
    product(t_both, lambda lanes: lhs[1, :, lanes], times_both)
    send_far(t_query)
    tick(jnp.int32(8))
    meet_core(t_both)
    send_far(t_both)
    feed_copy.wait_recv()
    here_copies = [load(feed_hbm, lhs.at[0], 9), load(feed_other, part_other, 10)]
    for copy in here_copies:
        copy.start()
    loads[5].wait()
    middle_copy.wait()
    for j in range(width // TILE):
        lanes = slice(j * TILE, (j + 1) * TILE)
        mid[:, lanes] = dot(cot[:, :q_cols], w_in[lanes, :q_cols], NT)
    kv_pass(1)
    tick(jnp.int32(9))


    for copy in here_copies:
        copy.wait()
    for half in range(rows // SIDE):
        here = slice(half * SIDE, (half + 1) * SIDE)
        pieces = [
            load(
                middle_hbm.at[pl.ds(half * SIDE, SIDE), pl.ds(j * TILE, TILE)],
                bias_ref.at[j], 11 + half * (width // TILE) + j,
            )
            for j in range(width // TILE)
        ]
        for copy in pieces:
            copy.start()
        for j, copy in enumerate(pieces):
            copy.wait()
            lanes = slice(j * TILE, (j + 1) * TILE)
            total = bias_ref[j] + lhs[0, here, lanes].astype(f32)
            lhs[0, here, lanes] = (total + part_other[here, lanes].astype(f32)).astype(bf16)
    result_copy = load(lhs.at[0], result_ref, 17)
    result_copy.start()
    tick(jnp.int32(10))

    kv_pass(2)
    for g in range(groups):
        cot[:, head_lanes(g, q_cols)] = turned(
            kv_sent[ctxs - 1, :, head_lanes(g)].astype(f32), cos_ref[...], sin_ref[...], -1
        ).astype(bf16)
    cot[:, q_cols + kv_width :] = kv_sent[ctxs - 1, :, kv_width:]
    x_copy.wait()
    x_rows = part[...].astype(f32)
    scale = lax.rsqrt(jnp.mean(x_rows * x_rows, axis=1, keepdims=True) + epsilon)
    for j in range(width // TILE):
        lanes = slice(j * TILE, (j + 1) * TILE)
        back = mid[:, lanes] + dot(cot[:, q_cols:], w_in[lanes, q_cols:], NT)
        part_other[:, lanes] = back.astype(bf16)
        gain_rows[0:1, lanes] += jnp.sum(back * (part[:, lanes].astype(f32) * scale), axis=0, keepdims=True)
    gain_copy = remote(gain_rows.at[pl.ds(0, 8)], gain_other, across, x_send.at[2], x_recv.at[2])
    gain_copy.start()
    part2_copy = remote(part_other, part2_other, across, x_send.at[3], x_recv.at[3])
    part2_copy.start()
    middle_back_copy = load(back_middle, mid, 18)
    middle_back_copy.start()
    product(
        t_key, lambda lanes: lhs[1, :, lanes], lambda start, left: dot(left, cot[:, q_cols : q_cols + TILE], TN).astype(bf16)
    )
    gain_copy.wait_recv()
    gain_copy.wait_send()
    gain_rows[0:1, :] += gain_other[0:1, :]
    gain_columns[...] = gain_rows[...].T

    def times_last(start, left):
        some = dot(left, cot[:, q_cols + TILE :], TN)
        gains = gain_columns[pl.ds(start, section), :]
        spare = jnp.zeros((section, TILE - tail - LANES), f32)
        return jnp.concatenate([some, gains, spare], axis=1).astype(bf16)

    meet_core(t_key)
    product(t_last, lambda lanes: lhs[1, :, lanes], times_last)
    send_far(t_key)
    meet_core(t_last)
    send_far(t_last)

    def drain(n, unused):
        tick(n)
        return unused

    lax.fori_loop(11, TILES, drain, 0)


    result_copy.wait()
    part2_copy.wait()
    other_copy = load(part2_other, lhs.at[0], 19)
    other_copy.start()
    middle_back_copy.wait()
    other_copy.wait()

    def token_rows(i, unused):
        here = pl.ds(pl.multiple_of(i * few, few), few)
        field = part[here, :].astype(f32)
        scale = lax.rsqrt(jnp.mean(field * field, axis=1, keepdims=True) + epsilon)
        unit = field * scale
        back = part_other[here, :].astype(f32) + lhs[0, here, :].astype(f32)
        inner = back * gain_ref[0:1, :]
        out = mid[here, :] + scale * (
            inner - unit * jnp.mean(inner * unit, axis=1, keepdims=True)
        )
        part_other[here, :] = out.astype(bf16)
        return unused

    lax.fori_loop(0, rows // few, token_rows, 0)
    token_copy = load(part_other, token_ref, 20)
    token_copy.start()
    lax.fori_loop(TILES, TILES + 5, drain, 0)

    for t in (TILES - 2, TILES - 1):
        core_copy(jnp.int32(t)).wait_send()

    def far_done(t, unused):
        far_copy(t).wait_send()
        return unused

    lax.fori_loop(0, TILES, far_done, 0)
    for s in range(ctxs - 1):
        kv_copy(s).wait_send()
    part_copy.wait_send()
    feed_copy.wait_send()
    token_copy.wait()


def back_all(part, feed, cotangent, middle, gains, act, mid_normed, x, normed, low, queries, kv, att, sums, qi, ki, cosine, sine, weights, ctxs):
    rows, width = x.shape
    q_cols = queries.shape[1]
    groups = kv.shape[2] // (2 * HEAD_SIZE)
    ratio = q_cols // (groups * HEAD_SIZE)
    tiles, lanes = dense_shapes(rows, groups, ratio)
    section = width // 4
    piece = section // ctxs
    vmem, hbm = pl.BlockSpec(memory_space=pltpu.VMEM), pl.BlockSpec(memory_space=pl.ANY)
    full = jax.ShapeDtypeStruct((rows, width), bf16)
    sems = lambda *n: pltpu.SemaphoreType.DMA(n)
    space = lambda *shape: pltpu.VMEM(shape, bf16)
    wide = lambda *shape: pltpu.VMEM(shape, f32)
    pairs = (rows // SIDE) * (rows // SIDE + 1) // 2
    return pl.pallas_call(
        back_kernel,
        in_specs=[hbm] * 4 + [vmem] + [hbm] * 14,
        out_specs=[hbm] * 5 + [vmem] + [hbm] * 2,
        out_shape=[
            full,
            jax.ShapeDtypeStruct((rows, width), f32),
            full,
            full,
            full,
            jax.ShapeDtypeStruct((TILES, piece, TILE), f32),
            jax.ShapeDtypeStruct((TILES, 2 * section, TILE), bf16),
            jax.ShapeDtypeStruct((TILES, section, TILE), bf16),
        ],
        scratch_shapes=[pltpu.VMEM(part_in.shape, part_in.dtype) for part_in in (low, queries, kv, att, sums, qi, ki, cosine, sine)]
        + [
            space(2, rows, width), wide(rows, width), space(rows, width), space(rows, width),
            space(width, q_cols), space(width, 2 * q_cols), space(2, rows, TILE),
            space(tiles, lanes, HEAD_SIZE), space(tiles, HEAD_SIZE, lanes),
            space(tiles, lanes, HEAD_SIZE), space(tiles, HEAD_SIZE, lanes),
            wide(tiles, 1, lanes), wide(pairs, SIDE, lanes), wide(tiles, HEAD_SIZE, lanes),
            space(ctxs, rows, q_cols), space(ctxs - 1, rows, q_cols), space(rows, 2 * q_cols),
            wide(LANES, width), wide(8, width), wide(width, LANES),
            space(2, 2 * section, TILE), space(2, 2 * section, TILE), space(4, 2 * section, TILE),
            space(2, 2 * section, TILE), space(SLOTS, section, TILE), space(2, section, TILE),
            space(TILES, (ctxs - 1) * piece, TILE),
            sems(30), sems(FEED_TILES), sems(4), sems(4), sems(TILES), sems(TILES),
            pltpu.SemaphoreType.REGULAR, sems(TILES), sems(TILES), sems(TILES), sems(TILES, 2),
            sems(TILES, 2), sems(TILES, 2), sems(ctxs - 1), sems(ctxs - 1),
        ],
        compiler_params=pltpu.CompilerParams(
            vmem_limit_bytes=63 * MIB, collective_id=1, has_side_effects=True
        ),
        cost_estimate=cost(4e10, 1e8),
        name="back_all",
    )(part, feed, cotangent, middle, gains, act, mid_normed, x, normed, low, queries, kv, att, sums, qi, ki, cosine, sine, weights)


def output_kernel(a_ref, w_ref, o_ref):
    o_ref[...] = dot(a_ref[...], w_ref[...], NT).astype(bf16)


def output_product(attended, weights, column, features):
    rows, inner = attended.shape
    return pl.pallas_call(
        output_kernel,
        grid=(2,),
        in_specs=[
            whole(attended.shape),
            pl.BlockSpec((features // 2, inner), lambda j: (j, column)),
        ],
        out_specs=pl.BlockSpec((rows, features // 2), lambda j: (0, j)),
        out_shape=jax.ShapeDtypeStruct((rows, features), bf16),
        compiler_params=params(40),
        cost_estimate=cost(2 * rows * inner * features, 2 * inner * features),
        name="output_product",
    )(attended, weights)


def feed_kernel(
    normed_ref, cot_ref, gate_ref, up_ref, down_ref,
    act_ref, back_ref, feed_ref, total_ref, feed_total,
):
    step = pl.program_id(0)
    gate = dot(normed_ref[...], gate_ref[...], NN)
    upward = dot(normed_ref[...], up_ref[...], NN)
    back_mixed = dot(cot_ref[...], down_ref[...], NN)
    sigmoid = 1.0 / (1.0 + jnp.exp(-gate))
    activated = gate * sigmoid
    mixed = (activated * upward).astype(bf16)
    back_gate = (back_mixed * upward * sigmoid * (1.0 + gate * (1.0 - sigmoid))).astype(bf16)
    back_up = (back_mixed * activated).astype(bf16)
    act_ref[0] = back_gate
    act_ref[1] = back_up
    act_ref[2] = mixed
    part = dot(back_gate, gate_ref[...], NT) + dot(back_up, up_ref[...], NT)
    feed = dot(mixed, down_ref[...], NT)

    @pl.when(step == 0)
    def _():
        total_ref[...] = part
        feed_total[...] = feed

    @pl.when(step > 0)
    def _():
        total_ref[...] += part
        feed_total[...] += feed

    @pl.when(step == pl.num_programs(0) - 1)
    def _():
        back_ref[...] = total_ref[...].astype(bf16)
        feed_ref[...] = feed_total[...].astype(bf16)


def feed_forward(normed, cotangent, gate, up, down):
    rows, width = normed.shape
    hidden = gate.shape[1]
    steps = hidden // FEED_TILE
    tile_of = pl.BlockSpec((width, FEED_TILE), lambda j: (0, j))
    acts_of = pl.BlockSpec((3, rows, FEED_TILE), lambda j: (0, 0, j))
    full = whole((rows, width))
    return pl.pallas_call(
        feed_kernel,
        grid=(steps,),
        in_specs=[full, full] + [tile_of] * 3,
        out_specs=[acts_of, full, full],
        out_shape=[
            jax.ShapeDtypeStruct((3, rows, hidden), bf16),
            jax.ShapeDtypeStruct((rows, width), bf16),
            jax.ShapeDtypeStruct((rows, width), bf16),
        ],
        scratch_shapes=[pltpu.VMEM((rows, width), f32)] * 2,
        compiler_params=params(56),
        cost_estimate=cost(12 * rows * width * hidden, 6 * width * hidden),
        name="feed_forward",
    )(normed, cotangent, gate, up, down)


def middle_kernel(cot_ref, mine_ref, other_ref, middle_ref, gain_ref, w_ref, bm_ref, bb_ref, ba_ref, grad_ref):
    middle = middle_ref[...]
    scale = lax.rsqrt(jnp.mean(middle * middle, axis=1, keepdims=True) + epsilon)
    unit = middle * scale
    back = mine_ref[...].astype(f32) + other_ref[...].astype(f32)
    grad_ref[...] = jnp.sum(back * unit, axis=0, keepdims=True)
    inner = back * gain_ref[1:2, :]
    out = cot_ref[...].astype(f32) + scale * (
        inner - unit * jnp.mean(inner * unit, axis=1, keepdims=True)
    )
    bm_ref[...] = out
    low = out.astype(bf16)
    bb_ref[...] = low
    ba_ref[...] = dot(low, w_ref[...], NN).astype(bf16)


def middle_back(cotangent, mine, other, middle, gains, weights, column, inner):
    rows, width = middle.shape
    full = whole((rows, width))
    return pl.pallas_call(
        middle_kernel,
        grid=(1,),
        in_specs=[full, full, full, full, whole(gains.shape)]
        + [pl.BlockSpec((width, inner), lambda j: (0, column))],
        out_specs=[full, full, whole((rows, inner)), whole((1, width))],
        out_shape=[
            jax.ShapeDtypeStruct((rows, width), f32),
            jax.ShapeDtypeStruct((rows, width), bf16),
            jax.ShapeDtypeStruct((rows, inner), bf16),
            jax.ShapeDtypeStruct((1, width), f32),
        ],
        compiler_params=params(56),
        cost_estimate=cost(2 * rows * width * inner, 1.5e7),
        name="middle_back",
    )(cotangent, mine, other, middle, gains, weights)


def inputs_kernel(count, x_ref, qc_ref, cos_ref, sin_ref, w_ref, *refs):
    parts = refs[:count]
    cot_ref, back_ref, grad_ref = refs[count:]
    half = qc_ref.shape[1] // 2
    cot_ref[:, : 2 * half] = qc_ref[...]
    total = parts[0][...].astype(f32)
    for part in parts[1:]:
        total += part[...].astype(f32)
    for h in range(half // HEAD_SIZE):
        lanes = slice(h * HEAD_SIZE, (h + 1) * HEAD_SIZE)
        there = slice(2 * half + h * HEAD_SIZE, 2 * half + (h + 1) * HEAD_SIZE)
        cot_ref[:, there] = turned(total[:, lanes], cos_ref[...], sin_ref[...], -1).astype(bf16)
    cot_ref[:, 3 * half :] = total[:, half:].astype(bf16)
    back = dot(cot_ref[...], w_ref[...], NT)
    back_ref[...] = back.astype(bf16)
    x = x_ref[...].astype(f32)
    unit = x * lax.rsqrt(jnp.mean(x * x, axis=1, keepdims=True) + epsilon)
    grad_ref[...] = jnp.sum(back * unit, axis=0, keepdims=True)


def inputs_back(x, qc, cosine, sine, weights, parts):
    rows, width = x.shape
    inner = 2 * qc.shape[1]
    full = whole((rows, width))
    return pl.pallas_call(
        functools.partial(inputs_kernel, len(parts)),
        grid=(1,),
        in_specs=[full, whole(qc.shape), whole(cosine.shape), whole(sine.shape)]
        + [pl.BlockSpec((width, inner), lambda j: (0, 0))]
        + [whole(parts[0].shape)] * len(parts),
        out_specs=[whole((rows, inner)), full, whole((1, width))],
        out_shape=[
            jax.ShapeDtypeStruct((rows, inner), bf16),
            jax.ShapeDtypeStruct((rows, width), bf16),
            jax.ShapeDtypeStruct((1, width), f32),
        ],
        compiler_params=params(56),
        cost_estimate=cost(2 * rows * width * inner, 1.5e7),
        name="inputs_back",
    )(x, qc, cosine, sine, weights, *parts)


def final_kernel(bm_ref, mine_ref, other_ref, x_ref, gain_ref, o_ref):
    x = x_ref[...].astype(f32)
    scale = lax.rsqrt(jnp.mean(x * x, axis=1, keepdims=True) + epsilon)
    unit = x * scale
    inner = (mine_ref[...].astype(f32) + other_ref[...].astype(f32)) * gain_ref[0:1, :]
    out = bm_ref[...] + scale * (inner - unit * jnp.mean(inner * unit, axis=1, keepdims=True))
    o_ref[...] = out.astype(bf16)


def final_back(back_middle, mine, other, x, gains):
    rows, width = x.shape
    block = pl.BlockSpec((rows // 4, width), lambda j: (j, 0))
    return pl.pallas_call(
        final_kernel,
        grid=(4,),
        in_specs=[block] * 4 + [whole(gains.shape)],
        out_specs=block,
        out_shape=jax.ShapeDtypeStruct((rows, width), bf16),
        compiler_params=params(40),
        cost_estimate=cost(1e6, 1e7),
        name="final_back",
    )(back_middle, mine, other, x, gains)


def relative(field, pairs, ctxs):
    dp, ctx = lax.axis_index("dp"), lax.axis_index("ctx")
    shaped = field.reshape((pairs, 2, ctxs, -1) + field.shape[1:])
    for axis, shift in ((0, dp // 2 + 1), (1, dp % 2 + 1), (2, ctx + 1)):
        shaped = jnp.roll(shaped, -shift, axis)
    return shaped.swapaxes(0, 1).reshape(field.shape)


def gradient_kernel(pairs, ctxs, place, a_ref, b_ref, send_ref, keep_ref):
    width = a_ref.shape[1]
    section = width // (2 * pairs)
    piece = section // ctxs
    for c, out in ((1, send_ref), (0, keep_ref)):
        for y in range(pairs):
            pair = lax.rem(place[0] + y + 1, pairs)
            core = lax.rem(place[1] + c, 2)
            lanes = pl.ds(pl.multiple_of((pair * 2 + core) * section, LANES), section)
            result = dot(a_ref[:, lanes], b_ref[...], TN).astype(bf16)
            for z in range(ctxs):
                far = lax.rem(z + ctxs - place[2] - 1 + ctxs, ctxs)
                rows = pl.ds(pl.multiple_of(y * section + far * piece, piece), piece)
                out[rows, :] = result[z * piece : (z + 1) * piece]


def gradient(a, b, pairs, ctxs):
    rows, width = a.shape
    columns = b.shape[1]
    section = width // (2 * pairs)
    if section % LANES or (section // ctxs) % 32:
        ordered = relative(dot(a, b, TN).astype(bf16), pairs, ctxs)
        return ordered[: width // 2], ordered[width // 2 :]
    dp, ctx = lax.axis_index("dp"), lax.axis_index("ctx")
    place = jnp.stack([dp // 2, dp % 2, ctx]).astype(jnp.int32)
    tile = TILE if columns % TILE == 0 else columns // 2
    block = pl.BlockSpec((width // 2, tile), lambda j: (0, j))
    return pl.pallas_call(
        functools.partial(gradient_kernel, pairs, ctxs),
        grid=(columns // tile,),
        in_specs=[SCALARS, whole(a.shape), pl.BlockSpec((rows, tile), lambda j: (0, j))],
        out_specs=[block, block],
        out_shape=[jax.ShapeDtypeStruct((width // 2, columns), bf16)] * 2,
        compiler_params=params(40),
        cost_estimate=cost(2 * rows * width * columns, 2 * width * columns),
        name="gradient",
    )(place, a, b)


def shifted(field, axis, steps, stride=1):
    count = lax.axis_size(axis)
    return lax.ppermute(
        field, axis, [(i, (i + steps * stride) % count) for i in range(count)]
    )


def other_core(field):
    return lax.ppermute(field, "dp", [(i, i ^ 1) for i in range(lax.axis_size("dp"))])


def sum_to_owner(send, keep, pairs, ctxs):
    columns = send.shape[1]
    got = other_core(send).reshape(pairs, -1, columns)
    keep = keep.reshape(pairs, -1, columns)
    total = got[-1].astype(f32) + keep[-1].astype(f32)
    for y in range(1, pairs):
        part = (got[y - 1].astype(f32) + keep[y - 1].astype(f32)).astype(bf16)
        total = total + shifted(part, "dp", y, 2).astype(f32)
    total = total.reshape(ctxs, -1, columns)
    result = total[-1]
    for z in range(1, ctxs):
        result = result + shifted(total[z - 1].astype(bf16), "ctx", z).astype(f32)
    return result


def swapped(field):
    count = lax.axis_size("tp")
    return lax.ppermute(field, "tp", [(i, count - 1 - i) for i in range(count)])


def body(
    tokens,
    cotangent,
    lengths,
    block_order,
    pre_gain,
    query_weight,
    key_weight,
    value_weight,
    output_weight,
    mid_gain,
    gate_weight,
    up_weight,
    down_weight,
):
    ctxs = lax.axis_size("ctx")
    pairs = lax.axis_size("dp") // 2
    ctx = lax.axis_index("ctx")
    order = block_order[0]
    ends = jnp.cumsum(lengths[0]).astype(jnp.int32)
    starts = ends - lengths[0]
    place = jnp.stack([ctx]).astype(jnp.int32)
    q_cols = query_weight.shape[1]
    features = tokens.shape[1]

    gain_columns = jnp.pad(jnp.stack([pre_gain, mid_gain], axis=1), ((0, 0), (0, LANES - 2)))
    packed = (query_weight, key_weight, value_weight, gain_columns, output_weight)
    stream = streams(order, ctx)
    lows = jnp.max(jnp.where(starts[None, :] <= stream[0][:, None], starts[None, :], 0), axis=1)
    if pairs == 2 and ctxs == 4 and query_weight.shape[0] % 32 == 0:
        own = jnp.stack([stream[0], lows])
        qi = jnp.concatenate([own, stream, jnp.zeros_like(own)], axis=0)
        (
            first, gate_full, up_full, down_full, queries, kv, normed, gains,
            attended_low, att, sums, middle, mid_normed, cosine, sine, ki,
        ) = forward_all(
            packed, gate_weight, up_weight, down_weight, tokens, frequencies(), qi, q_cols, ctxs
        )
        act, back_part, feed = feed_forward(mid_normed, cotangent, gate_full, up_full, down_full)
        _, _, _, result, token_gradient, grads, _, _ = back_all(
            back_part, feed, cotangent, middle, gains, act, mid_normed, tokens, normed,
            attended_low, queries, kv, att, sums, qi, ki, cosine, sine, first, ctxs,
        )
        wide = lambda *tiles: jnp.concatenate([grads[t] for t in tiles], axis=1)
        tail = q_cols - TILE
        qkv_gradient = jnp.concatenate(
            [grads[13], grads[14][:, :tail], grads[15], grads[16][:, :tail]], axis=1
        )
        output_gradient = jnp.concatenate([grads[12], grads[14][:, tail:]], axis=1)
        gain_sums = grads[16][:, tail : tail + LANES]
        gate_gradient, up_gradient = wide(0, 1, 2, 3), wide(4, 5, 6, 7)
        down_gradient = wide(8, 9, 10, 11)
    else:
        first, gate_full, up_full, down_full = (
            lax.all_gather(field, ROWS, axis=0, tiled=True)
            for field in (jnp.concatenate(packed, axis=1), gate_weight, up_weight, down_weight)
        )
        cosine, sine = angles(stream[0] - lows)
        gains = first[:, 2 * q_cols : 2 * q_cols + 8].T.astype(f32)
        queries, kv, normed = project(tokens, gains, cosine, sine, first, q_cols)
        pieces = [kv] + [shifted(kv, "ctx", k) for k in range(1, ctxs)]
        output_weights = first[:, 2 * q_cols + LANES :]
        attended_low, att, sums = attend(order, starts, place, queries, pieces)
        branch = output_product(attended_low, output_weights, 0, features)
        middle = tokens.astype(f32) + (branch.astype(f32) + swapped(branch).astype(f32))
        mid_scale = lax.rsqrt(jnp.mean(middle * middle, axis=1, keepdims=True) + epsilon)
        mid_normed = (middle * mid_scale * gains[1:2]).astype(bf16)
        act, back_part, feed = feed_forward(mid_normed, cotangent, gate_full, up_full, down_full)
        back_other = swapped(back_part)
        gate_parts = gradient(mid_normed, act[0], pairs, ctxs)
        up_parts = gradient(mid_normed, act[1], pairs, ctxs)
        down_parts = gradient(cotangent, act[2], pairs, ctxs)
        result = (middle + feed.astype(f32) + swapped(feed).astype(f32)).astype(bf16)

        back_middle, back_branch, back_attended, mid_grad = middle_back(
            cotangent, back_part, back_other, middle, gains, output_weights, 0, q_cols
        )
        output_parts = gradient(back_branch, attended_low, pairs, ctxs)
        back = attend_back(
            order, starts, place, queries, back_attended, att, sums, cosine, sine, pieces
        )
        own_parts = [back[1]] + [shifted(back[1 + k], "ctx", -k) for k in range(1, ctxs)]
        cot, normed_part, pre_grad = inputs_back(
            tokens, back[0], cosine, sine, first, own_parts
        )
        normed_other = swapped(normed_part)
        qkv_parts = gradient(normed, cot, pairs, ctxs)
        token_gradient = final_back(back_middle, normed_part, normed_other, tokens, gains)

        mid_once = jnp.where(lax.axis_index("tp") == 0, mid_grad, 0.0)
        pair = jnp.concatenate([pre_grad, mid_once], axis=0).astype(bf16)
        pair = jnp.pad(pair, ((0, 6), (0, 0))).T
        ordered = relative(pair, pairs, ctxs)
        gain_sums = sum_to_owner(
            ordered[: features // 2], ordered[features // 2 :], pairs, ctxs
        )
        gain_sums = gain_sums + swapped(gain_sums)
        gate_gradient = sum_to_owner(*gate_parts, pairs, ctxs)
        up_gradient = sum_to_owner(*up_parts, pairs, ctxs)
        down_gradient = sum_to_owner(*down_parts, pairs, ctxs)
        output_gradient = sum_to_owner(*output_parts, pairs, ctxs)
        qkv_gradient = sum_to_owner(*qkv_parts, pairs, ctxs)
    return (
        result,
        token_gradient,
        gain_sums[:, 0],
        qkv_gradient[:, :q_cols],
        qkv_gradient[:, q_cols : q_cols + q_cols // 2],
        qkv_gradient[:, q_cols + q_cols // 2 :],
        output_gradient,
        gain_sums[:, 1],
        gate_gradient,
        up_gradient,
        down_gradient,
    )


def solution(mesh):
    rows, split = P(ROWS, None), P(ROWS, "tp")
    return jax.shard_map(
        body,
        mesh=mesh,
        in_specs=(rows, rows, P("dp", None), P("dp", None, None), P(ROWS))
        + (split,) * 4
        + (P(ROWS),)
        + (split,) * 3,
        out_specs=(rows, rows, P(ROWS)) + (split,) * 4 + (P(ROWS),) + (split,) * 3,
        check_vma=False,
    )
```

```python
import functools
import math

import jax
import jax.numpy as jnp
import numpy as np
from jax import lax
from jax.experimental import pallas as pl
from jax.experimental.pallas import tpu as pltpu
from jax.sharding import PartitionSpec as P

HEAD_SIZE = 96
HALF = HEAD_SIZE // 2
BLOCK = 64
SPAN = 256
TILE = 512
FEED_TILE = 512
LANES = 128

epsilon = 1e-05
rotary_base = 100000.0
masked_score = -1e30
SCALE = HEAD_SIZE**-0.5
SCALE2 = SCALE / math.log(2.0)

f32 = jnp.float32
bf16 = jnp.bfloat16
ROWS = ("dp", "ctx")
MIB = 2**20


def dot(left, right, contract):
    return lax.dot_general(
        left, right, ((contract[:1], contract[1:]), ((), ())), preferred_element_type=f32
    )


NN, NT, TN = (1, 0), (1, 1), (0, 0)


def cost(flops, moved):
    return pl.CostEstimate(flops=int(flops), bytes_accessed=int(moved), transcendentals=0)


def params(mib):
    return pltpu.CompilerParams(vmem_limit_bytes=mib * MIB)


def whole(shape):
    return pl.BlockSpec(shape, lambda *_: (0,) * len(shape))


SCALARS = pl.BlockSpec(memory_space=pltpu.SMEM)


def frequencies():
    steps = np.arange(HALF, dtype=np.float64) * 2.0 / HEAD_SIZE
    return jnp.asarray(rotary_base ** -steps, f32)[None, :]


def angles(place):
    turn = place.astype(f32)[:, None] * frequencies()
    return (jnp.cos(turn), jnp.sin(turn))


def streams(order, ctx):
    rounds, count = order.shape
    owners = order[:, lax.rem(ctx - jnp.arange(count) + count, count)].T
    blocks = owners + (jnp.arange(rounds, dtype=jnp.int32) * count)[None, :]
    within = jnp.arange(BLOCK, dtype=jnp.int32)
    return (blocks[:, :, None] * BLOCK + within).reshape(count, rounds * BLOCK).astype(jnp.int32)


def turned(head, cosine, sine, sign):
    first, second = head[:, :HALF], head[:, HALF:]
    along = sine if sign > 0 else -sine
    return jnp.concatenate(
        [first * cosine - second * along, second * cosine + first * along], axis=1
    )


def project_kernel(x_ref, gain_ref, cos_ref, sin_ref, w_ref, q_ref, kv_ref, normed_ref):
    step = pl.program_id(0)
    tile = w_ref.shape[1]

    @pl.when(step == 0)
    def _():
        x = x_ref[...].astype(f32)
        scale = lax.rsqrt(jnp.mean(x * x, axis=1, keepdims=True) + epsilon)
        normed_ref[...] = (x * scale * gain_ref[0:1, :]).astype(bf16)

    out = dot(normed_ref[...], w_ref[...], NN)

    def rotated(ref):
        for h in range(tile // HEAD_SIZE):
            lanes = slice(h * HEAD_SIZE, (h + 1) * HEAD_SIZE)
            ref[:, lanes] = turned(out[:, lanes], cos_ref[...], sin_ref[...], 1).astype(bf16)

    @pl.when(step < 2)
    def _():
        rotated(q_ref)

    @pl.when(step == 2)
    def _():
        rotated(kv_ref)

    @pl.when(step == 3)
    def _():
        kv_ref[...] = out.astype(bf16)


def project(x, gains, cosine, sine, weights, q_cols):
    rows, width = x.shape
    tile = q_cols // 2
    return pl.pallas_call(
        project_kernel,
        grid=(4,),
        in_specs=[
            whole(x.shape),
            whole(gains.shape),
            whole(cosine.shape),
            whole(sine.shape),
            pl.BlockSpec((width, tile), lambda j: (0, j)),
        ],
        out_specs=[
            pl.BlockSpec((rows, tile), lambda j: (0, jnp.minimum(j, 1))),
            pl.BlockSpec((rows, tile), lambda j: (0, jnp.maximum(j - 2, 0))),
            whole((rows, width)),
        ],
        out_shape=[
            jax.ShapeDtypeStruct((rows, q_cols), bf16),
            jax.ShapeDtypeStruct((rows, q_cols), bf16),
            jax.ShapeDtypeStruct((rows, width), bf16),
        ],
        compiler_params=params(40),
        cost_estimate=cost(2 * rows * width * 4 * tile, 2 * width * 4 * tile),
        name="project",
    )(x, gains, cosine, sine, weights)


MESH = pl.DeviceIdType.MESH


def forward_kernel(
    query_shard, key_shard, value_shard, gain_shard, out_shard, gate_shard, up_shard, down_shard,
    x_ref, frequency_ref, qi_ref,
    full_ref, gate_ref, up_ref, down_ref, q_out, kv_out, normed_out, gain_out, low_out, att_out, sum_out,
    middle_out, mid_normed_out, cos_out, sin_out, ki_out,
    q_ref, kv_ref, normed_ref, gain_ref, low_ref, att_ref, sum_ref,
    middle_ref, mid_normed_ref, cos_ref, sin_ref, ki_ref,
    branch_ref, other_ref, w_ref, qt_ref, top_ref, total_ref,
    z_send, z_recv, y_send, y_recv, c_send, c_recv, k_send, k_recv, x_send, x_recv, local, save_sem,
):
    ctxs = lax.axis_size("ctx")
    dp, ctx, tp = lax.axis_index("dp"), lax.axis_index("ctx"), lax.axis_index("tp")
    far, core = (lax.rem(dp + 2, 4), ctx, tp), (dp + 1 - 2 * lax.rem(dp, 2), ctx, tp)
    after, before = (dp, lax.rem(ctx + 1, ctxs), tp), (dp, lax.rem(ctx + ctxs - 1, ctxs), tp)
    across = (dp, ctx, 1 - tp)
    piece = query_shard.shape[0]
    mine = pl.ds(pl.multiple_of((dp * ctxs + ctx) * piece, piece), piece)
    packs, column = [], 0
    for j, part in enumerate((query_shard, key_shard, value_shard, gain_shard, out_shard)):
        target = w_ref.at[mine, pl.ds(column, part.shape[1])]
        packs.append(pltpu.make_async_copy(part, target, local.at[5 + j]))
        packs[-1].start()
        column += part.shape[1]
    barrier = pltpu.get_barrier_semaphore()
    for device in (after, before, far, core, across):
        pl.semaphore_signal(barrier, inc=1, device_id=device, device_id_type=MESH)
    pl.semaphore_wait(barrier, 5)
    shards = (w_ref.at[mine], gate_shard, up_shard, down_shard)
    wholes = (w_ref, gate_ref, up_ref, down_ref)
    last = ctxs - 1


    def place(group, pair, steps):
        owner = pair * ctxs + lax.rem(ctx - steps + ctxs, ctxs)
        return wholes[group].at[pl.ds(pl.multiple_of(owner * piece, piece), piece)]

    def source(group, steps):
        return place(group, dp, steps) if steps else shards[group]

    def remote(source, target, device, sent, got):
        return pltpu.make_async_remote_copy(source, target, device_id=device, device_id_type=MESH, send_sem=sent, recv_sem=got)

    def ring(group, s):
        return remote(
            source(group, s), place(group, dp, s), after, z_send.at[group, s], z_recv.at[group, s]
        )

    def over(group, s):
        return remote(
            source(group, s), place(group, dp, s), far, y_send.at[group, s], y_recv.at[group, s]
        )

    def aside(group, s):
        return remote(
            source(group, s), place(group, dp, s), core, c_send.at[group, s], c_recv.at[group, s]
        )

    def aside_far(group, s):
        there = place(group, far[0], s)
        return remote(
            there, there, core, c_send.at[group, ctxs + s], c_recv.at[group, ctxs + s]
        )

    def own_copy(group):
        return pltpu.make_async_copy(shards[group], place(group, dp, 0), local.at[group])

    def begin(group):
        over(group, 0).start()
        aside(group, 0).start()
        if group:
            own_copy(group).start()

    def along(group, s):
        ring(group, s - 1).wait_recv()
        if s < last:
            ring(group, s).start()
        over(group, s).start()
        aside(group, s).start()

    def came_over(group, s):
        over(group, s).wait_recv()
        aside_far(group, s).start()

    def gathered(group):
        if group:
            own_copy(group).wait()
        for s in range(ctxs):
            aside(group, s).wait_recv()
            aside_far(group, s).wait_recv()

    saves = []

    def save(*pairs):
        for have, out in pairs:
            saves.append(pltpu.make_async_copy(have, out, save_sem.at[len(saves)]))
            saves[-1].start()

    first, gate, up, down = range(4)
    for copy in packs:
        copy.wait()
    ring(first, 0).start()
    begin(first)
    columns = qi_ref[...].astype(f32).T
    turn = (columns[:, 0:1] - columns[:, 1:2]) * frequency_ref[...]
    cos_ref[...] = jnp.cos(turn)
    sin_ref[...] = jnp.sin(turn)
    for k in range(ctxs):
        ki_ref[k] = columns[:, 2 + k : 3 + k].astype(jnp.int32)
    x = x_ref[...].astype(f32)
    unit = x * lax.rsqrt(jnp.mean(x * x, axis=1, keepdims=True) + epsilon)
    for s in range(1, ctxs):
        along(first, s)
        came_over(first, s - 1)
    ring(gate, 0).start()
    begin(gate)
    came_over(first, last)
    begin(up)
    gathered(first)
    full = pltpu.make_async_copy(w_ref, full_ref, local.at[4])
    full.start()
    along(gate, 1)

    q_cols = q_ref.shape[1]
    tile = q_cols // 2
    groups = kv_ref.shape[2] // (2 * HEAD_SIZE)
    ratio = q_cols // (groups * HEAD_SIZE)
    gains = w_ref[:, 2 * q_cols : 2 * q_cols + LANES].astype(f32).T[:8]
    gain_ref[...] = gains
    normed_ref[...] = (unit * gains[0:1]).astype(bf16)
    save((gain_ref, gain_out), (normed_ref, normed_out), (cos_ref, cos_out), (sin_ref, sin_out), (ki_ref, ki_out))

    def product(step):
        return dot(normed_ref[...], w_ref[:, step * tile : (step + 1) * tile], NN)

    def rotated(out, store):
        for h in range(tile // HEAD_SIZE):
            lanes = slice(h * HEAD_SIZE, (h + 1) * HEAD_SIZE)
            store(lanes, turned(out[:, lanes], cos_ref[...], sin_ref[...], 1).astype(bf16))

    def key_store(lanes, value):
        kv_ref[0, :, lanes] = value

    rotated(product(2), key_store)
    kv_ref[0, :, tile:] = product(3).astype(bf16)

    def kv_copy(s):
        return remote(kv_ref.at[s], kv_ref.at[s + 1], after, k_send.at[s], k_recv.at[s])

    kv_copy(0).start()
    ring(up, 0).start()
    begin(down)
    for step in range(2):

        def query_store(lanes, value):
            q_ref[:, step * tile + lanes.start : step * tile + lanes.stop] = value

        rotated(product(step), query_store)

    def attention(k):
        dense_piece(k, kv_ref, qi_ref, ki_ref, groups, ratio, qt_ref, top_ref, total_ref, att_ref)

    dense_begin(q_ref, groups, ratio, qt_ref, top_ref, total_ref, att_ref)
    along(gate, 2)
    came_over(gate, 0)
    waits = [
        [lambda: along(up, 1), lambda: along(gate, last), lambda: came_over(gate, 1), lambda: came_over(up, 0)],
        [lambda: ring(down, 0).start(), lambda: came_over(down, 0), lambda: came_over(gate, 2)],
        [lambda: along(up, 2)],
    ]

    def attention_step(k, unused):
        for s in range(1, ctxs):

            @pl.when(k == s)
            def _(s=s):
                kv_copy(s - 1).wait_recv()
                if s < last:
                    kv_copy(s).start()
                for step in waits[s - 1] if s - 1 < len(waits) else []:
                    step()

        attention(k)
        return unused

    lax.fori_loop(0, ctxs, attention_step, 0)
    save((q_ref, q_out), (kv_ref, kv_out))
    dense_end(groups, ratio, top_ref, total_ref, att_ref, sum_ref, low_ref)
    save((low_ref, low_out), (att_ref, att_out), (sum_ref, sum_out))
    branch_ref[...] = dot(low_ref[...], w_ref[:, 2 * q_cols + LANES :], NT).astype(bf16)
    exchange = remote(branch_ref, other_ref, across, x_send.at[0], x_recv.at[0])
    exchange.start()

    along(down, 1)
    came_over(gate, last)
    came_over(up, 1)
    along(up, last)
    came_over(up, 2)
    along(down, 2)
    came_over(down, 1)
    came_over(up, last)
    along(down, last)
    came_over(down, 2)
    exchange.wait_recv()
    few = 64

    def middle_rows(i, unused):
        here = pl.ds(pl.multiple_of(i * few, few), few)
        middle = x_ref[here, :].astype(f32) + (
            branch_ref[here, :].astype(f32) + other_ref[here, :].astype(f32)
        )
        middle_ref[here, :] = middle
        scale = lax.rsqrt(jnp.mean(middle * middle, axis=1, keepdims=True) + epsilon)
        mid_normed_ref[here, :] = (middle * scale * gain_ref[1:2, :]).astype(bf16)
        return unused

    lax.fori_loop(0, x_ref.shape[0] // few, middle_rows, 0)
    save((middle_ref, middle_out), (mid_normed_ref, mid_normed_out))
    came_over(down, last)
    for group in (gate, up, down):
        gathered(group)
    for group in range(4):
        for s in range(ctxs):
            if s < last:
                ring(group, s).wait_send()
            over(group, s).wait_send()
            aside(group, s).wait_send()
            aside_far(group, s).wait_send()
    for s in range(last):
        kv_copy(s).wait_send()
    exchange.wait_send()
    full.wait()
    for copy in saves:
        copy.wait()


def forward_all(packed, gate, up, down, x, frequency, qi, q_cols, ctxs):
    rows, width = x.shape
    columns, hidden = sum(part.shape[1] for part in packed), gate.shape[1]
    groups = q_cols // 2 // HEAD_SIZE
    tiles, lanes = dense_shapes(rows, groups, 2)
    vmem, hbm = pl.BlockSpec(memory_space=pltpu.VMEM), pl.BlockSpec(memory_space=pl.ANY)
    sems = lambda *n: pltpu.SemaphoreType.DMA(n)
    shape = jax.ShapeDtypeStruct
    full = shape((rows, width), bf16)
    kept = [
        shape((rows, q_cols), bf16),
        shape((ctxs, rows, q_cols), bf16),
        full,
        shape((8, width), f32),
        shape((rows, q_cols), bf16),
        shape((tiles, HEAD_SIZE, lanes), f32),
        shape((tiles, 1, lanes), f32),
        shape((rows, width), f32),
        full,
        shape((rows, HALF), f32),
        shape((rows, HALF), f32),
        shape((ctxs, rows, 1), jnp.int32),
    ]
    return pl.pallas_call(
        forward_kernel,
        in_specs=[hbm] * (len(packed) + 3) + [vmem] * 3,
        out_specs=[hbm] * 16,
        out_shape=[
            shape((width, columns), bf16),
            shape((width, hidden), bf16),
            shape((width, hidden), bf16),
            shape((width, hidden), bf16),
        ]
        + kept,
        scratch_shapes=[pltpu.VMEM(part.shape, part.dtype) for part in kept]
        + [
            pltpu.VMEM((rows, width), bf16),
            pltpu.VMEM((rows, width), bf16),
            pltpu.VMEM((width, columns), bf16),
            pltpu.VMEM((tiles, HEAD_SIZE, lanes), bf16),
            pltpu.VMEM((tiles, 1, lanes), f32),
            pltpu.VMEM((tiles, 1, lanes), f32),
        ]
        + [sems(4, ctxs - 1)] * 2
        + [sems(4, ctxs)] * 2
        + [sems(4, 2 * ctxs)] * 2
        + [sems(ctxs - 1)] * 2
        + [sems(1)] * 2
        + [sems(5 + len(packed)), sems(len(kept))],
        compiler_params=pltpu.CompilerParams(
            vmem_limit_bytes=56 * MIB, collective_id=0, has_side_effects=True
        ),
        cost_estimate=cost(1e10, 1e8),
        name="forward_all",
    )(*packed, gate, up, down, x, frequency, qi)


def gather_stream(order, ctx, pieces, k_ref, v_ref):
    count, groups = len(pieces), k_ref.shape[0]
    width = groups * HEAD_SIZE

    def fill(i, unused):
        source = pl.ds(pl.multiple_of(i * BLOCK, BLOCK), BLOCK)
        for k, piece in enumerate(pieces):
            block = i * count + order[i, lax.rem(ctx - k + count, count)]
            target = pl.ds(pl.multiple_of(block * BLOCK, BLOCK), BLOCK)
            for g in range(groups):
                lanes = slice(g * HEAD_SIZE, (g + 1) * HEAD_SIZE)
                k_ref[g, target, :] = piece[source, lanes]
                v_ref[g, target, :] = piece[
                    source, width + g * HEAD_SIZE : width + (g + 1) * HEAD_SIZE
                ]
        return unused

    lax.fori_loop(0, order.shape[0], fill, 0)


def reach(starts, first):
    low = jnp.int32(0)
    for j in range(starts.shape[0]):
        low = jnp.where(starts[j] <= first, starts[j], low)
    return low


def row_limits(starts, first, lanes):
    row = first + lax.rem(lax.broadcasted_iota(jnp.int32, (1, lanes), 1), BLOCK)
    low = jnp.zeros((1, lanes), jnp.int32)
    for j in range(starts.shape[0]):
        low = jnp.where(row >= starts[j], starts[j], low)
    return row, low


def stacked(ref, rows, group, ratio):
    return jnp.concatenate(
        [
            ref[rows, (group * ratio + h) * HEAD_SIZE : (group * ratio + h + 1) * HEAD_SIZE]
            for h in range(ratio)
        ],
        axis=0,
    )


def attend_kernel(count, order, starts, place, q_ref, *refs):
    pieces = refs[:count]
    low_ref, att_ref, sum_ref, k_ref, v_ref = refs[count:]
    groups = k_ref.shape[0]
    ratio = q_ref.shape[1] // (groups * HEAD_SIZE)
    lanes = ratio * BLOCK
    ctx = place[0]
    gather_stream(order, ctx, pieces, k_ref, v_ref)

    def one(i, unused):
        first = (i * count + order[i, ctx]) * BLOCK
        row, low = row_limits(starts, first, lanes)
        begin = reach(starts, first) // SPAN
        end = (first + BLOCK - 1) // SPAN + 1
        rows = pl.ds(pl.multiple_of(i * BLOCK, BLOCK), BLOCK)
        queries = [stacked(q_ref, rows, g, ratio) for g in range(groups)]

        def chunk(c, carry):
            keys = pl.ds(pl.multiple_of(c * SPAN, SPAN), SPAN)
            index = c * SPAN + lax.broadcasted_iota(jnp.int32, (SPAN, lanes), 0)
            allowed = (index <= row) & (index >= low)
            new = []
            for g in range(groups):
                top, total, out = carry[g]
                raw = dot(k_ref[g, keys, :], queries[g], NT) * SCALE2
                raw = jnp.where(allowed, raw, masked_score)
                new_top = jnp.maximum(top, jnp.max(raw, axis=0, keepdims=True))
                weights = jnp.where(allowed, jnp.exp2(raw - new_top), 0.0)
                back = jnp.exp2(top - new_top)
                total = total * back + jnp.sum(weights, axis=0, keepdims=True)
                out = out * back + dot(v_ref[g, keys, :], weights.astype(bf16), TN)
                new.append((new_top, total, out))
            return tuple(new)

        blank = (
            jnp.full((1, lanes), masked_score, f32),
            jnp.zeros((1, lanes), f32),
            jnp.zeros((HEAD_SIZE, lanes), f32),
        )
        result = lax.fori_loop(begin, end, chunk, (blank,) * groups)
        for g in range(groups):
            top, total, out = result[g]
            out = out / total
            att_ref[i * groups + g] = out
            sum_ref[pl.ds(i * groups + g, 1), :] = top + jnp.log2(total)
            flat = out.T.astype(bf16)
            for h in range(ratio):
                head = g * ratio + h
                low_ref[rows, head * HEAD_SIZE : (head + 1) * HEAD_SIZE] = flat[
                    h * BLOCK : (h + 1) * BLOCK
                ]
        return unused

    lax.fori_loop(0, order.shape[0], one, 0)


def attend(order, starts, place, queries, pieces):
    count, rows = len(pieces), queries.shape[0]
    groups = pieces[0].shape[1] // (2 * HEAD_SIZE)
    ratio = queries.shape[1] // (groups * HEAD_SIZE)
    rounds, lanes = order.shape[0], ratio * BLOCK
    return pl.pallas_call(
        functools.partial(attend_kernel, count),
        in_specs=[SCALARS] * 3 + [pl.BlockSpec(memory_space=pltpu.VMEM)] * (1 + count),
        out_specs=[pl.BlockSpec(memory_space=pltpu.VMEM)] * 3,
        out_shape=[
            jax.ShapeDtypeStruct(queries.shape, bf16),
            jax.ShapeDtypeStruct((rounds * groups, HEAD_SIZE, lanes), f32),
            jax.ShapeDtypeStruct((rounds * groups, lanes), f32),
        ],
        scratch_shapes=[pltpu.VMEM((groups, count * rows, HEAD_SIZE), bf16)] * 2,
        compiler_params=params(40),
        cost_estimate=cost(8e9, 1e7),
        name="attend",
    )(order, starts, place, queries, *pieces)


def attend_back_kernel(count, order, starts, place, q_ref, d_ref, att_ref, sum_ref, cos_ref, sin_ref, *refs):
    pieces = refs[:count]
    qc_ref = refs[count]
    outs = refs[count + 1 : 2 * count + 1]
    k_ref, v_ref, dk_ref, dv_ref = refs[2 * count + 1 :]
    groups = k_ref.shape[0]
    ratio = q_ref.shape[1] // (groups * HEAD_SIZE)
    lanes = ratio * BLOCK
    width = groups * HEAD_SIZE
    ctx = place[0]
    gather_stream(order, ctx, pieces, k_ref, v_ref)
    dk_ref[...] = jnp.zeros_like(dk_ref)
    dv_ref[...] = jnp.zeros_like(dv_ref)

    def one(i, unused):
        first = (i * count + order[i, ctx]) * BLOCK
        row, low = row_limits(starts, first, lanes)
        begin = reach(starts, first) // SPAN
        end = (first + BLOCK - 1) // SPAN + 1
        rows = pl.ds(pl.multiple_of(i * BLOCK, BLOCK), BLOCK)
        queries = [stacked(q_ref, rows, g, ratio) for g in range(groups)]
        slopes = [stacked(d_ref, rows, g, ratio) for g in range(groups)]
        sums, deltas = [], []
        for g in range(groups):
            sums.append(sum_ref[pl.ds(i * groups + g, 1), :])
            across = slopes[g].astype(f32).T
            deltas.append(jnp.sum(across * att_ref[i * groups + g], axis=0, keepdims=True))

        def chunk(c, carry):
            keys = pl.ds(pl.multiple_of(c * SPAN, SPAN), SPAN)
            index = c * SPAN + lax.broadcasted_iota(jnp.int32, (SPAN, lanes), 0)
            allowed = (index <= row) & (index >= low)
            new = []
            for g in range(groups):
                key, value = k_ref[g, keys, :], v_ref[g, keys, :]
                raw = dot(key, queries[g], NT) * SCALE2
                share = jnp.where(allowed, jnp.exp2(jnp.minimum(raw - sums[g], 0.0)), 0.0)
                back_share = dot(value, slopes[g], NT)
                back = (share * (back_share - deltas[g])).astype(bf16)
                dv_ref[g, keys, :] += dot(share.astype(bf16), slopes[g], NN)
                dk_ref[g, keys, :] += dot(back, queries[g], NN)
                new.append(carry[g] + dot(key, back, TN))
            return tuple(new)

        blank = jnp.zeros((HEAD_SIZE, lanes), f32)
        result = lax.fori_loop(begin, end, chunk, (blank,) * groups)
        cosine, sine = cos_ref[rows, :], sin_ref[rows, :]
        for g in range(groups):
            flat = result[g].T * SCALE
            for h in range(ratio):
                head = g * ratio + h
                qc_ref[rows, head * HEAD_SIZE : (head + 1) * HEAD_SIZE] = turned(
                    flat[h * BLOCK : (h + 1) * BLOCK], cosine, sine, -1
                ).astype(bf16)
        return unused

    lax.fori_loop(0, order.shape[0], one, 0)

    def spread(i, unused):
        target = pl.ds(pl.multiple_of(i * BLOCK, BLOCK), BLOCK)
        for k, out in enumerate(outs):
            block = i * count + order[i, lax.rem(ctx - k + count, count)]
            source = pl.ds(pl.multiple_of(block * BLOCK, BLOCK), BLOCK)
            for g in range(groups):
                out[target, g * HEAD_SIZE : (g + 1) * HEAD_SIZE] = (
                    dk_ref[g, source, :] * SCALE
                ).astype(bf16)
                out[target, width + g * HEAD_SIZE : width + (g + 1) * HEAD_SIZE] = dv_ref[
                    g, source, :
                ].astype(bf16)
        return unused

    lax.fori_loop(0, order.shape[0], spread, 0)


def attend_back(order, starts, place, queries, slopes, att, sums, cosine, sine, pieces):
    count, rows = len(pieces), queries.shape[0]
    groups = pieces[0].shape[1] // (2 * HEAD_SIZE)
    keys = (groups, count * rows, HEAD_SIZE)
    return pl.pallas_call(
        functools.partial(attend_back_kernel, count),
        in_specs=[SCALARS] * 3 + [pl.BlockSpec(memory_space=pltpu.VMEM)] * (6 + count),
        out_specs=[pl.BlockSpec(memory_space=pltpu.VMEM)] * (1 + count),
        out_shape=[jax.ShapeDtypeStruct(queries.shape, bf16)]
        + [jax.ShapeDtypeStruct(pieces[0].shape, bf16)] * count,
        scratch_shapes=[pltpu.VMEM(keys, bf16)] * 2 + [pltpu.VMEM(keys, f32)] * 2,
        compiler_params=params(56),
        cost_estimate=cost(16e9, 2e7),
        name="attend_back",
    )(order, starts, place, queries, slopes, att, sums, cosine, sine, *pieces)


SIDE = 256


def tile_bias(qi_ref, ki_ref, k, q_tile, k_tile, ratio):
    rows = slice(q_tile * SIDE, (q_tile + 1) * SIDE)
    keys = ki_ref[k, k_tile * SIDE : (k_tile + 1) * SIDE, :]
    allowed = (keys <= qi_ref[0:1, rows]) & (keys >= qi_ref[1:2, rows])
    bias = jnp.where(allowed, 0.0, masked_score)
    return jnp.concatenate([bias] * ratio, axis=1)


def flat_heads(ref, q_tile, group, ratio):
    return jnp.concatenate(
        [
            ref[
                q_tile * SIDE : (q_tile + 1) * SIDE,
                (group * ratio + h) * HEAD_SIZE : (group * ratio + h + 1) * HEAD_SIZE,
            ]
            for h in range(ratio)
        ],
        axis=0,
    )


def head_lanes(g, offset=0):
    return slice(offset + g * HEAD_SIZE, offset + (g + 1) * HEAD_SIZE)


def dense_begin(q_ref, groups, ratio, qt_ref, top_ref, total_ref, att_ref):
    for q_tile in range(q_ref.shape[0] // SIDE):
        for g in range(groups):
            flat = flat_heads(q_ref, q_tile, g, ratio)
            qt_ref[q_tile * groups + g] = flat.astype(f32).T.astype(bf16)
    top_ref[...] = jnp.full(top_ref.shape, masked_score, f32)
    total_ref[...] = jnp.zeros(total_ref.shape, f32)
    att_ref[...] = jnp.zeros(att_ref.shape, f32)


def dense_piece(k, kv_ref, qi_ref, ki_ref, groups, ratio, qt_ref, top_ref, total_ref, att_ref):
    width = groups * HEAD_SIZE
    for q_tile in range(qi_ref.shape[1] // SIDE):
        for k_tile in range(q_tile, -1, -1):
            bias = tile_bias(qi_ref, ki_ref, k, q_tile, k_tile, ratio)
            rows = slice(k_tile * SIDE, (k_tile + 1) * SIDE)
            for g in range(groups):
                i = q_tile * groups + g
                raw = dot(kv_ref[k, rows, head_lanes(g)], qt_ref[i], NN) * SCALE2 + bias
                top = top_ref[i]
                new_top = jnp.maximum(top, jnp.max(raw, axis=0, keepdims=True))
                weights = jnp.exp2(raw - new_top)
                back = jnp.exp2(top - new_top)
                top_ref[i] = new_top
                total_ref[i] = total_ref[i] * back + jnp.sum(weights, axis=0, keepdims=True)
                att_ref[i] = att_ref[i] * back + dot(
                    kv_ref[k, rows, head_lanes(g, width)], weights.astype(bf16), TN
                )


def dense_end(groups, ratio, top_ref, total_ref, att_ref, sum_ref, low_ref):
    for i in range(att_ref.shape[0]):
        q_tile, g = divmod(i, groups)
        out = att_ref[i] * (1.0 / total_ref[i])
        att_ref[i] = out
        sum_ref[i] = top_ref[i] + jnp.log2(total_ref[i])
        flat = out.T.astype(bf16)
        for h in range(ratio):
            low_ref[q_tile * SIDE : (q_tile + 1) * SIDE, head_lanes(g * ratio + h)] = flat[
                h * SIDE : (h + 1) * SIDE
            ]


def dense_shapes(rows, groups, ratio):
    tiles = rows // SIDE * groups
    return tiles, ratio * SIDE


FEED_TILES = 12
TILES = 17
EARLY = 4
SLOTS = 6


def back_kernel(
    part_hbm, feed_hbm, cot_hbm, middle_hbm, gain_ref, act_hbm, mid_normed_hbm, x_hbm, normed_hbm,
    low_hbm, q_hbm, kv_hbm, att_hbm, sum_hbm, qi_hbm, ki_hbm, cos_hbm, sin_hbm, weight_hbm,
    feed_other, back_middle, part2_other, result_ref, token_ref, grads_ref, held_hbm, far_hbm,
    low_ref, q_ref, kv_ref, att_ref, sum_ref, qi_ref, ki_ref, cos_ref, sin_ref,
    lhs, mid, part, part_other, w_out, w_in, rhs, q2, q2t, d2, d2t, delta, bias_ref, dq_ref,
    kv_sent, kv_got, cot, gain_rows, gain_other, gain_columns,
    p_send, p_keep, c_got, s_one, own, y_got, z_got,
    load_sem, act_sem, x_send, x_recv, c_send, c_recv, c_free, held_sem, y_send, y_recv, own_sem,
    z_send, z_recv, k_send, k_recv,
):
    ctxs = lax.axis_size("ctx")
    dp, ctx, tp = lax.axis_index("dp"), lax.axis_index("ctx"), lax.axis_index("tp")
    pair_at, core_at = dp // 2, lax.rem(dp, 2)
    far, core = (lax.rem(dp + 2, 4), ctx, tp), (dp + 1 - 2 * core_at, ctx, tp)
    after, before = (dp, lax.rem(ctx + 1, ctxs), tp), (dp, lax.rem(ctx + ctxs - 1, ctxs), tp)
    beside, opposite = (dp, ctx + 1 - 2 * lax.rem(ctx, 2), tp), (dp, lax.rem(ctx + 2, 4), tp)
    across = (dp, ctx, 1 - tp)
    rows, width = mid.shape
    section = width // 4
    piece = section // ctxs
    groups = kv_ref.shape[2] // (2 * HEAD_SIZE)
    kv_width = groups * HEAD_SIZE
    ratio = q_ref.shape[1] // kv_width
    q_cols = q_ref.shape[1]

    barrier = pltpu.get_barrier_semaphore()
    for device in (after, before, opposite, far, core, across):
        pl.semaphore_signal(barrier, inc=1, device_id=device, device_id_type=MESH)
    pl.semaphore_wait(barrier, 6)

    def remote(source, target, device, sent, got):
        return pltpu.make_async_remote_copy(source, target, sent, got, device, MESH)

    def load(source, target, index):
        return pltpu.make_async_copy(source, target, load_sem.at[index])


    def product(t, lhs_of, rhs_of):
        slot = lax.rem(t, 2)

        @pl.when(t >= 2)
        def _():
            core_copy(t - 2).wait_send()

        for c, out in ((1, p_send), (0, p_keep)):
            for y in range(2):
                there = lax.rem(pair_at + y + 1, 2) * 2 + lax.rem(core_at + c, 2)
                start = pl.multiple_of(there * section, LANES)
                result = rhs_of(start, lhs_of(pl.ds(start, section)))
                for z in range(ctxs):
                    odd, half = lax.rem(z + ctx, 2), lax.rem(z // 2 + ctx // 2, 2)
                    place = 2 * (1 - odd) + odd * half + (1 - odd) * (1 - half)
                    target = pl.ds(pl.multiple_of(y * section + place * piece, piece), piece)
                    out[slot, target, :] = result[z * piece : (z + 1) * piece]

        @pl.when(t >= 4)
        def _():
            pl.semaphore_wait(c_free, 1)

        core_copy(t).start()

    def core_copy(t):
        return remote(
            p_send.at[lax.rem(t, 2)], c_got.at[lax.rem(t, 4)], core, c_send.at[t], c_recv.at[t]
        )

    def held_copy(t):
        return pltpu.make_async_copy(s_one.at[lax.rem(t, 2)], held_hbm.at[t], held_sem.at[t])

    def meet_core(t):
        core_copy(t).wait_recv()
        slot, got = lax.rem(t, 2), lax.rem(t, 4)

        def add(i, unused):
            part_rows = pl.ds(pl.multiple_of(i * piece, piece), piece)
            total = p_keep[slot, part_rows, :].astype(f32) + c_got[got, part_rows, :].astype(f32)
            s_one[slot, part_rows, :] = total.astype(bf16)
            return unused

        lax.fori_loop(0, 2 * section // piece, add, 0)

        @pl.when(t + 4 < TILES)
        def _():
            pl.semaphore_signal(c_free, inc=1, device_id=core, device_id_type=MESH)

        held_copy(t).start()

    def far_copy(t):
        return remote(
            held_hbm.at[t, pl.ds(0, section)], far_hbm.at[t], far, y_send.at[t], y_recv.at[t]
        )

    def send_far(t):
        held_copy(t).wait()
        far_copy(t).start()

    def own_copy(t):
        return pltpu.make_async_copy(
            held_hbm.at[t, pl.ds(section, section)], own.at[lax.rem(t, SLOTS)], own_sem.at[t, 0]
        )

    def got_copy(t):
        return pltpu.make_async_copy(far_hbm.at[t], y_got.at[lax.rem(t, 2)], own_sem.at[t, 1])


    def near_copy(t):
        return remote(
            own.at[lax.rem(t, SLOTS), pl.ds(0, 2 * piece)],
            z_got.at[t, pl.ds(0, 2 * piece)], beside, z_send.at[t, 0], z_recv.at[t, 0],
        )

    def last_copy(t):
        return remote(
            own.at[lax.rem(t, SLOTS), pl.ds(2 * piece, piece)],
            z_got.at[t, pl.ds(2 * piece, piece)], opposite, z_send.at[t, 1], z_recv.at[t, 1],
        )

    def meet_near(t):
        near_copy(t).wait_recv()
        near_copy(t).wait_send()
        slot = lax.rem(t, SLOTS)
        for target, came in ((2, 1), (3, 0)):
            here = pl.ds(target * piece, piece)
            total = own[slot, here, :].astype(f32) + z_got[t, came * piece : (came + 1) * piece].astype(f32)
            own[slot, here, :] = total.astype(bf16)
        last_copy(t).start()

    def meet_last(t):
        last_copy(t).wait_recv()
        last_copy(t).wait_send()
        mine = own[lax.rem(t, SLOTS), 3 * piece :, :].astype(f32)
        grads_ref[t] = mine + z_got[t, 2 * piece :].astype(f32)

    def fetch(t):
        far_copy(t).wait_recv()
        own_copy(t).start()
        got_copy(t).start()

    def meet_far(t):
        own_copy(t).wait()
        got_copy(t).wait()
        slot, got = lax.rem(t, SLOTS), lax.rem(t, 2)
        for z in range(ctxs):
            target = pl.ds(z * piece, piece)
            total = own[slot, target, :].astype(f32) + y_got[got, target, :].astype(f32)
            own[slot, target, :] = total.astype(bf16)
        near_copy(t).start()

    def when(test, step, t):
        @pl.when(test)
        def _():
            step(t)

    def tick(n):
        when((n - 1 > EARLY) & (n - 1 < TILES), meet_far, n - 1)
        when((n - 3 >= EARLY) & (n - 3 < TILES), meet_near, n - 3)
        when((n - 5 >= EARLY - 1) & (n - 5 < TILES), meet_last, n - 5)
        when(n < TILES, fetch, n)


    part_copy = remote(part_hbm, part_other, across, x_send.at[0], x_recv.at[0])
    part_copy.start()
    feed_copy = remote(feed_hbm, feed_other, across, x_send.at[1], x_recv.at[1])
    feed_copy.start()

    def act_copy(t):
        columns = pl.ds(pl.multiple_of(lax.rem(t, 4) * TILE, TILE), TILE)
        return pltpu.make_async_copy(
            act_hbm.at[t // 4, :, columns], rhs.at[lax.rem(t, 2)], act_sem.at[t]
        )

    loads = [
        load(mid_normed_hbm, lhs.at[0], 0),
        load(cot_hbm, lhs.at[1], 1),
        load(part_hbm, part, 2),
        load(middle_hbm, mid, 3),
        load(weight_hbm.at[:, pl.ds(2 * q_cols + LANES, q_cols)], w_out, 4),
        load(weight_hbm.at[:, pl.ds(0, 2 * q_cols)], w_in, 5),
    ]
    later = (
        (low_hbm, low_ref), (q_hbm, q_ref), (kv_hbm, kv_ref), (att_hbm, att_ref), (sum_hbm, sum_ref),
        (qi_hbm, qi_ref), (ki_hbm, ki_ref), (cos_hbm, cos_ref), (sin_hbm, sin_ref),
    )
    later = [load(have, into, 21 + j) for j, (have, into) in enumerate(later)]
    act_copy(0).start()
    for copy in loads + later:
        copy.start()
    loads[0].wait()
    loads[1].wait()

    def plain(t):
        def times(start, left):
            return dot(left, rhs[lax.rem(t, 2)], TN).astype(bf16)

        return times

    def feed_step(t, unused):
        act_copy(t).wait()

        @pl.when(t + 1 < FEED_TILES)
        def _():
            act_copy(t + 1).start()

        product(t, lambda lanes: lhs[t // 8, :, lanes], plain(t))

        @pl.when(t == 0)
        def _():
            meet_core(t)
            send_far(t)

        @pl.when(t >= 2)
        def _():
            meet_core(t - 1)

        @pl.when(t >= 3)
        def _():
            send_far(t - 2)

        n, turn = (t - 4) // 3, lax.rem(t, 3)
        when((t >= 4) & (turn == 1), fetch, n)
        when((t >= 7) & (turn == 1), meet_near, n - 1)
        when((t >= 4) & (turn == 2), meet_far, n)
        when((t >= 7) & (turn == 0), meet_last, n - 1)

        return unused

    lax.fori_loop(0, FEED_TILES, feed_step, 0)
    meet_core(FEED_TILES - 1)
    send_far(FEED_TILES - 2)
    send_far(FEED_TILES - 1)
    for copy in later:
        copy.wait()

    for q_tile in range(rows // SIDE):
        for g in range(groups):
            flat = flat_heads(q_ref, q_tile, g, ratio)
            q2[q_tile * groups + g] = flat
            q2t[q_tile * groups + g] = flat.astype(f32).T.astype(bf16)
    dq_ref[...] = jnp.zeros(dq_ref.shape, f32)
    gain_rows[...] = jnp.zeros(gain_rows.shape, f32)


    loads[2].wait()
    loads[3].wait()
    t_1, t_2, t_3, t_4 = (jnp.int32(j) for j in range(1, 5))
    fetch(t_3)
    meet_last(t_1)
    meet_near(t_2)
    part_copy.wait_recv()
    few = 64

    def norm_rows(i, unused):
        here = pl.ds(pl.multiple_of(i * few, few), few)
        field = mid[here, :]
        scale = lax.rsqrt(jnp.mean(field * field, axis=1, keepdims=True) + epsilon)
        unit = field * scale
        back = part[here, :].astype(f32) + part_other[here, :].astype(f32)
        gain_rows[1:2, :] += jnp.sum(back * unit, axis=0, keepdims=True)
        inner = back * gain_ref[1:2, :]
        out = lhs[1, here, :].astype(f32) + scale * (
            inner - unit * jnp.mean(inner * unit, axis=1, keepdims=True)
        )
        mid[here, :] = out
        lhs[0, here, :] = out.astype(bf16)
        return unused

    lax.fori_loop(0, rows // few, norm_rows, 0)
    meet_far(t_3)
    meet_last(t_2)
    fetch(t_4)
    middle_copy = load(mid, back_middle, 6)
    middle_copy.start()
    normed_copy = load(normed_hbm, lhs.at[1], 7)
    normed_copy.start()
    x_copy = load(x_hbm, part, 8)
    x_copy.start()
    loads[4].wait()
    cot[:, :q_cols] = dot(lhs[0], w_out[...], NN).astype(bf16)
    meet_far(t_4)
    meet_near(t_3)
    for q_tile in range(rows // SIDE):
        for g in range(groups):
            i = q_tile * groups + g
            flat = flat_heads(cot, q_tile, g, ratio)
            turned_flat = flat.astype(f32).T
            d2[i] = flat
            d2t[i] = turned_flat.astype(bf16)
            delta[i] = jnp.sum(turned_flat * att_ref[i], axis=0, keepdims=True)

    t_out = jnp.int32(FEED_TILES)
    product(
        t_out, lambda lanes: lhs[0, :, lanes], lambda start, left: dot(left, low_ref[:, :TILE], TN).astype(bf16)
    )


    def kv_copy(s):
        return remote(kv_sent.at[s], kv_got.at[s], after, k_send.at[s], k_recv.at[s])

    def back_piece(s, unused):
        k = lax.rem(s + 1, ctxs)
        pairs = [(q, kk) for kk in range(rows // SIDE) for q in range(kk, rows // SIDE)]
        for index, (q_tile, k_tile) in enumerate(pairs):
            bias_ref[index] = tile_bias(qi_ref, ki_ref, k, q_tile, k_tile, ratio)
        sums = []
        for k_tile in range(rows // SIDE):
            here = slice(k_tile * SIDE, (k_tile + 1) * SIDE)
            for g in range(groups):
                key, value = kv_ref[k, here, head_lanes(g)], kv_ref[k, here, head_lanes(g, kv_width)]
                d_key = d_value = None
                for index, (q_tile, which) in enumerate(pairs):
                    if which != k_tile:
                        continue
                    i = q_tile * groups + g
                    raw = dot(key, q2t[i], NN) * SCALE2 + bias_ref[index]
                    share = jnp.exp2(raw - sum_ref[i])
                    back_share = dot(value, d2t[i], NN)
                    back = (share * (back_share - delta[i])).astype(bf16)
                    one_value = dot(share.astype(bf16), d2[i], NN)
                    one_key = dot(back, q2[i], NN)
                    d_value = one_value if d_value is None else d_value + one_value
                    d_key = one_key if d_key is None else d_key + one_key
                    dq_ref[i] += dot(key, back, TN)
                kv_sent[s, here, head_lanes(g)] = (d_key * SCALE).astype(bf16)
                kv_sent[s, here, head_lanes(g, kv_width)] = d_value.astype(bf16)

        @pl.when(s == 0)
        def _():
            kv_copy(0).start()
            meet_core(t_out)
            send_far(t_out)

        @pl.when((s == 0) | (s == 2))
        def _():
            tick(5 + s // 2)

        return unused

    lax.fori_loop(0, ctxs, back_piece, 0)

    def kv_pass(s):
        kv_copy(s).wait_recv()

        def add(i, unused):
            here = pl.ds(pl.multiple_of(i * few, few), few)
            total = kv_sent[s + 1, here, :].astype(f32) + kv_got[s, here, :].astype(f32)
            kv_sent[s + 1, here, :] = total.astype(bf16)
            return unused

        lax.fori_loop(0, rows // few, add, 0)
        if s + 1 < ctxs - 1:
            kv_copy(s + 1).start()


    kv_pass(0)
    tick(jnp.int32(7))
    for i in range(dq_ref.shape[0]):
        q_tile, g = divmod(i, groups)
        here = slice(q_tile * SIDE, (q_tile + 1) * SIDE)
        flat = dq_ref[i].T * SCALE
        for h in range(ratio):
            cot[here, head_lanes(g * ratio + h)] = turned(
                flat[h * SIDE : (h + 1) * SIDE], cos_ref[here, :], sin_ref[here, :], -1
            ).astype(bf16)
    normed_copy.wait()
    tail = q_cols - TILE
    t_query, t_both, t_key, t_last = (jnp.int32(FEED_TILES + 1 + j) for j in range(4))
    product(
        t_query, lambda lanes: lhs[1, :, lanes], lambda start, left: dot(left, cot[:, :TILE], TN).astype(bf16)
    )

    def times_both(start, left):
        from_query = dot(left, cot[:, TILE:q_cols], TN)
        from_output = dot(lhs[0, :, pl.ds(start, section)], low_ref[:, TILE:], TN)
        return jnp.concatenate([from_query, from_output], axis=1).astype(bf16)

    meet_core(t_query)
    product(t_both, lambda lanes: lhs[1, :, lanes], times_both)
    send_far(t_query)
    tick(jnp.int32(8))
    meet_core(t_both)
    send_far(t_both)
    feed_copy.wait_recv()
    here_copies = [load(feed_hbm, lhs.at[0], 9), load(feed_other, part_other, 10)]
    for copy in here_copies:
        copy.start()
    loads[5].wait()
    middle_copy.wait()
    for j in range(width // TILE):
        lanes = slice(j * TILE, (j + 1) * TILE)
        mid[:, lanes] = dot(cot[:, :q_cols], w_in[lanes, :q_cols], NT)
    kv_pass(1)
    tick(jnp.int32(9))


    for copy in here_copies:
        copy.wait()
    for half in range(rows // SIDE):
        here = slice(half * SIDE, (half + 1) * SIDE)
        pieces = [
            load(
                middle_hbm.at[pl.ds(half * SIDE, SIDE), pl.ds(j * TILE, TILE)],
                bias_ref.at[j], 11 + half * (width // TILE) + j,
            )
            for j in range(width // TILE)
        ]
        for copy in pieces:
            copy.start()
        for j, copy in enumerate(pieces):
            copy.wait()
            lanes = slice(j * TILE, (j + 1) * TILE)
            total = bias_ref[j] + lhs[0, here, lanes].astype(f32)
            lhs[0, here, lanes] = (total + part_other[here, lanes].astype(f32)).astype(bf16)
    result_copy = load(lhs.at[0], result_ref, 17)
    result_copy.start()
    tick(jnp.int32(10))

    kv_pass(2)
    for g in range(groups):
        cot[:, head_lanes(g, q_cols)] = turned(
            kv_sent[ctxs - 1, :, head_lanes(g)].astype(f32), cos_ref[...], sin_ref[...], -1
        ).astype(bf16)
    cot[:, q_cols + kv_width :] = kv_sent[ctxs - 1, :, kv_width:]
    x_copy.wait()
    x_rows = part[...].astype(f32)
    scale = lax.rsqrt(jnp.mean(x_rows * x_rows, axis=1, keepdims=True) + epsilon)
    for j in range(width // TILE):
        lanes = slice(j * TILE, (j + 1) * TILE)
        back = mid[:, lanes] + dot(cot[:, q_cols:], w_in[lanes, q_cols:], NT)
        part_other[:, lanes] = back.astype(bf16)
        gain_rows[0:1, lanes] += jnp.sum(back * (part[:, lanes].astype(f32) * scale), axis=0, keepdims=True)
    gain_copy = remote(gain_rows.at[pl.ds(0, 8)], gain_other, across, x_send.at[2], x_recv.at[2])
    gain_copy.start()
    part2_copy = remote(part_other, part2_other, across, x_send.at[3], x_recv.at[3])
    part2_copy.start()
    middle_back_copy = load(back_middle, mid, 18)
    middle_back_copy.start()
    product(
        t_key, lambda lanes: lhs[1, :, lanes], lambda start, left: dot(left, cot[:, q_cols : q_cols + TILE], TN).astype(bf16)
    )
    gain_copy.wait_recv()
    gain_copy.wait_send()
    gain_rows[0:1, :] += gain_other[0:1, :]
    gain_columns[...] = gain_rows[...].T

    def times_last(start, left):
        some = dot(left, cot[:, q_cols + TILE :], TN)
        gains = gain_columns[pl.ds(start, section), :]
        spare = jnp.zeros((section, TILE - tail - LANES), f32)
        return jnp.concatenate([some, gains, spare], axis=1).astype(bf16)

    meet_core(t_key)
    product(t_last, lambda lanes: lhs[1, :, lanes], times_last)
    send_far(t_key)
    meet_core(t_last)
    send_far(t_last)

    def drain(n, unused):
        tick(n)
        return unused

    lax.fori_loop(11, TILES, drain, 0)


    result_copy.wait()
    part2_copy.wait()
    other_copy = load(part2_other, lhs.at[0], 19)
    other_copy.start()
    middle_back_copy.wait()
    other_copy.wait()

    def token_rows(i, unused):
        here = pl.ds(pl.multiple_of(i * few, few), few)
        field = part[here, :].astype(f32)
        scale = lax.rsqrt(jnp.mean(field * field, axis=1, keepdims=True) + epsilon)
        unit = field * scale
        back = part_other[here, :].astype(f32) + lhs[0, here, :].astype(f32)
        inner = back * gain_ref[0:1, :]
        out = mid[here, :] + scale * (
            inner - unit * jnp.mean(inner * unit, axis=1, keepdims=True)
        )
        part_other[here, :] = out.astype(bf16)
        return unused

    lax.fori_loop(0, rows // few, token_rows, 0)
    token_copy = load(part_other, token_ref, 20)
    token_copy.start()
    lax.fori_loop(TILES, TILES + 5, drain, 0)

    for t in (TILES - 2, TILES - 1):
        core_copy(jnp.int32(t)).wait_send()

    def far_done(t, unused):
        far_copy(t).wait_send()
        return unused

    lax.fori_loop(0, TILES, far_done, 0)
    for s in range(ctxs - 1):
        kv_copy(s).wait_send()
    part_copy.wait_send()
    feed_copy.wait_send()
    token_copy.wait()


def back_all(part, feed, cotangent, middle, gains, act, mid_normed, x, normed, low, queries, kv, att, sums, qi, ki, cosine, sine, weights, ctxs):
    rows, width = x.shape
    q_cols = queries.shape[1]
    groups = kv.shape[2] // (2 * HEAD_SIZE)
    ratio = q_cols // (groups * HEAD_SIZE)
    tiles, lanes = dense_shapes(rows, groups, ratio)
    section = width // 4
    piece = section // ctxs
    vmem, hbm = pl.BlockSpec(memory_space=pltpu.VMEM), pl.BlockSpec(memory_space=pl.ANY)
    full = jax.ShapeDtypeStruct((rows, width), bf16)
    sems = lambda *n: pltpu.SemaphoreType.DMA(n)
    space = lambda *shape: pltpu.VMEM(shape, bf16)
    wide = lambda *shape: pltpu.VMEM(shape, f32)
    pairs = (rows // SIDE) * (rows // SIDE + 1) // 2
    return pl.pallas_call(
        back_kernel,
        in_specs=[hbm] * 4 + [vmem] + [hbm] * 14,
        out_specs=[hbm] * 5 + [vmem] + [hbm] * 2,
        out_shape=[
            full,
            jax.ShapeDtypeStruct((rows, width), f32),
            full,
            full,
            full,
            jax.ShapeDtypeStruct((TILES, piece, TILE), f32),
            jax.ShapeDtypeStruct((TILES, 2 * section, TILE), bf16),
            jax.ShapeDtypeStruct((TILES, section, TILE), bf16),
        ],
        scratch_shapes=[pltpu.VMEM(part_in.shape, part_in.dtype) for part_in in (low, queries, kv, att, sums, qi, ki, cosine, sine)]
        + [
            space(2, rows, width), wide(rows, width), space(rows, width), space(rows, width),
            space(width, q_cols), space(width, 2 * q_cols), space(2, rows, TILE),
            space(tiles, lanes, HEAD_SIZE), space(tiles, HEAD_SIZE, lanes),
            space(tiles, lanes, HEAD_SIZE), space(tiles, HEAD_SIZE, lanes),
            wide(tiles, 1, lanes), wide(pairs, SIDE, lanes), wide(tiles, HEAD_SIZE, lanes),
            space(ctxs, rows, q_cols), space(ctxs - 1, rows, q_cols), space(rows, 2 * q_cols),
            wide(LANES, width), wide(8, width), wide(width, LANES),
            space(2, 2 * section, TILE), space(2, 2 * section, TILE), space(4, 2 * section, TILE),
            space(2, 2 * section, TILE), space(SLOTS, section, TILE), space(2, section, TILE),
            space(TILES, (ctxs - 1) * piece, TILE),
            sems(30), sems(FEED_TILES), sems(4), sems(4), sems(TILES), sems(TILES),
            pltpu.SemaphoreType.REGULAR, sems(TILES), sems(TILES), sems(TILES), sems(TILES, 2),
            sems(TILES, 2), sems(TILES, 2), sems(ctxs - 1), sems(ctxs - 1),
        ],
        compiler_params=pltpu.CompilerParams(
            vmem_limit_bytes=63 * MIB, collective_id=1, has_side_effects=True
        ),
        cost_estimate=cost(4e10, 1e8),
        name="back_all",
    )(part, feed, cotangent, middle, gains, act, mid_normed, x, normed, low, queries, kv, att, sums, qi, ki, cosine, sine, weights)


def output_kernel(a_ref, w_ref, o_ref):
    o_ref[...] = dot(a_ref[...], w_ref[...], NT).astype(bf16)


def output_product(attended, weights, column, features):
    rows, inner = attended.shape
    return pl.pallas_call(
        output_kernel,
        grid=(2,),
        in_specs=[
            whole(attended.shape),
            pl.BlockSpec((features // 2, inner), lambda j: (j, column)),
        ],
        out_specs=pl.BlockSpec((rows, features // 2), lambda j: (0, j)),
        out_shape=jax.ShapeDtypeStruct((rows, features), bf16),
        compiler_params=params(40),
        cost_estimate=cost(2 * rows * inner * features, 2 * inner * features),
        name="output_product",
    )(attended, weights)


def feed_kernel(
    normed_ref, cot_ref, gate_ref, up_ref, down_ref,
    act_ref, back_ref, feed_ref, total_ref, feed_total,
):
    step = pl.program_id(0)
    gate = dot(normed_ref[...], gate_ref[...], NN)
    upward = dot(normed_ref[...], up_ref[...], NN)
    back_mixed = dot(cot_ref[...], down_ref[...], NN)
    sigmoid = 1.0 / (1.0 + jnp.exp(-gate))
    activated = gate * sigmoid
    mixed = (activated * upward).astype(bf16)
    back_gate = (back_mixed * upward * sigmoid * (1.0 + gate * (1.0 - sigmoid))).astype(bf16)
    back_up = (back_mixed * activated).astype(bf16)
    act_ref[0] = back_gate
    act_ref[1] = back_up
    act_ref[2] = mixed
    part = dot(back_gate, gate_ref[...], NT) + dot(back_up, up_ref[...], NT)
    feed = dot(mixed, down_ref[...], NT)

    @pl.when(step == 0)
    def _():
        total_ref[...] = part
        feed_total[...] = feed

    @pl.when(step > 0)
    def _():
        total_ref[...] += part
        feed_total[...] += feed

    @pl.when(step == pl.num_programs(0) - 1)
    def _():
        back_ref[...] = total_ref[...].astype(bf16)
        feed_ref[...] = feed_total[...].astype(bf16)


def feed_forward(normed, cotangent, gate, up, down):
    rows, width = normed.shape
    hidden = gate.shape[1]
    steps = hidden // FEED_TILE
    tile_of = pl.BlockSpec((width, FEED_TILE), lambda j: (0, j))
    acts_of = pl.BlockSpec((3, rows, FEED_TILE), lambda j: (0, 0, j))
    full = whole((rows, width))
    return pl.pallas_call(
        feed_kernel,
        grid=(steps,),
        in_specs=[full, full] + [tile_of] * 3,
        out_specs=[acts_of, full, full],
        out_shape=[
            jax.ShapeDtypeStruct((3, rows, hidden), bf16),
            jax.ShapeDtypeStruct((rows, width), bf16),
            jax.ShapeDtypeStruct((rows, width), bf16),
        ],
        scratch_shapes=[pltpu.VMEM((rows, width), f32)] * 2,
        compiler_params=params(56),
        cost_estimate=cost(12 * rows * width * hidden, 6 * width * hidden),
        name="feed_forward",
    )(normed, cotangent, gate, up, down)


def middle_kernel(cot_ref, mine_ref, other_ref, middle_ref, gain_ref, w_ref, bm_ref, bb_ref, ba_ref, grad_ref):
    middle = middle_ref[...]
    scale = lax.rsqrt(jnp.mean(middle * middle, axis=1, keepdims=True) + epsilon)
    unit = middle * scale
    back = mine_ref[...].astype(f32) + other_ref[...].astype(f32)
    grad_ref[...] = jnp.sum(back * unit, axis=0, keepdims=True)
    inner = back * gain_ref[1:2, :]
    out = cot_ref[...].astype(f32) + scale * (
        inner - unit * jnp.mean(inner * unit, axis=1, keepdims=True)
    )
    bm_ref[...] = out
    low = out.astype(bf16)
    bb_ref[...] = low
    ba_ref[...] = dot(low, w_ref[...], NN).astype(bf16)


def middle_back(cotangent, mine, other, middle, gains, weights, column, inner):
    rows, width = middle.shape
    full = whole((rows, width))
    return pl.pallas_call(
        middle_kernel,
        grid=(1,),
        in_specs=[full, full, full, full, whole(gains.shape)]
        + [pl.BlockSpec((width, inner), lambda j: (0, column))],
        out_specs=[full, full, whole((rows, inner)), whole((1, width))],
        out_shape=[
            jax.ShapeDtypeStruct((rows, width), f32),
            jax.ShapeDtypeStruct((rows, width), bf16),
            jax.ShapeDtypeStruct((rows, inner), bf16),
            jax.ShapeDtypeStruct((1, width), f32),
        ],
        compiler_params=params(56),
        cost_estimate=cost(2 * rows * width * inner, 1.5e7),
        name="middle_back",
    )(cotangent, mine, other, middle, gains, weights)


def inputs_kernel(count, x_ref, qc_ref, cos_ref, sin_ref, w_ref, *refs):
    parts = refs[:count]
    cot_ref, back_ref, grad_ref = refs[count:]
    half = qc_ref.shape[1] // 2
    cot_ref[:, : 2 * half] = qc_ref[...]
    total = parts[0][...].astype(f32)
    for part in parts[1:]:
        total += part[...].astype(f32)
    for h in range(half // HEAD_SIZE):
        lanes = slice(h * HEAD_SIZE, (h + 1) * HEAD_SIZE)
        there = slice(2 * half + h * HEAD_SIZE, 2 * half + (h + 1) * HEAD_SIZE)
        cot_ref[:, there] = turned(total[:, lanes], cos_ref[...], sin_ref[...], -1).astype(bf16)
    cot_ref[:, 3 * half :] = total[:, half:].astype(bf16)
    back = dot(cot_ref[...], w_ref[...], NT)
    back_ref[...] = back.astype(bf16)
    x = x_ref[...].astype(f32)
    unit = x * lax.rsqrt(jnp.mean(x * x, axis=1, keepdims=True) + epsilon)
    grad_ref[...] = jnp.sum(back * unit, axis=0, keepdims=True)


def inputs_back(x, qc, cosine, sine, weights, parts):
    rows, width = x.shape
    inner = 2 * qc.shape[1]
    full = whole((rows, width))
    return pl.pallas_call(
        functools.partial(inputs_kernel, len(parts)),
        grid=(1,),
        in_specs=[full, whole(qc.shape), whole(cosine.shape), whole(sine.shape)]
        + [pl.BlockSpec((width, inner), lambda j: (0, 0))]
        + [whole(parts[0].shape)] * len(parts),
        out_specs=[whole((rows, inner)), full, whole((1, width))],
        out_shape=[
            jax.ShapeDtypeStruct((rows, inner), bf16),
            jax.ShapeDtypeStruct((rows, width), bf16),
            jax.ShapeDtypeStruct((1, width), f32),
        ],
        compiler_params=params(56),
        cost_estimate=cost(2 * rows * width * inner, 1.5e7),
        name="inputs_back",
    )(x, qc, cosine, sine, weights, *parts)


def final_kernel(bm_ref, mine_ref, other_ref, x_ref, gain_ref, o_ref):
    x = x_ref[...].astype(f32)
    scale = lax.rsqrt(jnp.mean(x * x, axis=1, keepdims=True) + epsilon)
    unit = x * scale
    inner = (mine_ref[...].astype(f32) + other_ref[...].astype(f32)) * gain_ref[0:1, :]
    out = bm_ref[...] + scale * (inner - unit * jnp.mean(inner * unit, axis=1, keepdims=True))
    o_ref[...] = out.astype(bf16)


def final_back(back_middle, mine, other, x, gains):
    rows, width = x.shape
    block = pl.BlockSpec((rows // 4, width), lambda j: (j, 0))
    return pl.pallas_call(
        final_kernel,
        grid=(4,),
        in_specs=[block] * 4 + [whole(gains.shape)],
        out_specs=block,
        out_shape=jax.ShapeDtypeStruct((rows, width), bf16),
        compiler_params=params(40),
        cost_estimate=cost(1e6, 1e7),
        name="final_back",
    )(back_middle, mine, other, x, gains)


def relative(field, pairs, ctxs):
    dp, ctx = lax.axis_index("dp"), lax.axis_index("ctx")
    shaped = field.reshape((pairs, 2, ctxs, -1) + field.shape[1:])
    for axis, shift in ((0, dp // 2 + 1), (1, dp % 2 + 1), (2, ctx + 1)):
        shaped = jnp.roll(shaped, -shift, axis)
    return shaped.swapaxes(0, 1).reshape(field.shape)


def gradient_kernel(pairs, ctxs, place, a_ref, b_ref, send_ref, keep_ref):
    width = a_ref.shape[1]
    section = width // (2 * pairs)
    piece = section // ctxs
    for c, out in ((1, send_ref), (0, keep_ref)):
        for y in range(pairs):
            pair = lax.rem(place[0] + y + 1, pairs)
            core = lax.rem(place[1] + c, 2)
            lanes = pl.ds(pl.multiple_of((pair * 2 + core) * section, LANES), section)
            result = dot(a_ref[:, lanes], b_ref[...], TN).astype(bf16)
            for z in range(ctxs):
                far = lax.rem(z + ctxs - place[2] - 1 + ctxs, ctxs)
                rows = pl.ds(pl.multiple_of(y * section + far * piece, piece), piece)
                out[rows, :] = result[z * piece : (z + 1) * piece]


def gradient(a, b, pairs, ctxs):
    rows, width = a.shape
    columns = b.shape[1]
    section = width // (2 * pairs)
    if section % LANES or (section // ctxs) % 32:
        ordered = relative(dot(a, b, TN).astype(bf16), pairs, ctxs)
        return ordered[: width // 2], ordered[width // 2 :]
    dp, ctx = lax.axis_index("dp"), lax.axis_index("ctx")
    place = jnp.stack([dp // 2, dp % 2, ctx]).astype(jnp.int32)
    tile = TILE if columns % TILE == 0 else columns // 2
    block = pl.BlockSpec((width // 2, tile), lambda j: (0, j))
    return pl.pallas_call(
        functools.partial(gradient_kernel, pairs, ctxs),
        grid=(columns // tile,),
        in_specs=[SCALARS, whole(a.shape), pl.BlockSpec((rows, tile), lambda j: (0, j))],
        out_specs=[block, block],
        out_shape=[jax.ShapeDtypeStruct((width // 2, columns), bf16)] * 2,
        compiler_params=params(40),
        cost_estimate=cost(2 * rows * width * columns, 2 * width * columns),
        name="gradient",
    )(place, a, b)


def shifted(field, axis, steps, stride=1):
    count = lax.axis_size(axis)
    return lax.ppermute(
        field, axis, [(i, (i + steps * stride) % count) for i in range(count)]
    )


def other_core(field):
    return lax.ppermute(field, "dp", [(i, i ^ 1) for i in range(lax.axis_size("dp"))])


def sum_to_owner(send, keep, pairs, ctxs):
    columns = send.shape[1]
    got = other_core(send).reshape(pairs, -1, columns)
    keep = keep.reshape(pairs, -1, columns)
    total = got[-1].astype(f32) + keep[-1].astype(f32)
    for y in range(1, pairs):
        part = (got[y - 1].astype(f32) + keep[y - 1].astype(f32)).astype(bf16)
        total = total + shifted(part, "dp", y, 2).astype(f32)
    total = total.reshape(ctxs, -1, columns)
    result = total[-1]
    for z in range(1, ctxs):
        result = result + shifted(total[z - 1].astype(bf16), "ctx", z).astype(f32)
    return result


def swapped(field):
    count = lax.axis_size("tp")
    return lax.ppermute(field, "tp", [(i, count - 1 - i) for i in range(count)])


def body(
    tokens,
    cotangent,
    lengths,
    block_order,
    pre_gain,
    query_weight,
    key_weight,
    value_weight,
    output_weight,
    mid_gain,
    gate_weight,
    up_weight,
    down_weight,
):
    ctxs = lax.axis_size("ctx")
    pairs = lax.axis_size("dp") // 2
    ctx = lax.axis_index("ctx")
    order = block_order[0]
    ends = jnp.cumsum(lengths[0]).astype(jnp.int32)
    starts = ends - lengths[0]
    place = jnp.stack([ctx]).astype(jnp.int32)
    q_cols = query_weight.shape[1]
    features = tokens.shape[1]

    gain_columns = jnp.pad(jnp.stack([pre_gain, mid_gain], axis=1), ((0, 0), (0, LANES - 2)))
    packed = (query_weight, key_weight, value_weight, gain_columns, output_weight)
    stream = streams(order, ctx)
    lows = jnp.max(jnp.where(starts[None, :] <= stream[0][:, None], starts[None, :], 0), axis=1)
    if pairs == 2 and ctxs == 4 and query_weight.shape[0] % 32 == 0:
        own = jnp.stack([stream[0], lows])
        qi = jnp.concatenate([own, stream, jnp.zeros_like(own)], axis=0)
        (
            first, gate_full, up_full, down_full, queries, kv, normed, gains,
            attended_low, att, sums, middle, mid_normed, cosine, sine, ki,
        ) = forward_all(
            packed, gate_weight, up_weight, down_weight, tokens, frequencies(), qi, q_cols, ctxs
        )
        act, back_part, feed = feed_forward(mid_normed, cotangent, gate_full, up_full, down_full)
        _, _, _, result, token_gradient, grads, _, _ = back_all(
            back_part, feed, cotangent, middle, gains, act, mid_normed, tokens, normed,
            attended_low, queries, kv, att, sums, qi, ki, cosine, sine, first, ctxs,
        )
        wide = lambda *tiles: jnp.concatenate([grads[t] for t in tiles], axis=1)
        tail = q_cols - TILE
        qkv_gradient = jnp.concatenate(
            [grads[13], grads[14][:, :tail], grads[15], grads[16][:, :tail]], axis=1
        )
        output_gradient = jnp.concatenate([grads[12], grads[14][:, tail:]], axis=1)
        gain_sums = grads[16][:, tail : tail + LANES]
        gate_gradient, up_gradient = wide(0, 1, 2, 3), wide(4, 5, 6, 7)
        down_gradient = wide(8, 9, 10, 11)
    else:
        first, gate_full, up_full, down_full = (
            lax.all_gather(field, ROWS, axis=0, tiled=True)
            for field in (jnp.concatenate(packed, axis=1), gate_weight, up_weight, down_weight)
        )
        cosine, sine = angles(stream[0] - lows)
        gains = first[:, 2 * q_cols : 2 * q_cols + 8].T.astype(f32)
        queries, kv, normed = project(tokens, gains, cosine, sine, first, q_cols)
        pieces = [kv] + [shifted(kv, "ctx", k) for k in range(1, ctxs)]
        output_weights = first[:, 2 * q_cols + LANES :]
        attended_low, att, sums = attend(order, starts, place, queries, pieces)
        branch = output_product(attended_low, output_weights, 0, features)
        middle = tokens.astype(f32) + (branch.astype(f32) + swapped(branch).astype(f32))
        mid_scale = lax.rsqrt(jnp.mean(middle * middle, axis=1, keepdims=True) + epsilon)
        mid_normed = (middle * mid_scale * gains[1:2]).astype(bf16)
        act, back_part, feed = feed_forward(mid_normed, cotangent, gate_full, up_full, down_full)
        back_other = swapped(back_part)
        gate_parts = gradient(mid_normed, act[0], pairs, ctxs)
        up_parts = gradient(mid_normed, act[1], pairs, ctxs)
        down_parts = gradient(cotangent, act[2], pairs, ctxs)
        result = (middle + feed.astype(f32) + swapped(feed).astype(f32)).astype(bf16)

        back_middle, back_branch, back_attended, mid_grad = middle_back(
            cotangent, back_part, back_other, middle, gains, output_weights, 0, q_cols
        )
        output_parts = gradient(back_branch, attended_low, pairs, ctxs)
        back = attend_back(
            order, starts, place, queries, back_attended, att, sums, cosine, sine, pieces
        )
        own_parts = [back[1]] + [shifted(back[1 + k], "ctx", -k) for k in range(1, ctxs)]
        cot, normed_part, pre_grad = inputs_back(
            tokens, back[0], cosine, sine, first, own_parts
        )
        normed_other = swapped(normed_part)
        qkv_parts = gradient(normed, cot, pairs, ctxs)
        token_gradient = final_back(back_middle, normed_part, normed_other, tokens, gains)

        mid_once = jnp.where(lax.axis_index("tp") == 0, mid_grad, 0.0)
        pair = jnp.concatenate([pre_grad, mid_once], axis=0).astype(bf16)
        pair = jnp.pad(pair, ((0, 6), (0, 0))).T
        ordered = relative(pair, pairs, ctxs)
        gain_sums = sum_to_owner(
            ordered[: features // 2], ordered[features // 2 :], pairs, ctxs
        )
        gain_sums = gain_sums + swapped(gain_sums)
        gate_gradient = sum_to_owner(*gate_parts, pairs, ctxs)
        up_gradient = sum_to_owner(*up_parts, pairs, ctxs)
        down_gradient = sum_to_owner(*down_parts, pairs, ctxs)
        output_gradient = sum_to_owner(*output_parts, pairs, ctxs)
        qkv_gradient = sum_to_owner(*qkv_parts, pairs, ctxs)
    return (
        result,
        token_gradient,
        gain_sums[:, 0],
        qkv_gradient[:, :q_cols],
        qkv_gradient[:, q_cols : q_cols + q_cols // 2],
        qkv_gradient[:, q_cols + q_cols // 2 :],
        output_gradient,
        gain_sums[:, 1],
        gate_gradient,
        up_gradient,
        down_gradient,
    )


def solution(mesh):
    rows, split = P(ROWS, None), P(ROWS, "tp")
    return jax.shard_map(
        body,
        mesh=mesh,
        in_specs=(rows, rows, P("dp", None), P("dp", None, None), P(ROWS))
        + (split,) * 4
        + (P(ROWS),)
        + (split,) * 3,
        out_specs=(rows, rows, P(ROWS)) + (split,) * 4 + (P(ROWS),) + (split,) * 3,
        check_vma=False,
    )
```
